32 devices in a mesh: tm: 16 (over z, y, core), row: 2 (over x).
Axes of the slice: x: 2, y: 2, z: 4, core: 2. Of those that a mesh axis runs over, the one named last changes fastest.
Arguments:
- normals: float32 [16, 32, 1024], P('tm', None, 'row'), may hold values from -6 to 6
- inv_diag: float32 [16, 4, 256, 256], P('tm', 'row'), may hold values from -0.4 to 1.4, as said below
- lag_coupling: float32 [16, 4, 512, 256], P('tm', 'row'), may hold values from -0.25 to 0.25
- fill_mask: int32 [16, 4, 3], P('tm', 'row'), may hold values 0 or 1
Outputs:
- posterior: float32 [16, 32, 1024], P('tm', None, 'row')
The draws below stay inside these ranges and needn't reach their ends.
Inputs may be any that keep to these rules, and one draw needn't show every extreme that they name: inv_diag[t, i] is the transposed inverse of the diagonal block of the factor for time t and spatial block i.
All inputs are finite; a program needn't handle non-finite values. No bound on the sum of `fill_mask` on one device may be relied on, other than what follows from the above.
Results may differ from the reference program's by a relative error of at most 0.00025.
Values sent between devices are 32-bit elements; how exact they have to be, the bound alone decides.
No kernel may reach another device: no remote copies, remote signals or barrier semaphores. Data moves between devices by JAX's collectives and lax.ppermute only.
A program may use at most 64 MiB of HBM per device.

```python
import jax
import jax.numpy as jnp
from jax import lax

SB = 256
RIM = 128
NC = 32
TIMES = 16
NBLK = 4
SITES = 1024


def draw_inv_diag(key, part):
    shape = (TIMES, NBLK, SB, SB)
    values = jax.random.truncated_normal(key, -4.0, 4.0, shape, jnp.float32) * (0.5 / SB ** 0.5)
    return values + jnp.eye(SB, dtype=jnp.float32)


def touch_ends(result, own_key, low, top_value):
    place = [jax.random.randint(jax.random.fold_in(own_key, axis), (), 0, length) for axis, length in enumerate(result.shape)]
    widest = result.shape.index(max(result.shape))
    next_to = place[:widest] + [(place[widest] + 1) % result.shape[widest]] + place[widest + 1:]
    return result.at[tuple(place)].set(low).at[tuple(next_to)].set(top_value)


def levels(key, shape, cuts, smallest, top_value):
    loudness = 1.0
    for dim, parts in cuts:
        heights = jax.random.uniform(jax.random.fold_in(jax.random.fold_in(key, 6), dim), (parts,), jnp.float32, smallest / len(cuts), top_value / len(cuts))
        loudness = loudness * jnp.repeat(jnp.exp(heights), shape[dim] // parts).reshape((-1,) + (1,) * (len(shape) - 1 - dim))
    return loudness


def bell_draw(stream_key, shape, scale, bound, pieces=(), kind=jnp.bfloat16):
    entries = scale * jax.random.normal(stream_key, shape, jnp.float32)
    if pieces:
        entries = entries * levels(stream_key, shape, pieces, -0.22, 0.18)
    return jnp.clip(entries, -bound, bound).astype(kind)


def setup_inputs(seed: int = 0) -> dict:
    arg_keys = jax.random.split(jax.random.key(seed), 5)
    return {
        "normals": bell_draw(arg_keys[0], (TIMES, NC, SITES), 1.0, 6.0, ((0, 16), (2, 2)), jnp.float32),
        "inv_diag": draw_inv_diag(jax.random.fold_in(arg_keys[4], 71), 0),
        "lag_coupling": bell_draw(arg_keys[2], (TIMES, NBLK, SB + 2 * RIM, SB), ((SB + 2 * RIM) * 11 // 10) ** -0.5, 0.25, ((0, 16), (1, 2)), jnp.float32),
        "fill_mask": touch_ends((jax.random.randint(arg_keys[3], (TIMES, NBLK, 3), 0, 4) < 3).astype(jnp.int32), jax.random.fold_in(arg_keys[3], 1), 0, 1),
    }


def rim_weights(fill_mask, block_len, rim_len):
    flags = fill_mask.astype(jnp.float32)
    return jnp.concatenate([jnp.repeat(flags[..., 0:1], rim_len, axis=-1), jnp.repeat(flags[..., 1:2], block_len, axis=-1), jnp.repeat(flags[..., 2:3], rim_len, axis=-1)], axis=-1)


def reference(normals, inv_diag, lag_coupling, fill_mask):
    columns = normals.shape[1]
    site_count = normals.shape[2]
    block_count = inv_diag.shape[1]
    block_len = inv_diag.shape[2]
    rim_len = (lag_coupling.shape[2] - block_len) // 2
    weights = rim_weights(fill_mask, block_len, rim_len)

    def backward(following, inputs):
        normals_now, inverse_now, lag_now, weight_now = inputs
        padded = jnp.pad(following, ((0, 0), (rim_len, rim_len)))
        windows = jnp.stack([padded[:, position * block_len: position * block_len + block_len + 2 * rim_len] for position in range(block_count)], axis=1)
        coupled = jnp.einsum("cbw,bwk->cbk", windows * weight_now[None], lag_now, precision=lax.Precision.HIGHEST)
        residue = normals_now.reshape(columns, block_count, block_len) - coupled
        solved = jnp.einsum("cbk,bkj->cbj", residue, inverse_now, precision=lax.Precision.HIGHEST)
        solved = solved.reshape(columns, site_count)
        return solved, solved

    start_field = jnp.zeros((columns, site_count), jnp.float32)
    _, fields = lax.scan(backward, start_field, (normals, inv_diag, lag_coupling, weights), reverse=True)
    return fields
```

```python
import functools

import jax
import jax.numpy as jnp
from jax import lax
from jax.experimental import pallas as pl
from jax.experimental.pallas import tpu as pltpu
from jax.sharding import PartitionSpec as P

BOTH = ("tm", "row")
VMEM = pl.BlockSpec(memory_space=pltpu.VMEM)
SMEM = pl.BlockSpec(memory_space=pltpu.SMEM)
PARAMS = pltpu.CompilerParams(vmem_limit_bytes=32 * 1024 * 1024)


def halves(value):
    high = value.astype(jnp.bfloat16)
    low = (value - high.astype(jnp.float32)).astype(jnp.bfloat16)
    return high, low


def dot(a, b):
    return jnp.dot(a, b, preferred_element_type=jnp.float32)


def stacked_dot(pair, cols, high, low):
    rows = pair.shape[0] // 2
    wide = dot(pair[:, cols], high)
    return wide[:rows] + wide[rows:] + dot(pair[:rows, cols], low)


def fuse_kernel(sides, place, mask, normals, inv, lag, own, rim):
    blocks, length = inv.shape[1], inv.shape[2]
    window = lag.shape[2]
    edge = (window - length) // 2
    cols = normals.shape[1]
    cuts = (0, edge, edge + length, window)
    for b in range(blocks):
        inv_high, inv_low = halves(inv[0, b])
        for part in range(3):
            lo, hi = cuts[part], cuts[part + 1]
            flag = mask[0, b, part].astype(jnp.float32)
            high, low = halves(lag[0, b, lo:hi] * flag)
            own[b * window + lo : b * window + hi] = (
                dot(high, inv_high) + dot(low, inv_high) + dot(high, inv_low)
            )
        high, low = halves(normals[0, :, b * length : (b + 1) * length])
        at = blocks * window + b * cols
        own[at : at + cols] = dot(high, inv_high) + dot(low, inv_high) + dot(high, inv_low)

    def put(slot, block, start):
        rim[slot, :window] = own[block * window : (block + 1) * window, start : start + edge]
        at = blocks * window + block * cols
        rim[slot, window:] = own[at : at + cols, start : start + edge]

    if sides == 1:
        pl.when(place[1] == 0)(lambda: put(0, blocks - 1, length - edge))
        pl.when(place[1] != 0)(lambda: put(0, 0, 0))
    else:
        put(0, blocks - 1, length - edge)
        put(1, 0, 0)


def split_kernel(far, rim, near, far_high, far_low, rim_high, rim_low, near_high, near_low):
    count = far_high.shape[0]
    far_high[...], far_low[...] = halves(far[:count])
    near_high[...], near_low[...] = halves(near[:count])
    for side in range(rim.shape[0]):
        rim_high[side], rim_low[side] = halves(rim[side, : rim_high.shape[1]])


def turn_kernel(
    mine, first, sides, blocks, window, place, own_in, halo_in, far, rim, near,
    far_high, far_low, rim_high, rim_low, near_high, near_low,
    _upper, _lower, _send, upper, lower, send, late, mid,
):
    length = far.shape[1]
    edge = (window - length) // 2
    cols, sites = lower.shape
    halo = length + edge

    @pl.when(place[0] == mine)
    def _():
        def keep(ref, start, value):
            width = value.shape[1]
            high, low = halves(value)
            ref[:cols, pl.ds(start, width)] = high
            ref[cols:, pl.ds(start, width)] = low

        def const(pack, b):
            at = blocks * window + b * cols
            return pack[at : at + cols]

        mid[...] = jnp.zeros_like(mid)
        if not first:
            late[...] = jnp.zeros_like(late)
            keep(late, halo, own_in[...])
        right = jnp.int32(1) - jnp.minimum(place[1], 1)
        for side in range(sides):
            on_right = right if sides == 1 else side
            if not first:
                keep(late, pl.multiple_of(on_right * (halo + sites), 128), halo_in[side])
            value = rim[side, window:]
            if not first:
                start = pl.multiple_of(on_right * (2 * halo + sites - window), 128)
                value -= stacked_dot(late, pl.ds(start, window), rim_high[side], rim_low[side])
            keep(mid, pl.multiple_of(on_right * (edge + sites), 128), value)
        for b in range(blocks):
            value = const(far, b)
            if not first:
                at = halo - edge + b * length
                value -= stacked_dot(
                    late, pl.ds(at, window),
                    far_high[b * window : (b + 1) * window], far_low[b * window : (b + 1) * window],
                )
            keep(mid, edge + b * length, value)
            upper[:, b * length : (b + 1) * length] = value
        for b in range(blocks):
            lower[:, b * length : (b + 1) * length] = const(near, b) - stacked_dot(
                mid, pl.ds(b * length, window),
                near_high[b * window : (b + 1) * window], near_low[b * window : (b + 1) * window],
            )
        if sides == 1:
            start = pl.multiple_of(right * (sites - halo), 128)
            send[0] = lower[:, pl.ds(start, halo)]
        else:
            send[0] = lower[:, sites - halo :]
            send[1] = lower[:, :halo]


def local(normals, inv_diag, lag_coupling, fill_mask):
    times, rows = lax.axis_size("tm"), lax.axis_size("row")
    device, row = lax.axis_index("tm"), lax.axis_index("row")
    cols, sites = normals.shape[1:]
    blocks, length = inv_diag.shape[1:3]
    window = lag_coupling.shape[2]
    edge = (window - length) // 2
    halo = length + edge
    sides = 1 if rows == 2 else 2
    pairs = times // 2
    f32, bf16 = jnp.float32, jnp.bfloat16
    shape = jax.ShapeDtypeStruct
    place = jnp.stack([jnp.where(device % 2 == 0, device // 2, -1), row]).astype(jnp.int32)

    def link(source, target):
        return [(s * rows + r, t * rows + r) for s, t in zip(source, target) for r in range(rows)]

    def cross(value, source, target):
        if sides == 1:
            perm = [(s * rows + r, t * rows + 1 - r) for s, t in zip(source, target) for r in range(2)]
            return lax.ppermute(value, BOTH, perm)
        moved = []
        for side, step in enumerate((1, -1)):
            perm = [
                (s * rows + r, t * rows + r + step)
                for s, t in zip(source, target)
                for r in range(rows)
                if 0 <= r + step < rows
            ]
            moved.append(lax.ppermute(value[side : side + 1], BOTH, perm))
        return jnp.concatenate(moved)

    height = blocks * (window + cols)
    near, edges = pl.pallas_call(
        functools.partial(fuse_kernel, sides),
        out_shape=(shape((height, length), f32), shape((sides, window + cols, edge), f32)),
        in_specs=[SMEM, SMEM, VMEM, VMEM, VMEM],
        out_specs=(VMEM, VMEM),
        compiler_params=PARAMS,
    )(place, fill_mask, normals, inv_diag, lag_coupling)
    odd, even = range(1, times, 2), range(0, times, 2)
    far = lax.ppermute(near, BOTH, link(odd, even))
    rim = cross(edges, odd, even)
    tall = blocks * window
    parts = pl.pallas_call(
        split_kernel,
        out_shape=(
            shape((tall, length), bf16), shape((tall, length), bf16),
            shape((sides, window, edge), bf16), shape((sides, window, edge), bf16),
            shape((tall, length), bf16), shape((tall, length), bf16),
        ),
        in_specs=[VMEM] * 3,
        out_specs=(VMEM,) * 6,
        compiler_params=PARAMS,
    )(far, rim, near)

    state = (
        jnp.zeros((cols, sites), f32), jnp.zeros((cols, sites), f32), jnp.zeros((sides, cols, halo), f32)
    )
    own_in, halo_in = state[0], state[2]
    for step in range(pairs):
        mine = pairs - 1 - step
        state = pl.pallas_call(
            functools.partial(turn_kernel, mine, step == 0, sides, blocks, window),
            out_shape=tuple(shape(s.shape, f32) for s in state),
            in_specs=[SMEM] + [VMEM] * 14,
            out_specs=(VMEM,) * 3,
            scratch_shapes=[
                pltpu.VMEM((2 * cols, sites + 2 * halo), bf16),
                pltpu.VMEM((2 * cols, sites + 2 * edge), bf16),
            ],
            input_output_aliases={12: 0, 13: 1, 14: 2},
            compiler_params=PARAMS,
        )(place, own_in, halo_in, far, rim, near, *parts, *state)
        if mine:
            source, target = [2 * mine], [2 * mine - 2]
            own_in = lax.ppermute(state[1], BOTH, link(source, target))
            halo_in = cross(state[2], source, target)
    returned = lax.ppermute(state[0], BOTH, link(even, odd))
    return jnp.where(device % 2 == 0, state[1], returned)[None]


def solution(mesh):
    placed = (
        P("tm", None, "row"),
        P("tm", "row", None, None),
        P("tm", "row", None, None),
        P("tm", "row", None),
    )
    return jax.shard_map(
        local, mesh=mesh, in_specs=placed, out_specs=P("tm", None, "row"), check_vma=False
    )
```

```python
import functools

import jax
import jax.numpy as jnp
from jax import lax
from jax.experimental import pallas as pl
from jax.experimental.pallas import tpu as pltpu
from jax.sharding import PartitionSpec as P

BOTH = ("tm", "row")
VMEM = pl.BlockSpec(memory_space=pltpu.VMEM)
HBM = pl.BlockSpec(memory_space=pltpu.HBM)
PARAMS = pltpu.CompilerParams(vmem_limit_bytes=32 * 1024 * 1024)


def halves(value):
    high = value.astype(jnp.bfloat16)
    low = (value - high.astype(jnp.float32)).astype(jnp.bfloat16)
    return high, low


def dot(a, b):
    return jnp.dot(a, b, preferred_element_type=jnp.float32)


def stacked_dot(pair, cols, high, low):
    rows = pair.shape[0] // 2
    wide = dot(pair[:, cols], high)
    return wide[:rows] + wide[rows:] + dot(pair[:rows, cols], low)


def triple(high, low, inv_high, inv_low):
    return dot(high, inv_high) + dot(low, inv_high) + dot(high, inv_low)


def put_rim(sides, rim, columns):
    if sides == 1:
        row = lax.axis_index("row")

        @pl.when(row == 0)
        def _():
            rim[0] = columns(True)

        @pl.when(row != 0)
        def _():
            rim[0] = columns(False)
    else:
        rim[0] = columns(True)
        rim[1] = columns(False)


def const_kernel(
    sides, edge, mask, normals, inv, lag, const, rim, inv_high, inv_low, lag_out, mask_out, normals_in, inv_in, sems
):
    blocks, length = inv.shape[1], inv.shape[2]
    sites = normals.shape[2]
    moves = [pltpu.make_async_copy(normals.at[0], normals_in, sems.at[0])]
    for b in range(blocks):
        moves.append(pltpu.make_async_copy(inv.at[0, b], inv_in.at[b], sems.at[1 + b]))
    for b in range(blocks):
        moves.append(pltpu.make_async_copy(lag.at[0, b], lag_out.at[b], sems.at[1 + blocks + b]))
    moves.append(pltpu.make_async_copy(mask.at[0], mask_out, sems.at[1 + 2 * blocks]))
    for move in moves:
        move.start()
    moves[0].wait()
    for b in range(blocks):
        at = slice(b * length, (b + 1) * length)
        high, low = halves(normals_in[:, at])
        moves[1 + b].wait()
        inv_high[b], inv_low[b] = halves(inv_in[b])
        const[:, at] = triple(high, low, inv_high[b], inv_low[b])
    put_rim(sides, rim, lambda last: const[:, sites - edge :] if last else const[:, :edge])
    for move in moves[1 + blocks :]:
        move.wait()


def fuse_kernel(mask, const, inv_high, inv_low, lag, own, near_high, near_low):
    blocks, window, length = lag.shape
    edge = (window - length) // 2
    cols = const.shape[0]
    cuts = (0, edge, edge + length, window)
    flags = mask[...].astype(jnp.float32)
    for b in range(blocks):
        at = blocks * window + b * cols
        own[at : at + cols] = const[:, b * length : (b + 1) * length]
        for part in range(3):
            lo, hi = cuts[part], cuts[part + 1]
            rows = slice(b * window + lo, b * window + hi)
            high, low = halves(lag[b, lo:hi] * flags[b : b + 1, part : part + 1])
            value = triple(high, low, inv_high[b], inv_low[b])
            own[rows] = value
            near_high[rows], near_low[rows] = halves(value)


def edge_kernel(sides, blocks, cols, _own, _first_far, _first_rim, own, rim):
    length, edge = own.shape[1], rim.shape[2]
    window = length + 2 * edge

    def columns(last):
        b = blocks - 1 if last else 0
        cut = slice(length - edge, length) if last else slice(0, edge)
        at = blocks * window + b * cols
        return jnp.concatenate([own[b * window : (b + 1) * window, cut], own[at : at + cols, cut]])

    put_rim(sides, rim, columns)


def split_kernel(far, rim, far_high, far_low, rim_high, rim_low):
    far_high[...], far_low[...] = halves(far[: far_high.shape[0]])
    for side in range(rim.shape[0]):
        rim_high[side], rim_low[side] = halves(rim[side, : rim_high.shape[1]])


def turn_kernel(mine, sides, far_rows, rim_rows, next_in, own_in, far, rim, const, near_high, near_low, *rest):
    parts, (_upper, _lower, upper, lower, late, mid) = rest[:-6], rest[-6:]
    first = not parts
    cols, sites = lower.shape
    length = near_high.shape[1]
    blocks = sites // length
    window = near_high.shape[0] // blocks
    edge = (window - length) // 2
    halo = length + edge

    @pl.when(lax.axis_index("tm") == 2 * mine)
    def _():
        def keep(ref, start, value):
            width = value.shape[1]
            high, low = halves(value)
            ref[:cols, pl.ds(start, width)] = high
            ref[cols:, pl.ds(start, width)] = low

        mid[...] = jnp.zeros_like(mid)
        if not first:
            far_high, far_low, rim_high, rim_low = parts
            late[...] = jnp.zeros_like(late)
            keep(late, halo, own_in[...])
        right = jnp.int32(1) - lax.axis_index("row").astype(jnp.int32)
        for side in range(sides):
            on_right = right if sides == 1 else side
            if not first:
                start = pl.multiple_of((1 - on_right) * (sites - halo), 128)
                value = next_in[side, :, pl.ds(start, halo)]
                keep(late, pl.multiple_of(on_right * (halo + sites), 128), value)
            value = rim[side, rim_rows : rim_rows + cols]
            if not first:
                start = pl.multiple_of(on_right * (2 * halo + sites - window), 128)
                value -= stacked_dot(late, pl.ds(start, window), rim_high[side], rim_low[side])
            keep(mid, pl.multiple_of(on_right * (edge + sites), 128), value)
        for b in range(blocks):
            if first:
                value = far[:, b * length : (b + 1) * length]
            else:
                value = far[far_rows + b * cols : far_rows + (b + 1) * cols]
                at = halo - edge + b * length
                value -= stacked_dot(
                    late, pl.ds(at, window),
                    far_high[b * window : (b + 1) * window], far_low[b * window : (b + 1) * window],
                )
            keep(mid, edge + b * length, value)
            upper[:, b * length : (b + 1) * length] = value
        for b in range(blocks):
            lower[:, b * length : (b + 1) * length] = const[:, b * length : (b + 1) * length] - stacked_dot(
                mid, pl.ds(b * length, window),
                near_high[b * window : (b + 1) * window], near_low[b * window : (b + 1) * window],
            )


def local(normals, inv_diag, lag_coupling, fill_mask):
    times, rows = lax.axis_size("tm"), lax.axis_size("row")
    device = lax.axis_index("tm")
    cols, sites = normals.shape[1:]
    blocks, length = inv_diag.shape[1:3]
    window = lag_coupling.shape[2]
    edge = (window - length) // 2
    halo = length + edge
    sides = 1 if rows == 2 else 2
    pairs = times // 2
    f32, bf16 = jnp.float32, jnp.bfloat16
    shape = jax.ShapeDtypeStruct

    def link(source, target):
        return [(s * rows + r, t * rows + r) for s, t in zip(source, target) for r in range(rows)]

    def cross(value, source, target):
        if sides == 1:
            perm = [(s * rows + r, t * rows + 1 - r) for s, t in zip(source, target) for r in range(2)]
            return lax.ppermute(value, BOTH, perm)
        moved = []
        for side, step in enumerate((1, -1)):
            perm = [
                (s * rows + r, t * rows + r + step)
                for s, t in zip(source, target)
                for r in range(rows)
                if 0 <= r + step < rows
            ]
            moved.append(lax.ppermute(value[side : side + 1] if value.shape[0] > 1 else value, BOTH, perm))
        return jnp.concatenate(moved)

    tall = blocks * window
    const, const_rim, inv_high, inv_low, lag, mask = pl.pallas_call(
        functools.partial(const_kernel, sides, edge),
        out_shape=(
            shape((cols, sites), f32), shape((sides, cols, edge), f32),
            shape((blocks, length, length), bf16), shape((blocks, length, length), bf16),
            shape(lag_coupling.shape[1:], f32), shape(fill_mask.shape[1:], fill_mask.dtype),
        ),
        in_specs=[HBM] * 4,
        out_specs=(VMEM,) * 6,
        scratch_shapes=[
            pltpu.VMEM(normals.shape[1:], f32),
            pltpu.VMEM(inv_diag.shape[1:], f32),
            pltpu.SemaphoreType.DMA((2 + 2 * blocks,)),
        ],
        compiler_params=PARAMS,
    )(*[pltpu.with_memory_space_constraint(a, pltpu.HBM) for a in (fill_mask, normals, inv_diag, lag_coupling)])
    odd, even = range(1, times, 2), range(0, times, 2)
    first_rim = cross(const_rim, odd[-1:], even[-1:])
    first_far = lax.ppermute(const, BOTH, link(odd[-1:], even[-1:]))
    near, near_high, near_low = pl.pallas_call(
        fuse_kernel,
        out_shape=(
            shape((tall + blocks * cols, length), f32), shape((tall, length), bf16), shape((tall, length), bf16),
        ),
        in_specs=[VMEM] * 5,
        out_specs=(VMEM,) * 3,
        compiler_params=PARAMS,
        cost_estimate=pl.CostEstimate(
            flops=6 * (tall + cols * blocks) * length * length, bytes_accessed=16 * tall * length, transcendentals=0
        ),
    )(mask, const, inv_high, inv_low, lag)
    near, edges = pl.pallas_call(
        functools.partial(edge_kernel, sides, blocks, cols),
        out_shape=(shape(near.shape, f32), shape((sides, window + cols, edge), f32)),
        in_specs=[VMEM] * 3,
        out_specs=(VMEM,) * 2,
        input_output_aliases={0: 0},
        compiler_params=PARAMS,
    )(near, first_far, first_rim)
    rim = cross(edges, odd[:-1], even[:-1])
    far = lax.ppermute(near, BOTH, link(odd[:-1], even[:-1]))
    parts = pl.pallas_call(
        split_kernel,
        out_shape=(
            shape((tall, length), bf16), shape((tall, length), bf16),
            shape((sides, window, edge), bf16), shape((sides, window, edge), bf16),
        ),
        in_specs=[VMEM] * 2,
        out_specs=(VMEM,) * 4,
        compiler_params=PARAMS,
    )(far, rim)

    state = (jnp.zeros((cols, sites), f32), jnp.zeros((cols, sites), f32))
    own_in, next_in = state[0], jnp.zeros((sides, cols, sites), f32)
    for step in range(pairs):
        mine = pairs - 1 - step
        if step == 0:
            given = (next_in, own_in, first_far, first_rim, const, near_high, near_low)
            starts = (None, 0)
        else:
            given = (next_in, own_in, far, rim, const, near_high, near_low, *parts)
            starts = (tall, window)
        state = pl.pallas_call(
            functools.partial(turn_kernel, mine, sides, *starts),
            out_shape=tuple(shape(s.shape, f32) for s in state),
            in_specs=[VMEM] * (len(given) + len(state)),
            out_specs=(VMEM,) * 2,
            scratch_shapes=[
                pltpu.VMEM((2 * cols, sites + 2 * halo), bf16),
                pltpu.VMEM((2 * cols, sites + 2 * edge), bf16),
            ],
            input_output_aliases={len(given) + i: i for i in range(2)},
            compiler_params=PARAMS,
        )(*given, *state)
        if mine:
            source, target = [2 * mine], [2 * mine - 2]
            next_in = cross(state[1][None], source, target)
            own_in = lax.ppermute(state[1], BOTH, link(source, target))
    returned = lax.ppermute(state[0], BOTH, link(even, odd))
    return jnp.where(device % 2 == 0, state[1], returned)[None]


def solution(mesh):
    placed = (
        P("tm", None, "row"),
        P("tm", "row", None, None),
        P("tm", "row", None, None),
        P("tm", "row", None),
    )
    return jax.shard_map(
        local, mesh=mesh, in_specs=placed, out_specs=P("tm", None, "row"), check_vma=False
    )
```

```python
import functools

import jax
import jax.numpy as jnp
from jax import lax
from jax.experimental import pallas as pl
from jax.experimental.pallas import tpu as pltpu
from jax.sharding import PartitionSpec as P

BOTH = ("tm", "row")
VMEM = pl.BlockSpec(memory_space=pltpu.VMEM)
HBM = pl.BlockSpec(memory_space=pltpu.HBM)
PARAMS = pltpu.CompilerParams(vmem_limit_bytes=32 * 1024 * 1024)


def halves(value):
    high = value.astype(jnp.bfloat16)
    low = (value - high.astype(jnp.float32)).astype(jnp.bfloat16)
    return high, low


def dot(a, b):
    return jnp.dot(a, b, preferred_element_type=jnp.float32)


def stacked_dot(pair, cols, high, low):
    rows = pair.shape[0] // 2
    wide = dot(pair[:, cols], high)
    return wide[:rows] + wide[rows:] + dot(pair[:rows, cols], low)


def triple(high, low, inv_high, inv_low):
    return dot(high, inv_high) + dot(low, inv_high) + dot(high, inv_low)


def put_rim(sides, rim, columns):
    if sides == 1:
        row = lax.axis_index("row")

        @pl.when(row == 0)
        def _():
            rim[0] = columns(True)

        @pl.when(row != 0)
        def _():
            rim[0] = columns(False)
    else:
        rim[0] = columns(True)
        rim[1] = columns(False)


def const_kernel(
    mask, normals, inv, lag, const, inv_high, inv_low, lag_out, mask_out, normals_in, inv_in, sems
):
    blocks, length = inv.shape[1], inv.shape[2]
    moves = [pltpu.make_async_copy(normals.at[0], normals_in, sems.at[0])]
    for b in range(blocks):
        moves.append(pltpu.make_async_copy(inv.at[0, b], inv_in.at[b], sems.at[1 + b]))
    for b in range(blocks):
        moves.append(pltpu.make_async_copy(lag.at[0, b], lag_out.at[b], sems.at[1 + blocks + b]))
    moves.append(pltpu.make_async_copy(mask.at[0], mask_out, sems.at[1 + 2 * blocks]))
    for move in moves:
        move.start()
    moves[0].wait()
    for b in range(blocks):
        at = slice(b * length, (b + 1) * length)
        high, low = halves(normals_in[:, at])
        moves[1 + b].wait()
        inv_high[b], inv_low[b] = halves(inv_in[b])
        const[:, at] = triple(high, low, inv_high[b], inv_low[b])
    for move in moves[1 + blocks :]:
        move.wait()


def fuse_kernel(mask, const, inv_high, inv_low, lag, own, near_high, near_low):
    blocks, window, length = lag.shape
    edge = (window - length) // 2
    cols = const.shape[0]
    cuts = (0, edge, edge + length, window)
    flags = mask[...].astype(jnp.float32)
    for b in range(blocks):
        at = blocks * window + b * cols
        own[at : at + cols] = const[:, b * length : (b + 1) * length]
        for part in range(3):
            lo, hi = cuts[part], cuts[part + 1]
            rows = slice(b * window + lo, b * window + hi)
            high, low = halves(lag[b, lo:hi] * flags[b : b + 1, part : part + 1])
            value = triple(high, low, inv_high[b], inv_low[b])
            own[rows] = value
            near_high[rows], near_low[rows] = halves(value)


def edge_kernel(sides, blocks, cols, _own, _first_next, _first_far, own, rim):
    length, edge = own.shape[1], rim.shape[2]
    window = length + 2 * edge

    def columns(last):
        b = blocks - 1 if last else 0
        cut = slice(length - edge, length) if last else slice(0, edge)
        at = blocks * window + b * cols
        return jnp.concatenate([own[b * window : (b + 1) * window, cut], own[at : at + cols, cut]])

    put_rim(sides, rim, columns)


def pair_kernel(far, rim, near_high, near_low, const, high, low, both, far_high, far_low, total):
    cols, sites = const.shape
    length = far.shape[1]
    blocks = sites // length
    window = near_high.shape[0] // blocks
    edge = (window - length) // 2
    span = 2 * window
    tall = blocks * window
    far_high[...], far_low[...] = halves(far[:tall])
    if rim.shape[0] == 1:
        flag = jnp.minimum(lax.axis_index("row"), 1).astype(jnp.float32)
        left, right = rim[0] * flag, rim[0] * (1 - flag)
    else:
        left, right = rim[0], rim[1]
    left_pair, right_pair = halves(left[:window]), halves(right[:window])
    for b in range(blocks):
        here = slice(b * window, (b + 1) * window)
        column = slice(b * length, (b + 1) * length)

        def part(lo, hi):
            rows = slice(b * window + lo, b * window + hi)
            return near_high[rows], near_low[rows]

        def constant(block):
            if block < 0:
                return left[window:]
            if block == blocks:
                return right[window:]
            return far[tall + block * cols : tall + (block + 1) * cols]

        if b > 0:
            before = slice((b - 1) * window, b * window)
            low_pair = far_high[before, length - edge :], far_low[before, length - edge :]
            low_const = constant(b - 1)[:, length - edge :]
        else:
            low_pair, low_const = left_pair, constant(-1)
        if b + 1 < blocks:
            after = slice((b + 1) * window, (b + 2) * window)
            high_pair = far_high[after, :edge], far_low[after, :edge]
            high_const = constant(b + 1)[:, :edge]
        else:
            high_pair, high_const = right_pair, constant(blocks)
        first = triple(*low_pair, *part(0, edge))
        middle = triple(far_high[here], far_low[here], *part(edge, edge + length))
        last = triple(*high_pair, *part(edge + length, window))
        total[:window] = first
        total[window:] = last
        total[length : length + window] += middle
        high[b * span : (b + 1) * span], low[b * span : (b + 1) * span] = halves(total[...])
        both[:, column] = const[:, column] - (
            triple(*halves(low_const), *part(0, edge))
            + triple(*halves(constant(b)), *part(edge, edge + length))
            + triple(*halves(high_const), *part(edge + length, window))
        )


def keep(ref, start, value):
    cols, width = value.shape
    high, low = halves(value)
    ref[:cols, pl.ds(start, width)] = high
    ref[cols:, pl.ds(start, width)] = low


def load(sides, next_in, own_in, halo, ref):
    sites = own_in.shape[1]
    ref[...] = jnp.zeros_like(ref)
    keep(ref, halo, own_in[...])
    for side in range(sides):
        on_right = 1 - jnp.minimum(lax.axis_index("row"), 1).astype(jnp.int32) if sides == 1 else side
        start = pl.multiple_of((1 - on_right) * (sites - halo), 128)
        keep(ref, pl.multiple_of(on_right * (halo + sites), 128), next_in[side, :, pl.ds(start, halo)])


def top_kernel(mine, sides, next_in, own_in, const, near_high, near_low, _upper, _lower, upper, lower, mid):
    sites = lower.shape[1]
    length = near_high.shape[1]
    blocks = sites // length
    window = near_high.shape[0] // blocks
    edge = (window - length) // 2

    @pl.when(lax.axis_index("tm") == 2 * mine)
    def _():
        load(sides, next_in, own_in, edge, mid)
        upper[...] = own_in[...]
        for b in range(blocks):
            at, rows = slice(b * length, (b + 1) * length), slice(b * window, (b + 1) * window)
            product = stacked_dot(mid, slice(b * length, b * length + window), near_high[rows], near_low[rows])
            lower[:, at] = const[:, at] - product


def chain_kernel(mine, both, high, low, *rest):
    sides, given = rest[0], rest[1:]
    if sides:
        next_in, own_in, _late, _lower, late, lower = given
    else:
        late, _lower, lower = given
    sites = lower.shape[1]
    blocks = sites // high.shape[1]
    length, span = high.shape[1], high.shape[0] // blocks
    halo = (late.shape[1] - sites) // 2

    @pl.when(lax.axis_index("tm") == 2 * mine)
    def _():
        if sides:
            load(sides, next_in, own_in, halo, late)
        for b in range(blocks):
            at, rows = slice(b * length, (b + 1) * length), slice(b * span, (b + 1) * span)
            lower[:, at] = both[:, at] + stacked_dot(late, slice(b * length, b * length + span), high[rows], low[rows])


def upper_kernel(
    sides, top, next_in, own_in, far, far_high, far_low, _late, _upper, late, upper
):
    cols, sites = upper.shape
    length = far.shape[1]
    blocks = sites // length
    window = far_high.shape[0] // blocks
    halo = (late.shape[1] - sites) // 2
    at_window = halo - (window - length) // 2

    @pl.when(lax.axis_index("tm") == 0)
    def _():
        load(sides, next_in, own_in, halo, late)

    @pl.when(lax.axis_index("tm") != 2 * top)
    def _():
        for b in range(blocks):
            rows = slice(b * window, (b + 1) * window)
            at = blocks * window + b * cols
            start = at_window + b * length
            upper[:, b * length : (b + 1) * length] = far[at : at + cols] - stacked_dot(
                late, slice(start, start + window), far_high[rows], far_low[rows]
            )


def local(normals, inv_diag, lag_coupling, fill_mask):
    times, rows = lax.axis_size("tm"), lax.axis_size("row")
    device = lax.axis_index("tm")
    cols, sites = normals.shape[1:]
    blocks, length = inv_diag.shape[1:3]
    window = lag_coupling.shape[2]
    edge = (window - length) // 2
    halo = length + edge
    sides = 1 if rows == 2 else 2
    pairs = times // 2
    f32, bf16 = jnp.float32, jnp.bfloat16
    shape = jax.ShapeDtypeStruct

    def link(source, target):
        return [(s * rows + r, t * rows + r) for s, t in zip(source, target) for r in range(rows)]

    def cross(value, source, target):
        if sides == 1:
            perm = [(s * rows + r, t * rows + 1 - r) for s, t in zip(source, target) for r in range(2)]
            return lax.ppermute(value, BOTH, perm)
        moved = []
        for side, step in enumerate((1, -1)):
            perm = [
                (s * rows + r, t * rows + r + step)
                for s, t in zip(source, target)
                for r in range(rows)
                if 0 <= r + step < rows
            ]
            moved.append(lax.ppermute(value[side : side + 1] if value.shape[0] > 1 else value, BOTH, perm))
        return jnp.concatenate(moved)

    tall = blocks * window
    const, inv_high, inv_low, lag, mask = pl.pallas_call(
        const_kernel,
        out_shape=(
            shape((cols, sites), f32),
            shape((blocks, length, length), bf16), shape((blocks, length, length), bf16),
            shape(lag_coupling.shape[1:], f32), shape(fill_mask.shape[1:], fill_mask.dtype),
        ),
        in_specs=[HBM] * 4,
        out_specs=(VMEM,) * 5,
        scratch_shapes=[
            pltpu.VMEM(normals.shape[1:], f32),
            pltpu.VMEM(inv_diag.shape[1:], f32),
            pltpu.SemaphoreType.DMA((2 + 2 * blocks,)),
        ],
        compiler_params=PARAMS,
    )(*[pltpu.with_memory_space_constraint(a, pltpu.HBM) for a in (fill_mask, normals, inv_diag, lag_coupling)])
    odd, even = range(1, times, 2), range(0, times, 2)
    first_next = cross(const[None], odd[-1:], even[-1:])
    first_own = lax.ppermute(const, BOTH, link(odd[-1:], even[-1:]))
    near, near_high, near_low = pl.pallas_call(
        fuse_kernel,
        out_shape=(
            shape((tall + blocks * cols, length), f32), shape((tall, length), bf16), shape((tall, length), bf16),
        ),
        in_specs=[VMEM] * 5,
        out_specs=(VMEM,) * 3,
        compiler_params=PARAMS,
        cost_estimate=pl.CostEstimate(
            flops=6 * (tall + cols * blocks) * length * length, bytes_accessed=16 * tall * length, transcendentals=0
        ),
    )(mask, const, inv_high, inv_low, lag)
    near, edges = pl.pallas_call(
        functools.partial(edge_kernel, sides, blocks, cols),
        out_shape=(shape(near.shape, f32), shape((sides, window + cols, edge), f32)),
        in_specs=[VMEM] * 3,
        out_specs=(VMEM,) * 2,
        input_output_aliases={0: 0},
        compiler_params=PARAMS,
    )(near, first_next, first_own)
    rim = cross(edges, odd[:-1], even[:-1])
    far = lax.ppermute(near, BOTH, link(odd[:-1], even[:-1]))

    blank = jnp.zeros((cols, sites), f32)
    upper, lower = pl.pallas_call(
        functools.partial(top_kernel, pairs - 1, sides),
        out_shape=(shape((cols, sites), f32),) * 2,
        in_specs=[VMEM] * 7,
        out_specs=(VMEM,) * 2,
        scratch_shapes=[pltpu.VMEM((2 * cols, sites + 2 * edge), bf16)],
        input_output_aliases={5: 0, 6: 1},
        compiler_params=PARAMS,
    )(first_next, first_own, const, near_high, near_low, blank, blank)
    high, low, both, far_high, far_low = pl.pallas_call(
        pair_kernel,
        out_shape=(
            shape((2 * tall, length), bf16), shape((2 * tall, length), bf16), shape((cols, sites), f32),
            shape((tall, length), bf16), shape((tall, length), bf16),
        ),
        in_specs=[VMEM] * 5,
        out_specs=(VMEM,) * 5,
        scratch_shapes=[pltpu.VMEM((2 * window, length), f32)],
        compiler_params=PARAMS,
    )(far, rim, near_high, near_low, const)

    late = jnp.zeros((2 * cols, sites + 2 * halo), bf16)
    for mine in range(pairs - 1, 0, -1):
        source, target = [2 * mine], [2 * mine - 2]
        next_in = cross(lower[None], source, target)
        own_in = lax.ppermute(lower, BOTH, link(source, target))
        if mine > 1:
            late, lower = pl.pallas_call(
                lambda both, high, low, *rest, mine=mine: chain_kernel(mine - 1, both, high, low, sides, *rest),
                out_shape=(shape(late.shape, bf16), shape(lower.shape, f32)),
                in_specs=[VMEM] * 7,
                out_specs=(VMEM,) * 2,
                input_output_aliases={5: 0, 6: 1},
                compiler_params=PARAMS,
            )(both, high, low, next_in, own_in, late, lower)
    late, upper = pl.pallas_call(
        functools.partial(upper_kernel, sides, pairs - 1),
        out_shape=(shape(late.shape, bf16), shape(upper.shape, f32)),
        in_specs=[VMEM] * 7,
        out_specs=(VMEM,) * 2,
        input_output_aliases={5: 0, 6: 1},
        compiler_params=PARAMS,
    )(next_in, own_in, far, far_high, far_low, late, upper)
    returned = lax.ppermute(upper, BOTH, link(even, odd))
    lower = pl.pallas_call(
        lambda both, high, low, *rest: chain_kernel(0, both, high, low, 0, *rest),
        out_shape=shape(lower.shape, f32),
        in_specs=[VMEM] * 5,
        out_specs=VMEM,
        input_output_aliases={4: 0},
        compiler_params=PARAMS,
        cost_estimate=pl.CostEstimate(flops=12 * cols * tall * length, bytes_accessed=8 * tall * length, transcendentals=0),
    )(both, high, low, late, lower)
    return jnp.where(device % 2 == 0, lower, returned)[None]


def solution(mesh):
    placed = (
        P("tm", None, "row"),
        P("tm", "row", None, None),
        P("tm", "row", None, None),
        P("tm", "row", None),
    )
    return jax.shard_map(
        local, mesh=mesh, in_specs=placed, out_specs=P("tm", None, "row"), check_vma=False
    )
```

```python
import functools

import jax
import jax.numpy as jnp
from jax import lax
from jax.experimental import pallas as pl
from jax.experimental.pallas import tpu as pltpu
from jax.sharding import PartitionSpec as P

BOTH = ("tm", "row")
VMEM = pl.BlockSpec(memory_space=pltpu.VMEM)
HBM = pl.BlockSpec(memory_space=pltpu.HBM)
PARAMS = pltpu.CompilerParams(vmem_limit_bytes=32 * 1024 * 1024)


def halves(value):
    high = value.astype(jnp.bfloat16)
    low = (value - high.astype(jnp.float32)).astype(jnp.bfloat16)
    return high, low


def dot(a, b):
    return jnp.dot(a, b, preferred_element_type=jnp.float32)


def stacked_dot(pair, cols, high, low):
    rows = pair.shape[0] // 2
    wide = dot(pair[:, cols], high)
    return wide[:rows] + wide[rows:] + dot(pair[:rows, cols], low)


def triple(high, low, inv_high, inv_low):
    return dot(high, inv_high) + dot(low, inv_high) + dot(high, inv_low)


def put_rim(sides, rim, columns):
    if sides == 1:
        row = lax.axis_index("row")

        @pl.when(row == 0)
        def _():
            rim[0] = columns(True)

        @pl.when(row != 0)
        def _():
            rim[0] = columns(False)
    else:
        rim[0] = columns(True)
        rim[1] = columns(False)


def const_kernel(
    mask, normals, inv, lag, const, inv_high, inv_low, lag_out, mask_out, normals_in, inv_in, sems
):
    blocks, length = inv.shape[1], inv.shape[2]
    moves = [pltpu.make_async_copy(normals.at[0], normals_in, sems.at[0])]
    for b in range(blocks):
        moves.append(pltpu.make_async_copy(inv.at[0, b], inv_in.at[b], sems.at[1 + b]))
    for b in range(blocks):
        moves.append(pltpu.make_async_copy(lag.at[0, b], lag_out.at[b], sems.at[1 + blocks + b]))
    moves.append(pltpu.make_async_copy(mask.at[0], mask_out, sems.at[1 + 2 * blocks]))
    for move in moves:
        move.start()
    moves[0].wait()
    for b in range(blocks):
        at = slice(b * length, (b + 1) * length)
        high, low = halves(normals_in[:, at])
        moves[1 + b].wait()
        inv_high[b], inv_low[b] = halves(inv_in[b])
        const[:, at] = triple(high, low, inv_high[b], inv_low[b])
    for move in moves[1 + blocks :]:
        move.wait()


def fuse_kernel(mask, const, inv_high, inv_low, lag, own, near_high, near_low):
    blocks, window, length = lag.shape
    edge = (window - length) // 2
    cols = const.shape[0]
    cuts = (0, edge, edge + length, window)
    flags = mask[...].astype(jnp.float32)
    for b in range(blocks):
        at = blocks * window + b * cols
        own[at : at + cols] = const[:, b * length : (b + 1) * length]
        for part in range(3):
            lo, hi = cuts[part], cuts[part + 1]
            rows = slice(b * window + lo, b * window + hi)
            high, low = halves(lag[b, lo:hi] * flags[b : b + 1, part : part + 1])
            value = triple(high, low, inv_high[b], inv_low[b])
            own[rows] = value
            near_high[rows], near_low[rows] = halves(value)


def edge_kernel(sides, blocks, cols, _own, own, rim):
    length, edge = own.shape[1], rim.shape[2]
    window = length + 2 * edge

    def columns(last):
        b = blocks - 1 if last else 0
        cut = slice(length - edge, length) if last else slice(0, edge)
        at = blocks * window + b * cols
        return jnp.concatenate([own[b * window : (b + 1) * window, cut], own[at : at + cols, cut]])

    put_rim(sides, rim, columns)


def split_kernel(rim, far, far_high, far_low, rim_high, rim_low):
    far_high[...], far_low[...] = halves(far[: far_high.shape[0]])
    for side in range(rim.shape[0]):
        rim_high[side], rim_low[side] = halves(rim[side, : rim_high.shape[1]])


def pair_kernel(rim, far, far_high, far_low, near_high, near_low, const, high, low, both, total):
    cols, sites = const.shape
    length = far.shape[1]
    blocks = sites // length
    window = near_high.shape[0] // blocks
    edge = (window - length) // 2
    span = 2 * window
    tall = blocks * window
    if rim.shape[0] == 1:
        flag = jnp.minimum(lax.axis_index("row"), 1).astype(jnp.float32)
        left, right = rim[0] * flag, rim[0] * (1 - flag)
    else:
        left, right = rim[0], rim[1]
    left_pair, right_pair = halves(left[:window]), halves(right[:window])
    for b in range(blocks):
        here = slice(b * window, (b + 1) * window)
        column = slice(b * length, (b + 1) * length)

        def part(lo, hi):
            rows = slice(b * window + lo, b * window + hi)
            return near_high[rows], near_low[rows]

        def constant(block):
            if block < 0:
                return left[window:]
            if block == blocks:
                return right[window:]
            return far[tall + block * cols : tall + (block + 1) * cols]

        if b > 0:
            before = slice((b - 1) * window, b * window)
            low_pair = far_high[before, length - edge :], far_low[before, length - edge :]
            low_const = constant(b - 1)[:, length - edge :]
        else:
            low_pair, low_const = left_pair, constant(-1)
        if b + 1 < blocks:
            after = slice((b + 1) * window, (b + 2) * window)
            high_pair = far_high[after, :edge], far_low[after, :edge]
            high_const = constant(b + 1)[:, :edge]
        else:
            high_pair, high_const = right_pair, constant(blocks)
        first = triple(*low_pair, *part(0, edge))
        middle = triple(far_high[here], far_low[here], *part(edge, edge + length))
        last = triple(*high_pair, *part(edge + length, window))
        total[:window] = first
        total[window:] = last
        total[length : length + window] += middle
        high[b * span : (b + 1) * span], low[b * span : (b + 1) * span] = halves(total[...])
        both[:, column] = const[:, column] - (
            triple(*halves(low_const), *part(0, edge))
            + triple(*halves(constant(b)), *part(edge, edge + length))
            + triple(*halves(high_const), *part(edge + length, window))
        )


def keep(ref, start, value):
    cols, width = value.shape
    high, low = halves(value)
    ref[:cols, pl.ds(start, width)] = high
    ref[cols:, pl.ds(start, width)] = low


def load(sides, next_in, own_in, halo, ref):
    sites = own_in.shape[1]
    ref[...] = jnp.zeros_like(ref)
    keep(ref, halo, own_in[...])
    for side in range(sides):
        on_right = 1 - jnp.minimum(lax.axis_index("row"), 1).astype(jnp.int32) if sides == 1 else side
        start = pl.multiple_of((1 - on_right) * (sites - halo), 128)
        keep(ref, pl.multiple_of(on_right * (halo + sites), 128), next_in[side, :, pl.ds(start, halo)])


def top_kernel(mine, sides, next_in, own_in, const, near_high, near_low, _upper, _lower, upper, lower, mid):
    sites = lower.shape[1]
    length = near_high.shape[1]
    blocks = sites // length
    window = near_high.shape[0] // blocks
    edge = (window - length) // 2

    @pl.when(lax.axis_index("tm") == 2 * mine)
    def _():
        load(sides, next_in, own_in, edge, mid)
        upper[...] = own_in[...]
        for b in range(blocks):
            at, rows = slice(b * length, (b + 1) * length), slice(b * window, (b + 1) * window)
            product = stacked_dot(mid, slice(b * length, b * length + window), near_high[rows], near_low[rows])
            lower[:, at] = const[:, at] - product


def direct_kernel(
    mine, sides, next_in, own_in, rim, far, far_high, far_low, rim_high, rim_low, near_high, near_low, const,
    _late, _lower, late, lower, mid
):
    cols, sites = lower.shape
    length = near_high.shape[1]
    blocks = sites // length
    window = near_high.shape[0] // blocks
    edge = (window - length) // 2
    halo = length + edge

    @pl.when(lax.axis_index("tm") == 2 * mine)
    def _():
        load(sides, next_in, own_in, halo, late)
        mid[...] = jnp.zeros_like(mid)
        for side in range(sides):
            on_right = 1 - jnp.minimum(lax.axis_index("row"), 1).astype(jnp.int32) if sides == 1 else side
            start = pl.multiple_of(on_right * (2 * halo + sites - window), 128)
            product = stacked_dot(late, pl.ds(start, window), rim_high[side], rim_low[side])
            keep(mid, pl.multiple_of(on_right * (edge + sites), 128), rim[side, window:] - product)
        for b in range(blocks):
            rows, start = slice(b * window, (b + 1) * window), halo - edge + b * length
            at = blocks * window + b * cols
            product = stacked_dot(late, slice(start, start + window), far_high[rows], far_low[rows])
            keep(mid, edge + b * length, far[at : at + cols] - product)
        for b in range(blocks):
            at, rows = slice(b * length, (b + 1) * length), slice(b * window, (b + 1) * window)
            product = stacked_dot(mid, slice(b * length, b * length + window), near_high[rows], near_low[rows])
            lower[:, at] = const[:, at] - product


def step(both, high, low, late, lower):
    blocks = lower.shape[1] // high.shape[1]
    length, span = high.shape[1], high.shape[0] // blocks
    for b in range(blocks):
        at, rows = slice(b * length, (b + 1) * length), slice(b * span, (b + 1) * span)
        lower[:, at] = both[:, at] + stacked_dot(late, slice(b * length, b * length + span), high[rows], low[rows])


def chain_kernel(mine, sides, next_in, own_in, both, high, low, _late, _lower, late, lower):
    @pl.when(lax.axis_index("tm") == 2 * mine)
    def _():
        load(sides, next_in, own_in, (late.shape[1] - own_in.shape[1]) // 2, late)
        step(both, high, low, late, lower)


def last_kernel(both, high, low, late, _lower, lower):
    pl.when(lax.axis_index("tm") == 0)(lambda: step(both, high, low, late, lower))


def upper_kernel(
    sides, top, next_in, own_in, far, far_high, far_low, _late, _upper, late, upper
):
    cols, sites = upper.shape
    length = far.shape[1]
    blocks = sites // length
    window = far_high.shape[0] // blocks
    halo = (late.shape[1] - sites) // 2
    at_window = halo - (window - length) // 2

    @pl.when(lax.axis_index("tm") == 0)
    def _():
        load(sides, next_in, own_in, halo, late)

    @pl.when(lax.axis_index("tm") != 2 * top)
    def _():
        for b in range(blocks):
            rows = slice(b * window, (b + 1) * window)
            at = blocks * window + b * cols
            start = at_window + b * length
            upper[:, b * length : (b + 1) * length] = far[at : at + cols] - stacked_dot(
                late, slice(start, start + window), far_high[rows], far_low[rows]
            )


def local(normals, inv_diag, lag_coupling, fill_mask):
    times, rows = lax.axis_size("tm"), lax.axis_size("row")
    device = lax.axis_index("tm")
    cols, sites = normals.shape[1:]
    blocks, length = inv_diag.shape[1:3]
    window = lag_coupling.shape[2]
    edge = (window - length) // 2
    halo = length + edge
    sides = 1 if rows == 2 else 2
    pairs = times // 2
    f32, bf16 = jnp.float32, jnp.bfloat16
    shape = jax.ShapeDtypeStruct

    def link(source, target):
        return [(s * rows + r, t * rows + r) for s, t in zip(source, target) for r in range(rows)]

    def cross(value, source, target):
        if sides == 1:
            perm = [(s * rows + r, t * rows + 1 - r) for s, t in zip(source, target) for r in range(2)]
            return lax.ppermute(value, BOTH, perm)
        moved = []
        for side, step in enumerate((1, -1)):
            perm = [
                (s * rows + r, t * rows + r + step)
                for s, t in zip(source, target)
                for r in range(rows)
                if 0 <= r + step < rows
            ]
            moved.append(lax.ppermute(value[side : side + 1] if value.shape[0] > 1 else value, BOTH, perm))
        return jnp.concatenate(moved)

    tall = blocks * window
    const, inv_high, inv_low, lag, mask = pl.pallas_call(
        const_kernel,
        out_shape=(
            shape((cols, sites), f32),
            shape((blocks, length, length), bf16), shape((blocks, length, length), bf16),
            shape(lag_coupling.shape[1:], f32), shape(fill_mask.shape[1:], fill_mask.dtype),
        ),
        in_specs=[HBM] * 4,
        out_specs=(VMEM,) * 5,
        scratch_shapes=[
            pltpu.VMEM(normals.shape[1:], f32),
            pltpu.VMEM(inv_diag.shape[1:], f32),
            pltpu.SemaphoreType.DMA((2 + 2 * blocks,)),
        ],
        compiler_params=PARAMS,
    )(*[pltpu.with_memory_space_constraint(a, pltpu.HBM) for a in (fill_mask, normals, inv_diag, lag_coupling)])
    odd, even = range(1, times, 2), range(0, times, 2)
    first_next = cross(const[None], odd[-1:], even[-1:])
    first_own = lax.ppermute(const, BOTH, link(odd[-1:], even[-1:]))
    near, near_high, near_low = pl.pallas_call(
        fuse_kernel,
        out_shape=(
            shape((tall + blocks * cols, length), f32), shape((tall, length), bf16), shape((tall, length), bf16),
        ),
        in_specs=[VMEM] * 5,
        out_specs=(VMEM,) * 3,
        compiler_params=PARAMS,
        cost_estimate=pl.CostEstimate(
            flops=6 * (tall + cols * blocks) * length * length, bytes_accessed=16 * tall * length, transcendentals=0
        ),
    )(mask, const, inv_high, inv_low, lag)
    near, edges = pl.pallas_call(
        functools.partial(edge_kernel, sides, blocks, cols),
        out_shape=(shape(near.shape, f32), shape((sides, window + cols, edge), f32)),
        in_specs=[VMEM],
        out_specs=(VMEM,) * 2,
        input_output_aliases={0: 0},
        compiler_params=PARAMS,
    )(near)
    rim = cross(edges, odd[:-1], even[:-1])
    far = lax.ppermute(near, BOTH, link(odd[:-1], even[:-1]))

    blank = jnp.zeros((cols, sites), f32)
    upper, lower = pl.pallas_call(
        functools.partial(top_kernel, pairs - 1, sides),
        out_shape=(shape((cols, sites), f32),) * 2,
        in_specs=[VMEM] * 7,
        out_specs=(VMEM,) * 2,
        scratch_shapes=[pltpu.VMEM((2 * cols, sites + 2 * edge), bf16)],
        input_output_aliases={5: 0, 6: 1},
        compiler_params=PARAMS,
        cost_estimate=pl.CostEstimate(flops=50 * 10**9, bytes_accessed=0, transcendentals=0),
    )(first_next, first_own, const, near_high, near_low, blank, blank)
    far_high, far_low, rim_high, rim_low = pl.pallas_call(
        split_kernel,
        out_shape=(
            shape((tall, length), bf16), shape((tall, length), bf16),
            shape((sides, window, edge), bf16), shape((sides, window, edge), bf16),
        ),
        in_specs=[VMEM] * 2,
        out_specs=(VMEM,) * 4,
        compiler_params=PARAMS,
    )(rim, far)
    high, low, both = pl.pallas_call(
        pair_kernel,
        out_shape=(
            shape((2 * tall, length), bf16), shape((2 * tall, length), bf16), shape((cols, sites), f32),
        ),
        in_specs=[VMEM] * 7,
        out_specs=(VMEM,) * 3,
        scratch_shapes=[pltpu.VMEM((2 * window, length), f32)],
        compiler_params=PARAMS,
        cost_estimate=pl.CostEstimate(flops=10**9, bytes_accessed=0, transcendentals=0),
    )(rim, far, far_high, far_low, near_high, near_low, const)

    late = jnp.zeros((2 * cols, sites + 2 * halo), bf16)
    for mine in range(pairs - 1, 0, -1):
        source, target = [2 * mine], [2 * mine - 2]
        next_in = cross(lower[None], source, target)
        own_in = lax.ppermute(lower, BOTH, link(source, target))
        if mine == 1:
            break
        if mine == pairs - 1:
            kernel, given = functools.partial(direct_kernel, mine - 1, sides), (
                next_in, own_in, rim, far, far_high, far_low, rim_high, rim_low, near_high, near_low, const
            )
            scratch = [pltpu.VMEM((2 * cols, sites + 2 * edge), bf16)]
        else:
            kernel, given = functools.partial(chain_kernel, mine - 1, sides), (next_in, own_in, both, high, low)
            scratch = []
        late, lower = pl.pallas_call(
            kernel,
            out_shape=(shape(late.shape, bf16), shape(lower.shape, f32)),
            in_specs=[VMEM] * (len(given) + 2),
            out_specs=(VMEM,) * 2,
            scratch_shapes=scratch,
            input_output_aliases={len(given): 0, len(given) + 1: 1},
            compiler_params=PARAMS,
        )(*given, late, lower)
    late, upper = pl.pallas_call(
        functools.partial(upper_kernel, sides, pairs - 1),
        out_shape=(shape(late.shape, bf16), shape(upper.shape, f32)),
        in_specs=[VMEM] * 7,
        out_specs=(VMEM,) * 2,
        input_output_aliases={5: 0, 6: 1},
        compiler_params=PARAMS,
    )(next_in, own_in, far, far_high, far_low, late, upper)
    returned = lax.ppermute(upper, BOTH, link(even, odd))
    lower = pl.pallas_call(
        last_kernel,
        out_shape=shape(lower.shape, f32),
        in_specs=[VMEM] * 5,
        out_specs=VMEM,
        input_output_aliases={4: 0},
        compiler_params=PARAMS,
        cost_estimate=pl.CostEstimate(flops=12 * cols * tall * length, bytes_accessed=8 * tall * length, transcendentals=0),
    )(both, high, low, late, lower)
    return jnp.where(device % 2 == 0, lower, returned)[None]


def solution(mesh):
    placed = (
        P("tm", None, "row"),
        P("tm", "row", None, None),
        P("tm", "row", None, None),
        P("tm", "row", None),
    )
    return jax.shard_map(
        local, mesh=mesh, in_specs=placed, out_specs=P("tm", None, "row"), check_vma=False
    )
```

```python
import functools

import jax
import jax.numpy as jnp
from jax import lax
from jax.experimental import pallas as pl
from jax.experimental.pallas import tpu as pltpu
from jax.sharding import PartitionSpec as P

BOTH = ("tm", "row")
VMEM = pl.BlockSpec(memory_space=pltpu.VMEM)
HBM = pl.BlockSpec(memory_space=pltpu.HBM)
PARAMS = pltpu.CompilerParams(vmem_limit_bytes=32 * 1024 * 1024)


def halves(value):
    high = value.astype(jnp.bfloat16)
    low = (value - high.astype(jnp.float32)).astype(jnp.bfloat16)
    return high, low


def dot(a, b):
    return jnp.dot(a, b, preferred_element_type=jnp.float32)


def stacked_dot(pair, cols, high, low):
    rows = pair.shape[0] // 2
    wide = dot(pair[:, cols], high)
    return wide[:rows] + wide[rows:] + dot(pair[:rows, cols], low)


def triple(high, low, inv_high, inv_low):
    return dot(high, inv_high) + dot(low, inv_high) + dot(high, inv_low)


def put_rim(sides, rim, columns):
    if sides == 1:
        row = lax.axis_index("row")

        @pl.when(row == 0)
        def _():
            rim[0] = columns(True)

        @pl.when(row != 0)
        def _():
            rim[0] = columns(False)
    else:
        rim[0] = columns(True)
        rim[1] = columns(False)


def const_kernel(
    mask, normals, inv, lag, const, inv_high, inv_low, lag_out, mask_out, normals_in, inv_in, sems
):
    blocks, length = inv.shape[1], inv.shape[2]
    moves = [pltpu.make_async_copy(normals.at[0], normals_in, sems.at[0])]
    for b in range(blocks):
        moves.append(pltpu.make_async_copy(inv.at[0, b], inv_in.at[b], sems.at[1 + b]))
    for b in range(blocks):
        moves.append(pltpu.make_async_copy(lag.at[0, b], lag_out.at[b], sems.at[1 + blocks + b]))
    moves.append(pltpu.make_async_copy(mask.at[0], mask_out, sems.at[1 + 2 * blocks]))
    for move in moves:
        move.start()
    moves[0].wait()
    for b in range(blocks):
        at = slice(b * length, (b + 1) * length)
        high, low = halves(normals_in[:, at])
        moves[1 + b].wait()
        inv_high[b], inv_low[b] = halves(inv_in[b])
        const[:, at] = triple(high, low, inv_high[b], inv_low[b])
    for move in moves[1 + blocks :]:
        move.wait()


def fuse_kernel(mask, const, inv_high, inv_low, lag, own, near_high, near_low):
    blocks, window, length = lag.shape
    edge = (window - length) // 2
    cols = const.shape[0]
    cuts = (0, edge, edge + length, window)
    flags = mask[...].astype(jnp.float32)
    for b in range(blocks):
        at = blocks * window + b * cols
        own[at : at + cols] = const[:, b * length : (b + 1) * length]
        for part in range(3):
            lo, hi = cuts[part], cuts[part + 1]
            rows = slice(b * window + lo, b * window + hi)
            high, low = halves(lag[b, lo:hi] * flags[b : b + 1, part : part + 1])
            value = triple(high, low, inv_high[b], inv_low[b])
            own[rows] = value
            near_high[rows], near_low[rows] = halves(value)


def edge_kernel(sides, blocks, cols, _own, own, rim):
    length, edge = own.shape[1], rim.shape[2]
    window = length + 2 * edge

    def columns(last):
        b = blocks - 1 if last else 0
        cut = slice(length - edge, length) if last else slice(0, edge)
        at = blocks * window + b * cols
        return jnp.concatenate([own[b * window : (b + 1) * window, cut], own[at : at + cols, cut]])

    put_rim(sides, rim, columns)


def split_kernel(rim, far, far_high, far_low, rim_high, rim_low):
    far_high[...], far_low[...] = halves(far[: far_high.shape[0]])
    for side in range(rim.shape[0]):
        rim_high[side], rim_low[side] = halves(rim[side, : rim_high.shape[1]])


def cuts_of(blocks, length, sites, span, last):
    packed, cuts = 0, []
    for b in range(blocks):
        start = span // 2 - length // 2 - b * length
        lo, hi = (start + sites, span) if last else (0, start)
        cuts.append((lo, hi, packed))
        packed += hi - lo
    return cuts


def put_rows(b, start, sites, span, other_rows, total):
    length = total.shape[1]
    for last in (True, False):
        lo, hi, packed = cuts_of(sites // length, length, sites, span, last)[b]

        @pl.when((lax.axis_index("row") == 0) == last)
        def _():
            other_rows[packed : packed + hi - lo] = total[lo:hi]


def pair_kernel(jump, rim, far, far_high, far_low, near_high, near_low, const, high, low, both, *rest):
    cols, sites = const.shape
    length = far.shape[1]
    blocks = sites // length
    window = near_high.shape[0] // blocks
    edge = (window - length) // 2
    span = 2 * window
    tall = blocks * window
    total = rest[-1]
    if rim.shape[0] == 1:
        flag = jnp.minimum(lax.axis_index("row"), 1).astype(jnp.float32)
        left, right = rim[0] * flag, rim[0] * (1 - flag)
    else:
        left, right = rim[0], rim[1]
    left_pair, right_pair = halves(left[:window]), halves(right[:window])
    for b in range(blocks):
        here = slice(b * window, (b + 1) * window)
        column = slice(b * length, (b + 1) * length)

        def part(lo, hi):
            rows = slice(b * window + lo, b * window + hi)
            return near_high[rows], near_low[rows]

        def constant(block):
            if block < 0:
                return left[window:]
            if block == blocks:
                return right[window:]
            return far[tall + block * cols : tall + (block + 1) * cols]

        if b > 0:
            before = slice((b - 1) * window, b * window)
            low_pair = far_high[before, length - edge :], far_low[before, length - edge :]
            low_const = constant(b - 1)[:, length - edge :]
        else:
            low_pair, low_const = left_pair, constant(-1)
        if b + 1 < blocks:
            after = slice((b + 1) * window, (b + 2) * window)
            high_pair = far_high[after, :edge], far_low[after, :edge]
            high_const = constant(b + 1)[:, :edge]
        else:
            high_pair, high_const = right_pair, constant(blocks)
        first = triple(*low_pair, *part(0, edge))
        middle = triple(far_high[here], far_low[here], *part(edge, edge + length))
        last = triple(*high_pair, *part(edge + length, window))
        total[:window] = first
        total[window:] = last
        total[length : length + window] += middle
        high[b * span : (b + 1) * span], low[b * span : (b + 1) * span] = halves(total[...])
        if jump:
            own_rows, other_rows = rest[:2]
            start = length + edge - b * length
            own_rows[b * sites : (b + 1) * sites] = total[start : start + sites]
            put_rows(b, start, sites, span, other_rows, total)
        both[:, column] = const[:, column] - (
            triple(*halves(low_const), *part(0, edge))
            + triple(*halves(constant(b)), *part(edge, edge + length))
            + triple(*halves(high_const), *part(edge + length, window))
        )
        if jump:
            at = blocks * sites + b * cols
            own_rows[at : at + cols] = both[:, column]


def keep(ref, start, value):
    cols, width = value.shape
    high, low = halves(value)
    ref[:cols, pl.ds(start, width)] = high
    ref[cols:, pl.ds(start, width)] = low


def load(sides, pick, own, halo, ref):
    sites = own.shape[1]
    ref[...] = jnp.zeros_like(ref)
    keep(ref, halo, own)
    for side in range(sides):
        on_right = 1 - jnp.minimum(lax.axis_index("row"), 1).astype(jnp.int32) if sides == 1 else side
        start = pl.multiple_of((1 - on_right) * (sites - halo), 128)
        keep(ref, pl.multiple_of(on_right * (halo + sites), 128), pick(side, pl.ds(start, halo)))


def plain(next_in):
    return lambda side, cut: next_in[side, :, cut]


def top_kernel(mine, sides, next_in, own_in, const, near_high, near_low, _upper, _lower, upper, lower, mid):
    sites = lower.shape[1]
    length = near_high.shape[1]
    blocks = sites // length
    window = near_high.shape[0] // blocks
    edge = (window - length) // 2

    @pl.when(lax.axis_index("tm") == 2 * mine)
    def _():
        load(sides, plain(next_in), own_in[...], edge, mid)
        upper[...] = own_in[...]
        for b in range(blocks):
            at, rows = slice(b * length, (b + 1) * length), slice(b * window, (b + 1) * window)
            product = stacked_dot(mid, slice(b * length, b * length + window), near_high[rows], near_low[rows])
            lower[:, at] = const[:, at] - product


def direct_kernel(
    mine, sides, next_in, own_in, rim, far, far_high, far_low, rim_high, rim_low, near_high, near_low, const,
    _late, _lower, late, lower, mid
):
    cols, sites = lower.shape
    length = near_high.shape[1]
    blocks = sites // length
    window = near_high.shape[0] // blocks
    edge = (window - length) // 2
    halo = length + edge

    @pl.when(lax.axis_index("tm") == 2 * mine)
    def _():
        load(sides, plain(next_in), own_in[...], halo, late)
        mid[...] = jnp.zeros_like(mid)
        for side in range(sides):
            on_right = 1 - jnp.minimum(lax.axis_index("row"), 1).astype(jnp.int32) if sides == 1 else side
            start = pl.multiple_of(on_right * (2 * halo + sites - window), 128)
            product = stacked_dot(late, pl.ds(start, window), rim_high[side], rim_low[side])
            keep(mid, pl.multiple_of(on_right * (edge + sites), 128), rim[side, window:] - product)
        for b in range(blocks):
            rows, start = slice(b * window, (b + 1) * window), halo - edge + b * length
            at = blocks * window + b * cols
            product = stacked_dot(late, slice(start, start + window), far_high[rows], far_low[rows])
            keep(mid, edge + b * length, far[at : at + cols] - product)
        for b in range(blocks):
            at, rows = slice(b * length, (b + 1) * length), slice(b * window, (b + 1) * window)
            product = stacked_dot(mid, slice(b * length, b * length + window), near_high[rows], near_low[rows])
            lower[:, at] = const[:, at] - product


def step(both, high, low, late, lower):
    blocks = lower.shape[1] // high.shape[1]
    length, span = high.shape[1], high.shape[0] // blocks
    for b in range(blocks):
        at, rows = slice(b * length, (b + 1) * length), slice(b * span, (b + 1) * span)
        lower[:, at] = both[:, at] + stacked_dot(late, slice(b * length, b * length + span), high[rows], low[rows])


def chain_kernel(mine, sides, next_in, own_in, both, high, low, _late, _lower, late, lower):
    @pl.when(lax.axis_index("tm") == 2 * mine)
    def _():
        load(sides, plain(next_in), own_in[...], (late.shape[1] - own_in.shape[1]) // 2, late)
        step(both, high, low, late, lower)


def rows_kernel(own_rows, other_rows, own_high, own_low, other_high, other_low):
    own_high[...], own_low[...] = halves(own_rows[: own_high.shape[0]])
    other_high[...], other_low[...] = halves(other_rows[...])


def jump_kernel(
    mine, sides, next_in, own_in, both, high, low, own_rows, own_high, own_low, other_high, other_low,
    _late, _lower, late, lower, parts, mid
):
    cols, sites = lower.shape
    length = high.shape[1]
    blocks = sites // length
    span = high.shape[0] // blocks

    @pl.when(lax.axis_index("tm") != 2 * mine)
    def _():
        parts[...] = jnp.zeros_like(parts)

    @pl.when(lax.axis_index("tm") == 2 * mine)
    def _():
        load(sides, plain(next_in), own_in[...], (late.shape[1] - sites) // 2, late)
        step(both, high, low, late, lower)
        keep(mid, 0, lower[...])
        for b in range(blocks):
            at, rows = slice(b * length, (b + 1) * length), slice(b * sites, (b + 1) * sites)
            const = slice(blocks * sites + b * cols, blocks * sites + (b + 1) * cols)
            parts[:cols, at] = own_rows[const] + stacked_dot(mid, slice(0, sites), own_high[rows], own_low[rows])
        for last in (True, False):

            @pl.when((lax.axis_index("row") == 0) != last)
            def _():
                for b, (lo, hi, packed) in enumerate(cuts_of(blocks, length, sites, span, last)):
                    from_sites = slice(0, hi - lo) if last else slice(sites - (hi - lo), sites)
                    rows = slice(packed, packed + hi - lo)
                    parts[cols:, b * length : (b + 1) * length] = stacked_dot(
                        mid, from_sites, other_high[rows], other_low[rows]
                    )


def landing_kernel(mine, sides, next_in, own_in, both, high, low, _late, _lower, late, lower):
    cols, sites = lower.shape

    @pl.when(lax.axis_index("tm") == 2 * mine)
    def _():
        own = own_in[:cols] + next_in[cols:]
        pick = lambda side, cut: next_in[:cols, cut] + own_in[cols:, cut]
        load(sides, pick, own, (late.shape[1] - sites) // 2, late)
        step(both, high, low, late, lower)


def last_kernel(both, high, low, late, _lower, lower):
    pl.when(lax.axis_index("tm") == 0)(lambda: step(both, high, low, late, lower))


def upper_kernel(
    sides, top, next_in, own_in, far, far_high, far_low, _late, _upper, late, upper
):
    cols, sites = upper.shape
    length = far.shape[1]
    blocks = sites // length
    window = far_high.shape[0] // blocks
    halo = (late.shape[1] - sites) // 2
    at_window = halo - (window - length) // 2

    @pl.when(lax.axis_index("tm") == 0)
    def _():
        load(sides, plain(next_in), own_in[...], halo, late)

    @pl.when(lax.axis_index("tm") != 2 * top)
    def _():
        for b in range(blocks):
            rows = slice(b * window, (b + 1) * window)
            at = blocks * window + b * cols
            start = at_window + b * length
            upper[:, b * length : (b + 1) * length] = far[at : at + cols] - stacked_dot(
                late, slice(start, start + window), far_high[rows], far_low[rows]
            )


def local(normals, inv_diag, lag_coupling, fill_mask):
    times, rows = lax.axis_size("tm"), lax.axis_size("row")
    device = lax.axis_index("tm")
    cols, sites = normals.shape[1:]
    blocks, length = inv_diag.shape[1:3]
    window = lag_coupling.shape[2]
    edge = (window - length) // 2
    halo = length + edge
    sides = 1 if rows == 2 else 2
    pairs = times // 2
    f32, bf16 = jnp.float32, jnp.bfloat16
    shape = jax.ShapeDtypeStruct

    def link(source, target):
        return [(s * rows + r, t * rows + r) for s, t in zip(source, target) for r in range(rows)]

    def cross(value, source, target):
        if sides == 1:
            perm = [(s * rows + r, t * rows + 1 - r) for s, t in zip(source, target) for r in range(2)]
            return lax.ppermute(value, BOTH, perm)
        moved = []
        for side, step in enumerate((1, -1)):
            perm = [
                (s * rows + r, t * rows + r + step)
                for s, t in zip(source, target)
                for r in range(rows)
                if 0 <= r + step < rows
            ]
            moved.append(lax.ppermute(value[side : side + 1] if value.shape[0] > 1 else value, BOTH, perm))
        return jnp.concatenate(moved)

    tall = blocks * window
    jump = pairs // 2 - 1
    jumps = rows == 2 and 3 <= jump < pairs - 2
    const, inv_high, inv_low, lag, mask = pl.pallas_call(
        const_kernel,
        out_shape=(
            shape((cols, sites), f32),
            shape((blocks, length, length), bf16), shape((blocks, length, length), bf16),
            shape(lag_coupling.shape[1:], f32), shape(fill_mask.shape[1:], fill_mask.dtype),
        ),
        in_specs=[HBM] * 4,
        out_specs=(VMEM,) * 5,
        scratch_shapes=[
            pltpu.VMEM(normals.shape[1:], f32),
            pltpu.VMEM(inv_diag.shape[1:], f32),
            pltpu.SemaphoreType.DMA((2 + 2 * blocks,)),
        ],
        compiler_params=PARAMS,
    )(*[pltpu.with_memory_space_constraint(a, pltpu.HBM) for a in (fill_mask, normals, inv_diag, lag_coupling)])
    odd, even = range(1, times, 2), range(0, times, 2)
    first_next = cross(const[None], odd[-1:], even[-1:])
    first_own = lax.ppermute(const, BOTH, link(odd[-1:], even[-1:]))
    near, near_high, near_low = pl.pallas_call(
        fuse_kernel,
        out_shape=(
            shape((tall + blocks * cols, length), f32), shape((tall, length), bf16), shape((tall, length), bf16),
        ),
        in_specs=[VMEM] * 5,
        out_specs=(VMEM,) * 3,
        compiler_params=PARAMS,
        cost_estimate=pl.CostEstimate(
            flops=6 * (tall + cols * blocks) * length * length, bytes_accessed=16 * tall * length, transcendentals=0
        ),
    )(mask, const, inv_high, inv_low, lag)
    near, edges = pl.pallas_call(
        functools.partial(edge_kernel, sides, blocks, cols),
        out_shape=(shape(near.shape, f32), shape((sides, window + cols, edge), f32)),
        in_specs=[VMEM],
        out_specs=(VMEM,) * 2,
        input_output_aliases={0: 0},
        compiler_params=PARAMS,
    )(near)
    rim = cross(edges, odd[:-1], even[:-1])
    far = lax.ppermute(near, BOTH, link(odd[:-1], even[:-1]))

    blank = jnp.zeros((cols, sites), f32)
    upper, lower = pl.pallas_call(
        functools.partial(top_kernel, pairs - 1, sides),
        out_shape=(shape((cols, sites), f32),) * 2,
        in_specs=[VMEM] * 7,
        out_specs=(VMEM,) * 2,
        scratch_shapes=[pltpu.VMEM((2 * cols, sites + 2 * edge), bf16)],
        input_output_aliases={5: 0, 6: 1},
        compiler_params=PARAMS,
        cost_estimate=pl.CostEstimate(flops=50 * 10**9, bytes_accessed=0, transcendentals=0),
    )(first_next, first_own, const, near_high, near_low, blank, blank)
    far_high, far_low, rim_high, rim_low = pl.pallas_call(
        split_kernel,
        out_shape=(
            shape((tall, length), bf16), shape((tall, length), bf16),
            shape((sides, window, edge), bf16), shape((sides, window, edge), bf16),
        ),
        in_specs=[VMEM] * 2,
        out_specs=(VMEM,) * 4,
        compiler_params=PARAMS,
    )(rim, far)
    packs = (shape((blocks * (sites + cols), length), f32), shape((halo + edge, length), f32)) if jumps else ()
    high, low, both, *packs = pl.pallas_call(
        functools.partial(pair_kernel, jumps),
        out_shape=(
            shape((2 * tall, length), bf16), shape((2 * tall, length), bf16), shape((cols, sites), f32), *packs
        ),
        in_specs=[VMEM] * 7,
        out_specs=(VMEM,) * (3 + len(packs)),
        scratch_shapes=[pltpu.VMEM((2 * window, length), f32)],
        compiler_params=PARAMS,
        cost_estimate=pl.CostEstimate(flops=10**9, bytes_accessed=0, transcendentals=0),
    )(rim, far, far_high, far_low, near_high, near_low, const)
    if jumps:
        source, target = [2 * jump - 2], [2 * jump]
        own_rows = lax.ppermute(packs[0], BOTH, link(source, target))
        other_rows = cross(packs[1], source, target)
        ship = pl.pallas_call(
            rows_kernel,
            out_shape=(shape((blocks * sites, length), bf16),) * 2 + (shape(other_rows.shape, bf16),) * 2,
            in_specs=[VMEM] * 2,
            out_specs=(VMEM,) * 4,
            compiler_params=PARAMS,
        )(own_rows, other_rows)

    def turn(kernel, given, state, scratch=(), extra=(), flops=0):
        return pl.pallas_call(
            kernel,
            out_shape=tuple(shape(v.shape, v.dtype) for v in state) + tuple(extra),
            in_specs=[VMEM] * (len(given) + 2),
            out_specs=(VMEM,) * (2 + len(extra)),
            scratch_shapes=list(scratch),
            input_output_aliases={len(given): 0, len(given) + 1: 1},
            compiler_params=PARAMS,
            cost_estimate=pl.CostEstimate(flops=flops, bytes_accessed=0, transcendentals=0) if flops else None,
        )(*given, *state)

    late = jnp.zeros((2 * cols, sites + 2 * halo), bf16)
    mine = pairs - 1
    while mine > 0:
        if jumps and mine == jump:
            source, target = [2 * mine], [2 * mine - 4]
            next_in = cross(parts, source, target)
            own_in = lax.ppermute(parts, BOTH, link(source, target))
            beside_next = cross(lower[None], source, [2 * mine - 2])
            beside_own = lax.ppermute(lower, BOTH, link(source, [2 * mine - 2]))
            late, lower = turn(
                functools.partial(landing_kernel, mine - 2, sides), (next_in, own_in, both, high, low), (late, lower)
            )
            late, lower = turn(
                functools.partial(chain_kernel, mine - 1, sides),
                (beside_next, beside_own, both, high, low),
                (late, lower),
            )
            mine -= 2
            continue
        source, target = [2 * mine], [2 * mine - 2]
        next_in = cross(lower[None], source, target)
        own_in = lax.ppermute(lower, BOTH, link(source, target))
        mine -= 1
        if mine == 0:
            break
        if mine == pairs - 2:
            late, lower = turn(
                functools.partial(direct_kernel, mine, sides),
                (next_in, own_in, rim, far, far_high, far_low, rim_high, rim_low, near_high, near_low, const),
                (late, lower),
                [pltpu.VMEM((2 * cols, sites + 2 * edge), bf16)],
            )
        elif jumps and mine == jump:
            late, lower, parts = turn(
                functools.partial(jump_kernel, mine, sides),
                (next_in, own_in, both, high, low, own_rows, *ship),
                (late, lower),
                [pltpu.VMEM((2 * cols, sites), bf16)],
                [shape((2 * cols, sites), f32)],
            )
        else:
            late, lower = turn(
                functools.partial(chain_kernel, mine, sides),
                (next_in, own_in, both, high, low),
                (late, lower),
                flops=50 * 10**9 if jumps and mine == pairs - 3 else 0,
            )
    late, upper = pl.pallas_call(
        functools.partial(upper_kernel, sides, pairs - 1),
        out_shape=(shape(late.shape, bf16), shape(upper.shape, f32)),
        in_specs=[VMEM] * 7,
        out_specs=(VMEM,) * 2,
        input_output_aliases={5: 0, 6: 1},
        compiler_params=PARAMS,
    )(next_in, own_in, far, far_high, far_low, late, upper)
    returned = lax.ppermute(upper, BOTH, link(even, odd))
    lower = pl.pallas_call(
        last_kernel,
        out_shape=shape(lower.shape, f32),
        in_specs=[VMEM] * 5,
        out_specs=VMEM,
        input_output_aliases={4: 0},
        compiler_params=PARAMS,
        cost_estimate=pl.CostEstimate(flops=12 * cols * tall * length, bytes_accessed=8 * tall * length, transcendentals=0),
    )(both, high, low, late, lower)
    return jnp.where(device % 2 == 0, lower, returned)[None]


def solution(mesh):
    placed = (
        P("tm", None, "row"),
        P("tm", "row", None, None),
        P("tm", "row", None, None),
        P("tm", "row", None),
    )
    return jax.shard_map(
        local, mesh=mesh, in_specs=placed, out_specs=P("tm", None, "row"), check_vma=False
    )
```

```python
import functools

import jax
import jax.numpy as jnp
from jax import lax
from jax.experimental import pallas as pl
from jax.experimental.pallas import tpu as pltpu
from jax.sharding import PartitionSpec as P

BOTH = ("tm", "row")
VMEM = pl.BlockSpec(memory_space=pltpu.VMEM)
HBM = pl.BlockSpec(memory_space=pltpu.HBM)
PARAMS = pltpu.CompilerParams(vmem_limit_bytes=32 * 1024 * 1024)


def halves(value):
    high = value.astype(jnp.bfloat16)
    low = (value - high.astype(jnp.float32)).astype(jnp.bfloat16)
    return high, low


def dot(a, b):
    return jnp.dot(a, b, preferred_element_type=jnp.float32)


def stacked_dot(pair, cols, high, low):
    rows = pair.shape[0] // 2
    wide = dot(pair[:, cols], high)
    return wide[:rows] + wide[rows:] + dot(pair[:rows, cols], low)


def triple(high, low, inv_high, inv_low):
    return dot(high, inv_high) + dot(low, inv_high) + dot(high, inv_low)


def put_rim(sides, rim, columns):
    if sides == 1:
        row = lax.axis_index("row")

        @pl.when(row == 0)
        def _():
            rim[0] = columns(True)

        @pl.when(row != 0)
        def _():
            rim[0] = columns(False)
    else:
        rim[0] = columns(True)
        rim[1] = columns(False)


def const_kernel(
    mask, normals, inv, lag, const, inv_high, inv_low, lag_out, mask_out, normals_in, inv_in, sems
):
    blocks, length = inv.shape[1], inv.shape[2]
    moves = [pltpu.make_async_copy(normals.at[0], normals_in, sems.at[0])]
    for b in range(blocks):
        moves.append(pltpu.make_async_copy(inv.at[0, b], inv_in.at[b], sems.at[1 + b]))
    for b in range(blocks):
        moves.append(pltpu.make_async_copy(lag.at[0, b], lag_out.at[b], sems.at[1 + blocks + b]))
    moves.append(pltpu.make_async_copy(mask.at[0], mask_out, sems.at[1 + 2 * blocks]))
    for move in moves:
        move.start()
    moves[0].wait()
    for b in range(blocks):
        at = slice(b * length, (b + 1) * length)
        high, low = halves(normals_in[:, at])
        moves[1 + b].wait()
        inv_high[b], inv_low[b] = halves(inv_in[b])
        const[:, at] = triple(high, low, inv_high[b], inv_low[b])
    for move in moves[1 + blocks :]:
        move.wait()


def fuse_kernel(mask, const, inv_high, inv_low, lag, own, near_high, near_low):
    blocks, window, length = lag.shape
    edge = (window - length) // 2
    cols = const.shape[0]
    cuts = (0, edge, edge + length, window)
    flags = mask[...].astype(jnp.float32)
    for b in range(blocks):
        at = blocks * window + b * cols
        own[at : at + cols] = const[:, b * length : (b + 1) * length]
        for part in range(3):
            lo, hi = cuts[part], cuts[part + 1]
            rows = slice(b * window + lo, b * window + hi)
            high, low = halves(lag[b, lo:hi] * flags[b : b + 1, part : part + 1])
            value = triple(high, low, inv_high[b], inv_low[b])
            own[rows] = value
            near_high[rows], near_low[rows] = halves(value)


def edge_kernel(sides, blocks, cols, _own, own, rim):
    length, edge = own.shape[1], rim.shape[2]
    window = length + 2 * edge

    def columns(last):
        b = blocks - 1 if last else 0
        cut = slice(length - edge, length) if last else slice(0, edge)
        at = blocks * window + b * cols
        return jnp.concatenate([own[b * window : (b + 1) * window, cut], own[at : at + cols, cut]])

    put_rim(sides, rim, columns)


def split_kernel(rim, far, far_high, far_low, rim_high, rim_low):
    far_high[...], far_low[...] = halves(far[: far_high.shape[0]])
    for side in range(rim.shape[0]):
        rim_high[side], rim_low[side] = halves(rim[side, : rim_high.shape[1]])


def cuts_of(blocks, length, sites, span, last):
    packed, cuts = 0, []
    for b in range(blocks):
        start = span // 2 - length // 2 - b * length
        lo, hi = (start + sites, span) if last else (0, start)
        cuts.append((lo, hi, packed))
        packed += hi - lo
    return cuts


def pair_kernel(jump, rim, far, far_high, far_low, near_high, near_low, const, high, low, both, *rest):
    cols, sites = const.shape
    length = far.shape[1]
    blocks = sites // length
    window = near_high.shape[0] // blocks
    edge = (window - length) // 2
    span = 2 * window
    tall = blocks * window
    total = rest[-1]
    if rim.shape[0] == 1:
        flag = jnp.minimum(lax.axis_index("row"), 1).astype(jnp.float32)
        left, right = rim[0] * flag, rim[0] * (1 - flag)
    else:
        left, right = rim[0], rim[1]
    left_pair, right_pair = halves(left[:window]), halves(right[:window])
    for b in range(blocks):
        here = slice(b * window, (b + 1) * window)
        column = slice(b * length, (b + 1) * length)

        def part(lo, hi):
            rows = slice(b * window + lo, b * window + hi)
            return near_high[rows], near_low[rows]

        def constant(block):
            if block < 0:
                return left[window:]
            if block == blocks:
                return right[window:]
            return far[tall + block * cols : tall + (block + 1) * cols]

        if b > 0:
            before = slice((b - 1) * window, b * window)
            low_pair = far_high[before, length - edge :], far_low[before, length - edge :]
            low_const = constant(b - 1)[:, length - edge :]
        else:
            low_pair, low_const = left_pair, constant(-1)
        if b + 1 < blocks:
            after = slice((b + 1) * window, (b + 2) * window)
            high_pair = far_high[after, :edge], far_low[after, :edge]
            high_const = constant(b + 1)[:, :edge]
        else:
            high_pair, high_const = right_pair, constant(blocks)
        first = triple(*low_pair, *part(0, edge))
        middle = triple(far_high[here], far_low[here], *part(edge, edge + length))
        last = triple(*high_pair, *part(edge + length, window))
        total[:window] = first
        total[window:] = last
        total[length : length + window] += middle
        high[b * span : (b + 1) * span], low[b * span : (b + 1) * span] = halves(total[...])
        both[:, column] = const[:, column] - (
            triple(*halves(low_const), *part(0, edge))
            + triple(*halves(constant(b)), *part(edge, edge + length))
            + triple(*halves(high_const), *part(edge + length, window))
        )
    if jump:
        own_rows, other_rows = rest[:2]

        def value(start, count):
            rows = pl.ds(start, count)
            return high[rows].astype(jnp.float32) + low[rows].astype(jnp.float32)

        for b in range(blocks):
            own_rows[b * sites : (b + 1) * sites] = value(b * span + window - edge - b * length, sites)
            at = blocks * sites + b * cols
            own_rows[at : at + cols] = both[:, b * length : (b + 1) * length]
        starts = [
            [b * span + at for b, (lo, hi, _) in enumerate(cuts_of(blocks, length, sites, span, last)) for at in range(lo, hi, edge)]
            for last in (True, False)
        ]
        row = lax.axis_index("row")
        for chunk, (on_right, on_left) in enumerate(zip(*starts)):
            start = pl.multiple_of(jnp.where(row == 0, on_right, on_left), edge)
            other_rows[chunk * edge : (chunk + 1) * edge] = value(start, edge)


def keep(ref, start, value):
    cols, width = value.shape
    high, low = halves(value)
    ref[:cols, pl.ds(start, width)] = high
    ref[cols:, pl.ds(start, width)] = low


def load(sides, pick, own, halo, ref):
    sites = own.shape[1]
    ref[...] = jnp.zeros_like(ref)
    keep(ref, halo, own)
    for side in range(sides):
        on_right = 1 - jnp.minimum(lax.axis_index("row"), 1).astype(jnp.int32) if sides == 1 else side
        start = pl.multiple_of((1 - on_right) * (sites - halo), 128)
        keep(ref, pl.multiple_of(on_right * (halo + sites), 128), pick(side, pl.ds(start, halo)))


def plain(next_in):
    return lambda side, cut: next_in[side, :, cut]


def top_kernel(mine, sides, next_in, own_in, const, near_high, near_low, _upper, _lower, upper, lower, mid):
    sites = lower.shape[1]
    length = near_high.shape[1]
    blocks = sites // length
    window = near_high.shape[0] // blocks
    edge = (window - length) // 2

    @pl.when(lax.axis_index("tm") == 2 * mine)
    def _():
        load(sides, plain(next_in), own_in[...], edge, mid)
        upper[...] = own_in[...]
        for b in range(blocks):
            at, rows = slice(b * length, (b + 1) * length), slice(b * window, (b + 1) * window)
            product = stacked_dot(mid, slice(b * length, b * length + window), near_high[rows], near_low[rows])
            lower[:, at] = const[:, at] - product


def direct_kernel(
    mine, sides, next_in, own_in, rim, far, far_high, far_low, rim_high, rim_low, near_high, near_low, const,
    _late, _lower, late, lower, mid
):
    cols, sites = lower.shape
    length = near_high.shape[1]
    blocks = sites // length
    window = near_high.shape[0] // blocks
    edge = (window - length) // 2
    halo = length + edge

    @pl.when(lax.axis_index("tm") == 2 * mine)
    def _():
        load(sides, plain(next_in), own_in[...], halo, late)
        mid[...] = jnp.zeros_like(mid)
        for side in range(sides):
            on_right = 1 - jnp.minimum(lax.axis_index("row"), 1).astype(jnp.int32) if sides == 1 else side
            start = pl.multiple_of(on_right * (2 * halo + sites - window), 128)
            product = stacked_dot(late, pl.ds(start, window), rim_high[side], rim_low[side])
            keep(mid, pl.multiple_of(on_right * (edge + sites), 128), rim[side, window:] - product)
        for b in range(blocks):
            rows, start = slice(b * window, (b + 1) * window), halo - edge + b * length
            at = blocks * window + b * cols
            product = stacked_dot(late, slice(start, start + window), far_high[rows], far_low[rows])
            keep(mid, edge + b * length, far[at : at + cols] - product)
        for b in range(blocks):
            at, rows = slice(b * length, (b + 1) * length), slice(b * window, (b + 1) * window)
            product = stacked_dot(mid, slice(b * length, b * length + window), near_high[rows], near_low[rows])
            lower[:, at] = const[:, at] - product


def step(both, high, low, late, lower):
    blocks = lower.shape[1] // high.shape[1]
    length, span = high.shape[1], high.shape[0] // blocks
    for b in range(blocks):
        at, rows = slice(b * length, (b + 1) * length), slice(b * span, (b + 1) * span)
        lower[:, at] = both[:, at] + stacked_dot(late, slice(b * length, b * length + span), high[rows], low[rows])


def chain_kernel(mine, sides, next_in, own_in, both, high, low, _late, _lower, late, lower):
    @pl.when(lax.axis_index("tm") == 2 * mine)
    def _():
        load(sides, plain(next_in), own_in[...], (late.shape[1] - own_in.shape[1]) // 2, late)
        step(both, high, low, late, lower)


def rows_kernel(own_rows, other_rows, own_high, own_low, other_high, other_low):
    own_high[...], own_low[...] = halves(own_rows[: own_high.shape[0]])
    other_high[...], other_low[...] = halves(other_rows[...])


def jump_kernel(
    mine, sides, next_in, own_in, both, high, low, own_rows, own_high, own_low, other_high, other_low,
    _late, _lower, late, lower, parts, mid
):
    cols, sites = lower.shape
    length = high.shape[1]
    blocks = sites // length
    span = high.shape[0] // blocks

    @pl.when(lax.axis_index("tm") != 2 * mine)
    def _():
        parts[...] = jnp.zeros_like(parts)

    @pl.when(lax.axis_index("tm") == 2 * mine)
    def _():
        load(sides, plain(next_in), own_in[...], (late.shape[1] - sites) // 2, late)
        step(both, high, low, late, lower)
        keep(mid, 0, lower[...])
        for b in range(blocks):
            at, rows = slice(b * length, (b + 1) * length), slice(b * sites, (b + 1) * sites)
            const = slice(blocks * sites + b * cols, blocks * sites + (b + 1) * cols)
            parts[:cols, at] = own_rows[const] + stacked_dot(mid, slice(0, sites), own_high[rows], own_low[rows])
        for last in (True, False):

            @pl.when((lax.axis_index("row") == 0) != last)
            def _():
                for b, (lo, hi, packed) in enumerate(cuts_of(blocks, length, sites, span, last)):
                    from_sites = slice(0, hi - lo) if last else slice(sites - (hi - lo), sites)
                    rows = slice(packed, packed + hi - lo)
                    parts[cols:, b * length : (b + 1) * length] = stacked_dot(
                        mid, from_sites, other_high[rows], other_low[rows]
                    )


def last_kernel(jumps, both, high, low, late, _lower, lower):
    device = lax.axis_index("tm")
    pl.when((device == 0) | (device == 2) if jumps else device == 0)(lambda: step(both, high, low, late, lower))


def upper_kernel(sides, top, jumps, next_in, own_in, *rest):
    if jumps:
        beside_next, beside_own = rest[:2]
    far, far_high, far_low, _late, _upper, late, upper = rest[-7:]
    cols, sites = upper.shape
    length = far.shape[1]
    blocks = sites // length
    window = far_high.shape[0] // blocks
    halo = (late.shape[1] - sites) // 2
    at_window = halo - (window - length) // 2

    @pl.when(lax.axis_index("tm") == 0)
    def _():
        if jumps:
            own = own_in[:cols] + next_in[cols:]
            load(sides, lambda side, cut: next_in[:cols, cut] + own_in[cols:, cut], own, halo, late)
        else:
            load(sides, plain(next_in), own_in[...], halo, late)

    if jumps:

        @pl.when(lax.axis_index("tm") == 2)
        def _():
            load(sides, plain(beside_next), beside_own[...], halo, late)

    @pl.when(lax.axis_index("tm") != 2 * top)
    def _():
        for b in range(blocks):
            rows = slice(b * window, (b + 1) * window)
            at = blocks * window + b * cols
            start = at_window + b * length
            upper[:, b * length : (b + 1) * length] = far[at : at + cols] - stacked_dot(
                late, slice(start, start + window), far_high[rows], far_low[rows]
            )


def local(normals, inv_diag, lag_coupling, fill_mask):
    times, rows = lax.axis_size("tm"), lax.axis_size("row")
    device = lax.axis_index("tm")
    cols, sites = normals.shape[1:]
    blocks, length = inv_diag.shape[1:3]
    window = lag_coupling.shape[2]
    edge = (window - length) // 2
    halo = length + edge
    sides = 1 if rows == 2 else 2
    pairs = times // 2
    f32, bf16 = jnp.float32, jnp.bfloat16
    shape = jax.ShapeDtypeStruct

    def link(source, target):
        return [(s * rows + r, t * rows + r) for s, t in zip(source, target) for r in range(rows)]

    def cross(value, source, target):
        if sides == 1:
            perm = [(s * rows + r, t * rows + 1 - r) for s, t in zip(source, target) for r in range(2)]
            return lax.ppermute(value, BOTH, perm)
        moved = []
        for side, step in enumerate((1, -1)):
            perm = [
                (s * rows + r, t * rows + r + step)
                for s, t in zip(source, target)
                for r in range(rows)
                if 0 <= r + step < rows
            ]
            moved.append(lax.ppermute(value[side : side + 1] if value.shape[0] > 1 else value, BOTH, perm))
        return jnp.concatenate(moved)

    tall = blocks * window
    jump = 2
    jumps = rows == 2 and pairs > 5
    const, inv_high, inv_low, lag, mask = pl.pallas_call(
        const_kernel,
        out_shape=(
            shape((cols, sites), f32),
            shape((blocks, length, length), bf16), shape((blocks, length, length), bf16),
            shape(lag_coupling.shape[1:], f32), shape(fill_mask.shape[1:], fill_mask.dtype),
        ),
        in_specs=[HBM] * 4,
        out_specs=(VMEM,) * 5,
        scratch_shapes=[
            pltpu.VMEM(normals.shape[1:], f32),
            pltpu.VMEM(inv_diag.shape[1:], f32),
            pltpu.SemaphoreType.DMA((2 + 2 * blocks,)),
        ],
        compiler_params=PARAMS,
    )(*[pltpu.with_memory_space_constraint(a, pltpu.HBM) for a in (fill_mask, normals, inv_diag, lag_coupling)])
    odd, even = range(1, times, 2), range(0, times, 2)
    first_next = cross(const[None], odd[-1:], even[-1:])
    first_own = lax.ppermute(const, BOTH, link(odd[-1:], even[-1:]))
    near, near_high, near_low = pl.pallas_call(
        fuse_kernel,
        out_shape=(
            shape((tall + blocks * cols, length), f32), shape((tall, length), bf16), shape((tall, length), bf16),
        ),
        in_specs=[VMEM] * 5,
        out_specs=(VMEM,) * 3,
        compiler_params=PARAMS,
        cost_estimate=pl.CostEstimate(
            flops=6 * (tall + cols * blocks) * length * length, bytes_accessed=16 * tall * length, transcendentals=0
        ),
    )(mask, const, inv_high, inv_low, lag)
    near, edges = pl.pallas_call(
        functools.partial(edge_kernel, sides, blocks, cols),
        out_shape=(shape(near.shape, f32), shape((sides, window + cols, edge), f32)),
        in_specs=[VMEM],
        out_specs=(VMEM,) * 2,
        input_output_aliases={0: 0},
        compiler_params=PARAMS,
    )(near)
    rim = cross(edges, odd[:-1], even[:-1])
    far = lax.ppermute(near, BOTH, link(odd[:-1], even[:-1]))

    blank = jnp.zeros((cols, sites), f32)
    upper, lower = pl.pallas_call(
        functools.partial(top_kernel, pairs - 1, sides),
        out_shape=(shape((cols, sites), f32),) * 2,
        in_specs=[VMEM] * 7,
        out_specs=(VMEM,) * 2,
        scratch_shapes=[pltpu.VMEM((2 * cols, sites + 2 * edge), bf16)],
        input_output_aliases={5: 0, 6: 1},
        compiler_params=PARAMS,
        cost_estimate=pl.CostEstimate(flops=50 * 10**9, bytes_accessed=0, transcendentals=0),
    )(first_next, first_own, const, near_high, near_low, blank, blank)
    far_high, far_low, rim_high, rim_low = pl.pallas_call(
        split_kernel,
        out_shape=(
            shape((tall, length), bf16), shape((tall, length), bf16),
            shape((sides, window, edge), bf16), shape((sides, window, edge), bf16),
        ),
        in_specs=[VMEM] * 2,
        out_specs=(VMEM,) * 4,
        compiler_params=PARAMS,
    )(rim, far)
    packs = (shape((blocks * (sites + cols), length), f32), shape((halo + edge, length), f32)) if jumps else ()
    high, low, both, *packs = pl.pallas_call(
        functools.partial(pair_kernel, jumps),
        out_shape=(
            shape((2 * tall, length), bf16), shape((2 * tall, length), bf16), shape((cols, sites), f32), *packs
        ),
        in_specs=[VMEM] * 7,
        out_specs=(VMEM,) * (3 + len(packs)),
        scratch_shapes=[pltpu.VMEM((2 * window, length), f32)],
        compiler_params=PARAMS,
        cost_estimate=pl.CostEstimate(flops=10**9, bytes_accessed=0, transcendentals=0),
    )(rim, far, far_high, far_low, near_high, near_low, const)
    if jumps:
        source, target = [2 * jump - 2], [2 * jump]
        own_rows = lax.ppermute(packs[0], BOTH, link(source, target))
        other_rows = cross(packs[1], source, target)
        ship = pl.pallas_call(
            rows_kernel,
            out_shape=(shape((blocks * sites, length), bf16),) * 2 + (shape(other_rows.shape, bf16),) * 2,
            in_specs=[VMEM] * 2,
            out_specs=(VMEM,) * 4,
            compiler_params=PARAMS,
        )(own_rows, other_rows)

    def turn(kernel, given, state, scratch=(), extra=(), flops=0):
        return pl.pallas_call(
            kernel,
            out_shape=tuple(shape(v.shape, v.dtype) for v in state) + tuple(extra),
            in_specs=[VMEM] * (len(given) + 2),
            out_specs=(VMEM,) * (2 + len(extra)),
            scratch_shapes=list(scratch),
            input_output_aliases={len(given): 0, len(given) + 1: 1},
            compiler_params=PARAMS,
            cost_estimate=pl.CostEstimate(flops=flops, bytes_accessed=0, transcendentals=0) if flops else None,
        )(*given, *state)

    late = jnp.zeros((2 * cols, sites + 2 * halo), bf16)
    mine = pairs - 1
    while mine > 0:
        if jumps and mine == jump:
            source, target = [2 * mine], [2 * mine - 4]
            next_in = cross(parts, source, target)
            own_in = lax.ppermute(parts, BOTH, link(source, target))
            beside_next = cross(lower[None], source, [2 * mine - 2])
            beside_own = lax.ppermute(lower, BOTH, link(source, [2 * mine - 2]))
            break
        source, target = [2 * mine], [2 * mine - 2]
        next_in = cross(lower[None], source, target)
        own_in = lax.ppermute(lower, BOTH, link(source, target))
        mine -= 1
        if mine == 0:
            break
        if mine == pairs - 2:
            late, lower = turn(
                functools.partial(direct_kernel, mine, sides),
                (next_in, own_in, rim, far, far_high, far_low, rim_high, rim_low, near_high, near_low, const),
                (late, lower),
                [pltpu.VMEM((2 * cols, sites + 2 * edge), bf16)],
            )
        elif jumps and mine == jump:
            late, lower, parts = turn(
                functools.partial(jump_kernel, mine, sides),
                (next_in, own_in, both, high, low, own_rows, *ship),
                (late, lower),
                [pltpu.VMEM((2 * cols, sites), bf16)],
                [shape((2 * cols, sites), f32)],
            )
        else:
            late, lower = turn(
                functools.partial(chain_kernel, mine, sides),
                (next_in, own_in, both, high, low),
                (late, lower),
                flops=50 * 10**9 if jumps and mine == pairs - 3 else 0,
            )
    given = (next_in, own_in) + ((beside_next, beside_own) if jumps else ())
    late, upper = turn(
        functools.partial(upper_kernel, sides, pairs - 1, jumps), (*given, far, far_high, far_low), (late, upper)
    )
    returned = lax.ppermute(upper, BOTH, link(even, odd))
    lower = pl.pallas_call(
        functools.partial(last_kernel, jumps),
        out_shape=shape(lower.shape, f32),
        in_specs=[VMEM] * 5,
        out_specs=VMEM,
        input_output_aliases={4: 0},
        compiler_params=PARAMS,
        cost_estimate=pl.CostEstimate(flops=12 * cols * tall * length, bytes_accessed=8 * tall * length, transcendentals=0),
    )(both, high, low, late, lower)
    return jnp.where(device % 2 == 0, lower, returned)[None]


def solution(mesh):
    placed = (
        P("tm", None, "row"),
        P("tm", "row", None, None),
        P("tm", "row", None, None),
        P("tm", "row", None),
    )
    return jax.shard_map(
        local, mesh=mesh, in_specs=placed, out_specs=P("tm", None, "row"), check_vma=False
    )
```

```python
import functools

import jax
import jax.numpy as jnp
from jax import lax
from jax.experimental import pallas as pl
from jax.experimental.pallas import tpu as pltpu
from jax.sharding import PartitionSpec as P

BOTH = ("tm", "row")
VMEM = pl.BlockSpec(memory_space=pltpu.VMEM)
HBM = pl.BlockSpec(memory_space=pltpu.HBM)
PARAMS = pltpu.CompilerParams(vmem_limit_bytes=32 * 1024 * 1024)


def halves(value):
    high = value.astype(jnp.bfloat16)
    low = (value - high.astype(jnp.float32)).astype(jnp.bfloat16)
    return high, low


def dot(a, b):
    return jnp.dot(a, b, preferred_element_type=jnp.float32)


def stacked_dot(pair, cols, high, low):
    rows = pair.shape[0] // 2
    wide = dot(pair[:, cols], high)
    return wide[:rows] + wide[rows:] + dot(pair[:rows, cols], low)


def triple(high, low, inv_high, inv_low):
    return dot(high, inv_high) + dot(low, inv_high) + dot(high, inv_low)


def put_rim(sides, rim, columns):
    if sides == 1:
        row = lax.axis_index("row")

        @pl.when(row == 0)
        def _():
            rim[0] = columns(True)

        @pl.when(row != 0)
        def _():
            rim[0] = columns(False)
    else:
        rim[0] = columns(True)
        rim[1] = columns(False)


def const_kernel(
    mask, normals, inv, lag, const, inv_high, inv_low, lag_out, mask_out, normals_in, inv_in, sems
):
    blocks, length = inv.shape[1], inv.shape[2]
    moves = [pltpu.make_async_copy(normals.at[0], normals_in, sems.at[0])]
    for b in range(blocks):
        moves.append(pltpu.make_async_copy(inv.at[0, b], inv_in.at[b], sems.at[1 + b]))
    for b in range(blocks):
        moves.append(pltpu.make_async_copy(lag.at[0, b], lag_out.at[b], sems.at[1 + blocks + b]))
    moves.append(pltpu.make_async_copy(mask.at[0], mask_out, sems.at[1 + 2 * blocks]))
    for move in moves:
        move.start()
    moves[0].wait()
    for b in range(blocks):
        at = slice(b * length, (b + 1) * length)
        high, low = halves(normals_in[:, at])
        moves[1 + b].wait()
        inv_high[b], inv_low[b] = halves(inv_in[b])
        const[:, at] = triple(high, low, inv_high[b], inv_low[b])
    for move in moves[1 + blocks :]:
        move.wait()


def fuse_kernel(mask, const, inv_high, inv_low, lag, own, near_high, near_low):
    blocks, window, length = lag.shape
    edge = (window - length) // 2
    cols = const.shape[0]
    cuts = (0, edge, edge + length, window)
    flags = mask[...].astype(jnp.float32)
    for b in range(blocks):
        at = blocks * window + b * cols
        own[at : at + cols] = const[:, b * length : (b + 1) * length]
        for part in range(3):
            lo, hi = cuts[part], cuts[part + 1]
            rows = slice(b * window + lo, b * window + hi)
            high, low = halves(lag[b, lo:hi] * flags[b : b + 1, part : part + 1])
            value = triple(high, low, inv_high[b], inv_low[b])
            own[rows] = value
            near_high[rows], near_low[rows] = halves(value)


def edge_kernel(sides, blocks, cols, _own, own, rim):
    length, edge = own.shape[1], rim.shape[2]
    window = length + 2 * edge

    def columns(last):
        b = blocks - 1 if last else 0
        cut = slice(length - edge, length) if last else slice(0, edge)
        at = blocks * window + b * cols
        return jnp.concatenate([own[b * window : (b + 1) * window, cut], own[at : at + cols, cut]])

    put_rim(sides, rim, columns)


def split_kernel(rim, far, far_high, far_low, rim_high, rim_low):
    far_high[...], far_low[...] = halves(far[: far_high.shape[0]])
    for side in range(rim.shape[0]):
        rim_high[side], rim_low[side] = halves(rim[side, : rim_high.shape[1]])


def cuts_of(blocks, length, sites, span, last):
    packed, cuts = 0, []
    for b in range(blocks):
        start = span // 2 - length // 2 - b * length
        lo, hi = (start + sites, span) if last else (0, start)
        cuts.append((lo, hi, packed))
        packed += hi - lo
    return cuts


def pair_kernel(jump, rim, far, far_high, far_low, near_high, near_low, const, high, low, both, *rest):
    cols, sites = const.shape
    length = far.shape[1]
    blocks = sites // length
    window = near_high.shape[0] // blocks
    edge = (window - length) // 2
    span = 2 * window
    tall = blocks * window
    total = rest[-1]
    if rim.shape[0] == 1:
        flag = jnp.minimum(lax.axis_index("row"), 1).astype(jnp.float32)
        left, right = rim[0] * flag, rim[0] * (1 - flag)
    else:
        left, right = rim[0], rim[1]
    left_pair, right_pair = halves(left[:window]), halves(right[:window])
    for b in range(blocks):
        here = slice(b * window, (b + 1) * window)
        column = slice(b * length, (b + 1) * length)

        def part(lo, hi):
            rows = slice(b * window + lo, b * window + hi)
            return near_high[rows], near_low[rows]

        def constant(block):
            if block < 0:
                return left[window:]
            if block == blocks:
                return right[window:]
            return far[tall + block * cols : tall + (block + 1) * cols]

        if b > 0:
            before = slice((b - 1) * window, b * window)
            low_pair = far_high[before, length - edge :], far_low[before, length - edge :]
            low_const = constant(b - 1)[:, length - edge :]
        else:
            low_pair, low_const = left_pair, constant(-1)
        if b + 1 < blocks:
            after = slice((b + 1) * window, (b + 2) * window)
            high_pair = far_high[after, :edge], far_low[after, :edge]
            high_const = constant(b + 1)[:, :edge]
        else:
            high_pair, high_const = right_pair, constant(blocks)
        first = triple(*low_pair, *part(0, edge))
        middle = triple(far_high[here], far_low[here], *part(edge, edge + length))
        last = triple(*high_pair, *part(edge + length, window))
        total[:window] = first
        total[window:] = last
        total[length : length + window] += middle
        high[b * span : (b + 1) * span], low[b * span : (b + 1) * span] = halves(total[...])
        both[:, column] = const[:, column] - (
            triple(*halves(low_const), *part(0, edge))
            + triple(*halves(constant(b)), *part(edge, edge + length))
            + triple(*halves(high_const), *part(edge + length, window))
        )
    if jump:
        own_rows, other_rows = rest[:2]

        def value(start, count):
            rows = pl.ds(start, count)
            return high[rows].astype(jnp.float32) + low[rows].astype(jnp.float32)

        for b in range(blocks):
            own_rows[b * sites : (b + 1) * sites] = value(b * span + window - edge - b * length, sites)
            at = blocks * sites + b * cols
            own_rows[at : at + cols] = both[:, b * length : (b + 1) * length]
        starts = [
            [b * span + at for b, (lo, hi, _) in enumerate(cuts_of(blocks, length, sites, span, last)) for at in range(lo, hi, edge)]
            for last in (True, False)
        ]
        row = lax.axis_index("row")
        for chunk, (on_right, on_left) in enumerate(zip(*starts)):
            start = pl.multiple_of(jnp.where(row == 0, on_right, on_left), edge)
            other_rows[chunk * edge : (chunk + 1) * edge] = value(start, edge)


def keep(ref, start, value):
    cols, width = value.shape
    high, low = halves(value)
    ref[:cols, pl.ds(start, width)] = high
    ref[cols:, pl.ds(start, width)] = low


def load(sides, pick, own, halo, ref):
    sites = own.shape[1]
    ref[...] = jnp.zeros_like(ref)
    keep(ref, halo, own)
    for side in range(sides):
        on_right = 1 - jnp.minimum(lax.axis_index("row"), 1).astype(jnp.int32) if sides == 1 else side
        start = pl.multiple_of((1 - on_right) * (sites - halo), 128)
        keep(ref, pl.multiple_of(on_right * (halo + sites), 128), pick(side, pl.ds(start, halo)))


def plain(next_in):
    return lambda side, cut: next_in[:, cut] if len(next_in.shape) == 2 else next_in[side, :, cut]


def top_kernel(mine, sides, own_in, next_in, const, near_high, near_low, _upper, _lower, upper, lower, mid):
    sites = lower.shape[1]
    length = near_high.shape[1]
    blocks = sites // length
    window = near_high.shape[0] // blocks
    edge = (window - length) // 2

    @pl.when(lax.axis_index("tm") == 2 * mine)
    def _():
        load(sides, plain(next_in), own_in[...], edge, mid)
        upper[...] = own_in[...]
        for b in range(blocks):
            at, rows = slice(b * length, (b + 1) * length), slice(b * window, (b + 1) * window)
            product = stacked_dot(mid, slice(b * length, b * length + window), near_high[rows], near_low[rows])
            lower[:, at] = const[:, at] - product


def direct_kernel(
    mine, sides, own_in, next_in, rim, far, far_high, far_low, rim_high, rim_low, near_high, near_low, const,
    _late, _lower, late, lower, mid
):
    cols, sites = lower.shape
    length = near_high.shape[1]
    blocks = sites // length
    window = near_high.shape[0] // blocks
    edge = (window - length) // 2
    halo = length + edge

    @pl.when(lax.axis_index("tm") == 2 * mine)
    def _():
        load(sides, plain(next_in), own_in[...], halo, late)
        mid[...] = jnp.zeros_like(mid)
        for side in range(sides):
            on_right = 1 - jnp.minimum(lax.axis_index("row"), 1).astype(jnp.int32) if sides == 1 else side
            start = pl.multiple_of(on_right * (2 * halo + sites - window), 128)
            product = stacked_dot(late, pl.ds(start, window), rim_high[side], rim_low[side])
            keep(mid, pl.multiple_of(on_right * (edge + sites), 128), rim[side, window:] - product)
        for b in range(blocks):
            rows, start = slice(b * window, (b + 1) * window), halo - edge + b * length
            at = blocks * window + b * cols
            product = stacked_dot(late, slice(start, start + window), far_high[rows], far_low[rows])
            keep(mid, edge + b * length, far[at : at + cols] - product)
        for b in range(blocks):
            at, rows = slice(b * length, (b + 1) * length), slice(b * window, (b + 1) * window)
            product = stacked_dot(mid, slice(b * length, b * length + window), near_high[rows], near_low[rows])
            lower[:, at] = const[:, at] - product


def step(both, high, low, late, lower):
    blocks = lower.shape[1] // high.shape[1]
    length, span = high.shape[1], high.shape[0] // blocks
    for b in range(blocks):
        at, rows = slice(b * length, (b + 1) * length), slice(b * span, (b + 1) * span)
        lower[:, at] = both[:, at] + stacked_dot(late, slice(b * length, b * length + span), high[rows], low[rows])


def chain_kernel(mine, sides, own_in, next_in, both, high, low, _late, _lower, late, lower):
    @pl.when(lax.axis_index("tm") == 2 * mine)
    def _():
        load(sides, plain(next_in), own_in[...], (late.shape[1] - own_in.shape[1]) // 2, late)
        step(both, high, low, late, lower)


def rows_kernel(own_rows, other_rows, own_high, own_low, other_high, other_low):
    own_high[...], own_low[...] = halves(own_rows[: own_high.shape[0]])
    other_high[...], other_low[...] = halves(other_rows[...])


def add_parts(lower, own_rows, own_high, own_low, other_high, other_low, parts, mid, span):
    cols, sites = lower.shape
    length = own_rows.shape[1]
    blocks = sites // length
    keep(mid, 0, lower[...])
    for b in range(blocks):
        at, rows = slice(b * length, (b + 1) * length), slice(b * sites, (b + 1) * sites)
        const = slice(blocks * sites + b * cols, blocks * sites + (b + 1) * cols)
        parts[:cols, at] = own_rows[const] + stacked_dot(mid, slice(0, sites), own_high[rows], own_low[rows])
    for last in (True, False):

        @pl.when((lax.axis_index("row") == 0) != last)
        def _():
            for b, (lo, hi, packed) in enumerate(cuts_of(blocks, length, sites, span, last)):
                from_sites = slice(0, hi - lo) if last else slice(sites - (hi - lo), sites)
                rows = slice(packed, packed + hi - lo)
                parts[cols:, b * length : (b + 1) * length] = stacked_dot(
                    mid, from_sites, other_high[rows], other_low[rows]
                )


def jump_kernel(mine, sides, own_in, next_in, both, high, low, *rest):
    ship, (_late, _lower, late, lower, parts, mid) = rest[:-6], rest[-6:]

    @pl.when(lax.axis_index("tm") == 2 * mine)
    def _():
        load(sides, plain(next_in), own_in[...], (late.shape[1] - own_in.shape[1]) // 2, late)
        step(both, high, low, late, lower)
        add_parts(lower, *ship, parts, mid, high.shape[0] * high.shape[1] // own_in.shape[1])

    @pl.when(lax.axis_index("tm") != 2 * mine)
    def _():
        parts[...] = jnp.zeros_like(parts)


def parts_kernel(mine, span, lower, *rest):
    ship, (parts, mid) = rest[:-2], rest[-2:]

    @pl.when(lax.axis_index("tm") == 2 * mine)
    def _():
        add_parts(lower, *ship, parts, mid, span)

    @pl.when(lax.axis_index("tm") != 2 * mine)
    def _():
        parts[...] = jnp.zeros_like(parts)


def last_kernel(jumps, both, high, low, late, _lower, lower):
    device = lax.axis_index("tm")
    pl.when((device == 0) | (device == 2) if jumps else device == 0)(lambda: step(both, high, low, late, lower))


def upper_kernel(sides, top, *rest):
    far, far_high, far_low, _late, _upper, late, upper = rest[-7:]
    cols, sites = upper.shape
    length = far.shape[1]
    blocks = sites // length
    window = far_high.shape[0] // blocks
    halo = (late.shape[1] - sites) // 2
    at_window = halo - (window - length) // 2

    def take(mine, own_in, next_in):
        @pl.when(lax.axis_index("tm") == 2 * mine)
        def _():
            if own_in.shape[0] == cols:
                load(sides, plain(next_in), own_in[...], halo, late)
            else:
                own = own_in[:cols] + next_in[cols:]
                load(sides, lambda side, cut: next_in[:cols, cut] + own_in[cols:, cut], own, halo, late)

    messages = rest[:-7]
    for mine in range(len(messages) // 2):
        take(mine, *messages[2 * mine : 2 * mine + 2])

    @pl.when(lax.axis_index("tm") != 2 * top)
    def _():
        for b in range(blocks):
            rows = slice(b * window, (b + 1) * window)
            at = blocks * window + b * cols
            start = at_window + b * length
            upper[:, b * length : (b + 1) * length] = far[at : at + cols] - stacked_dot(
                late, slice(start, start + window), far_high[rows], far_low[rows]
            )


def local(normals, inv_diag, lag_coupling, fill_mask):
    times, rows = lax.axis_size("tm"), lax.axis_size("row")
    device = lax.axis_index("tm")
    cols, sites = normals.shape[1:]
    blocks, length = inv_diag.shape[1:3]
    window = lag_coupling.shape[2]
    edge = (window - length) // 2
    halo = length + edge
    sides = 1 if rows == 2 else 2
    pairs = times // 2
    f32, bf16 = jnp.float32, jnp.bfloat16
    shape = jax.ShapeDtypeStruct

    def link(source, target):
        return [(s * rows + r, t * rows + r) for s, t in zip(source, target) for r in range(rows)]

    def cross(value, source, target, split=False):
        if sides == 1:
            perm = [(s * rows + r, t * rows + 1 - r) for s, t in zip(source, target) for r in range(2)]
            return lax.ppermute(value, BOTH, perm)
        moved = []
        for side, step in enumerate((1, -1)):
            perm = [
                (s * rows + r, t * rows + r + step)
                for s, t in zip(source, target)
                for r in range(rows)
                if 0 <= r + step < rows
            ]
            moved.append(lax.ppermute(value[side : side + 1] if split else value[None], BOTH, perm))
        return jnp.concatenate(moved)

    tall = blocks * window
    jump = 2
    jumps = rows == 2 and pairs > 5
    const, inv_high, inv_low, lag, mask = pl.pallas_call(
        const_kernel,
        out_shape=(
            shape((cols, sites), f32),
            shape((blocks, length, length), bf16), shape((blocks, length, length), bf16),
            shape(lag_coupling.shape[1:], f32), shape(fill_mask.shape[1:], fill_mask.dtype),
        ),
        in_specs=[HBM] * 4,
        out_specs=(VMEM,) * 5,
        scratch_shapes=[
            pltpu.VMEM(normals.shape[1:], f32),
            pltpu.VMEM(inv_diag.shape[1:], f32),
            pltpu.SemaphoreType.DMA((2 + 2 * blocks,)),
        ],
        compiler_params=PARAMS,
    )(*[pltpu.with_memory_space_constraint(a, pltpu.HBM) for a in (fill_mask, normals, inv_diag, lag_coupling)])
    odd, even = range(1, times, 2), range(0, times, 2)
    first_next = cross(const, odd[-1:], even[-1:])
    first_own = lax.ppermute(const, BOTH, link(odd[-1:], even[-1:]))
    near, near_high, near_low = pl.pallas_call(
        fuse_kernel,
        out_shape=(
            shape((tall + blocks * cols, length), f32), shape((tall, length), bf16), shape((tall, length), bf16),
        ),
        in_specs=[VMEM] * 5,
        out_specs=(VMEM,) * 3,
        compiler_params=PARAMS,
        cost_estimate=pl.CostEstimate(
            flops=6 * (tall + cols * blocks) * length * length, bytes_accessed=16 * tall * length, transcendentals=0
        ),
    )(mask, const, inv_high, inv_low, lag)
    near, edges = pl.pallas_call(
        functools.partial(edge_kernel, sides, blocks, cols),
        out_shape=(shape(near.shape, f32), shape((sides, window + cols, edge), f32)),
        in_specs=[VMEM],
        out_specs=(VMEM,) * 2,
        input_output_aliases={0: 0},
        compiler_params=PARAMS,
    )(near)
    rim = cross(edges, odd[:-1], even[:-1], True)
    far = lax.ppermute(near, BOTH, link(odd[:-1], even[:-1]))

    blank = jnp.zeros((cols, sites), f32)
    upper, lower = pl.pallas_call(
        functools.partial(top_kernel, pairs - 1, sides),
        out_shape=(shape((cols, sites), f32),) * 2,
        in_specs=[VMEM] * 7,
        out_specs=(VMEM,) * 2,
        scratch_shapes=[pltpu.VMEM((2 * cols, sites + 2 * edge), bf16)],
        input_output_aliases={5: 0, 6: 1},
        compiler_params=PARAMS,
        cost_estimate=pl.CostEstimate(flops=50 * 10**9, bytes_accessed=0, transcendentals=0),
    )(first_own, first_next, const, near_high, near_low, blank, blank)
    far_high, far_low, rim_high, rim_low = pl.pallas_call(
        split_kernel,
        out_shape=(
            shape((tall, length), bf16), shape((tall, length), bf16),
            shape((sides, window, edge), bf16), shape((sides, window, edge), bf16),
        ),
        in_specs=[VMEM] * 2,
        out_specs=(VMEM,) * 4,
        compiler_params=PARAMS,
    )(rim, far)
    packs = (shape((blocks * (sites + cols), length), f32), shape((halo + edge, length), f32)) if jumps else ()
    high, low, both, *packs = pl.pallas_call(
        functools.partial(pair_kernel, jumps),
        out_shape=(
            shape((2 * tall, length), bf16), shape((2 * tall, length), bf16), shape((cols, sites), f32), *packs
        ),
        in_specs=[VMEM] * 7,
        out_specs=(VMEM,) * (3 + len(packs)),
        scratch_shapes=[pltpu.VMEM((2 * window, length), f32)],
        compiler_params=PARAMS,
        cost_estimate=pl.CostEstimate(flops=10**9, bytes_accessed=0, transcendentals=0),
    )(rim, far, far_high, far_low, near_high, near_low, const)
    if jumps:
        source, target = [2 * jump - 2, 2 * jump], [2 * jump, 2 * jump + 2]
        own_rows = lax.ppermute(packs[0], BOTH, link(source, target))
        other_rows = cross(packs[1], source, target)
        ship = pl.pallas_call(
            rows_kernel,
            out_shape=(shape((blocks * sites, length), bf16),) * 2 + (shape(other_rows.shape, bf16),) * 2,
            in_specs=[VMEM] * 2,
            out_specs=(VMEM,) * 4,
            compiler_params=PARAMS,
        )(own_rows, other_rows)

    def turn(kernel, given, state, scratch=(), extra=(), flops=0):
        return pl.pallas_call(
            kernel,
            out_shape=tuple(shape(v.shape, v.dtype) for v in state) + tuple(extra),
            in_specs=[VMEM] * (len(given) + 2),
            out_specs=(VMEM,) * (2 + len(extra)),
            scratch_shapes=list(scratch),
            input_output_aliases={len(given): 0, len(given) + 1: 1},
            compiler_params=PARAMS,
            cost_estimate=pl.CostEstimate(flops=flops, bytes_accessed=0, transcendentals=0) if flops else None,
        )(*given, *state)

    late = jnp.zeros((2 * cols, sites + 2 * halo), bf16)
    mine = pairs - 1
    while mine > 0:
        if jumps and mine == jump:
            source, target = [2 * mine], [2 * mine - 4]
            next_in = cross(parts, source, target)
            own_in = lax.ppermute(parts, BOTH, link(source, target))
            break
        source, target = [2 * mine], [2 * mine - 2]
        next_in = cross(lower, source, target)
        own_in = lax.ppermute(lower, BOTH, link(source, target))
        if jumps and mine == jump + 1:
            beside = pl.pallas_call(
                functools.partial(parts_kernel, mine, 2 * window),
                out_shape=shape((2 * cols, sites), f32),
                in_specs=[VMEM] * 6,
                out_specs=VMEM,
                scratch_shapes=[pltpu.VMEM((2 * cols, sites), bf16)],
                compiler_params=PARAMS,
            )(lower, own_rows, *ship)
            source, target = [2 * mine], [2 * mine - 4]
            beside_next = cross(beside, source, target)
            beside_own = lax.ppermute(beside, BOTH, link(source, target))
        mine -= 1
        if mine == 0:
            break
        if mine == pairs - 2:
            late, lower = turn(
                functools.partial(direct_kernel, mine, sides),
                (own_in, next_in, rim, far, far_high, far_low, rim_high, rim_low, near_high, near_low, const),
                (late, lower),
                [pltpu.VMEM((2 * cols, sites + 2 * edge), bf16)],
            )
        elif jumps and mine == jump:
            late, lower, parts = turn(
                functools.partial(jump_kernel, mine, sides),
                (own_in, next_in, both, high, low, own_rows, *ship),
                (late, lower),
                [pltpu.VMEM((2 * cols, sites), bf16)],
                [shape((2 * cols, sites), f32)],
            )
        else:
            early = jumps and mine == pairs - 3
            late, lower = turn(
                functools.partial(chain_kernel, mine, sides),
                (own_in, next_in, both, high, low),
                (late, lower),
                flops=50 * 10**9 if early else 0,
            )
    given = (own_in, next_in) + ((beside_own, beside_next) if jumps else ())
    late, upper = turn(
        functools.partial(upper_kernel, sides, pairs - 1), (*given, far, far_high, far_low), (late, upper)
    )
    returned = lax.ppermute(upper, BOTH, link(even, odd))
    lower = pl.pallas_call(
        functools.partial(last_kernel, jumps),
        out_shape=shape(lower.shape, f32),
        in_specs=[VMEM] * 5,
        out_specs=VMEM,
        input_output_aliases={4: 0},
        compiler_params=PARAMS,
        cost_estimate=pl.CostEstimate(flops=12 * cols * tall * length, bytes_accessed=8 * tall * length, transcendentals=0),
    )(both, high, low, late, lower)
    return jnp.where(device % 2 == 0, lower, returned)[None]


def solution(mesh):
    placed = (
        P("tm", None, "row"),
        P("tm", "row", None, None),
        P("tm", "row", None, None),
        P("tm", "row", None),
    )
    return jax.shard_map(
        local, mesh=mesh, in_specs=placed, out_specs=P("tm", None, "row"), check_vma=False
    )
```

```python
import functools

import jax
import jax.numpy as jnp
from jax import lax
from jax.experimental import pallas as pl
from jax.experimental.pallas import tpu as pltpu
from jax.sharding import PartitionSpec as P

BOTH = ("tm", "row")
VMEM = pl.BlockSpec(memory_space=pltpu.VMEM)
HBM = pl.BlockSpec(memory_space=pltpu.HBM)
PARAMS = pltpu.CompilerParams(vmem_limit_bytes=32 * 1024 * 1024)


def halves(value):
    high = value.astype(jnp.bfloat16)
    low = (value - high.astype(jnp.float32)).astype(jnp.bfloat16)
    return high, low


def dot(a, b):
    return jnp.dot(a, b, preferred_element_type=jnp.float32)


def stacked_dot(pair, cols, high, low):
    rows = pair.shape[0] // 2
    wide = dot(pair[:, cols], high)
    return wide[:rows] + wide[rows:] + dot(pair[:rows, cols], low)


def triple(high, low, inv_high, inv_low):
    return dot(high, inv_high) + dot(low, inv_high) + dot(high, inv_low)


def put_rim(sides, rim, columns):
    if sides == 1:
        row = lax.axis_index("row")

        @pl.when(row == 0)
        def _():
            rim[0] = columns(True)

        @pl.when(row != 0)
        def _():
            rim[0] = columns(False)
    else:
        rim[0] = columns(True)
        rim[1] = columns(False)


def const_kernel(normals, inv, const, inv_high, inv_low, normals_in, inv_in, sems):
    blocks, length = inv.shape[1], inv.shape[2]
    moves = [pltpu.make_async_copy(normals.at[0], normals_in, sems.at[0])]
    for b in range(blocks):
        moves.append(pltpu.make_async_copy(inv.at[0, b], inv_in.at[b], sems.at[1 + b]))
    for move in moves:
        move.start()
    moves[0].wait()
    for b in range(blocks):
        at = slice(b * length, (b + 1) * length)
        high, low = halves(normals_in[:, at])
        moves[1 + b].wait()
        inv_high[b], inv_low[b] = halves(inv_in[b])
        const[:, at] = triple(high, low, inv_high[b], inv_low[b])


def fuse_kernel(mask, const, inv_high, inv_low, lag, own, near_high, near_low):
    blocks, window, length = lag.shape[1:]
    edge = (window - length) // 2
    cols = const.shape[0]
    cuts = (0, edge, edge + length, window)
    flags = mask[0].astype(jnp.float32)
    for b in range(blocks):
        at = blocks * window + b * cols
        own[at : at + cols] = const[:, b * length : (b + 1) * length]
        for part in range(3):
            lo, hi = cuts[part], cuts[part + 1]
            rows = slice(b * window + lo, b * window + hi)
            high, low = halves(lag[0, b, lo:hi] * flags[b : b + 1, part : part + 1])
            value = triple(high, low, inv_high[b], inv_low[b])
            own[rows] = value
            near_high[rows], near_low[rows] = halves(value)


def edge_kernel(sides, blocks, cols, _own, own, rim):
    length, edge = own.shape[1], rim.shape[2]
    window = length + 2 * edge

    def columns(last):
        b = blocks - 1 if last else 0
        cut = slice(length - edge, length) if last else slice(0, edge)
        at = blocks * window + b * cols
        return jnp.concatenate([own[b * window : (b + 1) * window, cut], own[at : at + cols, cut]])

    put_rim(sides, rim, columns)


def split_kernel(rim, far, far_high, far_low, rim_high, rim_low):
    far_high[...], far_low[...] = halves(far[: far_high.shape[0]])
    for side in range(rim.shape[0]):
        rim_high[side], rim_low[side] = halves(rim[side, : rim_high.shape[1]])


def cuts_of(blocks, length, sites, span, last):
    packed, cuts = 0, []
    for b in range(blocks):
        start = span // 2 - length // 2 - b * length
        lo, hi = (start + sites, span) if last else (0, start)
        cuts.append((lo, hi, packed))
        packed += hi - lo
    return cuts


def pair_kernel(jump, rim, far, far_high, far_low, near_high, near_low, const, high, low, both, *rest):
    cols, sites = const.shape
    length = far.shape[1]
    blocks = sites // length
    window = near_high.shape[0] // blocks
    edge = (window - length) // 2
    span = 2 * window
    tall = blocks * window
    total = rest[-1]
    if rim.shape[0] == 1:
        flag = jnp.minimum(lax.axis_index("row"), 1).astype(jnp.float32)
        left, right = rim[0] * flag, rim[0] * (1 - flag)
    else:
        left, right = rim[0], rim[1]
    left_pair, right_pair = halves(left[:window]), halves(right[:window])
    for b in range(blocks):
        here = slice(b * window, (b + 1) * window)
        column = slice(b * length, (b + 1) * length)

        def part(lo, hi):
            rows = slice(b * window + lo, b * window + hi)
            return near_high[rows], near_low[rows]

        def constant(block):
            if block < 0:
                return left[window:]
            if block == blocks:
                return right[window:]
            return far[tall + block * cols : tall + (block + 1) * cols]

        if b > 0:
            before = slice((b - 1) * window, b * window)
            low_pair = far_high[before, length - edge :], far_low[before, length - edge :]
            low_const = constant(b - 1)[:, length - edge :]
        else:
            low_pair, low_const = left_pair, constant(-1)
        if b + 1 < blocks:
            after = slice((b + 1) * window, (b + 2) * window)
            high_pair = far_high[after, :edge], far_low[after, :edge]
            high_const = constant(b + 1)[:, :edge]
        else:
            high_pair, high_const = right_pair, constant(blocks)
        first = triple(*low_pair, *part(0, edge))
        middle = triple(far_high[here], far_low[here], *part(edge, edge + length))
        last = triple(*high_pair, *part(edge + length, window))
        total[:window] = first
        total[window:] = last
        total[length : length + window] += middle
        high[b * span : (b + 1) * span], low[b * span : (b + 1) * span] = halves(total[...])
        both[:, column] = const[:, column] - (
            triple(*halves(low_const), *part(0, edge))
            + triple(*halves(constant(b)), *part(edge, edge + length))
            + triple(*halves(high_const), *part(edge + length, window))
        )
    if jump:
        own_rows, other_rows = rest[:2]

        def value(start, count):
            rows = pl.ds(start, count)
            return high[rows].astype(jnp.float32) + low[rows].astype(jnp.float32)

        for b in range(blocks):
            own_rows[b * sites : (b + 1) * sites] = value(b * span + window - edge - b * length, sites)
            at = blocks * sites + b * cols
            own_rows[at : at + cols] = both[:, b * length : (b + 1) * length]
        starts = [
            [b * span + at for b, (lo, hi, _) in enumerate(cuts_of(blocks, length, sites, span, last)) for at in range(lo, hi, edge)]
            for last in (True, False)
        ]
        row = lax.axis_index("row")
        for chunk, (on_right, on_left) in enumerate(zip(*starts)):
            start = pl.multiple_of(jnp.where(row == 0, on_right, on_left), edge)
            other_rows[chunk * edge : (chunk + 1) * edge] = value(start, edge)


def keep(ref, start, value):
    cols, width = value.shape
    high, low = halves(value)
    ref[:cols, pl.ds(start, width)] = high
    ref[cols:, pl.ds(start, width)] = low


def load(sides, pick, own, halo, ref):
    sites = own.shape[1]
    keep(ref, halo, own)
    for side in range(sides):
        on_right = 1 - jnp.minimum(lax.axis_index("row"), 1).astype(jnp.int32) if sides == 1 else side
        start = pl.multiple_of((1 - on_right) * (sites - halo), 128)
        keep(ref, pl.multiple_of(on_right * (halo + sites), 128), pick(side, pl.ds(start, halo)))


def plain(next_in):
    return lambda side, cut: next_in[:, cut] if len(next_in.shape) == 2 else next_in[side, :, cut]


def top_kernel(mine, sides, own_in, next_in, const, near_high, near_low, _upper, _lower, upper, lower, mid):
    sites = lower.shape[1]
    length = near_high.shape[1]
    blocks = sites // length
    window = near_high.shape[0] // blocks
    edge = (window - length) // 2

    @pl.when(lax.axis_index("tm") == 2 * mine)
    def _():
        mid[...] = jnp.zeros_like(mid)
        load(sides, plain(next_in), own_in[...], edge, mid)
        upper[...] = own_in[...]
        for b in range(blocks):
            at, rows = slice(b * length, (b + 1) * length), slice(b * window, (b + 1) * window)
            product = stacked_dot(mid, slice(b * length, b * length + window), near_high[rows], near_low[rows])
            lower[:, at] = const[:, at] - product


def direct_kernel(
    mine, sides, own_in, next_in, rim, far, far_high, far_low, rim_high, rim_low, near_high, near_low, const,
    _late, _lower, late, lower, mid
):
    cols, sites = lower.shape
    length = near_high.shape[1]
    blocks = sites // length
    window = near_high.shape[0] // blocks
    edge = (window - length) // 2
    halo = length + edge

    @pl.when(lax.axis_index("tm") == 2 * mine)
    def _():
        load(sides, plain(next_in), own_in[...], halo, late)
        mid[...] = jnp.zeros_like(mid)
        for side in range(sides):
            on_right = 1 - jnp.minimum(lax.axis_index("row"), 1).astype(jnp.int32) if sides == 1 else side
            start = pl.multiple_of(on_right * (2 * halo + sites - window), 128)
            product = stacked_dot(late, pl.ds(start, window), rim_high[side], rim_low[side])
            keep(mid, pl.multiple_of(on_right * (edge + sites), 128), rim[side, window:] - product)
        for b in range(blocks):
            rows, start = slice(b * window, (b + 1) * window), halo - edge + b * length
            at = blocks * window + b * cols
            product = stacked_dot(late, slice(start, start + window), far_high[rows], far_low[rows])
            keep(mid, edge + b * length, far[at : at + cols] - product)
        for b in range(blocks):
            at, rows = slice(b * length, (b + 1) * length), slice(b * window, (b + 1) * window)
            product = stacked_dot(mid, slice(b * length, b * length + window), near_high[rows], near_low[rows])
            lower[:, at] = const[:, at] - product


def step(both, high, low, late, lower):
    blocks = lower.shape[1] // high.shape[1]
    length, span = high.shape[1], high.shape[0] // blocks
    for b in range(blocks):
        at, rows = slice(b * length, (b + 1) * length), slice(b * span, (b + 1) * span)
        lower[:, at] = both[:, at] + stacked_dot(late, slice(b * length, b * length + span), high[rows], low[rows])


def chain_kernel(mine, sides, own_in, next_in, both, high, low, _late, _lower, late, lower):
    @pl.when(lax.axis_index("tm") == 2 * mine)
    def _():
        load(sides, plain(next_in), own_in[...], (late.shape[1] - own_in.shape[1]) // 2, late)
        step(both, high, low, late, lower)


def rows_kernel(own_rows, other_rows, own_high, own_low, other_high, other_low):
    own_high[...], own_low[...] = halves(own_rows[: own_high.shape[0]])
    other_high[...], other_low[...] = halves(other_rows[...])


def add_parts(lower, own_rows, own_high, own_low, other_high, other_low, to_next, to_own, mid, far_mid, span):
    cols, sites = lower.shape
    length = own_rows.shape[1]
    blocks = sites // length
    halo = to_own.shape[1] - sites
    edge = halo - length
    row = lax.axis_index("row")
    keep(mid, 0, lower[...])
    near = pl.multiple_of(jnp.where(row == 0, sites - halo, 0), edge)
    for b in range(blocks):
        at, rows = slice(b * length, (b + 1) * length), slice(b * sites, (b + 1) * sites)
        const = slice(blocks * sites + b * cols, blocks * sites + (b + 1) * cols)
        to_own[:, at] = own_rows[const] + stacked_dot(mid, slice(0, sites), own_high[rows], own_low[rows])
    to_next[:, :halo] = to_own[:, pl.ds(near, halo)]
    for b in range(blocks):
        value = None
        cuts = [cuts_of(blocks, length, sites, span, last)[b] for last in (True, False)]
        for chunk in range(0, max(hi - lo for lo, hi, _ in cuts), edge):
            starts, froms, there = [], [], []
            for last, (lo, hi, packed) in zip((True, False), cuts):
                count = hi - lo
                there.append(chunk < count)
                starts.append(packed + chunk if chunk < count else 0)
                froms.append((0 if last else sites - count) + chunk if chunk < count else 0)
            start = pl.multiple_of(jnp.where(row == 0, starts[1], starts[0]), edge)
            source = pl.multiple_of(jnp.where(row == 0, froms[1], froms[0]), edge)
            rows = pl.ds(start, edge)
            product = stacked_dot(mid, pl.ds(source, edge), other_high[rows], other_low[rows])
            if not all(there):
                product = jnp.where((row == 0) == there[1], product, 0.0)
            value = product if value is None else value + product
        far_mid[:, b * length : (b + 1) * length] = value
    to_next[:, halo:] = far_mid[...]
    away = pl.multiple_of(jnp.where(row == 0, 0, sites - halo), edge)
    to_own[:, sites:] = far_mid[:, pl.ds(away, halo)]


def jump_kernel(mine, sides, own_in, next_in, both, high, low, *rest):
    ship, (_late, _lower, late, lower, to_next, to_own, to_last, *scratch) = rest[:-9], rest[-9:]

    @pl.when(lax.axis_index("tm") == 2 * mine)
    def _():
        load(sides, plain(next_in), own_in[...], (late.shape[1] - own_in.shape[1]) // 2, late)
        step(both, high, low, late, lower)
        add_parts(lower, *ship, to_next, to_own, *scratch, high.shape[0] * high.shape[1] // own_in.shape[1])
        to_last[...] = to_next[...]

    @pl.when(lax.axis_index("tm") != 2 * mine)
    def _():
        for part in (to_next, to_own, to_last):
            part[...] = jnp.zeros_like(part)


def parts_kernel(mine, span, lower, *rest):
    ship, parts = rest[:-4], rest[-4:]

    @pl.when(lax.axis_index("tm") == 2 * mine)
    def _():
        add_parts(lower, *ship, *parts, span)

    @pl.when(lax.axis_index("tm") != 2 * mine)
    def _():
        for part in parts[:2]:
            part[...] = jnp.zeros_like(part)


def last_kernel(jumps, both, high, low, late, _lower, lower):
    device = lax.axis_index("tm")
    pl.when((device == 0) | (device == 2) if jumps else device == 0)(lambda: step(both, high, low, late, lower))


def upper_kernel(sides, top, *rest):
    far, far_high, far_low, _late, _upper, late, upper = rest[-7:]
    cols, sites = upper.shape
    length = far.shape[1]
    blocks = sites // length
    window = far_high.shape[0] // blocks
    halo = (late.shape[1] - sites) // 2
    at_window = halo - (window - length) // 2
    messages = rest[:-7]

    if len(messages) == 2:

        @pl.when(lax.axis_index("tm") == 0)
        def _():
            load(sides, plain(messages[1]), messages[0][...], halo, late)

    for mine, (*next_in, own_in) in enumerate(((messages[0], messages[2], messages[1]), messages[3:]) if len(messages) > 2 else ()):

        @pl.when(lax.axis_index("tm") == 2 * mine)
        def _():
            from_next = next_in[0][...] + next_in[1][...] if len(next_in) == 2 else next_in[0][...]
            own = own_in[:, :sites] + from_next[:, halo:]
            near = own_in[:, sites:] + from_next[:, :halo]
            load(sides, lambda side, cut: near, own, halo, late)

    @pl.when(lax.axis_index("tm") != 2 * top)
    def _():
        for b in range(blocks):
            rows = slice(b * window, (b + 1) * window)
            at = blocks * window + b * cols
            start = at_window + b * length
            upper[:, b * length : (b + 1) * length] = far[at : at + cols] - stacked_dot(
                late, slice(start, start + window), far_high[rows], far_low[rows]
            )


def local(normals, inv_diag, lag_coupling, fill_mask):
    times, rows = lax.axis_size("tm"), lax.axis_size("row")
    device = lax.axis_index("tm")
    cols, sites = normals.shape[1:]
    blocks, length = inv_diag.shape[1:3]
    window = lag_coupling.shape[2]
    edge = (window - length) // 2
    halo = length + edge
    sides = 1 if rows == 2 else 2
    pairs = times // 2
    f32, bf16 = jnp.float32, jnp.bfloat16
    shape = jax.ShapeDtypeStruct

    def link(source, target):
        return [(s * rows + r, t * rows + r) for s, t in zip(source, target) for r in range(rows)]

    def cross(value, source, target, split=False):
        if sides == 1:
            perm = [(s * rows + r, t * rows + 1 - r) for s, t in zip(source, target) for r in range(2)]
            return lax.ppermute(value, BOTH, perm)
        moved = []
        for side, step in enumerate((1, -1)):
            perm = [
                (s * rows + r, t * rows + r + step)
                for s, t in zip(source, target)
                for r in range(rows)
                if 0 <= r + step < rows
            ]
            moved.append(lax.ppermute(value[side : side + 1] if split else value[None], BOTH, perm))
        return jnp.concatenate(moved)

    tall = blocks * window
    jump = 2
    jumps = rows == 2 and pairs > 5
    const, inv_high, inv_low = pl.pallas_call(
        const_kernel,
        out_shape=(
            shape((cols, sites), f32),
            shape((blocks, length, length), bf16), shape((blocks, length, length), bf16),
        ),
        in_specs=[HBM] * 2,
        out_specs=(VMEM,) * 3,
        scratch_shapes=[
            pltpu.VMEM(normals.shape[1:], f32),
            pltpu.VMEM(inv_diag.shape[1:], f32),
            pltpu.SemaphoreType.DMA((1 + blocks,)),
        ],
        compiler_params=PARAMS,
        cost_estimate=pl.CostEstimate(flops=5*10**9, bytes_accessed=0, transcendentals=0),
    )(*[pltpu.with_memory_space_constraint(a, pltpu.HBM) for a in (normals, inv_diag)])
    odd, even = range(1, times, 2), range(0, times, 2)
    first_next = cross(const, odd[-1:], even[-1:])
    first_own = lax.ppermute(const, BOTH, link(odd[-1:], even[-1:]))
    near, near_high, near_low = pl.pallas_call(
        fuse_kernel,
        out_shape=(
            shape((tall + blocks * cols, length), f32), shape((tall, length), bf16), shape((tall, length), bf16),
        ),
        in_specs=[VMEM] * 5,
        out_specs=(VMEM,) * 3,
        compiler_params=PARAMS,
        cost_estimate=pl.CostEstimate(
            flops=6 * (tall + cols * blocks) * length * length, bytes_accessed=16 * tall * length, transcendentals=0
        ),
    )(fill_mask, const, inv_high, inv_low, lag_coupling)
    near, edges = pl.pallas_call(
        functools.partial(edge_kernel, sides, blocks, cols),
        out_shape=(shape(near.shape, f32), shape((sides, window + cols, edge), f32)),
        in_specs=[VMEM],
        out_specs=(VMEM,) * 2,
        input_output_aliases={0: 0},
        compiler_params=PARAMS,
    )(near)
    rim = cross(edges, odd[:-1], even[:-1], True)
    far = lax.ppermute(near, BOTH, link(odd[:-1], even[:-1]))

    blank = jnp.zeros((cols, sites), f32)
    upper, lower = pl.pallas_call(
        functools.partial(top_kernel, pairs - 1, sides),
        out_shape=(shape((cols, sites), f32),) * 2,
        in_specs=[VMEM] * 7,
        out_specs=(VMEM,) * 2,
        scratch_shapes=[pltpu.VMEM((2 * cols, sites + 2 * edge), bf16)],
        input_output_aliases={5: 0, 6: 1},
        compiler_params=PARAMS,
        cost_estimate=pl.CostEstimate(flops=50 * 10**9, bytes_accessed=0, transcendentals=0),
    )(first_own, first_next, const, near_high, near_low, blank, blank)
    far_high, far_low, rim_high, rim_low = pl.pallas_call(
        split_kernel,
        out_shape=(
            shape((tall, length), bf16), shape((tall, length), bf16),
            shape((sides, window, edge), bf16), shape((sides, window, edge), bf16),
        ),
        in_specs=[VMEM] * 2,
        out_specs=(VMEM,) * 4,
        compiler_params=PARAMS,
    )(rim, far)
    packs = (shape((blocks * (sites + cols), length), f32), shape((halo + edge, length), f32)) if jumps else ()
    high, low, both, *packs = pl.pallas_call(
        functools.partial(pair_kernel, jumps),
        out_shape=(
            shape((2 * tall, length), bf16), shape((2 * tall, length), bf16), shape((cols, sites), f32), *packs
        ),
        in_specs=[VMEM] * 7,
        out_specs=(VMEM,) * (3 + len(packs)),
        scratch_shapes=[pltpu.VMEM((2 * window, length), f32)],
        compiler_params=PARAMS,
        cost_estimate=pl.CostEstimate(flops=10**9, bytes_accessed=0, transcendentals=0),
    )(rim, far, far_high, far_low, near_high, near_low, const)
    if jumps:
        source, target = [2 * jump - 2, 2 * jump], [2 * jump, 2 * jump + 2]
        own_rows = lax.ppermute(packs[0], BOTH, link(source, target))
        other_rows = cross(packs[1], source, target)
        ship = pl.pallas_call(
            rows_kernel,
            out_shape=(shape((blocks * sites, length), bf16),) * 2 + (shape(other_rows.shape, bf16),) * 2,
            in_specs=[VMEM] * 2,
            out_specs=(VMEM,) * 4,
            compiler_params=PARAMS,
        )(own_rows, other_rows)

    def turn(kernel, given, state, scratch=(), extra=(), flops=0):
        return pl.pallas_call(
            kernel,
            out_shape=tuple(shape(v.shape, v.dtype) for v in state) + tuple(extra),
            in_specs=[VMEM] * (len(given) + 2),
            out_specs=(VMEM,) * (2 + len(extra)),
            scratch_shapes=list(scratch),
            input_output_aliases={len(given): 0, len(given) + 1: 1},
            compiler_params=PARAMS,
            cost_estimate=pl.CostEstimate(flops=flops, bytes_accessed=0, transcendentals=0) if flops else None,
        )(*given, *state)

    parts = (shape((cols, sites + halo), f32),) * 2
    parts_scratch = [pltpu.VMEM((2 * cols, sites), bf16), pltpu.VMEM((cols, sites), f32)]
    late = jnp.zeros((2 * cols, sites + 2 * halo), bf16)
    mine = pairs - 1
    while mine > 0:
        if jumps and mine == jump:
            source, target = [2 * mine], [2 * mine - 4]
            first_in = lax.ppermute(to_next, BOTH, [(2 * source[0] + 1, 2 * target[0])])
            own_in = lax.ppermute(to_own, BOTH, link(source, target))
            next_in = lax.ppermute(to_last, BOTH, [(2 * source[0], 2 * target[0] + 1)])
            break
        source, target = [2 * mine], [2 * mine - 2]
        next_in = cross(lower, source, target)
        own_in = lax.ppermute(lower, BOTH, link(source, target))
        if jumps and mine == jump + 1:
            beside = pl.pallas_call(
                functools.partial(parts_kernel, mine, 2 * window),
                out_shape=parts,
                in_specs=[VMEM] * 6,
                out_specs=(VMEM,) * 2,
                scratch_shapes=parts_scratch,
                compiler_params=PARAMS,
            )(lower, own_rows, *ship)
            source, target = [2 * mine], [2 * mine - 4]
            beside_next = cross(beside[0], source, target)
            beside_own = lax.ppermute(beside[1], BOTH, link(source, target))
        mine -= 1
        if mine == 0:
            break
        if mine == pairs - 2:
            late, lower = turn(
                functools.partial(direct_kernel, mine, sides),
                (own_in, next_in, rim, far, far_high, far_low, rim_high, rim_low, near_high, near_low, const),
                (late, lower),
                [pltpu.VMEM((2 * cols, sites + 2 * edge), bf16)],
            )
        elif jumps and mine == jump:
            late, lower, to_next, to_own, to_last = turn(
                functools.partial(jump_kernel, mine, sides),
                (own_in, next_in, both, high, low, own_rows, *ship),
                (late, lower),
                parts_scratch,
                parts + parts[:1],
            )
        else:
            early = jumps and mine == pairs - 3
            late, lower = turn(
                functools.partial(chain_kernel, mine, sides),
                (own_in, next_in, both, high, low),
                (late, lower),
                flops=50 * 10**9 if early else 0,
            )
    given = (first_in, own_in, next_in, beside_next, beside_own) if jumps else (own_in, next_in)
    late, upper = turn(
        functools.partial(upper_kernel, sides, pairs - 1), (*given, far, far_high, far_low), (late, upper)
    )
    returned = lax.ppermute(upper, BOTH, link(even, odd))
    lower = pl.pallas_call(
        functools.partial(last_kernel, jumps),
        out_shape=shape(lower.shape, f32),
        in_specs=[VMEM] * 5,
        out_specs=VMEM,
        input_output_aliases={4: 0},
        compiler_params=PARAMS,
        cost_estimate=pl.CostEstimate(flops=12 * cols * tall * length, bytes_accessed=8 * tall * length, transcendentals=0),
    )(both, high, low, late, lower)
    return jnp.where(device % 2 == 0, lower, returned)[None]


def solution(mesh):
    placed = (
        P("tm", None, "row"),
        P("tm", "row", None, None),
        P("tm", "row", None, None),
        P("tm", "row", None),
    )
    return jax.shard_map(
        local, mesh=mesh, in_specs=placed, out_specs=P("tm", None, "row"), check_vma=False
    )
```

```python
import functools

import jax
import jax.numpy as jnp
from jax import lax
from jax.experimental import pallas as pl
from jax.experimental.pallas import tpu as pltpu
from jax.sharding import PartitionSpec as P

BOTH = ("tm", "row")
VMEM = pl.BlockSpec(memory_space=pltpu.VMEM)
HBM = pl.BlockSpec(memory_space=pltpu.HBM)
PARAMS = pltpu.CompilerParams(vmem_limit_bytes=32 * 1024 * 1024)


def halves(value):
    high = value.astype(jnp.bfloat16)
    low = (value - high.astype(jnp.float32)).astype(jnp.bfloat16)
    return high, low


def dot(a, b):
    return jnp.dot(a, b, preferred_element_type=jnp.float32)


def stacked_dot(pair, cols, high, low):
    rows = pair.shape[0] // 2
    wide = dot(pair[:, cols], high)
    return wide[:rows] + wide[rows:] + dot(pair[:rows, cols], low)


def triple(high, low, inv_high, inv_low):
    return dot(high, inv_high) + dot(low, inv_high) + dot(high, inv_low)


def put_rim(sides, rim, columns):
    if sides == 1:
        row = lax.axis_index("row")

        @pl.when(row == 0)
        def _():
            rim[0] = columns(True)

        @pl.when(row != 0)
        def _():
            rim[0] = columns(False)
    else:
        rim[0] = columns(True)
        rim[1] = columns(False)


def const_kernel(normals, inv, const, inv_high, inv_low, normals_in, inv_in, sems):
    blocks, length = inv.shape[1], inv.shape[2]
    moves = [pltpu.make_async_copy(normals.at[0], normals_in, sems.at[0])]
    for b in range(blocks):
        moves.append(pltpu.make_async_copy(inv.at[0, b], inv_in.at[b], sems.at[1 + b]))
    for move in moves:
        move.start()
    moves[0].wait()
    for b in range(blocks):
        at = slice(b * length, (b + 1) * length)
        high, low = halves(normals_in[:, at])
        moves[1 + b].wait()
        inv_high[b], inv_low[b] = halves(inv_in[b])
        const[:, at] = triple(high, low, inv_high[b], inv_low[b])


def fuse_kernel(mask, const, inv_high, inv_low, lag, own, near_high, near_low):
    blocks, window, length = lag.shape[1:]
    edge = (window - length) // 2
    cols = const.shape[0]
    cuts = (0, edge, edge + length, window)
    flags = mask[0].astype(jnp.float32)
    for b in range(blocks):
        at = blocks * window + b * cols
        own[at : at + cols] = const[:, b * length : (b + 1) * length]
        for part in range(3):
            lo, hi = cuts[part], cuts[part + 1]
            rows = slice(b * window + lo, b * window + hi)
            high, low = halves(lag[0, b, lo:hi] * flags[b : b + 1, part : part + 1])
            value = triple(high, low, inv_high[b], inv_low[b])
            own[rows] = value
            near_high[rows], near_low[rows] = halves(value)


def edge_kernel(sides, blocks, cols, own, rim):
    length, edge = own.shape[1], rim.shape[2]
    window = length + 2 * edge

    def columns(last):
        b = blocks - 1 if last else 0
        cut = slice(length - edge, length) if last else slice(0, edge)
        at = blocks * window + b * cols
        return jnp.concatenate([own[b * window : (b + 1) * window, cut], own[at : at + cols, cut]])

    put_rim(sides, rim, columns)


def split_kernel(rim, far, far_high, far_low, rim_high, rim_low):
    far_high[...], far_low[...] = halves(far[: far_high.shape[0]])
    for side in range(rim.shape[0]):
        rim_high[side], rim_low[side] = halves(rim[side, : rim_high.shape[1]])


def cuts_of(blocks, length, sites, span, last):
    packed, cuts = 0, []
    for b in range(blocks):
        start = span // 2 - length // 2 - b * length
        lo, hi = (start + sites, span) if last else (0, start)
        cuts.append((lo, hi, packed))
        packed += hi - lo
    return cuts


def pair_kernel(jump, far, rim, far_high, far_low, near_high, near_low, const, high, low, both, *rest):
    cols, sites = const.shape
    length = far.shape[1]
    blocks = sites // length
    window = near_high.shape[0] // blocks
    edge = (window - length) // 2
    span = 2 * window
    tall = blocks * window
    total = rest[-1]
    if rim.shape[0] == 1:
        flag = jnp.minimum(lax.axis_index("row"), 1).astype(jnp.float32)
        left, right = rim[0] * flag, rim[0] * (1 - flag)
    else:
        left, right = rim[0], rim[1]
    left_pair, right_pair = halves(left[:window]), halves(right[:window])
    for b in range(blocks):
        here = slice(b * window, (b + 1) * window)
        column = slice(b * length, (b + 1) * length)

        def part(lo, hi):
            rows = slice(b * window + lo, b * window + hi)
            return near_high[rows], near_low[rows]

        def constant(block):
            if block < 0:
                return left[window:]
            if block == blocks:
                return right[window:]
            return far[tall + block * cols : tall + (block + 1) * cols]

        if b > 0:
            before = slice((b - 1) * window, b * window)
            low_pair = far_high[before, length - edge :], far_low[before, length - edge :]
            low_const = constant(b - 1)[:, length - edge :]
        else:
            low_pair, low_const = left_pair, constant(-1)
        if b + 1 < blocks:
            after = slice((b + 1) * window, (b + 2) * window)
            high_pair = far_high[after, :edge], far_low[after, :edge]
            high_const = constant(b + 1)[:, :edge]
        else:
            high_pair, high_const = right_pair, constant(blocks)
        first = triple(*low_pair, *part(0, edge))
        middle = triple(far_high[here], far_low[here], *part(edge, edge + length))
        last = triple(*high_pair, *part(edge + length, window))
        total[:window] = first
        total[window:] = last
        total[length : length + window] += middle
        high[b * span : (b + 1) * span], low[b * span : (b + 1) * span] = halves(total[...])
        both[:, column] = const[:, column] - (
            triple(*halves(low_const), *part(0, edge))
            + triple(*halves(constant(b)), *part(edge, edge + length))
            + triple(*halves(high_const), *part(edge + length, window))
        )
    if jump:
        own_rows, other_rows = rest[:2]

        def value(start, count):
            rows = pl.ds(start, count)
            return high[rows].astype(jnp.float32) + low[rows].astype(jnp.float32)

        for b in range(blocks):
            own_rows[b * sites : (b + 1) * sites] = value(b * span + window - edge - b * length, sites)
            at = blocks * sites + b * cols
            own_rows[at : at + cols] = both[:, b * length : (b + 1) * length]
        starts = [
            [b * span + at for b, (lo, hi, _) in enumerate(cuts_of(blocks, length, sites, span, last)) for at in range(lo, hi, edge)]
            for last in (True, False)
        ]
        row = lax.axis_index("row")
        for chunk, (on_right, on_left) in enumerate(zip(*starts)):
            start = pl.multiple_of(jnp.where(row == 0, on_right, on_left), edge)
            other_rows[chunk * edge : (chunk + 1) * edge] = value(start, edge)


def keep(ref, start, value):
    cols, width = value.shape
    high, low = halves(value)
    ref[:cols, pl.ds(start, width)] = high
    ref[cols:, pl.ds(start, width)] = low


def load(sides, pick, own, halo, ref):
    sites = own.shape[1]
    keep(ref, halo, own)
    for side in range(sides):
        on_right = 1 - jnp.minimum(lax.axis_index("row"), 1).astype(jnp.int32) if sides == 1 else side
        start = pl.multiple_of((1 - on_right) * (sites - halo), 128)
        keep(ref, pl.multiple_of(on_right * (halo + sites), 128), pick(side, pl.ds(start, halo)))


def plain(next_in):
    return lambda side, cut: next_in[:, cut] if len(next_in.shape) == 2 else next_in[side, :, cut]


def top_kernel(mine, sides, next_in, own_in, const, near_high, near_low, _upper, _lower, upper, lower, mid):
    sites = lower.shape[1]
    length = near_high.shape[1]
    blocks = sites // length
    window = near_high.shape[0] // blocks
    edge = (window - length) // 2

    @pl.when(lax.axis_index("tm") == 2 * mine)
    def _():
        mid[...] = jnp.zeros_like(mid)
        load(sides, plain(next_in), own_in[...], edge, mid)
        upper[...] = own_in[...]
        for b in range(blocks):
            at, rows = slice(b * length, (b + 1) * length), slice(b * window, (b + 1) * window)
            product = stacked_dot(mid, slice(b * length, b * length + window), near_high[rows], near_low[rows])
            lower[:, at] = const[:, at] - product


def direct_kernel(
    mine, sides, next_in, own_in, far, rim, far_high, far_low, rim_high, rim_low, near_high, near_low, const,
    _late, _lower, late, lower, mid
):
    cols, sites = lower.shape
    length = near_high.shape[1]
    blocks = sites // length
    window = near_high.shape[0] // blocks
    edge = (window - length) // 2
    halo = length + edge

    @pl.when(lax.axis_index("tm") == 2 * mine)
    def _():
        load(sides, plain(next_in), own_in[...], halo, late)
        mid[...] = jnp.zeros_like(mid)
        for side in range(sides):
            on_right = 1 - jnp.minimum(lax.axis_index("row"), 1).astype(jnp.int32) if sides == 1 else side
            start = pl.multiple_of(on_right * (2 * halo + sites - window), 128)
            product = stacked_dot(late, pl.ds(start, window), rim_high[side], rim_low[side])
            keep(mid, pl.multiple_of(on_right * (edge + sites), 128), rim[side, window:] - product)
        for b in range(blocks):
            rows, start = slice(b * window, (b + 1) * window), halo - edge + b * length
            at = blocks * window + b * cols
            product = stacked_dot(late, slice(start, start + window), far_high[rows], far_low[rows])
            keep(mid, edge + b * length, far[at : at + cols] - product)
        for b in range(blocks):
            at, rows = slice(b * length, (b + 1) * length), slice(b * window, (b + 1) * window)
            product = stacked_dot(mid, slice(b * length, b * length + window), near_high[rows], near_low[rows])
            lower[:, at] = const[:, at] - product


def step(both, high, low, late, lower):
    blocks = lower.shape[1] // high.shape[1]
    length, span = high.shape[1], high.shape[0] // blocks
    for b in range(blocks):
        at, rows = slice(b * length, (b + 1) * length), slice(b * span, (b + 1) * span)
        lower[:, at] = both[:, at] + stacked_dot(late, slice(b * length, b * length + span), high[rows], low[rows])


def load_rims(sides, next_in, sites, halo, late):
    for side in range(sides):
        on_right = 1 - jnp.minimum(lax.axis_index("row"), 1).astype(jnp.int32) if sides == 1 else side
        start = pl.multiple_of((1 - on_right) * (sites - halo), 128)
        keep(late, pl.multiple_of(on_right * (halo + sites), 128), plain(next_in)(side, pl.ds(start, halo)))


def rim_kernel(mine, sides, next_in, both, high, low, _late, late, base):
    sites, length = base.shape[1], high.shape[1]
    blocks = sites // length
    span = high.shape[0] // blocks
    halo = (late.shape[1] - sites) // 2
    edge = halo - length

    @pl.when(lax.axis_index("tm") == 2 * mine)
    def _():
        load_rims(sides, next_in, sites, halo, late)
        cuts = [cuts_of(blocks, length, sites, span, last) for last in (False, True)]
        for b in range(blocks):
            value = both[:, b * length : (b + 1) * length]
            if sides == 2:
                for lo, hi, _ in (cuts[0][b], cuts[1][b]):
                    rows = slice(b * span + lo, b * span + hi)
                    value += stacked_dot(late, slice(b * length + lo, b * length + hi), high[rows], low[rows])
            else:
                on_left = lax.axis_index("row") != 0
                counts = [cut[b][1] - cut[b][0] for cut in cuts]
                for chunk in range(0, max(counts), edge):
                    starts = [cut[b][0] + chunk if chunk < count else 0 for cut, count in zip(cuts, counts)]
                    start = pl.multiple_of(jnp.where(on_left, starts[0], starts[1]), edge)
                    rows = pl.ds(b * span + start, edge)
                    product = stacked_dot(late, pl.ds(b * length + start, edge), high[rows], low[rows])
                    if chunk >= min(counts):
                        product = jnp.where(on_left == (counts[0] > counts[1]), product, 0.0)
                    value += product
            base[:, b * length : (b + 1) * length] = value


def add_own(own_in, base, high, low, late, lower):
    sites, length = lower.shape[1], high.shape[1]
    blocks = sites // length
    span = high.shape[0] // blocks
    halo = (late.shape[1] - sites) // 2
    keep(late, halo, own_in[...])
    for b in range(blocks):
        at, start = slice(b * length, (b + 1) * length), halo - b * length
        rows = slice(b * span + start, b * span + start + sites)
        lower[:, at] = base[:, at] + stacked_dot(late, slice(halo, halo + sites), high[rows], low[rows])


def chain_kernel(mine, own_in, base, high, low, _late, _lower, late, lower):
    pl.when(lax.axis_index("tm") == 2 * mine)(lambda: add_own(own_in, base, high, low, late, lower))


def rows_kernel(own_rows, other_rows, own_high, own_low, other_high, other_low):
    own_high[...], own_low[...] = halves(own_rows[: own_high.shape[0]])
    other_high[...], other_low[...] = halves(other_rows[...])


def add_parts(lower, own_rows, own_high, own_low, other_high, other_low, to_next, to_own, mid, far_mid, span):
    cols, sites = lower.shape
    length = own_rows.shape[1]
    blocks = sites // length
    halo = to_own.shape[1] - sites
    edge = halo - length
    row = lax.axis_index("row")
    keep(mid, 0, lower[...])
    near = pl.multiple_of(jnp.where(row == 0, sites - halo, 0), edge)
    for b in range(blocks):
        at, rows = slice(b * length, (b + 1) * length), slice(b * sites, (b + 1) * sites)
        const = slice(blocks * sites + b * cols, blocks * sites + (b + 1) * cols)
        to_own[:, at] = own_rows[const] + stacked_dot(mid, slice(0, sites), own_high[rows], own_low[rows])
    to_next[:, :halo] = to_own[:, pl.ds(near, halo)]
    for b in range(blocks):
        value = None
        cuts = [cuts_of(blocks, length, sites, span, last)[b] for last in (True, False)]
        for chunk in range(0, max(hi - lo for lo, hi, _ in cuts), edge):
            starts, froms, there = [], [], []
            for last, (lo, hi, packed) in zip((True, False), cuts):
                count = hi - lo
                there.append(chunk < count)
                starts.append(packed + chunk if chunk < count else 0)
                froms.append((0 if last else sites - count) + chunk if chunk < count else 0)
            start = pl.multiple_of(jnp.where(row == 0, starts[1], starts[0]), edge)
            source = pl.multiple_of(jnp.where(row == 0, froms[1], froms[0]), edge)
            rows = pl.ds(start, edge)
            product = stacked_dot(mid, pl.ds(source, edge), other_high[rows], other_low[rows])
            if not all(there):
                product = jnp.where((row == 0) == there[1], product, 0.0)
            value = product if value is None else value + product
        far_mid[:, b * length : (b + 1) * length] = value
    to_next[:, halo:] = far_mid[...]
    away = pl.multiple_of(jnp.where(row == 0, 0, sites - halo), edge)
    to_own[:, sites:] = far_mid[:, pl.ds(away, halo)]


def jump_kernel(mine, own_in, base, high, low, *rest):
    ship, (_late, _lower, late, lower, to_next, to_own, to_last, *scratch) = rest[:-9], rest[-9:]

    @pl.when(lax.axis_index("tm") == 2 * mine)
    def _():
        add_own(own_in, base, high, low, late, lower)
        add_parts(lower, *ship, to_next, to_own, *scratch, high.shape[0] * high.shape[1] // own_in.shape[1])
        to_last[...] = to_next[...]

    @pl.when(lax.axis_index("tm") != 2 * mine)
    def _():
        for part in (to_next, to_own, to_last):
            part[...] = jnp.zeros_like(part)


def parts_kernel(mine, span, lower, *rest):
    ship, parts = rest[:-4], rest[-4:]

    @pl.when(lax.axis_index("tm") == 2 * mine)
    def _():
        add_parts(lower, *ship, *parts, span)

    @pl.when(lax.axis_index("tm") != 2 * mine)
    def _():
        for part in parts[:2]:
            part[...] = jnp.zeros_like(part)


def last_kernel(jumps, both, high, low, late, _lower, lower):
    device = lax.axis_index("tm")
    pl.when((device == 0) | (device == 2) if jumps else device == 0)(lambda: step(both, high, low, late, lower))


def upper_kernel(sides, top, *rest):
    far, far_high, far_low, _late, _upper, late, upper = rest[-7:]
    cols, sites = upper.shape
    length = far.shape[1]
    blocks = sites // length
    window = far_high.shape[0] // blocks
    halo = (late.shape[1] - sites) // 2
    at_window = halo - (window - length) // 2
    messages = rest[:-7]

    if len(messages) == 2:

        @pl.when(lax.axis_index("tm") == 0)
        def _():
            load(sides, plain(messages[1]), messages[0][...], halo, late)

    for mine, (*next_in, own_in) in enumerate(((messages[0], messages[2], messages[1]), messages[3:]) if len(messages) > 2 else ()):

        @pl.when(lax.axis_index("tm") == 2 * mine)
        def _():
            from_next = next_in[0][...] + next_in[1][...] if len(next_in) == 2 else next_in[0][...]
            own = own_in[:, :sites] + from_next[:, halo:]
            near = own_in[:, sites:] + from_next[:, :halo]
            load(sides, lambda side, cut: near, own, halo, late)

    @pl.when(lax.axis_index("tm") != 2 * top)
    def _():
        for b in range(blocks):
            rows = slice(b * window, (b + 1) * window)
            at = blocks * window + b * cols
            start = at_window + b * length
            upper[:, b * length : (b + 1) * length] = far[at : at + cols] - stacked_dot(
                late, slice(start, start + window), far_high[rows], far_low[rows]
            )


def local(normals, inv_diag, lag_coupling, fill_mask):
    times, rows = lax.axis_size("tm"), lax.axis_size("row")
    device = lax.axis_index("tm")
    cols, sites = normals.shape[1:]
    blocks, length = inv_diag.shape[1:3]
    window = lag_coupling.shape[2]
    edge = (window - length) // 2
    halo = length + edge
    sides = 1 if rows == 2 else 2
    pairs = times // 2
    f32, bf16 = jnp.float32, jnp.bfloat16
    shape = jax.ShapeDtypeStruct

    def link(source, target):
        return [(s * rows + r, t * rows + r) for s, t in zip(source, target) for r in range(rows)]

    def cross(value, source, target, split=False):
        if sides == 1:
            perm = [(s * rows + r, t * rows + 1 - r) for s, t in zip(source, target) for r in range(2)]
            return lax.ppermute(value, BOTH, perm)
        moved = []
        for side, step in enumerate((1, -1)):
            perm = [
                (s * rows + r, t * rows + r + step)
                for s, t in zip(source, target)
                for r in range(rows)
                if 0 <= r + step < rows
            ]
            moved.append(lax.ppermute(value[side : side + 1] if split else value[None], BOTH, perm))
        return jnp.concatenate(moved)

    tall = blocks * window
    jump = 2
    jumps = rows == 2 and pairs > 5
    const, inv_high, inv_low = pl.pallas_call(
        const_kernel,
        out_shape=(
            shape((cols, sites), f32),
            shape((blocks, length, length), bf16), shape((blocks, length, length), bf16),
        ),
        in_specs=[HBM] * 2,
        out_specs=(VMEM,) * 3,
        scratch_shapes=[
            pltpu.VMEM(normals.shape[1:], f32),
            pltpu.VMEM(inv_diag.shape[1:], f32),
            pltpu.SemaphoreType.DMA((1 + blocks,)),
        ],
        compiler_params=PARAMS,
        cost_estimate=pl.CostEstimate(flops=5*10**9, bytes_accessed=0, transcendentals=0),
    )(*[pltpu.with_memory_space_constraint(a, pltpu.HBM) for a in (normals, inv_diag)])
    odd, even = range(1, times, 2), range(0, times, 2)
    first_next = cross(const, odd[-1:], even[-1:])
    first_own = lax.ppermute(const, BOTH, link(odd[-1:], even[-1:]))
    near, near_high, near_low = pl.pallas_call(
        fuse_kernel,
        out_shape=(
            shape((tall + blocks * cols, length), f32), shape((tall, length), bf16), shape((tall, length), bf16),
        ),
        in_specs=[VMEM] * 5,
        out_specs=(VMEM,) * 3,
        compiler_params=PARAMS,
        cost_estimate=pl.CostEstimate(
            flops=6 * (tall + cols * blocks) * length * length, bytes_accessed=16 * tall * length, transcendentals=0
        ),
    )(fill_mask, const, inv_high, inv_low, lag_coupling)
    edges = pl.pallas_call(
        functools.partial(edge_kernel, sides, blocks, cols),
        out_shape=shape((sides, window + cols, edge), f32),
        in_specs=[VMEM],
        out_specs=VMEM,
        compiler_params=PARAMS,
    )(near)
    near = pl.pallas_call(
        lambda _own, _edges, own: None,
        out_shape=shape(near.shape, f32),
        in_specs=[VMEM] * 2,
        out_specs=VMEM,
        input_output_aliases={0: 0},
        compiler_params=PARAMS,
    )(near, edges)
    rim = cross(edges, odd[:-1], even[:-1], True)
    far = lax.ppermute(near, BOTH, link(odd[:-1], even[:-1]))

    blank = jnp.zeros((cols, sites), f32)
    upper, lower = pl.pallas_call(
        functools.partial(top_kernel, pairs - 1, sides),
        out_shape=(shape((cols, sites), f32),) * 2,
        in_specs=[VMEM] * 7,
        out_specs=(VMEM,) * 2,
        scratch_shapes=[pltpu.VMEM((2 * cols, sites + 2 * edge), bf16)],
        input_output_aliases={5: 0, 6: 1},
        compiler_params=PARAMS,
        cost_estimate=pl.CostEstimate(flops=50 * 10**9, bytes_accessed=0, transcendentals=0),
    )(first_next, first_own, const, near_high, near_low, blank, blank)
    far_high, far_low, rim_high, rim_low = pl.pallas_call(
        split_kernel,
        out_shape=(
            shape((tall, length), bf16), shape((tall, length), bf16),
            shape((sides, window, edge), bf16), shape((sides, window, edge), bf16),
        ),
        in_specs=[VMEM] * 2,
        out_specs=(VMEM,) * 4,
        compiler_params=PARAMS,
    )(rim, far)
    packs = (shape((blocks * (sites + cols), length), f32), shape((halo + edge, length), f32)) if jumps else ()
    high, low, both, *packs = pl.pallas_call(
        functools.partial(pair_kernel, jumps),
        out_shape=(
            shape((2 * tall, length), bf16), shape((2 * tall, length), bf16), shape((cols, sites), f32), *packs
        ),
        in_specs=[VMEM] * 7,
        out_specs=(VMEM,) * (3 + len(packs)),
        scratch_shapes=[pltpu.VMEM((2 * window, length), f32)],
        compiler_params=PARAMS,
        cost_estimate=pl.CostEstimate(flops=10**9, bytes_accessed=0, transcendentals=0),
    )(far, rim, far_high, far_low, near_high, near_low, const)
    if jumps:
        source, target = [2 * jump - 2, 2 * jump], [2 * jump, 2 * jump + 2]
        own_rows = lax.ppermute(packs[0], BOTH, link(source, target))
        other_rows = cross(packs[1], source, target)
        ship = pl.pallas_call(
            rows_kernel,
            out_shape=(shape((blocks * sites, length), bf16),) * 2 + (shape(other_rows.shape, bf16),) * 2,
            in_specs=[VMEM] * 2,
            out_specs=(VMEM,) * 4,
            compiler_params=PARAMS,
        )(own_rows, other_rows)

    def turn(kernel, given, state, scratch=(), extra=(), flops=0):
        return pl.pallas_call(
            kernel,
            out_shape=tuple(shape(v.shape, v.dtype) for v in state) + tuple(extra),
            in_specs=[VMEM] * (len(given) + len(state)),
            out_specs=(VMEM,) * (len(state) + len(extra)),
            scratch_shapes=list(scratch),
            input_output_aliases={len(given) + i: i for i in range(len(state))},
            compiler_params=PARAMS,
            cost_estimate=pl.CostEstimate(flops=flops, bytes_accessed=0, transcendentals=0) if flops else None,
        )(*given, *state)

    parts = (shape((cols, sites + halo), f32),) * 2
    parts_scratch = [pltpu.VMEM((2 * cols, sites), bf16), pltpu.VMEM((cols, sites), f32)]
    late = jnp.zeros((2 * cols, sites + 2 * halo), bf16)
    mine = pairs - 1
    while mine > 0:
        if jumps and mine == jump:
            source, target = [2 * mine], [2 * mine - 4]
            first_in = lax.ppermute(to_next, BOTH, [(2 * source[0] + 1, 2 * target[0])])
            own_in = lax.ppermute(to_own, BOTH, link(source, target))
            next_in = lax.ppermute(to_last, BOTH, [(2 * source[0], 2 * target[0] + 1)])
            break
        source, target = [2 * mine], [2 * mine - 2]
        next_in = cross(lower, source, target)
        own_in = lax.ppermute(lower, BOTH, link(source, target))
        if jumps and mine == jump + 1:
            beside = pl.pallas_call(
                functools.partial(parts_kernel, mine, 2 * window),
                out_shape=parts,
                in_specs=[VMEM] * 6,
                out_specs=(VMEM,) * 2,
                scratch_shapes=parts_scratch,
                compiler_params=PARAMS,
            )(lower, own_rows, *ship)
            source, target = [2 * mine], [2 * mine - 4]
            beside_next = cross(beside[0], source, target)
            beside_own = lax.ppermute(beside[1], BOTH, link(source, target))
        mine -= 1
        if mine == 0:
            break
        if mine == pairs - 2:
            late, lower = turn(
                functools.partial(direct_kernel, mine, sides),
                (next_in, own_in, far, rim, far_high, far_low, rim_high, rim_low, near_high, near_low, const),
                (late, lower),
                [pltpu.VMEM((2 * cols, sites + 2 * edge), bf16)],
            )
            continue
        late, base = turn(
            functools.partial(rim_kernel, mine, sides),
            (next_in, both, high, low),
            (late,),
            extra=[shape((cols, sites), f32)],
        )
        if jumps and mine == jump:
            late, lower, to_next, to_own, to_last = turn(
                functools.partial(jump_kernel, mine),
                (own_in, base, high, low, own_rows, *ship),
                (late, lower),
                parts_scratch,
                parts + parts[:1],
            )
        else:
            late, lower = turn(
                functools.partial(chain_kernel, mine),
                (own_in, base, high, low),
                (late, lower),
                flops=50 * 10**9 if jumps and mine == pairs - 3 else 0,
            )
    given = (first_in, own_in, next_in, beside_next, beside_own) if jumps else (own_in, next_in)
    late, upper = turn(
        functools.partial(upper_kernel, sides, pairs - 1), (*given, far, far_high, far_low), (late, upper)
    )
    returned = lax.ppermute(upper, BOTH, link(even, odd))
    lower = pl.pallas_call(
        functools.partial(last_kernel, jumps),
        out_shape=shape(lower.shape, f32),
        in_specs=[VMEM] * 5,
        out_specs=VMEM,
        input_output_aliases={4: 0},
        compiler_params=PARAMS,
        cost_estimate=pl.CostEstimate(flops=12 * cols * tall * length, bytes_accessed=8 * tall * length, transcendentals=0),
    )(both, high, low, late, lower)
    return jnp.where(device % 2 == 0, lower, returned)[None]


def solution(mesh):
    placed = (
        P("tm", None, "row"),
        P("tm", "row", None, None),
        P("tm", "row", None, None),
        P("tm", "row", None),
    )
    return jax.shard_map(
        local, mesh=mesh, in_specs=placed, out_specs=P("tm", None, "row"), check_vma=False
    )
```

```python
import functools

import jax
import jax.numpy as jnp
from jax import lax
from jax.experimental import pallas as pl
from jax.experimental.pallas import tpu as pltpu
from jax.sharding import PartitionSpec as P

BOTH = ("tm", "row")
VMEM = pl.BlockSpec(memory_space=pltpu.VMEM)
HBM = pl.BlockSpec(memory_space=pltpu.HBM)
PARAMS = pltpu.CompilerParams(vmem_limit_bytes=32 * 1024 * 1024)


def halves(value):
    high = value.astype(jnp.bfloat16)
    low = (value - high.astype(jnp.float32)).astype(jnp.bfloat16)
    return high, low


def dot(a, b):
    return jnp.dot(a, b, preferred_element_type=jnp.float32)


def stacked_dot(pair, cols, high, low):
    rows = pair.shape[0] // 2
    wide = dot(pair[:, cols], high)
    return wide[:rows] + wide[rows:] + dot(pair[:rows, cols], low)


def triple(high, low, inv_high, inv_low):
    return dot(high, inv_high) + dot(low, inv_high) + dot(high, inv_low)


def put_rim(sides, rim, columns):
    if sides == 1:
        row = lax.axis_index("row")

        @pl.when(row == 0)
        def _():
            rim[0] = columns(True)

        @pl.when(row != 0)
        def _():
            rim[0] = columns(False)
    else:
        rim[0] = columns(True)
        rim[1] = columns(False)


def const_kernel(normals, inv, const, again, inv_high, inv_low, normals_in, inv_in, sems):
    blocks, length = inv.shape[1], inv.shape[2]
    moves = [pltpu.make_async_copy(normals.at[0], normals_in, sems.at[0])]
    for b in range(blocks):
        moves.append(pltpu.make_async_copy(inv.at[0, b], inv_in.at[b], sems.at[1 + b]))
    for move in moves:
        move.start()
    moves[0].wait()
    for b in range(blocks):
        at = slice(b * length, (b + 1) * length)
        high, low = halves(normals_in[:, at])
        moves[1 + b].wait()
        inv_high[b], inv_low[b] = halves(inv_in[b])
        const[:, at] = triple(high, low, inv_high[b], inv_low[b])
    again[...] = const[...]


def fuse_kernel(mask, const, inv_high, inv_low, lag, own, near_high, near_low):
    blocks, window, length = lag.shape[1:]
    edge = (window - length) // 2
    cols = const.shape[0]
    cuts = (0, edge, edge + length, window)
    flags = mask[0].astype(jnp.float32)
    for b in range(blocks):
        at = blocks * window + b * cols
        own[at : at + cols] = const[:, b * length : (b + 1) * length]
        for part in range(3):
            lo, hi = cuts[part], cuts[part + 1]
            rows = slice(b * window + lo, b * window + hi)
            high, low = halves(lag[0, b, lo:hi] * flags[b : b + 1, part : part + 1])
            value = triple(high, low, inv_high[b], inv_low[b])
            own[rows] = value
            near_high[rows], near_low[rows] = halves(value)


def edge_kernel(sides, blocks, cols, own, rim):
    length, edge = own.shape[1], rim.shape[2]
    window = length + 2 * edge

    def columns(last):
        b = blocks - 1 if last else 0
        cut = slice(length - edge, length) if last else slice(0, edge)
        at = blocks * window + b * cols
        return jnp.concatenate([own[b * window : (b + 1) * window, cut], own[at : at + cols, cut]])

    put_rim(sides, rim, columns)


def split_kernel(far, far_high, far_low):
    far_high[...], far_low[...] = halves(far[: far_high.shape[0]])


def cuts_of(blocks, length, sites, span, last):
    packed, cuts = 0, []
    for b in range(blocks):
        start = span // 2 - length // 2 - b * length
        lo, hi = (start + sites, span) if last else (0, start)
        cuts.append((lo, hi, packed))
        packed += hi - lo
    return cuts


def pair_kernel(first, jump, *refs):
    here = lax.axis_index("tm") == 2 * first[0]
    pl.when(here if first[1] else jnp.logical_not(here))(lambda: make_pair(jump, *refs))


def make_pair(jump, far, rim, far_high, far_low, near_high, near_low, const, high, low, both, *rest):
    cols, sites = const.shape
    length = far.shape[1]
    blocks = sites // length
    window = near_high.shape[0] // blocks
    edge = (window - length) // 2
    span = 2 * window
    tall = blocks * window
    total = rest[-1]
    if rim.shape[0] == 1:
        flag = jnp.minimum(lax.axis_index("row"), 1).astype(jnp.float32)
        left, right = rim[0] * flag, rim[0] * (1 - flag)
    else:
        left, right = rim[0], rim[1]
    left_pair, right_pair = halves(left[:window]), halves(right[:window])
    for b in range(blocks):
        here = slice(b * window, (b + 1) * window)
        column = slice(b * length, (b + 1) * length)

        def part(lo, hi):
            rows = slice(b * window + lo, b * window + hi)
            return near_high[rows], near_low[rows]

        def constant(block):
            if block < 0:
                return left[window:]
            if block == blocks:
                return right[window:]
            return far[tall + block * cols : tall + (block + 1) * cols]

        if b > 0:
            before = slice((b - 1) * window, b * window)
            low_pair = far_high[before, length - edge :], far_low[before, length - edge :]
            low_const = constant(b - 1)[:, length - edge :]
        else:
            low_pair, low_const = left_pair, constant(-1)
        if b + 1 < blocks:
            after = slice((b + 1) * window, (b + 2) * window)
            high_pair = far_high[after, :edge], far_low[after, :edge]
            high_const = constant(b + 1)[:, :edge]
        else:
            high_pair, high_const = right_pair, constant(blocks)
        first = triple(*low_pair, *part(0, edge))
        middle = triple(far_high[here], far_low[here], *part(edge, edge + length))
        last = triple(*high_pair, *part(edge + length, window))
        total[:window] = first
        total[window:] = last
        total[length : length + window] += middle
        high[b * span : (b + 1) * span], low[b * span : (b + 1) * span] = halves(total[...])
        both[:, column] = const[:, column] - (
            triple(*halves(low_const), *part(0, edge))
            + triple(*halves(constant(b)), *part(edge, edge + length))
            + triple(*halves(high_const), *part(edge + length, window))
        )
    if jump:
        own_rows, other_rows = rest[:2]

        def value(start, count):
            rows = pl.ds(start, count)
            return high[rows].astype(jnp.float32) + low[rows].astype(jnp.float32)

        for b in range(blocks):
            own_rows[b * sites : (b + 1) * sites] = value(b * span + window - edge - b * length, sites)
            at = blocks * sites + b * cols
            own_rows[at : at + cols] = both[:, b * length : (b + 1) * length]
        starts = [
            [b * span + at for b, (lo, hi, _) in enumerate(cuts_of(blocks, length, sites, span, last)) for at in range(lo, hi, edge)]
            for last in (True, False)
        ]
        row = lax.axis_index("row")
        for chunk, (on_right, on_left) in enumerate(zip(*starts)):
            start = pl.multiple_of(jnp.where(row == 0, on_right, on_left), edge)
            other_rows[chunk * edge : (chunk + 1) * edge] = value(start, edge)


def keep(ref, start, value):
    cols, width = value.shape
    high, low = halves(value)
    ref[:cols, pl.ds(start, width)] = high
    ref[cols:, pl.ds(start, width)] = low


def load(sides, pick, own, halo, ref):
    sites = own.shape[1]
    keep(ref, halo, own)
    for side in range(sides):
        on_right = 1 - jnp.minimum(lax.axis_index("row"), 1).astype(jnp.int32) if sides == 1 else side
        start = pl.multiple_of((1 - on_right) * (sites - halo), 128)
        keep(ref, pl.multiple_of(on_right * (halo + sites), 128), pick(side, pl.ds(start, halo)))


def plain(next_in):
    return lambda side, cut: next_in[:, cut] if len(next_in.shape) == 2 else next_in[side, :, cut]


def top_kernel(mine, sides, next_in, own_in, const, near_high, near_low, _upper, _lower, upper, lower, mid):
    sites = lower.shape[1]
    length = near_high.shape[1]
    blocks = sites // length
    window = near_high.shape[0] // blocks
    edge = (window - length) // 2

    @pl.when(lax.axis_index("tm") == 2 * mine)
    def _():
        mid[...] = jnp.zeros_like(mid)
        load(sides, plain(next_in), own_in[...], edge, mid)
        upper[...] = own_in[...]
        for b in range(blocks):
            at, rows = slice(b * length, (b + 1) * length), slice(b * window, (b + 1) * window)
            product = stacked_dot(mid, slice(b * length, b * length + window), near_high[rows], near_low[rows])
            lower[:, at] = const[:, at] - product


def step(both, high, low, late, lower):
    blocks = lower.shape[1] // high.shape[1]
    length, span = high.shape[1], high.shape[0] // blocks
    for b in range(blocks):
        at, rows = slice(b * length, (b + 1) * length), slice(b * span, (b + 1) * span)
        lower[:, at] = both[:, at] + stacked_dot(late, slice(b * length, b * length + span), high[rows], low[rows])


def load_rims(sides, next_in, sites, halo, late):
    for side in range(sides):
        on_right = 1 - jnp.minimum(lax.axis_index("row"), 1).astype(jnp.int32) if sides == 1 else side
        start = pl.multiple_of((1 - on_right) * (sites - halo), 128)
        keep(late, pl.multiple_of(on_right * (halo + sites), 128), plain(next_in)(side, pl.ds(start, halo)))


def rim_kernel(mine, sides, next_in, both, high, low, _late, late, base):
    sites, length = base.shape[1], high.shape[1]
    blocks = sites // length
    span = high.shape[0] // blocks
    halo = (late.shape[1] - sites) // 2
    edge = halo - length

    @pl.when(lax.axis_index("tm") == 2 * mine)
    def _():
        load_rims(sides, next_in, sites, halo, late)
        cuts = [cuts_of(blocks, length, sites, span, last) for last in (False, True)]
        for b in range(blocks):
            value = both[:, b * length : (b + 1) * length]
            if sides == 2:
                for lo, hi, _ in (cuts[0][b], cuts[1][b]):
                    rows = slice(b * span + lo, b * span + hi)
                    value += stacked_dot(late, slice(b * length + lo, b * length + hi), high[rows], low[rows])
            else:
                on_left = lax.axis_index("row") != 0
                counts = [cut[b][1] - cut[b][0] for cut in cuts]
                for chunk in range(0, max(counts), edge):
                    starts = [cut[b][0] + chunk if chunk < count else 0 for cut, count in zip(cuts, counts)]
                    start = pl.multiple_of(jnp.where(on_left, starts[0], starts[1]), edge)
                    rows = pl.ds(b * span + start, edge)
                    product = stacked_dot(late, pl.ds(b * length + start, edge), high[rows], low[rows])
                    if chunk >= min(counts):
                        product = jnp.where(on_left == (counts[0] > counts[1]), product, 0.0)
                    value += product
            base[:, b * length : (b + 1) * length] = value


def add_own(own_in, base, high, low, late, lower):
    sites, length = lower.shape[1], high.shape[1]
    blocks = sites // length
    span = high.shape[0] // blocks
    halo = (late.shape[1] - sites) // 2
    keep(late, halo, own_in[...])
    for b in range(blocks):
        at, start = slice(b * length, (b + 1) * length), halo - b * length
        rows = slice(b * span + start, b * span + start + sites)
        lower[:, at] = base[:, at] + stacked_dot(late, slice(halo, halo + sites), high[rows], low[rows])


def chain_kernel(mine, own_in, base, high, low, _late, _lower, late, lower):
    pl.when(lax.axis_index("tm") == 2 * mine)(lambda: add_own(own_in, base, high, low, late, lower))


def rows_kernel(own_rows, other_rows, own_high, own_low, other_high, other_low):
    own_high[...], own_low[...] = halves(own_rows[: own_high.shape[0]])
    other_high[...], other_low[...] = halves(other_rows[...])


def add_parts(lower, own_rows, own_high, own_low, other_high, other_low, to_next, to_own, mid, far_mid, span):
    cols, sites = lower.shape
    length = own_rows.shape[1]
    blocks = sites // length
    halo = to_own.shape[1] - sites
    edge = halo - length
    row = lax.axis_index("row")
    keep(mid, 0, lower[...])
    near = pl.multiple_of(jnp.where(row == 0, sites - halo, 0), edge)
    for b in range(blocks):
        at, rows = slice(b * length, (b + 1) * length), slice(b * sites, (b + 1) * sites)
        const = slice(blocks * sites + b * cols, blocks * sites + (b + 1) * cols)
        to_own[:, at] = own_rows[const] + stacked_dot(mid, slice(0, sites), own_high[rows], own_low[rows])
    to_next[:, :halo] = to_own[:, pl.ds(near, halo)]
    for b in range(blocks):
        value = None
        cuts = [cuts_of(blocks, length, sites, span, last)[b] for last in (True, False)]
        for chunk in range(0, max(hi - lo for lo, hi, _ in cuts), edge):
            starts, froms, there = [], [], []
            for last, (lo, hi, packed) in zip((True, False), cuts):
                count = hi - lo
                there.append(chunk < count)
                starts.append(packed + chunk if chunk < count else 0)
                froms.append((0 if last else sites - count) + chunk if chunk < count else 0)
            start = pl.multiple_of(jnp.where(row == 0, starts[1], starts[0]), edge)
            source = pl.multiple_of(jnp.where(row == 0, froms[1], froms[0]), edge)
            rows = pl.ds(start, edge)
            product = stacked_dot(mid, pl.ds(source, edge), other_high[rows], other_low[rows])
            if not all(there):
                product = jnp.where((row == 0) == there[1], product, 0.0)
            value = product if value is None else value + product
        far_mid[:, b * length : (b + 1) * length] = value
    to_next[:, halo:] = far_mid[...]
    away = pl.multiple_of(jnp.where(row == 0, 0, sites - halo), edge)
    to_own[:, sites:] = far_mid[:, pl.ds(away, halo)]


def jump_kernel(mine, own_in, base, high, low, *rest):
    ship, (_late, _lower, late, lower, to_next, to_own, to_last, *scratch) = rest[:-9], rest[-9:]

    @pl.when(lax.axis_index("tm") == 2 * mine)
    def _():
        add_own(own_in, base, high, low, late, lower)
        add_parts(lower, *ship, to_next, to_own, *scratch, high.shape[0] * high.shape[1] // own_in.shape[1])
        to_last[...] = to_next[...]

    @pl.when(lax.axis_index("tm") != 2 * mine)
    def _():
        for part in (to_next, to_own, to_last):
            part[...] = jnp.zeros_like(part)


def parts_kernel(mine, span, lower, *rest):
    ship, parts = rest[:-4], rest[-4:]

    @pl.when(lax.axis_index("tm") == 2 * mine)
    def _():
        add_parts(lower, *ship, *parts, span)

    @pl.when(lax.axis_index("tm") != 2 * mine)
    def _():
        for part in parts[:2]:
            part[...] = jnp.zeros_like(part)


def last_kernel(jumps, both, high, low, late, _lower, lower):
    device = lax.axis_index("tm")
    pl.when((device == 0) | (device == 2) if jumps else device == 0)(lambda: step(both, high, low, late, lower))


def upper_kernel(sides, top, *rest):
    far, far_high, far_low, _late, _upper, late, upper = rest[-7:]
    cols, sites = upper.shape
    length = far.shape[1]
    blocks = sites // length
    window = far_high.shape[0] // blocks
    halo = (late.shape[1] - sites) // 2
    at_window = halo - (window - length) // 2
    messages = rest[:-7]

    if len(messages) == 2:

        @pl.when(lax.axis_index("tm") == 0)
        def _():
            load(sides, plain(messages[1]), messages[0][...], halo, late)

    for mine, (*next_in, own_in) in enumerate(((messages[0], messages[2], messages[1]), messages[3:]) if len(messages) > 2 else ()):

        @pl.when(lax.axis_index("tm") == 2 * mine)
        def _():
            from_next = next_in[0][...] + next_in[1][...] if len(next_in) == 2 else next_in[0][...]
            own = own_in[:, :sites] + from_next[:, halo:]
            near = own_in[:, sites:] + from_next[:, :halo]
            load(sides, lambda side, cut: near, own, halo, late)

    @pl.when(lax.axis_index("tm") != 2 * top)
    def _():
        for b in range(blocks):
            rows = slice(b * window, (b + 1) * window)
            at = blocks * window + b * cols
            start = at_window + b * length
            upper[:, b * length : (b + 1) * length] = far[at : at + cols] - stacked_dot(
                late, slice(start, start + window), far_high[rows], far_low[rows]
            )


def local(normals, inv_diag, lag_coupling, fill_mask):
    times, rows = lax.axis_size("tm"), lax.axis_size("row")
    device = lax.axis_index("tm")
    cols, sites = normals.shape[1:]
    blocks, length = inv_diag.shape[1:3]
    window = lag_coupling.shape[2]
    edge = (window - length) // 2
    halo = length + edge
    sides = 1 if rows == 2 else 2
    pairs = times // 2
    f32, bf16 = jnp.float32, jnp.bfloat16
    shape = jax.ShapeDtypeStruct

    def link(source, target):
        return [(s * rows + r, t * rows + r) for s, t in zip(source, target) for r in range(rows)]

    def cross(value, source, target, split=False):
        if sides == 1:
            perm = [(s * rows + r, t * rows + 1 - r) for s, t in zip(source, target) for r in range(2)]
            return lax.ppermute(value, BOTH, perm)
        moved = []
        for side, step in enumerate((1, -1)):
            perm = [
                (s * rows + r, t * rows + r + step)
                for s, t in zip(source, target)
                for r in range(rows)
                if 0 <= r + step < rows
            ]
            moved.append(lax.ppermute(value[side : side + 1] if split else value[None], BOTH, perm))
        return jnp.concatenate(moved)

    tall = blocks * window
    jump = 2
    jumps = rows == 2 and pairs > 5
    const, again, inv_high, inv_low = pl.pallas_call(
        const_kernel,
        out_shape=(
            shape((cols, sites), f32), shape((cols, sites), f32),
            shape((blocks, length, length), bf16), shape((blocks, length, length), bf16),
        ),
        in_specs=[HBM] * 2,
        out_specs=(VMEM,) * 4,
        scratch_shapes=[
            pltpu.VMEM(normals.shape[1:], f32),
            pltpu.VMEM(inv_diag.shape[1:], f32),
            pltpu.SemaphoreType.DMA((1 + blocks,)),
        ],
        compiler_params=PARAMS,
        cost_estimate=pl.CostEstimate(flops=5*10**9, bytes_accessed=0, transcendentals=0),
    )(*[pltpu.with_memory_space_constraint(a, pltpu.HBM) for a in (normals, inv_diag)])
    odd, even = range(1, times, 2), range(0, times, 2)
    first_next = cross(const, odd[-1:], even[-1:])
    first_own = lax.ppermute(again, BOTH, link(odd[-1:], even[-1:]))
    near, near_high, near_low = pl.pallas_call(
        fuse_kernel,
        out_shape=(
            shape((tall + blocks * cols, length), f32), shape((tall, length), bf16), shape((tall, length), bf16),
        ),
        in_specs=[VMEM] * 5,
        out_specs=(VMEM,) * 3,
        compiler_params=PARAMS,
        cost_estimate=pl.CostEstimate(
            flops=6 * (tall + cols * blocks) * length * length, bytes_accessed=16 * tall * length, transcendentals=0
        ),
    )(fill_mask, const, inv_high, inv_low, lag_coupling)
    edges = pl.pallas_call(
        functools.partial(edge_kernel, sides, blocks, cols),
        out_shape=shape((sides, window + cols, edge), f32),
        in_specs=[VMEM],
        out_specs=VMEM,
        compiler_params=PARAMS,
    )(near)
    near = pl.pallas_call(
        lambda _own, _edges, own: None,
        out_shape=shape(near.shape, f32),
        in_specs=[VMEM] * 2,
        out_specs=VMEM,
        input_output_aliases={0: 0},
        compiler_params=PARAMS,
    )(near, edges)
    rim = cross(edges, odd[:-1], even[:-1], True)
    far = lax.ppermute(near, BOTH, link(odd[:-1], even[:-1]))

    blank = jnp.zeros((cols, sites), f32)
    upper, lower = pl.pallas_call(
        functools.partial(top_kernel, pairs - 1, sides),
        out_shape=(shape((cols, sites), f32),) * 2,
        in_specs=[VMEM] * 7,
        out_specs=(VMEM,) * 2,
        scratch_shapes=[pltpu.VMEM((2 * cols, sites + 2 * edge), bf16)],
        input_output_aliases={5: 0, 6: 1},
        compiler_params=PARAMS,
        cost_estimate=pl.CostEstimate(flops=50 * 10**9, bytes_accessed=0, transcendentals=0),
    )(first_next, first_own, const, near_high, near_low, blank, blank)
    far_high, far_low = pl.pallas_call(
        split_kernel,
        out_shape=(shape((tall, length), bf16), shape((tall, length), bf16)),
        in_specs=[VMEM],
        out_specs=(VMEM,) * 2,
        compiler_params=PARAMS,
    )(far)
    packs = (shape((blocks * (sites + cols), length), f32), shape((halo + edge, length), f32)) if jumps else ()

    def pair_matrix(first, jumps, packs):
        return pl.pallas_call(
            functools.partial(pair_kernel, (pairs - 2, first), jumps),
            out_shape=(
                shape((2 * tall, length), bf16), shape((2 * tall, length), bf16), shape((cols, sites), f32), *packs
            ),
            in_specs=[VMEM] * 7,
            out_specs=(VMEM,) * (3 + len(packs)),
            scratch_shapes=[pltpu.VMEM((2 * window, length), f32)],
            compiler_params=PARAMS,
            cost_estimate=pl.CostEstimate(flops=10**9, bytes_accessed=0, transcendentals=0),
        )(far, rim, far_high, far_low, near_high, near_low, const)

    early = pair_matrix(True, False, ())
    high, low, both, *packs = pair_matrix(False, jumps, packs)
    if jumps:
        source, target = [2 * jump - 2, 2 * jump], [2 * jump, 2 * jump + 2]
        own_rows = lax.ppermute(packs[0], BOTH, link(source, target))
        other_rows = cross(packs[1], source, target)
        ship = pl.pallas_call(
            rows_kernel,
            out_shape=(shape((blocks * sites, length), bf16),) * 2 + (shape(other_rows.shape, bf16),) * 2,
            in_specs=[VMEM] * 2,
            out_specs=(VMEM,) * 4,
            compiler_params=PARAMS,
        )(own_rows, other_rows)

    def turn(kernel, given, state, scratch=(), extra=(), flops=0):
        return pl.pallas_call(
            kernel,
            out_shape=tuple(shape(v.shape, v.dtype) for v in state) + tuple(extra),
            in_specs=[VMEM] * (len(given) + len(state)),
            out_specs=(VMEM,) * (len(state) + len(extra)),
            scratch_shapes=list(scratch),
            input_output_aliases={len(given) + i: i for i in range(len(state))},
            compiler_params=PARAMS,
            cost_estimate=pl.CostEstimate(flops=flops, bytes_accessed=0, transcendentals=0) if flops else None,
        )(*given, *state)

    parts = (shape((cols, sites + halo), f32),) * 2
    parts_scratch = [pltpu.VMEM((2 * cols, sites), bf16), pltpu.VMEM((cols, sites), f32)]
    late = jnp.zeros((2 * cols, sites + 2 * halo), bf16)
    mine = pairs - 1
    while mine > 0:
        if jumps and mine == jump:
            source, target = [2 * mine], [2 * mine - 4]
            first_in = lax.ppermute(to_next, BOTH, [(2 * source[0] + 1, 2 * target[0])])
            own_in = lax.ppermute(to_own, BOTH, link(source, target))
            next_in = lax.ppermute(to_last, BOTH, [(2 * source[0], 2 * target[0] + 1)])
            break
        source, target = [2 * mine], [2 * mine - 2]
        next_in = cross(lower, source, target)
        own_in = lax.ppermute(lower, BOTH, link(source, target))
        if jumps and mine == jump + 1:
            beside = pl.pallas_call(
                functools.partial(parts_kernel, mine, 2 * window),
                out_shape=parts,
                in_specs=[VMEM] * 6,
                out_specs=(VMEM,) * 2,
                scratch_shapes=parts_scratch,
                compiler_params=PARAMS,
            )(lower, own_rows, *ship)
            source, target = [2 * mine], [2 * mine - 4]
            beside_next = cross(beside[0], source, target)
            beside_own = lax.ppermute(beside[1], BOTH, link(source, target))
        mine -= 1
        if mine == 0:
            break
        here = early if mine == pairs - 2 else (high, low, both)
        late, base = turn(
            functools.partial(rim_kernel, mine, sides),
            (next_in, here[2], *here[:2]),
            (late,),
            extra=[shape((cols, sites), f32)],
        )
        if jumps and mine == jump:
            late, lower, to_next, to_own, to_last = turn(
                functools.partial(jump_kernel, mine),
                (own_in, base, high, low, own_rows, *ship),
                (late, lower),
                parts_scratch,
                parts + parts[:1],
            )
        else:
            late, lower = turn(
                functools.partial(chain_kernel, mine),
                (own_in, base, *here[:2]),
                (late, lower),
                flops=50 * 10**9 if jumps and mine == pairs - 3 else 0,
            )
    given = (first_in, own_in, next_in, beside_next, beside_own) if jumps else (own_in, next_in)
    late, upper = turn(
        functools.partial(upper_kernel, sides, pairs - 1), (*given, far, far_high, far_low), (late, upper)
    )
    returned = lax.ppermute(upper, BOTH, link(even, odd))
    lower = pl.pallas_call(
        functools.partial(last_kernel, jumps),
        out_shape=shape(lower.shape, f32),
        in_specs=[VMEM] * 5,
        out_specs=VMEM,
        input_output_aliases={4: 0},
        compiler_params=PARAMS,
        cost_estimate=pl.CostEstimate(flops=12 * cols * tall * length, bytes_accessed=8 * tall * length, transcendentals=0),
    )(both, high, low, late, lower)
    return jnp.where(device % 2 == 0, lower, returned)[None]


def solution(mesh):
    placed = (
        P("tm", None, "row"),
        P("tm", "row", None, None),
        P("tm", "row", None, None),
        P("tm", "row", None),
    )
    return jax.shard_map(
        local, mesh=mesh, in_specs=placed, out_specs=P("tm", None, "row"), check_vma=False
    )
```

```python
import functools

import jax
import jax.numpy as jnp
from jax import lax
from jax.experimental import pallas as pl
from jax.experimental.pallas import tpu as pltpu
from jax.sharding import PartitionSpec as P

BOTH = ("tm", "row")
VMEM = pl.BlockSpec(memory_space=pltpu.VMEM)
HBM = pl.BlockSpec(memory_space=pltpu.HBM)
PARAMS = pltpu.CompilerParams(vmem_limit_bytes=32 * 1024 * 1024)


def halves(value):
    high = value.astype(jnp.bfloat16)
    low = (value - high.astype(jnp.float32)).astype(jnp.bfloat16)
    return high, low


def dot(a, b):
    return jnp.dot(a, b, preferred_element_type=jnp.float32)


def stacked_dot(pair, cols, high, low):
    rows = pair.shape[0] // 2
    wide = dot(pair[:, cols], high)
    return wide[:rows] + wide[rows:] + dot(pair[:rows, cols], low)


def triple(high, low, inv_high, inv_low):
    return dot(high, inv_high) + dot(low, inv_high) + dot(high, inv_low)


def put_rim(sides, rim, columns):
    if sides == 1:
        row = lax.axis_index("row")

        @pl.when(row == 0)
        def _():
            rim[0] = columns(True)

        @pl.when(row != 0)
        def _():
            rim[0] = columns(False)
    else:
        rim[0] = columns(True)
        rim[1] = columns(False)


def fuse_kernel(
    mask, normals, inv, lag, const, again, own, near_high, near_low, mask_in, normals_in, inv_in, lag_in, sems
):
    blocks, length = inv.shape[1], inv.shape[2]
    window, cols = lag.shape[2], normals.shape[1]
    edge = (window - length) // 2
    cuts = (0, edge, edge + length, window)
    moves = [pltpu.make_async_copy(normals.at[0], normals_in, sems.at[0])]
    for b in range(blocks):
        moves.append(pltpu.make_async_copy(inv.at[0, b], inv_in.at[b], sems.at[1 + b]))
    moves.append(pltpu.make_async_copy(mask.at[0], mask_in, sems.at[1 + blocks]))
    for b in range(blocks):
        moves.append(pltpu.make_async_copy(lag.at[0, b], lag_in.at[b], sems.at[2 + blocks + b]))
    for move in moves:
        move.start()
    moves[0].wait()
    pairs = []
    for b in range(blocks):
        at = slice(b * length, (b + 1) * length)
        high, low = halves(normals_in[:, at])
        moves[1 + b].wait()
        pairs.append(halves(inv_in[b]))
        value = triple(high, low, *pairs[b])
        const[:, at] = value
        again[:, at] = value
        own[blocks * window + b * cols : blocks * window + (b + 1) * cols] = value
    moves[1 + blocks].wait()
    flags = mask_in[...].astype(jnp.float32)
    for b in range(blocks):
        moves[2 + blocks + b].wait()
        for part in range(3):
            lo, hi = cuts[part], cuts[part + 1]
            rows = slice(b * window + lo, b * window + hi)
            high, low = halves(lag_in[b, lo:hi] * flags[b : b + 1, part : part + 1])
            value = triple(high, low, *pairs[b])
            own[rows] = value
            near_high[rows], near_low[rows] = halves(value)


def edge_kernel(sides, blocks, cols, own, rim):
    length, edge = own.shape[1], rim.shape[2]
    window = length + 2 * edge

    def columns(last):
        b = blocks - 1 if last else 0
        cut = slice(length - edge, length) if last else slice(0, edge)
        at = blocks * window + b * cols
        return jnp.concatenate([own[b * window : (b + 1) * window, cut], own[at : at + cols, cut]])

    put_rim(sides, rim, columns)


def split_kernel(far, far_high, far_low):
    far_high[...], far_low[...] = halves(far[: far_high.shape[0]])


def cuts_of(blocks, length, sites, span, last):
    packed, cuts = 0, []
    for b in range(blocks):
        start = span // 2 - length // 2 - b * length
        lo, hi = (start + sites, span) if last else (0, start)
        cuts.append((lo, hi, packed))
        packed += hi - lo
    return cuts


def pair_kernel(first, jump, *refs):
    here = lax.axis_index("tm") == 2 * first[0]
    pl.when(here if first[1] else jnp.logical_not(here))(lambda: make_pair(jump, *refs))


def make_pair(jump, far, rim, far_high, far_low, near_high, near_low, const, high, low, both, *rest):
    cols, sites = const.shape
    length = far.shape[1]
    blocks = sites // length
    window = near_high.shape[0] // blocks
    edge = (window - length) // 2
    span = 2 * window
    tall = blocks * window
    total = rest[-1]
    if rim.shape[0] == 1:
        flag = jnp.minimum(lax.axis_index("row"), 1).astype(jnp.float32)
        left, right = rim[0] * flag, rim[0] * (1 - flag)
    else:
        left, right = rim[0], rim[1]
    left_pair, right_pair = halves(left[:window]), halves(right[:window])
    for b in range(blocks):
        here = slice(b * window, (b + 1) * window)
        column = slice(b * length, (b + 1) * length)

        def part(lo, hi):
            rows = slice(b * window + lo, b * window + hi)
            return near_high[rows], near_low[rows]

        def constant(block):
            if block < 0:
                return left[window:]
            if block == blocks:
                return right[window:]
            return far[tall + block * cols : tall + (block + 1) * cols]

        if b > 0:
            before = slice((b - 1) * window, b * window)
            low_pair = far_high[before, length - edge :], far_low[before, length - edge :]
            low_const = constant(b - 1)[:, length - edge :]
        else:
            low_pair, low_const = left_pair, constant(-1)
        if b + 1 < blocks:
            after = slice((b + 1) * window, (b + 2) * window)
            high_pair = far_high[after, :edge], far_low[after, :edge]
            high_const = constant(b + 1)[:, :edge]
        else:
            high_pair, high_const = right_pair, constant(blocks)
        first = triple(*low_pair, *part(0, edge))
        middle = triple(far_high[here], far_low[here], *part(edge, edge + length))
        last = triple(*high_pair, *part(edge + length, window))
        total[:window] = first
        total[window:] = last
        total[length : length + window] += middle
        high[b * span : (b + 1) * span], low[b * span : (b + 1) * span] = halves(total[...])
        both[:, column] = const[:, column] - (
            triple(*halves(low_const), *part(0, edge))
            + triple(*halves(constant(b)), *part(edge, edge + length))
            + triple(*halves(high_const), *part(edge + length, window))
        )
    if jump:
        own_rows, other_rows = rest[:2]

        def value(start, count):
            rows = pl.ds(start, count)
            return high[rows].astype(jnp.float32) + low[rows].astype(jnp.float32)

        for b in range(blocks):
            own_rows[b * sites : (b + 1) * sites] = value(b * span + window - edge - b * length, sites)
            at = blocks * sites + b * cols
            own_rows[at : at + cols] = both[:, b * length : (b + 1) * length]
        starts = [
            [b * span + at for b, (lo, hi, _) in enumerate(cuts_of(blocks, length, sites, span, last)) for at in range(lo, hi, edge)]
            for last in (True, False)
        ]
        row = lax.axis_index("row")
        for chunk, (on_right, on_left) in enumerate(zip(*starts)):
            start = pl.multiple_of(jnp.where(row == 0, on_right, on_left), edge)
            other_rows[chunk * edge : (chunk + 1) * edge] = value(start, edge)


def keep(ref, start, value):
    cols, width = value.shape
    high, low = halves(value)
    ref[:cols, pl.ds(start, width)] = high
    ref[cols:, pl.ds(start, width)] = low


def load(sides, pick, own, halo, ref):
    sites = own.shape[1]
    keep(ref, halo, own)
    for side in range(sides):
        on_right = 1 - jnp.minimum(lax.axis_index("row"), 1).astype(jnp.int32) if sides == 1 else side
        start = pl.multiple_of((1 - on_right) * (sites - halo), 128)
        keep(ref, pl.multiple_of(on_right * (halo + sites), 128), pick(side, pl.ds(start, halo)))


def plain(next_in):
    return lambda side, cut: next_in[:, cut] if len(next_in.shape) == 2 else next_in[side, :, cut]


def top_kernel(mine, sides, next_in, own_in, const, near_high, near_low, _upper, _lower, upper, lower, mid):
    sites = lower.shape[1]
    length = near_high.shape[1]
    blocks = sites // length
    window = near_high.shape[0] // blocks
    edge = (window - length) // 2

    @pl.when(lax.axis_index("tm") == 2 * mine)
    def _():
        mid[...] = jnp.zeros_like(mid)
        load(sides, plain(next_in), own_in[...], edge, mid)
        upper[...] = own_in[...]
        for b in range(blocks):
            at, rows = slice(b * length, (b + 1) * length), slice(b * window, (b + 1) * window)
            product = stacked_dot(mid, slice(b * length, b * length + window), near_high[rows], near_low[rows])
            lower[:, at] = const[:, at] - product


def step(both, high, low, late, lower):
    blocks = lower.shape[1] // high.shape[1]
    length, span = high.shape[1], high.shape[0] // blocks
    for b in range(blocks):
        at, rows = slice(b * length, (b + 1) * length), slice(b * span, (b + 1) * span)
        lower[:, at] = both[:, at] + stacked_dot(late, slice(b * length, b * length + span), high[rows], low[rows])


def load_rims(sides, next_in, sites, halo, late):
    for side in range(sides):
        on_right = 1 - jnp.minimum(lax.axis_index("row"), 1).astype(jnp.int32) if sides == 1 else side
        start = pl.multiple_of((1 - on_right) * (sites - halo), 128)
        keep(late, pl.multiple_of(on_right * (halo + sites), 128), plain(next_in)(side, pl.ds(start, halo)))


def rim_kernel(mine, sides, next_in, both, high, low, _late, late, base):
    sites, length = base.shape[1], high.shape[1]
    blocks = sites // length
    span = high.shape[0] // blocks
    halo = (late.shape[1] - sites) // 2
    edge = halo - length

    @pl.when(lax.axis_index("tm") == 2 * mine)
    def _():
        load_rims(sides, next_in, sites, halo, late)
        cuts = [cuts_of(blocks, length, sites, span, last) for last in (False, True)]
        for b in range(blocks):
            value = both[:, b * length : (b + 1) * length]
            if sides == 2:
                for lo, hi, _ in (cuts[0][b], cuts[1][b]):
                    rows = slice(b * span + lo, b * span + hi)
                    value += stacked_dot(late, slice(b * length + lo, b * length + hi), high[rows], low[rows])
            else:
                on_left = lax.axis_index("row") != 0
                counts = [cut[b][1] - cut[b][0] for cut in cuts]
                for chunk in range(0, max(counts), edge):
                    starts = [cut[b][0] + chunk if chunk < count else 0 for cut, count in zip(cuts, counts)]
                    start = pl.multiple_of(jnp.where(on_left, starts[0], starts[1]), edge)
                    rows = pl.ds(b * span + start, edge)
                    product = stacked_dot(late, pl.ds(b * length + start, edge), high[rows], low[rows])
                    if chunk >= min(counts):
                        product = jnp.where(on_left == (counts[0] > counts[1]), product, 0.0)
                    value += product
            base[:, b * length : (b + 1) * length] = value


def add_own(own_in, base, high, low, late, lower):
    sites, length = lower.shape[1], high.shape[1]
    blocks = sites // length
    span = high.shape[0] // blocks
    halo = (late.shape[1] - sites) // 2
    keep(late, halo, own_in[...])
    for b in range(blocks):
        at, start = slice(b * length, (b + 1) * length), halo - b * length
        rows = slice(b * span + start, b * span + start + sites)
        lower[:, at] = base[:, at] + stacked_dot(late, slice(halo, halo + sites), high[rows], low[rows])


def chain_kernel(mine, own_in, base, high, low, _late, _lower, late, lower):
    pl.when(lax.axis_index("tm") == 2 * mine)(lambda: add_own(own_in, base, high, low, late, lower))


def rows_kernel(own_rows, other_rows, own_high, own_low, other_high, other_low):
    own_high[...], own_low[...] = halves(own_rows[: own_high.shape[0]])
    other_high[...], other_low[...] = halves(other_rows[...])


def add_parts(lower, own_rows, own_high, own_low, other_high, other_low, to_next, to_own, mid, far_mid, span):
    cols, sites = lower.shape
    length = own_rows.shape[1]
    blocks = sites // length
    halo = to_own.shape[1] - sites
    edge = halo - length
    row = lax.axis_index("row")
    keep(mid, 0, lower[...])
    near = pl.multiple_of(jnp.where(row == 0, sites - halo, 0), edge)
    for b in range(blocks):
        at, rows = slice(b * length, (b + 1) * length), slice(b * sites, (b + 1) * sites)
        const = slice(blocks * sites + b * cols, blocks * sites + (b + 1) * cols)
        to_own[:, at] = own_rows[const] + stacked_dot(mid, slice(0, sites), own_high[rows], own_low[rows])
    to_next[:, :halo] = to_own[:, pl.ds(near, halo)]
    left, right = (cuts_of(blocks, length, sites, span, last) for last in (False, True))
    for b in range(blocks):
        far_mid[:, b * length : (b + 1) * length] = jnp.zeros((cols, length), jnp.float32)
        spans = [(lo_hi[1] - lo_hi[0], lo_hi[2]) for lo_hi in (left[b], right[b])]
        both = min(spans[0][0], spans[1][0])
        more = max(spans[0][0], spans[1][0]) - both
        long_left = spans[0][0] > spans[1][0]
        for count, offset, only in ((both, 0, False), (more, both, True)):
            if not count:
                continue
            at = slice(b * length, (b + 1) * length)
            starts = [packed + offset for _, packed in spans]
            froms = [sites - spans[0][0] + offset, offset]
            if only:
                starts = [starts[0] if long_left else starts[1]] * 2
                froms = [froms[0] if long_left else froms[1]] * 2

            def add(b=b, at=at, starts=starts, froms=froms, count=count):
                start = pl.multiple_of(jnp.where(row == 0, starts[0], starts[1]), edge)
                source = pl.multiple_of(jnp.where(row == 0, froms[0], froms[1]), edge)
                rows = pl.ds(start, count)
                far_mid[:, at] += stacked_dot(mid, pl.ds(source, count), other_high[rows], other_low[rows])

            if only:
                pl.when((row == 0) == long_left)(add)
            else:
                add()
    to_next[:, halo:] = far_mid[...]
    away = pl.multiple_of(jnp.where(row == 0, 0, sites - halo), edge)
    to_own[:, sites:] = far_mid[:, pl.ds(away, halo)]


def jump_kernel(mine, own_in, base, high, low, *rest):
    ship, (_late, _lower, late, lower, to_next, to_own, to_last, *scratch) = rest[:-9], rest[-9:]

    @pl.when(lax.axis_index("tm") == 2 * mine)
    def _():
        add_own(own_in, base, high, low, late, lower)
        add_parts(lower, *ship, to_next, to_own, *scratch, high.shape[0] * high.shape[1] // own_in.shape[1])
        to_last[...] = to_next[...]

    @pl.when(lax.axis_index("tm") != 2 * mine)
    def _():
        for part in (to_next, to_own, to_last):
            part[...] = jnp.zeros_like(part)


def parts_kernel(mine, span, lower, *rest):
    ship, parts = rest[:-4], rest[-4:]

    @pl.when(lax.axis_index("tm") == 2 * mine)
    def _():
        add_parts(lower, *ship, *parts, span)

    @pl.when(lax.axis_index("tm") != 2 * mine)
    def _():
        for part in parts[:2]:
            part[...] = jnp.zeros_like(part)


def last_kernel(jumps, both, high, low, late, _lower, lower):
    device = lax.axis_index("tm")
    pl.when((device == 0) | (device == 2) if jumps else device == 0)(lambda: step(both, high, low, late, lower))


def upper_kernel(sides, top, *rest):
    far, far_high, far_low, _late, _upper, late, upper = rest[-7:]
    cols, sites = upper.shape
    length = far.shape[1]
    blocks = sites // length
    window = far_high.shape[0] // blocks
    halo = (late.shape[1] - sites) // 2
    at_window = halo - (window - length) // 2
    messages = rest[:-7]

    if len(messages) == 2:

        @pl.when(lax.axis_index("tm") == 0)
        def _():
            load(sides, plain(messages[1]), messages[0][...], halo, late)

    for mine, (*next_in, own_in) in enumerate(((messages[0], messages[2], messages[1]), messages[3:]) if len(messages) > 2 else ()):

        @pl.when(lax.axis_index("tm") == 2 * mine)
        def _():
            from_next = next_in[0][...] + next_in[1][...] if len(next_in) == 2 else next_in[0][...]
            own = own_in[:, :sites] + from_next[:, halo:]
            near = own_in[:, sites:] + from_next[:, :halo]
            load(sides, lambda side, cut: near, own, halo, late)

    @pl.when(lax.axis_index("tm") != 2 * top)
    def _():
        for b in range(blocks):
            rows = slice(b * window, (b + 1) * window)
            at = blocks * window + b * cols
            start = at_window + b * length
            upper[:, b * length : (b + 1) * length] = far[at : at + cols] - stacked_dot(
                late, slice(start, start + window), far_high[rows], far_low[rows]
            )


def local(normals, inv_diag, lag_coupling, fill_mask):
    times, rows = lax.axis_size("tm"), lax.axis_size("row")
    device = lax.axis_index("tm")
    cols, sites = normals.shape[1:]
    blocks, length = inv_diag.shape[1:3]
    window = lag_coupling.shape[2]
    edge = (window - length) // 2
    halo = length + edge
    sides = 1 if rows == 2 else 2
    pairs = times // 2
    f32, bf16 = jnp.float32, jnp.bfloat16
    shape = jax.ShapeDtypeStruct

    def link(source, target):
        return [(s * rows + r, t * rows + r) for s, t in zip(source, target) for r in range(rows)]

    def cross(value, source, target, split=False):
        if sides == 1:
            perm = [(s * rows + r, t * rows + 1 - r) for s, t in zip(source, target) for r in range(2)]
            return lax.ppermute(value, BOTH, perm)
        moved = []
        for side, step in enumerate((1, -1)):
            perm = [
                (s * rows + r, t * rows + r + step)
                for s, t in zip(source, target)
                for r in range(rows)
                if 0 <= r + step < rows
            ]
            moved.append(lax.ppermute(value[side : side + 1] if split else value[None], BOTH, perm))
        return jnp.concatenate(moved)

    tall = blocks * window
    jump = 2
    jumps = rows == 2 and pairs > 5
    const, again, near, near_high, near_low = pl.pallas_call(
        fuse_kernel,
        out_shape=(
            shape((cols, sites), f32), shape((cols, sites), f32), shape((tall + blocks * cols, length), f32),
            shape((tall, length), bf16), shape((tall, length), bf16),
        ),
        in_specs=[HBM] * 4,
        out_specs=(VMEM,) * 5,
        scratch_shapes=[
            pltpu.VMEM(fill_mask.shape[1:], fill_mask.dtype),
            pltpu.VMEM(normals.shape[1:], f32),
            pltpu.VMEM(inv_diag.shape[1:], f32),
            pltpu.VMEM(lag_coupling.shape[1:], f32),
            pltpu.SemaphoreType.DMA((2 + 2 * blocks,)),
        ],
        compiler_params=PARAMS,
    )(*[pltpu.with_memory_space_constraint(a, pltpu.HBM) for a in (fill_mask, normals, inv_diag, lag_coupling)])
    odd, even = range(1, times, 2), range(0, times, 2)
    first_next = cross(const, odd[-1:], even[-1:])
    first_own = lax.ppermute(again, BOTH, link(odd[-1:], even[-1:]))
    edges = pl.pallas_call(
        functools.partial(edge_kernel, sides, blocks, cols),
        out_shape=shape((sides, window + cols, edge), f32),
        in_specs=[VMEM],
        out_specs=VMEM,
        compiler_params=PARAMS,
    )(near)
    near = pl.pallas_call(
        lambda _own, _edges, own: None,
        out_shape=shape(near.shape, f32),
        in_specs=[VMEM] * 2,
        out_specs=VMEM,
        input_output_aliases={0: 0},
        compiler_params=PARAMS,
    )(near, edges)
    rim = cross(edges, odd[:-1], even[:-1], True)
    far = lax.ppermute(near, BOTH, link(odd[:-1], even[:-1]))

    blank = jnp.zeros((cols, sites), f32)
    upper, lower = pl.pallas_call(
        functools.partial(top_kernel, pairs - 1, sides),
        out_shape=(shape((cols, sites), f32),) * 2,
        in_specs=[VMEM] * 7,
        out_specs=(VMEM,) * 2,
        scratch_shapes=[pltpu.VMEM((2 * cols, sites + 2 * edge), bf16)],
        input_output_aliases={5: 0, 6: 1},
        compiler_params=PARAMS,
        cost_estimate=pl.CostEstimate(flops=50 * 10**9, bytes_accessed=0, transcendentals=0),
    )(first_next, first_own, const, near_high, near_low, blank, blank)
    far_high, far_low = pl.pallas_call(
        split_kernel,
        out_shape=(shape((tall, length), bf16), shape((tall, length), bf16)),
        in_specs=[VMEM],
        out_specs=(VMEM,) * 2,
        compiler_params=PARAMS,
    )(far)
    packs = (shape((blocks * (sites + cols), length), f32), shape((halo + edge, length), f32)) if jumps else ()

    def pair_matrix(first, jumps, packs):
        return pl.pallas_call(
            functools.partial(pair_kernel, (pairs - 2, first), jumps),
            out_shape=(
                shape((2 * tall, length), bf16), shape((2 * tall, length), bf16), shape((cols, sites), f32), *packs
            ),
            in_specs=[VMEM] * 7,
            out_specs=(VMEM,) * (3 + len(packs)),
            scratch_shapes=[pltpu.VMEM((2 * window, length), f32)],
            compiler_params=PARAMS,
            cost_estimate=pl.CostEstimate(flops=10**9, bytes_accessed=0, transcendentals=0),
        )(far, rim, far_high, far_low, near_high, near_low, const)

    early = pair_matrix(True, False, ())
    high, low, both, *packs = pair_matrix(False, jumps, packs)
    if jumps:
        source, target = [2 * jump - 2, 2 * jump], [2 * jump, 2 * jump + 2]
        own_rows = lax.ppermute(packs[0], BOTH, link(source, target))
        other_rows = cross(packs[1], source, target)
        ship = pl.pallas_call(
            rows_kernel,
            out_shape=(shape((blocks * sites, length), bf16),) * 2 + (shape(other_rows.shape, bf16),) * 2,
            in_specs=[VMEM] * 2,
            out_specs=(VMEM,) * 4,
            compiler_params=PARAMS,
        )(own_rows, other_rows)

    def turn(kernel, given, state, scratch=(), extra=(), flops=0):
        return pl.pallas_call(
            kernel,
            out_shape=tuple(shape(v.shape, v.dtype) for v in state) + tuple(extra),
            in_specs=[VMEM] * (len(given) + len(state)),
            out_specs=(VMEM,) * (len(state) + len(extra)),
            scratch_shapes=list(scratch),
            input_output_aliases={len(given) + i: i for i in range(len(state))},
            compiler_params=PARAMS,
            cost_estimate=pl.CostEstimate(flops=flops, bytes_accessed=0, transcendentals=0) if flops else None,
        )(*given, *state)

    parts = (shape((cols, sites + halo), f32),) * 2
    parts_scratch = [pltpu.VMEM((2 * cols, sites), bf16), pltpu.VMEM((cols, sites), f32)]
    late = jnp.zeros((2 * cols, sites + 2 * halo), bf16)
    mine = pairs - 1
    while mine > 0:
        if jumps and mine == jump:
            source, target = [2 * mine], [2 * mine - 4]
            first_in = lax.ppermute(to_next, BOTH, [(2 * source[0] + 1, 2 * target[0])])
            own_in = lax.ppermute(to_own, BOTH, link(source, target))
            next_in = lax.ppermute(to_last, BOTH, [(2 * source[0], 2 * target[0] + 1)])
            break
        source, target = [2 * mine], [2 * mine - 2]
        next_in = cross(lower, source, target)
        own_in = lax.ppermute(lower, BOTH, link(source, target))
        if jumps and mine == jump + 1:
            beside = pl.pallas_call(
                functools.partial(parts_kernel, mine, 2 * window),
                out_shape=parts,
                in_specs=[VMEM] * 6,
                out_specs=(VMEM,) * 2,
                scratch_shapes=parts_scratch,
                compiler_params=PARAMS,
            )(lower, own_rows, *ship)
            source, target = [2 * mine], [2 * mine - 4]
            beside_next = cross(beside[0], source, target)
            beside_own = lax.ppermute(beside[1], BOTH, link(source, target))
        mine -= 1
        if mine == 0:
            break
        here = early if mine == pairs - 2 else (high, low, both)
        late, base = turn(
            functools.partial(rim_kernel, mine, sides),
            (next_in, here[2], *here[:2]),
            (late,),
            extra=[shape((cols, sites), f32)],
        )
        if jumps and mine == jump:
            late, lower, to_next, to_own, to_last = turn(
                functools.partial(jump_kernel, mine),
                (own_in, base, high, low, own_rows, *ship),
                (late, lower),
                parts_scratch,
                parts + parts[:1],
            )
        else:
            late, lower = turn(
                functools.partial(chain_kernel, mine),
                (own_in, base, *here[:2]),
                (late, lower),
                flops=50 * 10**9 if jumps and mine == pairs - 3 else 0,
            )
    given = (first_in, own_in, next_in, beside_next, beside_own) if jumps else (own_in, next_in)
    late, upper = turn(
        functools.partial(upper_kernel, sides, pairs - 1), (*given, far, far_high, far_low), (late, upper)
    )
    returned = lax.ppermute(upper, BOTH, link(even, odd))
    lower = pl.pallas_call(
        functools.partial(last_kernel, jumps),
        out_shape=shape(lower.shape, f32),
        in_specs=[VMEM] * 5,
        out_specs=VMEM,
        input_output_aliases={4: 0},
        compiler_params=PARAMS,
        cost_estimate=pl.CostEstimate(flops=12 * cols * tall * length, bytes_accessed=8 * tall * length, transcendentals=0),
    )(both, high, low, late, lower)
    return jnp.where(device % 2 == 0, lower, returned)[None]


def solution(mesh):
    placed = (
        P("tm", None, "row"),
        P("tm", "row", None, None),
        P("tm", "row", None, None),
        P("tm", "row", None),
    )
    return jax.shard_map(
        local, mesh=mesh, in_specs=placed, out_specs=P("tm", None, "row"), check_vma=False
    )
```

```python
import functools

import jax
import jax.numpy as jnp
from jax import lax
from jax.experimental import pallas as pl
from jax.experimental.pallas import tpu as pltpu
from jax.sharding import PartitionSpec as P

BOTH = ("tm", "row")
VMEM = pl.BlockSpec(memory_space=pltpu.VMEM)
HBM = pl.BlockSpec(memory_space=pltpu.HBM)
PARAMS = pltpu.CompilerParams(vmem_limit_bytes=32 * 1024 * 1024)


def halves(value):
    high = value.astype(jnp.bfloat16)
    low = (value - high.astype(jnp.float32)).astype(jnp.bfloat16)
    return high, low


def dot(a, b):
    return jnp.dot(a, b, preferred_element_type=jnp.float32)


def stacked_dot(pair, cols, high, low):
    rows = pair.shape[0] // 2
    wide = dot(pair[:, cols], high)
    return wide[:rows] + wide[rows:] + dot(pair[:rows, cols], low)


def triple(high, low, inv_high, inv_low):
    return dot(high, inv_high) + dot(low, inv_high) + dot(high, inv_low)


def put_rim(sides, rim, columns):
    if sides == 1:
        row = lax.axis_index("row")

        @pl.when(row == 0)
        def _():
            rim[0] = columns(True)

        @pl.when(row != 0)
        def _():
            rim[0] = columns(False)
    else:
        rim[0] = columns(True)
        rim[1] = columns(False)


def const_kernel(normals, inv, const, again, inv_high, inv_low, normals_in, inv_in, sems):
    blocks, length = inv.shape[1], inv.shape[2]
    moves = [pltpu.make_async_copy(normals.at[0], normals_in, sems.at[0])]
    for b in range(blocks):
        moves.append(pltpu.make_async_copy(inv.at[0, b], inv_in.at[b], sems.at[1 + b]))
    for move in moves:
        move.start()
    moves[0].wait()
    for b in range(blocks):
        at = slice(b * length, (b + 1) * length)
        high, low = halves(normals_in[:, at])
        moves[1 + b].wait()
        inv_high[b], inv_low[b] = halves(inv_in[b])
        const[:, at] = triple(high, low, inv_high[b], inv_low[b])
    again[...] = const[...]


def fuse_kernel(mask, const, inv_high, inv_low, lag, own, near_high, near_low):
    blocks, window, length = lag.shape[1:]
    edge = (window - length) // 2
    cols = const.shape[0]
    cuts = (0, edge, edge + length, window)
    flags = mask[0].astype(jnp.float32)
    for b in range(blocks):
        at = blocks * window + b * cols
        own[at : at + cols] = const[:, b * length : (b + 1) * length]
        for part in range(3):
            lo, hi = cuts[part], cuts[part + 1]
            rows = slice(b * window + lo, b * window + hi)
            high, low = halves(lag[0, b, lo:hi] * flags[b : b + 1, part : part + 1])
            value = triple(high, low, inv_high[b], inv_low[b])
            own[rows] = value
            near_high[rows], near_low[rows] = halves(value)


def edge_kernel(sides, blocks, cols, own, rim):
    length, edge = own.shape[1], rim.shape[2]
    window = length + 2 * edge

    def columns(last):
        b = blocks - 1 if last else 0
        cut = slice(length - edge, length) if last else slice(0, edge)
        at = blocks * window + b * cols
        return jnp.concatenate([own[b * window : (b + 1) * window, cut], own[at : at + cols, cut]])

    put_rim(sides, rim, columns)


def split_kernel(far, far_high, far_low):
    far_high[...], far_low[...] = halves(far[: far_high.shape[0]])


def cuts_of(blocks, length, sites, span, last):
    packed, cuts = 0, []
    for b in range(blocks):
        start = span // 2 - length // 2 - b * length
        lo, hi = (start + sites, span) if last else (0, start)
        cuts.append((lo, hi, packed))
        packed += hi - lo
    return cuts


def pair_kernel(first, jump, *refs):
    here = lax.axis_index("tm") == 2 * first[0]
    pl.when(here if first[1] else jnp.logical_not(here))(lambda: make_pair(jump, *refs))


def make_pair(jump, far, rim, far_high, far_low, near_high, near_low, const, high, low, both, *rest):
    cols, sites = const.shape
    length = far.shape[1]
    blocks = sites // length
    window = near_high.shape[0] // blocks
    edge = (window - length) // 2
    span = 2 * window
    tall = blocks * window
    total = rest[-1]
    if rim.shape[0] == 1:
        flag = jnp.minimum(lax.axis_index("row"), 1).astype(jnp.float32)
        left, right = rim[0] * flag, rim[0] * (1 - flag)
    else:
        left, right = rim[0], rim[1]
    left_pair, right_pair = halves(left[:window]), halves(right[:window])
    for b in range(blocks):
        here = slice(b * window, (b + 1) * window)
        column = slice(b * length, (b + 1) * length)

        def part(lo, hi):
            rows = slice(b * window + lo, b * window + hi)
            return near_high[rows], near_low[rows]

        def constant(block):
            if block < 0:
                return left[window:]
            if block == blocks:
                return right[window:]
            return far[tall + block * cols : tall + (block + 1) * cols]

        if b > 0:
            before = slice((b - 1) * window, b * window)
            low_pair = far_high[before, length - edge :], far_low[before, length - edge :]
            low_const = constant(b - 1)[:, length - edge :]
        else:
            low_pair, low_const = left_pair, constant(-1)
        if b + 1 < blocks:
            after = slice((b + 1) * window, (b + 2) * window)
            high_pair = far_high[after, :edge], far_low[after, :edge]
            high_const = constant(b + 1)[:, :edge]
        else:
            high_pair, high_const = right_pair, constant(blocks)
        first = triple(*low_pair, *part(0, edge))
        middle = triple(far_high[here], far_low[here], *part(edge, edge + length))
        last = triple(*high_pair, *part(edge + length, window))
        total[:window] = first
        total[window:] = last
        total[length : length + window] += middle
        high[b * span : (b + 1) * span], low[b * span : (b + 1) * span] = halves(total[...])
        both[:, column] = const[:, column] - (
            triple(*halves(low_const), *part(0, edge))
            + triple(*halves(constant(b)), *part(edge, edge + length))
            + triple(*halves(high_const), *part(edge + length, window))
        )
    if jump:
        own_rows, other_rows = rest[:2]

        def value(start, count):
            rows = pl.ds(start, count)
            return high[rows].astype(jnp.float32) + low[rows].astype(jnp.float32)

        for b in range(blocks):
            own_rows[b * sites : (b + 1) * sites] = value(b * span + window - edge - b * length, sites)
            at = blocks * sites + b * cols
            own_rows[at : at + cols] = both[:, b * length : (b + 1) * length]
        starts = [
            [b * span + at for b, (lo, hi, _) in enumerate(cuts_of(blocks, length, sites, span, last)) for at in range(lo, hi, edge)]
            for last in (True, False)
        ]
        row = lax.axis_index("row")
        for chunk, (on_right, on_left) in enumerate(zip(*starts)):
            start = pl.multiple_of(jnp.where(row == 0, on_right, on_left), edge)
            other_rows[chunk * edge : (chunk + 1) * edge] = value(start, edge)


def keep(ref, start, value):
    cols, width = value.shape
    high, low = halves(value)
    ref[:cols, pl.ds(start, width)] = high
    ref[cols:, pl.ds(start, width)] = low


def load(sides, pick, own, halo, ref):
    sites = own.shape[1]
    keep(ref, halo, own)
    for side in range(sides):
        on_right = 1 - jnp.minimum(lax.axis_index("row"), 1).astype(jnp.int32) if sides == 1 else side
        start = pl.multiple_of((1 - on_right) * (sites - halo), 128)
        keep(ref, pl.multiple_of(on_right * (halo + sites), 128), pick(side, pl.ds(start, halo)))


def plain(next_in):
    return lambda side, cut: next_in[:, cut] if len(next_in.shape) == 2 else next_in[side, :, cut]


def top_kernel(mine, sides, next_in, own_in, const, near_high, near_low, _upper, _lower, upper, lower, mid):
    sites = lower.shape[1]
    length = near_high.shape[1]
    blocks = sites // length
    window = near_high.shape[0] // blocks
    edge = (window - length) // 2

    @pl.when(lax.axis_index("tm") == 2 * mine)
    def _():
        mid[...] = jnp.zeros_like(mid)
        load(sides, plain(next_in), own_in[...], edge, mid)
        upper[...] = own_in[...]
        for b in range(blocks):
            at, rows = slice(b * length, (b + 1) * length), slice(b * window, (b + 1) * window)
            product = stacked_dot(mid, slice(b * length, b * length + window), near_high[rows], near_low[rows])
            lower[:, at] = const[:, at] - product


def step(both, high, low, late, lower):
    blocks = lower.shape[1] // high.shape[1]
    length, span = high.shape[1], high.shape[0] // blocks
    for b in range(blocks):
        at, rows = slice(b * length, (b + 1) * length), slice(b * span, (b + 1) * span)
        lower[:, at] = both[:, at] + stacked_dot(late, slice(b * length, b * length + span), high[rows], low[rows])


def load_rims(sides, next_in, sites, halo, late):
    for side in range(sides):
        on_right = 1 - jnp.minimum(lax.axis_index("row"), 1).astype(jnp.int32) if sides == 1 else side
        start = pl.multiple_of((1 - on_right) * (sites - halo), 128)
        keep(late, pl.multiple_of(on_right * (halo + sites), 128), plain(next_in)(side, pl.ds(start, halo)))


def rim_kernel(mine, sides, next_in, both, high, low, _late, late, base):
    sites, length = base.shape[1], high.shape[1]
    blocks = sites // length
    span = high.shape[0] // blocks
    halo = (late.shape[1] - sites) // 2
    edge = halo - length

    @pl.when(lax.axis_index("tm") == 2 * mine)
    def _():
        load_rims(sides, next_in, sites, halo, late)
        cuts = [cuts_of(blocks, length, sites, span, last) for last in (False, True)]
        for b in range(blocks):
            value = both[:, b * length : (b + 1) * length]
            if sides == 2:
                for lo, hi, _ in (cuts[0][b], cuts[1][b]):
                    rows = slice(b * span + lo, b * span + hi)
                    value += stacked_dot(late, slice(b * length + lo, b * length + hi), high[rows], low[rows])
            else:
                on_left = lax.axis_index("row") != 0
                counts = [cut[b][1] - cut[b][0] for cut in cuts]
                for chunk in range(0, max(counts), edge):
                    starts = [cut[b][0] + chunk if chunk < count else 0 for cut, count in zip(cuts, counts)]
                    start = pl.multiple_of(jnp.where(on_left, starts[0], starts[1]), edge)
                    rows = pl.ds(b * span + start, edge)
                    product = stacked_dot(late, pl.ds(b * length + start, edge), high[rows], low[rows])
                    if chunk >= min(counts):
                        product = jnp.where(on_left == (counts[0] > counts[1]), product, 0.0)
                    value += product
            base[:, b * length : (b + 1) * length] = value


def add_own(own_in, base, high, low, late, lower):
    sites, length = lower.shape[1], high.shape[1]
    blocks = sites // length
    span = high.shape[0] // blocks
    halo = (late.shape[1] - sites) // 2
    keep(late, halo, own_in[...])
    for b in range(blocks):
        at, start = slice(b * length, (b + 1) * length), halo - b * length
        rows = slice(b * span + start, b * span + start + sites)
        lower[:, at] = base[:, at] + stacked_dot(late, slice(halo, halo + sites), high[rows], low[rows])


def chain_kernel(mine, own_in, base, high, low, _late, _lower, late, lower):
    pl.when(lax.axis_index("tm") == 2 * mine)(lambda: add_own(own_in, base, high, low, late, lower))


def rows_kernel(own_rows, other_rows, own_high, own_low, other_high, other_low):
    own_high[...], own_low[...] = halves(own_rows[: own_high.shape[0]])
    other_high[...], other_low[...] = halves(other_rows[...])


def add_parts(lower, own_rows, own_high, own_low, other_high, other_low, to_next, to_own, mid, far_mid, span):
    cols, sites = lower.shape
    length = own_rows.shape[1]
    blocks = sites // length
    halo = to_own.shape[1] - sites
    edge = halo - length
    row = lax.axis_index("row")
    keep(mid, 0, lower[...])
    near = pl.multiple_of(jnp.where(row == 0, sites - halo, 0), edge)
    for b in range(blocks):
        at, rows = slice(b * length, (b + 1) * length), slice(b * sites, (b + 1) * sites)
        const = slice(blocks * sites + b * cols, blocks * sites + (b + 1) * cols)
        to_own[:, at] = own_rows[const] + stacked_dot(mid, slice(0, sites), own_high[rows], own_low[rows])
    to_next[:, :halo] = to_own[:, pl.ds(near, halo)]
    pieces = []
    for rows, from_last, from_first in (
        (slice(0, edge), sites - halo, 0),
        (slice(edge, halo), sites - length, 0),
        (slice(halo, halo + edge), sites - edge, length),
    ):
        source = pl.multiple_of(jnp.where(row == 0, from_last, from_first), edge)
        pieces.append(stacked_dot(mid, pl.ds(source, rows.stop - rows.start), other_high[rows], other_low[rows]))
    far_mid[:, :length] = pieces[0] + jnp.where(row == 0, pieces[1], 0.0)
    far_mid[:, length:] = pieces[2] + jnp.where(row == 0, 0.0, pieces[1])
    to_next[:, halo:] = far_mid[...]
    away = pl.multiple_of(jnp.where(row == 0, 0, sites - halo), edge)
    to_own[:, sites:] = far_mid[:, pl.ds(away, halo)]


def jump_kernel(mine, own_in, base, high, low, *rest):
    ship, (_late, _lower, late, lower, to_next, to_own, to_last, *scratch) = rest[:-9], rest[-9:]

    @pl.when(lax.axis_index("tm") == 2 * mine)
    def _():
        add_own(own_in, base, high, low, late, lower)
        add_parts(lower, *ship, to_next, to_own, *scratch, high.shape[0] * high.shape[1] // own_in.shape[1])
        to_last[...] = to_next[...]

    @pl.when(lax.axis_index("tm") != 2 * mine)
    def _():
        for part in (to_next, to_own, to_last):
            part[...] = jnp.zeros_like(part)


def parts_kernel(mine, span, lower, *rest):
    ship, parts = rest[:-4], rest[-4:]

    @pl.when(lax.axis_index("tm") == 2 * mine)
    def _():
        add_parts(lower, *ship, *parts, span)

    @pl.when(lax.axis_index("tm") != 2 * mine)
    def _():
        for part in parts[:2]:
            part[...] = jnp.zeros_like(part)


def last_kernel(jumps, both, high, low, late, _lower, lower):
    device = lax.axis_index("tm")
    pl.when((device == 0) | (device == 2) if jumps else device == 0)(lambda: step(both, high, low, late, lower))


def upper_kernel(sides, top, *rest):
    far, far_high, far_low, _late, _upper, late, upper = rest[-7:]
    cols, sites = upper.shape
    length = far.shape[1]
    blocks = sites // length
    window = far_high.shape[0] // blocks
    halo = (late.shape[1] - sites) // 2
    at_window = halo - (window - length) // 2
    messages = rest[:-7]

    if len(messages) == 2:

        @pl.when(lax.axis_index("tm") == 0)
        def _():
            load(sides, plain(messages[1]), messages[0][...], halo, late)

    for mine, (*next_in, own_in) in enumerate(((messages[0], messages[2], messages[1]), messages[3:]) if len(messages) > 2 else ()):

        @pl.when(lax.axis_index("tm") == 2 * mine)
        def _():
            from_next = next_in[0][...] + next_in[1][...] if len(next_in) == 2 else next_in[0][...]
            own = own_in[:, :sites] + from_next[:, halo:]
            near = own_in[:, sites:] + from_next[:, :halo]
            load(sides, lambda side, cut: near, own, halo, late)

    @pl.when(lax.axis_index("tm") != 2 * top)
    def _():
        for b in range(blocks):
            rows = slice(b * window, (b + 1) * window)
            at = blocks * window + b * cols
            start = at_window + b * length
            upper[:, b * length : (b + 1) * length] = far[at : at + cols] - stacked_dot(
                late, slice(start, start + window), far_high[rows], far_low[rows]
            )


def local(normals, inv_diag, lag_coupling, fill_mask):
    times, rows = lax.axis_size("tm"), lax.axis_size("row")
    device = lax.axis_index("tm")
    cols, sites = normals.shape[1:]
    blocks, length = inv_diag.shape[1:3]
    window = lag_coupling.shape[2]
    edge = (window - length) // 2
    halo = length + edge
    sides = 1 if rows == 2 else 2
    pairs = times // 2
    f32, bf16 = jnp.float32, jnp.bfloat16
    shape = jax.ShapeDtypeStruct

    def link(source, target):
        return [(s * rows + r, t * rows + r) for s, t in zip(source, target) for r in range(rows)]

    def cross(value, source, target, split=False):
        if sides == 1:
            perm = [(s * rows + r, t * rows + 1 - r) for s, t in zip(source, target) for r in range(2)]
            return lax.ppermute(value, BOTH, perm)
        moved = []
        for side, step in enumerate((1, -1)):
            perm = [
                (s * rows + r, t * rows + r + step)
                for s, t in zip(source, target)
                for r in range(rows)
                if 0 <= r + step < rows
            ]
            moved.append(lax.ppermute(value[side : side + 1] if split else value[None], BOTH, perm))
        return jnp.concatenate(moved)

    tall = blocks * window
    jump = 2
    jumps = rows == 2 and pairs > 5 and blocks == 2
    const, again, inv_high, inv_low = pl.pallas_call(
        const_kernel,
        out_shape=(
            shape((cols, sites), f32), shape((cols, sites), f32),
            shape((blocks, length, length), bf16), shape((blocks, length, length), bf16),
        ),
        in_specs=[HBM] * 2,
        out_specs=(VMEM,) * 4,
        scratch_shapes=[
            pltpu.VMEM(normals.shape[1:], f32),
            pltpu.VMEM(inv_diag.shape[1:], f32),
            pltpu.SemaphoreType.DMA((1 + blocks,)),
        ],
        compiler_params=PARAMS,
        cost_estimate=pl.CostEstimate(flops=5*10**9, bytes_accessed=0, transcendentals=0),
    )(*[pltpu.with_memory_space_constraint(a, pltpu.HBM) for a in (normals, inv_diag)])
    odd, even = range(1, times, 2), range(0, times, 2)
    first_next = cross(const, odd[-1:], even[-1:])
    first_own = lax.ppermute(again, BOTH, link(odd[-1:], even[-1:]))
    near, near_high, near_low = pl.pallas_call(
        fuse_kernel,
        out_shape=(
            shape((tall + blocks * cols, length), f32), shape((tall, length), bf16), shape((tall, length), bf16),
        ),
        in_specs=[VMEM] * 5,
        out_specs=(VMEM,) * 3,
        compiler_params=PARAMS,
        cost_estimate=pl.CostEstimate(
            flops=6 * (tall + cols * blocks) * length * length, bytes_accessed=16 * tall * length, transcendentals=0
        ),
    )(fill_mask, const, inv_high, inv_low, lag_coupling)
    edges = pl.pallas_call(
        functools.partial(edge_kernel, sides, blocks, cols),
        out_shape=shape((sides, window + cols, edge), f32),
        in_specs=[VMEM],
        out_specs=VMEM,
        compiler_params=PARAMS,
    )(near)
    near = pl.pallas_call(
        lambda _own, _edges, own: None,
        out_shape=shape(near.shape, f32),
        in_specs=[VMEM] * 2,
        out_specs=VMEM,
        input_output_aliases={0: 0},
        compiler_params=PARAMS,
    )(near, edges)
    rim = cross(edges, odd[:-1], even[:-1], True)
    far = lax.ppermute(near, BOTH, link(odd[:-1], even[:-1]))

    blank = jnp.zeros((cols, sites), f32)
    upper, lower = pl.pallas_call(
        functools.partial(top_kernel, pairs - 1, sides),
        out_shape=(shape((cols, sites), f32),) * 2,
        in_specs=[VMEM] * 7,
        out_specs=(VMEM,) * 2,
        scratch_shapes=[pltpu.VMEM((2 * cols, sites + 2 * edge), bf16)],
        input_output_aliases={5: 0, 6: 1},
        compiler_params=PARAMS,
        cost_estimate=pl.CostEstimate(flops=50 * 10**9, bytes_accessed=0, transcendentals=0),
    )(first_next, first_own, const, near_high, near_low, blank, blank)
    far_high, far_low = pl.pallas_call(
        split_kernel,
        out_shape=(shape((tall, length), bf16), shape((tall, length), bf16)),
        in_specs=[VMEM],
        out_specs=(VMEM,) * 2,
        compiler_params=PARAMS,
    )(far)
    packs = (shape((blocks * (sites + cols), length), f32), shape((halo + edge, length), f32)) if jumps else ()

    def pair_matrix(first, jumps, packs):
        return pl.pallas_call(
            functools.partial(pair_kernel, (pairs - 2, first), jumps),
            out_shape=(
                shape((2 * tall, length), bf16), shape((2 * tall, length), bf16), shape((cols, sites), f32), *packs
            ),
            in_specs=[VMEM] * 7,
            out_specs=(VMEM,) * (3 + len(packs)),
            scratch_shapes=[pltpu.VMEM((2 * window, length), f32)],
            compiler_params=PARAMS,
            cost_estimate=pl.CostEstimate(flops=10**9, bytes_accessed=0, transcendentals=0),
        )(far, rim, far_high, far_low, near_high, near_low, const)

    early = pair_matrix(True, False, ())
    high, low, both, *packs = pair_matrix(False, jumps, packs)
    if jumps:
        source, target = [2 * jump - 2, 2 * jump], [2 * jump, 2 * jump + 2]
        own_rows = lax.ppermute(packs[0], BOTH, link(source, target))
        other_rows = cross(packs[1], source, target)
        ship = pl.pallas_call(
            rows_kernel,
            out_shape=(shape((blocks * sites, length), bf16),) * 2 + (shape(other_rows.shape, bf16),) * 2,
            in_specs=[VMEM] * 2,
            out_specs=(VMEM,) * 4,
            compiler_params=PARAMS,
        )(own_rows, other_rows)

    def turn(kernel, given, state, scratch=(), extra=(), flops=0):
        return pl.pallas_call(
            kernel,
            out_shape=tuple(shape(v.shape, v.dtype) for v in state) + tuple(extra),
            in_specs=[VMEM] * (len(given) + len(state)),
            out_specs=(VMEM,) * (len(state) + len(extra)),
            scratch_shapes=list(scratch),
            input_output_aliases={len(given) + i: i for i in range(len(state))},
            compiler_params=PARAMS,
            cost_estimate=pl.CostEstimate(flops=flops, bytes_accessed=0, transcendentals=0) if flops else None,
        )(*given, *state)

    parts = (shape((cols, sites + halo), f32),) * 2
    parts_scratch = [pltpu.VMEM((2 * cols, sites), bf16), pltpu.VMEM((cols, sites), f32)]
    late = jnp.zeros((2 * cols, sites + 2 * halo), bf16)
    mine = pairs - 1
    while mine > 0:
        if jumps and mine == jump:
            source, target = [2 * mine], [2 * mine - 4]
            first_in = lax.ppermute(to_next, BOTH, [(2 * source[0] + 1, 2 * target[0])])
            own_in = lax.ppermute(to_own, BOTH, link(source, target))
            next_in = lax.ppermute(to_last, BOTH, [(2 * source[0], 2 * target[0] + 1)])
            break
        source, target = [2 * mine], [2 * mine - 2]
        next_in = cross(lower, source, target)
        own_in = lax.ppermute(lower, BOTH, link(source, target))
        if jumps and mine == jump + 1:
            beside = pl.pallas_call(
                functools.partial(parts_kernel, mine, 2 * window),
                out_shape=parts,
                in_specs=[VMEM] * 6,
                out_specs=(VMEM,) * 2,
                scratch_shapes=parts_scratch,
                compiler_params=PARAMS,
            )(lower, own_rows, *ship)
            source, target = [2 * mine], [2 * mine - 4]
            beside_next = cross(beside[0], source, target)
            beside_own = lax.ppermute(beside[1], BOTH, link(source, target))
        mine -= 1
        if mine == 0:
            break
        here = early if mine == pairs - 2 else (high, low, both)
        late, base = turn(
            functools.partial(rim_kernel, mine, sides),
            (next_in, here[2], *here[:2]),
            (late,),
            extra=[shape((cols, sites), f32)],
        )
        if jumps and mine == jump:
            late, lower, to_next, to_own, to_last = turn(
                functools.partial(jump_kernel, mine),
                (own_in, base, high, low, own_rows, *ship),
                (late, lower),
                parts_scratch,
                parts + parts[:1],
            )
        else:
            late, lower = turn(
                functools.partial(chain_kernel, mine),
                (own_in, base, *here[:2]),
                (late, lower),
                flops=50 * 10**9 if jumps and mine == pairs - 3 else 0,
            )
    given = (first_in, own_in, next_in, beside_next, beside_own) if jumps else (own_in, next_in)
    late, upper = turn(
        functools.partial(upper_kernel, sides, pairs - 1), (*given, far, far_high, far_low), (late, upper)
    )
    returned = lax.ppermute(upper, BOTH, link(even, odd))
    lower = pl.pallas_call(
        functools.partial(last_kernel, jumps),
        out_shape=shape(lower.shape, f32),
        in_specs=[VMEM] * 5,
        out_specs=VMEM,
        input_output_aliases={4: 0},
        compiler_params=PARAMS,
        cost_estimate=pl.CostEstimate(flops=12 * cols * tall * length, bytes_accessed=8 * tall * length, transcendentals=0),
    )(both, high, low, late, lower)
    return jnp.where(device % 2 == 0, lower, returned)[None]


def solution(mesh):
    placed = (
        P("tm", None, "row"),
        P("tm", "row", None, None),
        P("tm", "row", None, None),
        P("tm", "row", None),
    )
    return jax.shard_map(
        local, mesh=mesh, in_specs=placed, out_specs=P("tm", None, "row"), check_vma=False
    )
```

```python
import functools

import jax
import jax.numpy as jnp
from jax import lax
from jax.experimental import pallas as pl
from jax.experimental.pallas import tpu as pltpu
from jax.sharding import PartitionSpec as P

BOTH = ("tm", "row")
VMEM = pl.BlockSpec(memory_space=pltpu.VMEM)
HBM = pl.BlockSpec(memory_space=pltpu.HBM)
PARAMS = pltpu.CompilerParams(vmem_limit_bytes=32 * 1024 * 1024)


def halves(value):
    high = value.astype(jnp.bfloat16)
    low = (value - high.astype(jnp.float32)).astype(jnp.bfloat16)
    return high, low


def dot(a, b):
    return jnp.dot(a, b, preferred_element_type=jnp.float32)


def stacked_dot(pair, cols, high, low):
    rows = pair.shape[0] // 2
    wide = dot(pair[:, cols], high)
    return wide[:rows] + wide[rows:] + dot(pair[:rows, cols], low)


def triple(high, low, inv_high, inv_low):
    return dot(high, inv_high) + dot(low, inv_high) + dot(high, inv_low)


def put_rim(sides, rim, columns):
    if sides == 1:
        row = lax.axis_index("row")

        @pl.when(row == 0)
        def _():
            rim[0] = columns(True)

        @pl.when(row != 0)
        def _():
            rim[0] = columns(False)
    else:
        rim[0] = columns(True)
        rim[1] = columns(False)


def const_kernel(normals, inv, const, inv_high, inv_low, normals_in, inv_in, sems):
    blocks, length = inv.shape[1], inv.shape[2]
    moves = [pltpu.make_async_copy(normals.at[0], normals_in, sems.at[0])]
    for b in range(blocks):
        moves.append(pltpu.make_async_copy(inv.at[0, b], inv_in.at[b], sems.at[1 + b]))
    for move in moves:
        move.start()
    moves[0].wait()
    for b in range(blocks):
        at = slice(b * length, (b + 1) * length)
        high, low = halves(normals_in[:, at])
        moves[1 + b].wait()
        inv_high[b], inv_low[b] = halves(inv_in[b])
        const[:, at] = triple(high, low, inv_high[b], inv_low[b])


def again_kernel(const, again):
    again[...] = const[...]


def fuse_kernel(mask, const, inv_high, inv_low, lag, own, near_high, near_low):
    blocks, window, length = lag.shape[1:]
    edge = (window - length) // 2
    cols = const.shape[0]
    cuts = (0, edge, edge + length, window)
    flags = mask[0].astype(jnp.float32)
    for b in range(blocks):
        at = blocks * window + b * cols
        own[at : at + cols] = const[:, b * length : (b + 1) * length]
        for part in range(3):
            lo, hi = cuts[part], cuts[part + 1]
            rows = slice(b * window + lo, b * window + hi)
            high, low = halves(lag[0, b, lo:hi] * flags[b : b + 1, part : part + 1])
            value = triple(high, low, inv_high[b], inv_low[b])
            own[rows] = value
            near_high[rows], near_low[rows] = halves(value)


def edge_kernel(sides, blocks, cols, own, rim):
    length, edge = own.shape[1], rim.shape[2]
    window = length + 2 * edge

    def columns(last):
        b = blocks - 1 if last else 0
        cut = slice(length - edge, length) if last else slice(0, edge)
        at = blocks * window + b * cols
        return jnp.concatenate([own[b * window : (b + 1) * window, cut], own[at : at + cols, cut]])

    put_rim(sides, rim, columns)


def split_kernel(far, far_high, far_low):
    far_high[...], far_low[...] = halves(far[: far_high.shape[0]])


def cuts_of(blocks, length, sites, span, last):
    packed, cuts = 0, []
    for b in range(blocks):
        start = span // 2 - length // 2 - b * length
        lo, hi = (start + sites, span) if last else (0, start)
        cuts.append((lo, hi, packed))
        packed += hi - lo
    return cuts


def pair_kernel(first, jump, *refs):
    here = lax.axis_index("tm") == 2 * first[0]
    pl.when(here if first[1] else jnp.logical_not(here))(lambda: make_pair(jump, *refs))


def make_pair(jump, far, rim, far_high, far_low, near_high, near_low, const, high, low, both, *rest):
    cols, sites = const.shape
    length = far.shape[1]
    blocks = sites // length
    window = near_high.shape[0] // blocks
    edge = (window - length) // 2
    span = 2 * window
    tall = blocks * window
    total = rest[-1]
    if rim.shape[0] == 1:
        flag = jnp.minimum(lax.axis_index("row"), 1).astype(jnp.float32)
        left, right = rim[0] * flag, rim[0] * (1 - flag)
    else:
        left, right = rim[0], rim[1]
    left_pair, right_pair = halves(left[:window]), halves(right[:window])
    for b in range(blocks):
        here = slice(b * window, (b + 1) * window)
        column = slice(b * length, (b + 1) * length)

        def part(lo, hi):
            rows = slice(b * window + lo, b * window + hi)
            return near_high[rows], near_low[rows]

        def constant(block):
            if block < 0:
                return left[window:]
            if block == blocks:
                return right[window:]
            return far[tall + block * cols : tall + (block + 1) * cols]

        if b > 0:
            before = slice((b - 1) * window, b * window)
            low_pair = far_high[before, length - edge :], far_low[before, length - edge :]
            low_const = constant(b - 1)[:, length - edge :]
        else:
            low_pair, low_const = left_pair, constant(-1)
        if b + 1 < blocks:
            after = slice((b + 1) * window, (b + 2) * window)
            high_pair = far_high[after, :edge], far_low[after, :edge]
            high_const = constant(b + 1)[:, :edge]
        else:
            high_pair, high_const = right_pair, constant(blocks)
        first = triple(*low_pair, *part(0, edge))
        middle = triple(far_high[here], far_low[here], *part(edge, edge + length))
        last = triple(*high_pair, *part(edge + length, window))
        total[:window] = first
        total[window:] = last
        total[length : length + window] += middle
        high[b * span : (b + 1) * span], low[b * span : (b + 1) * span] = halves(total[...])
        both[:, column] = const[:, column] - (
            triple(*halves(low_const), *part(0, edge))
            + triple(*halves(constant(b)), *part(edge, edge + length))
            + triple(*halves(high_const), *part(edge + length, window))
        )
    if jump:
        own_rows, other_rows = rest[:2]

        def value(start, count):
            rows = pl.ds(start, count)
            return high[rows].astype(jnp.float32) + low[rows].astype(jnp.float32)

        for b in range(blocks):
            own_rows[b * sites : (b + 1) * sites] = value(b * span + window - edge - b * length, sites)
            at = blocks * sites + b * cols
            own_rows[at : at + cols] = both[:, b * length : (b + 1) * length]
        starts = [
            [b * span + at for b, (lo, hi, _) in enumerate(cuts_of(blocks, length, sites, span, last)) for at in range(lo, hi, edge)]
            for last in (True, False)
        ]
        row = lax.axis_index("row")
        for chunk, (on_right, on_left) in enumerate(zip(*starts)):
            start = pl.multiple_of(jnp.where(row == 0, on_right, on_left), edge)
            other_rows[chunk * edge : (chunk + 1) * edge] = value(start, edge)


def keep(ref, start, value):
    cols, width = value.shape
    high, low = halves(value)
    ref[:cols, pl.ds(start, width)] = high
    ref[cols:, pl.ds(start, width)] = low


def load(sides, pick, own, halo, ref):
    sites = own.shape[1]
    keep(ref, halo, own)
    for side in range(sides):
        on_right = 1 - jnp.minimum(lax.axis_index("row"), 1).astype(jnp.int32) if sides == 1 else side
        start = pl.multiple_of((1 - on_right) * (sites - halo), 128)
        keep(ref, pl.multiple_of(on_right * (halo + sites), 128), pick(side, pl.ds(start, halo)))


def plain(next_in):
    return lambda side, cut: next_in[:, cut] if len(next_in.shape) == 2 else next_in[side, :, cut]


def top_kernel(mine, sides, next_in, own_in, const, near_high, near_low, _upper, _lower, upper, lower, mid):
    sites = lower.shape[1]
    length = near_high.shape[1]
    blocks = sites // length
    window = near_high.shape[0] // blocks
    edge = (window - length) // 2

    @pl.when(lax.axis_index("tm") == 2 * mine)
    def _():
        mid[...] = jnp.zeros_like(mid)
        load(sides, plain(next_in), own_in[...], edge, mid)
        upper[...] = own_in[...]
        for b in range(blocks):
            at, rows = slice(b * length, (b + 1) * length), slice(b * window, (b + 1) * window)
            product = stacked_dot(mid, slice(b * length, b * length + window), near_high[rows], near_low[rows])
            lower[:, at] = const[:, at] - product


def step(both, high, low, late, lower):
    blocks = lower.shape[1] // high.shape[1]
    length, span = high.shape[1], high.shape[0] // blocks
    for b in range(blocks):
        at, rows = slice(b * length, (b + 1) * length), slice(b * span, (b + 1) * span)
        lower[:, at] = both[:, at] + stacked_dot(late, slice(b * length, b * length + span), high[rows], low[rows])


def load_rims(sides, next_in, sites, halo, late):
    for side in range(sides):
        on_right = 1 - jnp.minimum(lax.axis_index("row"), 1).astype(jnp.int32) if sides == 1 else side
        start = pl.multiple_of((1 - on_right) * (sites - halo), 128)
        keep(late, pl.multiple_of(on_right * (halo + sites), 128), plain(next_in)(side, pl.ds(start, halo)))


def rim_kernel(mine, sides, next_in, both, high, low, _late, late, base):
    sites, length = base.shape[1], high.shape[1]
    blocks = sites // length
    span = high.shape[0] // blocks
    halo = (late.shape[1] - sites) // 2
    edge = halo - length

    @pl.when(lax.axis_index("tm") == 2 * mine)
    def _():
        load_rims(sides, next_in, sites, halo, late)
        cuts = [cuts_of(blocks, length, sites, span, last) for last in (False, True)]
        for b in range(blocks):
            value = both[:, b * length : (b + 1) * length]
            if sides == 2:
                for lo, hi, _ in (cuts[0][b], cuts[1][b]):
                    rows = slice(b * span + lo, b * span + hi)
                    value += stacked_dot(late, slice(b * length + lo, b * length + hi), high[rows], low[rows])
            else:
                on_left = lax.axis_index("row") != 0
                counts = [cut[b][1] - cut[b][0] for cut in cuts]
                for chunk in range(0, max(counts), edge):
                    starts = [cut[b][0] + chunk if chunk < count else 0 for cut, count in zip(cuts, counts)]
                    start = pl.multiple_of(jnp.where(on_left, starts[0], starts[1]), edge)
                    rows = pl.ds(b * span + start, edge)
                    product = stacked_dot(late, pl.ds(b * length + start, edge), high[rows], low[rows])
                    if chunk >= min(counts):
                        product = jnp.where(on_left == (counts[0] > counts[1]), product, 0.0)
                    value += product
            base[:, b * length : (b + 1) * length] = value


def add_own(own_in, base, high, low, late, lower):
    sites, length = lower.shape[1], high.shape[1]
    blocks = sites // length
    span = high.shape[0] // blocks
    halo = (late.shape[1] - sites) // 2
    keep(late, halo, own_in[...])
    for b in range(blocks):
        at, start = slice(b * length, (b + 1) * length), halo - b * length
        rows = slice(b * span + start, b * span + start + sites)
        lower[:, at] = base[:, at] + stacked_dot(late, slice(halo, halo + sites), high[rows], low[rows])


def chain_kernel(mine, own_in, base, high, low, _late, _lower, late, lower):
    pl.when(lax.axis_index("tm") == 2 * mine)(lambda: add_own(own_in, base, high, low, late, lower))


def rows_kernel(own_rows, other_rows, own_high, own_low, other_high, other_low):
    own_high[...], own_low[...] = halves(own_rows[: own_high.shape[0]])
    other_high[...], other_low[...] = halves(other_rows[...])


def add_parts(lower, own_rows, own_high, own_low, other_high, other_low, to_next, to_own, mid, far_mid, span):
    cols, sites = lower.shape
    length = own_rows.shape[1]
    blocks = sites // length
    halo = to_own.shape[1] - sites
    edge = halo - length
    row = lax.axis_index("row")
    keep(mid, 0, lower[...])
    near = pl.multiple_of(jnp.where(row == 0, sites - halo, 0), edge)
    for b in range(blocks):
        at, rows = slice(b * length, (b + 1) * length), slice(b * sites, (b + 1) * sites)
        const = slice(blocks * sites + b * cols, blocks * sites + (b + 1) * cols)
        to_own[:, at] = own_rows[const] + stacked_dot(mid, slice(0, sites), own_high[rows], own_low[rows])
    to_next[:, :halo] = to_own[:, pl.ds(near, halo)]
    pieces = []
    for rows, from_last, from_first in (
        (slice(0, edge), sites - halo, 0),
        (slice(edge, halo), sites - length, 0),
        (slice(halo, halo + edge), sites - edge, length),
    ):
        source = pl.multiple_of(jnp.where(row == 0, from_last, from_first), edge)
        pieces.append(stacked_dot(mid, pl.ds(source, rows.stop - rows.start), other_high[rows], other_low[rows]))
    far_mid[:, :length] = pieces[0] + jnp.where(row == 0, pieces[1], 0.0)
    far_mid[:, length:] = pieces[2] + jnp.where(row == 0, 0.0, pieces[1])
    to_next[:, halo:] = far_mid[...]
    away = pl.multiple_of(jnp.where(row == 0, 0, sites - halo), edge)
    to_own[:, sites:] = far_mid[:, pl.ds(away, halo)]


def jump_kernel(mine, own_in, base, high, low, *rest):
    ship, (_late, _lower, late, lower, to_next, to_own, to_last, *scratch) = rest[:-9], rest[-9:]

    @pl.when(lax.axis_index("tm") == 2 * mine)
    def _():
        add_own(own_in, base, high, low, late, lower)
        add_parts(lower, *ship, to_next, to_own, *scratch, high.shape[0] * high.shape[1] // own_in.shape[1])
        to_last[...] = to_next[...]

    @pl.when(lax.axis_index("tm") != 2 * mine)
    def _():
        for part in (to_next, to_own, to_last):
            part[...] = jnp.zeros_like(part)


def parts_kernel(mine, span, lower, *rest):
    ship, parts = rest[:-4], rest[-4:]

    @pl.when(lax.axis_index("tm") == 2 * mine)
    def _():
        add_parts(lower, *ship, *parts, span)

    @pl.when(lax.axis_index("tm") != 2 * mine)
    def _():
        for part in parts[:2]:
            part[...] = jnp.zeros_like(part)


def last_kernel(jumps, both, high, low, late, _lower, lower):
    device = lax.axis_index("tm")
    pl.when((device == 0) | (device == 2) if jumps else device == 0)(lambda: step(both, high, low, late, lower))


def upper_kernel(sides, top, *rest):
    far, far_high, far_low, _late, _upper, late, upper = rest[-7:]
    cols, sites = upper.shape
    length = far.shape[1]
    blocks = sites // length
    window = far_high.shape[0] // blocks
    halo = (late.shape[1] - sites) // 2
    at_window = halo - (window - length) // 2
    messages = rest[:-7]

    if len(messages) == 2:

        @pl.when(lax.axis_index("tm") == 0)
        def _():
            load(sides, plain(messages[1]), messages[0][...], halo, late)

    for mine, (*next_in, own_in) in enumerate(((messages[0], messages[2], messages[1]), messages[3:]) if len(messages) > 2 else ()):

        @pl.when(lax.axis_index("tm") == 2 * mine)
        def _():
            from_next = next_in[0][...] + next_in[1][...] if len(next_in) == 2 else next_in[0][...]
            own = own_in[:, :sites] + from_next[:, halo:]
            near = own_in[:, sites:] + from_next[:, :halo]
            load(sides, lambda side, cut: near, own, halo, late)

    @pl.when(lax.axis_index("tm") != 2 * top)
    def _():
        for b in range(blocks):
            rows = slice(b * window, (b + 1) * window)
            at = blocks * window + b * cols
            start = at_window + b * length
            upper[:, b * length : (b + 1) * length] = far[at : at + cols] - stacked_dot(
                late, slice(start, start + window), far_high[rows], far_low[rows]
            )


def local(normals, inv_diag, lag_coupling, fill_mask):
    times, rows = lax.axis_size("tm"), lax.axis_size("row")
    device = lax.axis_index("tm")
    cols, sites = normals.shape[1:]
    blocks, length = inv_diag.shape[1:3]
    window = lag_coupling.shape[2]
    edge = (window - length) // 2
    halo = length + edge
    sides = 1 if rows == 2 else 2
    pairs = times // 2
    f32, bf16 = jnp.float32, jnp.bfloat16
    shape = jax.ShapeDtypeStruct

    def link(source, target):
        return [(s * rows + r, t * rows + r) for s, t in zip(source, target) for r in range(rows)]

    def cross(value, source, target, split=False):
        if sides == 1:
            perm = [(s * rows + r, t * rows + 1 - r) for s, t in zip(source, target) for r in range(2)]
            return lax.ppermute(value, BOTH, perm)
        moved = []
        for side, step in enumerate((1, -1)):
            perm = [
                (s * rows + r, t * rows + r + step)
                for s, t in zip(source, target)
                for r in range(rows)
                if 0 <= r + step < rows
            ]
            moved.append(lax.ppermute(value[side : side + 1] if split else value[None], BOTH, perm))
        return jnp.concatenate(moved)

    tall = blocks * window
    jump = 2
    jumps = rows == 2 and pairs > 5 and blocks == 2
    const, inv_high, inv_low = pl.pallas_call(
        const_kernel,
        out_shape=(
            shape((cols, sites), f32),
            shape((blocks, length, length), bf16), shape((blocks, length, length), bf16),
        ),
        in_specs=[HBM] * 2,
        out_specs=(VMEM,) * 3,
        scratch_shapes=[
            pltpu.VMEM(normals.shape[1:], f32),
            pltpu.VMEM(inv_diag.shape[1:], f32),
            pltpu.SemaphoreType.DMA((1 + blocks,)),
        ],
        compiler_params=PARAMS,
    )(*[pltpu.with_memory_space_constraint(a, pltpu.HBM) for a in (normals, inv_diag)])
    again = pl.pallas_call(
        again_kernel,
        out_shape=shape((cols, sites), f32),
        in_specs=[VMEM],
        out_specs=VMEM,
        compiler_params=PARAMS,
        cost_estimate=pl.CostEstimate(flops=5 * 10**9, bytes_accessed=0, transcendentals=0),
    )(const)
    odd, even = range(1, times, 2), range(0, times, 2)
    first_next = cross(again, odd[-1:], even[-1:])
    first_own = lax.ppermute(const, BOTH, link(odd[-1:], even[-1:]))
    near, near_high, near_low = pl.pallas_call(
        fuse_kernel,
        out_shape=(
            shape((tall + blocks * cols, length), f32), shape((tall, length), bf16), shape((tall, length), bf16),
        ),
        in_specs=[VMEM] * 5,
        out_specs=(VMEM,) * 3,
        compiler_params=PARAMS,
        cost_estimate=pl.CostEstimate(
            flops=6 * (tall + cols * blocks) * length * length, bytes_accessed=16 * tall * length, transcendentals=0
        ),
    )(fill_mask, const, inv_high, inv_low, lag_coupling)
    edges = pl.pallas_call(
        functools.partial(edge_kernel, sides, blocks, cols),
        out_shape=shape((sides, window + cols, edge), f32),
        in_specs=[VMEM],
        out_specs=VMEM,
        compiler_params=PARAMS,
    )(near)
    near = pl.pallas_call(
        lambda _own, _edges, own: None,
        out_shape=shape(near.shape, f32),
        in_specs=[VMEM] * 2,
        out_specs=VMEM,
        input_output_aliases={0: 0},
        compiler_params=PARAMS,
    )(near, edges)
    rim = cross(edges, odd[:-1], even[:-1], True)
    far = lax.ppermute(near, BOTH, link(odd[:-1], even[:-1]))

    blank = jnp.zeros((cols, sites), f32)
    upper, lower = pl.pallas_call(
        functools.partial(top_kernel, pairs - 1, sides),
        out_shape=(shape((cols, sites), f32),) * 2,
        in_specs=[VMEM] * 7,
        out_specs=(VMEM,) * 2,
        scratch_shapes=[pltpu.VMEM((2 * cols, sites + 2 * edge), bf16)],
        input_output_aliases={5: 0, 6: 1},
        compiler_params=PARAMS,
        cost_estimate=pl.CostEstimate(flops=50 * 10**9, bytes_accessed=0, transcendentals=0),
    )(first_next, first_own, const, near_high, near_low, blank, blank)
    far_high, far_low = pl.pallas_call(
        split_kernel,
        out_shape=(shape((tall, length), bf16), shape((tall, length), bf16)),
        in_specs=[VMEM],
        out_specs=(VMEM,) * 2,
        compiler_params=PARAMS,
    )(far)
    packs = (shape((blocks * (sites + cols), length), f32), shape((halo + edge, length), f32)) if jumps else ()

    def pair_matrix(first, jumps, packs):
        return pl.pallas_call(
            functools.partial(pair_kernel, (pairs - 2, first), jumps),
            out_shape=(
                shape((2 * tall, length), bf16), shape((2 * tall, length), bf16), shape((cols, sites), f32), *packs
            ),
            in_specs=[VMEM] * 7,
            out_specs=(VMEM,) * (3 + len(packs)),
            scratch_shapes=[pltpu.VMEM((2 * window, length), f32)],
            compiler_params=PARAMS,
            cost_estimate=pl.CostEstimate(flops=10**9, bytes_accessed=0, transcendentals=0),
        )(far, rim, far_high, far_low, near_high, near_low, const)

    early = pair_matrix(True, False, ())
    high, low, both, *packs = pair_matrix(False, jumps, packs)
    if jumps:
        source, target = [2 * jump - 2, 2 * jump], [2 * jump, 2 * jump + 2]
        own_rows = lax.ppermute(packs[0], BOTH, link(source, target))
        other_rows = cross(packs[1], source, target)
        ship = pl.pallas_call(
            rows_kernel,
            out_shape=(shape((blocks * sites, length), bf16),) * 2 + (shape(other_rows.shape, bf16),) * 2,
            in_specs=[VMEM] * 2,
            out_specs=(VMEM,) * 4,
            compiler_params=PARAMS,
        )(own_rows, other_rows)

    def turn(kernel, given, state, scratch=(), extra=(), flops=0):
        return pl.pallas_call(
            kernel,
            out_shape=tuple(shape(v.shape, v.dtype) for v in state) + tuple(extra),
            in_specs=[VMEM] * (len(given) + len(state)),
            out_specs=(VMEM,) * (len(state) + len(extra)),
            scratch_shapes=list(scratch),
            input_output_aliases={len(given) + i: i for i in range(len(state))},
            compiler_params=PARAMS,
            cost_estimate=pl.CostEstimate(flops=flops, bytes_accessed=0, transcendentals=0) if flops else None,
        )(*given, *state)

    parts = (shape((cols, sites + halo), f32),) * 2
    parts_scratch = [pltpu.VMEM((2 * cols, sites), bf16), pltpu.VMEM((cols, sites), f32)]
    late = jnp.zeros((2 * cols, sites + 2 * halo), bf16)
    mine = pairs - 1
    while mine > 0:
        if jumps and mine == jump:
            source, target = [2 * mine], [2 * mine - 4]
            first_in = lax.ppermute(to_next, BOTH, [(2 * source[0] + 1, 2 * target[0])])
            own_in = lax.ppermute(to_own, BOTH, link(source, target))
            next_in = lax.ppermute(to_last, BOTH, [(2 * source[0], 2 * target[0] + 1)])
            break
        source, target = [2 * mine], [2 * mine - 2]
        next_in = cross(lower, source, target)
        own_in = lax.ppermute(lower, BOTH, link(source, target))
        if jumps and mine == jump + 1:
            beside = pl.pallas_call(
                functools.partial(parts_kernel, mine, 2 * window),
                out_shape=parts,
                in_specs=[VMEM] * 6,
                out_specs=(VMEM,) * 2,
                scratch_shapes=parts_scratch,
                compiler_params=PARAMS,
            )(lower, own_rows, *ship)
            source, target = [2 * mine], [2 * mine - 4]
            beside_next = cross(beside[0], source, target)
            beside_own = lax.ppermute(beside[1], BOTH, link(source, target))
        mine -= 1
        if mine == 0:
            break
        here = early if mine == pairs - 2 else (high, low, both)
        late, base = turn(
            functools.partial(rim_kernel, mine, sides),
            (next_in, here[2], *here[:2]),
            (late,),
            extra=[shape((cols, sites), f32)],
        )
        if jumps and mine == jump:
            late, lower, to_next, to_own, to_last = turn(
                functools.partial(jump_kernel, mine),
                (own_in, base, high, low, own_rows, *ship),
                (late, lower),
                parts_scratch,
                parts + parts[:1],
            )
        else:
            late, lower = turn(
                functools.partial(chain_kernel, mine),
                (own_in, base, *here[:2]),
                (late, lower),
                flops=50 * 10**9 if jumps and mine == pairs - 3 else 0,
            )
    given = (first_in, own_in, next_in, beside_next, beside_own) if jumps else (own_in, next_in)
    late, upper = turn(
        functools.partial(upper_kernel, sides, pairs - 1), (*given, far, far_high, far_low), (late, upper)
    )
    returned = lax.ppermute(upper, BOTH, link(even, odd))
    lower = pl.pallas_call(
        functools.partial(last_kernel, jumps),
        out_shape=shape(lower.shape, f32),
        in_specs=[VMEM] * 5,
        out_specs=VMEM,
        input_output_aliases={4: 0},
        compiler_params=PARAMS,
        cost_estimate=pl.CostEstimate(flops=12 * cols * tall * length, bytes_accessed=8 * tall * length, transcendentals=0),
    )(both, high, low, late, lower)
    return jnp.where(device % 2 == 0, lower, returned)[None]


def solution(mesh):
    placed = (
        P("tm", None, "row"),
        P("tm", "row", None, None),
        P("tm", "row", None, None),
        P("tm", "row", None),
    )
    return jax.shard_map(
        local, mesh=mesh, in_specs=placed, out_specs=P("tm", None, "row"), check_vma=False
    )
```

```python
import functools

import jax
import jax.numpy as jnp
from jax import lax
from jax.experimental import pallas as pl
from jax.experimental.pallas import tpu as pltpu
from jax.sharding import PartitionSpec as P

BOTH = ("tm", "row")
VMEM = pl.BlockSpec(memory_space=pltpu.VMEM)
HBM = pl.BlockSpec(memory_space=pltpu.HBM)
PARAMS = pltpu.CompilerParams(vmem_limit_bytes=32 * 1024 * 1024)


def halves(value):
    high = value.astype(jnp.bfloat16)
    low = (value - high.astype(jnp.float32)).astype(jnp.bfloat16)
    return high, low


def dot(a, b):
    return jnp.dot(a, b, preferred_element_type=jnp.float32)


def stacked_dot(pair, cols, high, low):
    rows = pair.shape[0] // 2
    wide = dot(pair[:, cols], high)
    return wide[:rows] + wide[rows:] + dot(pair[:rows, cols], low)


def triple(high, low, inv_high, inv_low):
    return dot(high, inv_high) + dot(low, inv_high) + dot(high, inv_low)


def put_rim(sides, rim, columns):
    if sides == 1:
        row = lax.axis_index("row")

        @pl.when(row == 0)
        def _():
            rim[0] = columns(True)

        @pl.when(row != 0)
        def _():
            rim[0] = columns(False)
    else:
        rim[0] = columns(True)
        rim[1] = columns(False)


def const_kernel(normals, inv, const, inv_high, inv_low, normals_in, inv_in, sems):
    blocks, length = inv.shape[1], inv.shape[2]
    moves = [pltpu.make_async_copy(normals.at[0], normals_in, sems.at[0])]
    for b in range(blocks):
        moves.append(pltpu.make_async_copy(inv.at[0, b], inv_in.at[b], sems.at[1 + b]))
    for move in moves:
        move.start()
    moves[0].wait()
    for b in range(blocks):
        at = slice(b * length, (b + 1) * length)
        high, low = halves(normals_in[:, at])
        moves[1 + b].wait()
        inv_high[b], inv_low[b] = halves(inv_in[b])
        const[:, at] = triple(high, low, inv_high[b], inv_low[b])


def again_kernel(const, again):
    again[...] = const[...]


def fuse_kernel(late, *refs):
    here = lax.axis_index("tm") == late[0]
    given = refs[:5] + refs[6:] if late[1] else refs
    pl.when(here if late[1] else jnp.logical_not(here))(lambda: make_fused(*given))


def make_fused(mask, const, inv_high, inv_low, lag, near_high, near_low, own=None):
    blocks, window, length = lag.shape[1:]
    edge = (window - length) // 2
    cols = const.shape[0]
    cuts = (0, edge, edge + length, window)
    flags = mask[0].astype(jnp.float32)
    for b in range(blocks):
        at = blocks * window + b * cols
        if own is not None:
            own[at : at + cols] = const[:, b * length : (b + 1) * length]
        for part in range(3):
            lo, hi = cuts[part], cuts[part + 1]
            rows = slice(b * window + lo, b * window + hi)
            high, low = halves(lag[0, b, lo:hi] * flags[b : b + 1, part : part + 1])
            value = triple(high, low, inv_high[b], inv_low[b])
            if own is not None:
                own[rows] = value
            near_high[rows], near_low[rows] = halves(value)


def edge_kernel(sides, blocks, cols, own, rim):
    length, edge = own.shape[1], rim.shape[2]
    window = length + 2 * edge

    def columns(last):
        b = blocks - 1 if last else 0
        cut = slice(length - edge, length) if last else slice(0, edge)
        at = blocks * window + b * cols
        return jnp.concatenate([own[b * window : (b + 1) * window, cut], own[at : at + cols, cut]])

    put_rim(sides, rim, columns)


def split_kernel(far, far_high, far_low):
    far_high[...], far_low[...] = halves(far[: far_high.shape[0]])


def cuts_of(blocks, length, sites, span, last):
    packed, cuts = 0, []
    for b in range(blocks):
        start = span // 2 - length // 2 - b * length
        lo, hi = (start + sites, span) if last else (0, start)
        cuts.append((lo, hi, packed))
        packed += hi - lo
    return cuts


def pair_kernel(first, jump, *refs):
    here = lax.axis_index("tm") == 2 * first[0]
    pl.when(here if first[1] else jnp.logical_not(here))(lambda: make_pair(jump, *refs))


def make_pair(jump, far, rim, far_high, far_low, near_high, near_low, const, high, low, both, *rest):
    cols, sites = const.shape
    length = far.shape[1]
    blocks = sites // length
    window = near_high.shape[0] // blocks
    edge = (window - length) // 2
    span = 2 * window
    tall = blocks * window
    total = rest[-1]
    if rim.shape[0] == 1:
        flag = jnp.minimum(lax.axis_index("row"), 1).astype(jnp.float32)
        left, right = rim[0] * flag, rim[0] * (1 - flag)
    else:
        left, right = rim[0], rim[1]
    left_pair, right_pair = halves(left[:window]), halves(right[:window])
    for b in range(blocks):
        here = slice(b * window, (b + 1) * window)
        column = slice(b * length, (b + 1) * length)

        def part(lo, hi):
            rows = slice(b * window + lo, b * window + hi)
            return near_high[rows], near_low[rows]

        def constant(block):
            if block < 0:
                return left[window:]
            if block == blocks:
                return right[window:]
            return far[tall + block * cols : tall + (block + 1) * cols]

        if b > 0:
            before = slice((b - 1) * window, b * window)
            low_pair = far_high[before, length - edge :], far_low[before, length - edge :]
            low_const = constant(b - 1)[:, length - edge :]
        else:
            low_pair, low_const = left_pair, constant(-1)
        if b + 1 < blocks:
            after = slice((b + 1) * window, (b + 2) * window)
            high_pair = far_high[after, :edge], far_low[after, :edge]
            high_const = constant(b + 1)[:, :edge]
        else:
            high_pair, high_const = right_pair, constant(blocks)
        first = triple(*low_pair, *part(0, edge))
        middle = triple(far_high[here], far_low[here], *part(edge, edge + length))
        last = triple(*high_pair, *part(edge + length, window))
        total[:window] = first
        total[window:] = last
        total[length : length + window] += middle
        high[b * span : (b + 1) * span], low[b * span : (b + 1) * span] = halves(total[...])
        both[:, column] = const[:, column] - (
            triple(*halves(low_const), *part(0, edge))
            + triple(*halves(constant(b)), *part(edge, edge + length))
            + triple(*halves(high_const), *part(edge + length, window))
        )
    if jump:
        own_rows, other_rows = rest[:2]

        def value(start, count):
            rows = pl.ds(start, count)
            return high[rows].astype(jnp.float32) + low[rows].astype(jnp.float32)

        for b in range(blocks):
            own_rows[b * sites : (b + 1) * sites] = value(b * span + window - edge - b * length, sites)
            at = blocks * sites + b * cols
            own_rows[at : at + cols] = both[:, b * length : (b + 1) * length]
        starts = [
            [b * span + at for b, (lo, hi, _) in enumerate(cuts_of(blocks, length, sites, span, last)) for at in range(lo, hi, edge)]
            for last in (True, False)
        ]
        row = lax.axis_index("row")
        for chunk, (on_right, on_left) in enumerate(zip(*starts)):
            start = pl.multiple_of(jnp.where(row == 0, on_right, on_left), edge)
            other_rows[chunk * edge : (chunk + 1) * edge] = value(start, edge)


def keep(ref, start, value):
    cols, width = value.shape
    high, low = halves(value)
    ref[:cols, pl.ds(start, width)] = high
    ref[cols:, pl.ds(start, width)] = low


def load(sides, pick, own, halo, ref):
    sites = own.shape[1]
    keep(ref, halo, own)
    for side in range(sides):
        on_right = 1 - jnp.minimum(lax.axis_index("row"), 1).astype(jnp.int32) if sides == 1 else side
        start = pl.multiple_of((1 - on_right) * (sites - halo), 128)
        keep(ref, pl.multiple_of(on_right * (halo + sites), 128), pick(side, pl.ds(start, halo)))


def plain(next_in):
    return lambda side, cut: next_in[:, cut] if len(next_in.shape) == 2 else next_in[side, :, cut]


def top_kernel(mine, sides, next_in, own_in, const, near_high, near_low, _upper, _lower, upper, lower, mid):
    sites = lower.shape[1]
    length = near_high.shape[1]
    blocks = sites // length
    window = near_high.shape[0] // blocks
    edge = (window - length) // 2

    @pl.when(lax.axis_index("tm") == 2 * mine)
    def _():
        mid[...] = jnp.zeros_like(mid)
        load(sides, plain(next_in), own_in[...], edge, mid)
        upper[...] = own_in[...]
        for b in range(blocks):
            at, rows = slice(b * length, (b + 1) * length), slice(b * window, (b + 1) * window)
            product = stacked_dot(mid, slice(b * length, b * length + window), near_high[rows], near_low[rows])
            lower[:, at] = const[:, at] - product


def step(both, high, low, late, lower):
    blocks = lower.shape[1] // high.shape[1]
    length, span = high.shape[1], high.shape[0] // blocks
    for b in range(blocks):
        at, rows = slice(b * length, (b + 1) * length), slice(b * span, (b + 1) * span)
        lower[:, at] = both[:, at] + stacked_dot(late, slice(b * length, b * length + span), high[rows], low[rows])


def load_rims(sides, next_in, sites, halo, late):
    for side in range(sides):
        on_right = 1 - jnp.minimum(lax.axis_index("row"), 1).astype(jnp.int32) if sides == 1 else side
        start = pl.multiple_of((1 - on_right) * (sites - halo), 128)
        keep(late, pl.multiple_of(on_right * (halo + sites), 128), plain(next_in)(side, pl.ds(start, halo)))


def rim_kernel(mine, sides, next_in, both, high, low, _late, late, base):
    sites, length = base.shape[1], high.shape[1]
    blocks = sites // length
    span = high.shape[0] // blocks
    halo = (late.shape[1] - sites) // 2
    edge = halo - length

    @pl.when(lax.axis_index("tm") == 2 * mine)
    def _():
        load_rims(sides, next_in, sites, halo, late)
        cuts = [cuts_of(blocks, length, sites, span, last) for last in (False, True)]
        for b in range(blocks):
            value = both[:, b * length : (b + 1) * length]
            if sides == 2:
                for lo, hi, _ in (cuts[0][b], cuts[1][b]):
                    rows = slice(b * span + lo, b * span + hi)
                    value += stacked_dot(late, slice(b * length + lo, b * length + hi), high[rows], low[rows])
            else:
                on_left = lax.axis_index("row") != 0
                counts = [cut[b][1] - cut[b][0] for cut in cuts]
                for chunk in range(0, max(counts), edge):
                    starts = [cut[b][0] + chunk if chunk < count else 0 for cut, count in zip(cuts, counts)]
                    start = pl.multiple_of(jnp.where(on_left, starts[0], starts[1]), edge)
                    rows = pl.ds(b * span + start, edge)
                    product = stacked_dot(late, pl.ds(b * length + start, edge), high[rows], low[rows])
                    if chunk >= min(counts):
                        product = jnp.where(on_left == (counts[0] > counts[1]), product, 0.0)
                    value += product
            base[:, b * length : (b + 1) * length] = value


def add_own(own_in, base, high, low, late, lower):
    sites, length = lower.shape[1], high.shape[1]
    blocks = sites // length
    span = high.shape[0] // blocks
    halo = (late.shape[1] - sites) // 2
    keep(late, halo, own_in[...])
    for b in range(blocks):
        at, start = slice(b * length, (b + 1) * length), halo - b * length
        rows = slice(b * span + start, b * span + start + sites)
        lower[:, at] = base[:, at] + stacked_dot(late, slice(halo, halo + sites), high[rows], low[rows])


def chain_kernel(mine, own_in, base, high, low, _late, _lower, late, lower):
    pl.when(lax.axis_index("tm") == 2 * mine)(lambda: add_own(own_in, base, high, low, late, lower))


def rows_kernel(own_rows, other_rows, own_high, own_low, other_high, other_low):
    own_high[...], own_low[...] = halves(own_rows[: own_high.shape[0]])
    other_high[...], other_low[...] = halves(other_rows[...])


def add_parts(lower, own_rows, own_high, own_low, other_high, other_low, to_next, to_own, mid, far_mid, span):
    cols, sites = lower.shape
    length = own_rows.shape[1]
    blocks = sites // length
    halo = to_own.shape[1] - sites
    edge = halo - length
    row = lax.axis_index("row")
    keep(mid, 0, lower[...])
    near = pl.multiple_of(jnp.where(row == 0, sites - halo, 0), edge)
    for b in range(blocks):
        at, rows = slice(b * length, (b + 1) * length), slice(b * sites, (b + 1) * sites)
        const = slice(blocks * sites + b * cols, blocks * sites + (b + 1) * cols)
        to_own[:, at] = own_rows[const] + stacked_dot(mid, slice(0, sites), own_high[rows], own_low[rows])
    to_next[:, :halo] = to_own[:, pl.ds(near, halo)]
    pieces = []
    for rows, from_last, from_first in (
        (slice(0, edge), sites - halo, 0),
        (slice(edge, halo), sites - length, 0),
        (slice(halo, halo + edge), sites - edge, length),
    ):
        source = pl.multiple_of(jnp.where(row == 0, from_last, from_first), edge)
        pieces.append(stacked_dot(mid, pl.ds(source, rows.stop - rows.start), other_high[rows], other_low[rows]))
    far_mid[:, :length] = pieces[0] + jnp.where(row == 0, pieces[1], 0.0)
    far_mid[:, length:] = pieces[2] + jnp.where(row == 0, 0.0, pieces[1])
    to_next[:, halo:] = far_mid[...]
    away = pl.multiple_of(jnp.where(row == 0, 0, sites - halo), edge)
    to_own[:, sites:] = far_mid[:, pl.ds(away, halo)]


def jump_kernel(mine, own_in, base, high, low, *rest):
    ship, (_late, _lower, late, lower, to_next, to_own, *scratch) = rest[:-8], rest[-8:]

    @pl.when(lax.axis_index("tm") == 2 * mine)
    def _():
        add_own(own_in, base, high, low, late, lower)
        add_parts(lower, *ship, to_next, to_own, *scratch, high.shape[0] * high.shape[1] // own_in.shape[1])

    @pl.when(lax.axis_index("tm") != 2 * mine)
    def _():
        for part in (to_next, to_own):
            part[...] = jnp.zeros_like(part)


def parts_kernel(mine, span, lower, *rest):
    ship, parts = rest[:-4], rest[-4:]

    @pl.when(lax.axis_index("tm") == 2 * mine)
    def _():
        add_parts(lower, *ship, *parts, span)

    @pl.when(lax.axis_index("tm") != 2 * mine)
    def _():
        for part in parts[:2]:
            part[...] = jnp.zeros_like(part)


def last_kernel(jumps, both, high, low, late, _lower, lower):
    device = lax.axis_index("tm")
    pl.when((device == 0) | (device == 2) if jumps else device == 0)(lambda: step(both, high, low, late, lower))


def upper_kernel(sides, top, *rest):
    far, far_high, far_low, _late, _upper, late, upper = rest[-7:]
    cols, sites = upper.shape
    length = far.shape[1]
    blocks = sites // length
    window = far_high.shape[0] // blocks
    halo = (late.shape[1] - sites) // 2
    at_window = halo - (window - length) // 2
    messages = rest[:-7]

    if len(messages) == 2:

        @pl.when(lax.axis_index("tm") == 0)
        def _():
            load(sides, plain(messages[1]), messages[0][...], halo, late)

    for mine, (from_next, own_in) in enumerate((messages[:2], messages[2:]) if len(messages) > 2 else ()):

        @pl.when(lax.axis_index("tm") == 2 * mine)
        def _():
            own = own_in[:, :sites] + from_next[:, halo:]
            near = own_in[:, sites:] + from_next[:, :halo]
            load(sides, lambda side, cut: near, own, halo, late)

    @pl.when(lax.axis_index("tm") != 2 * top)
    def _():
        for b in range(blocks):
            rows = slice(b * window, (b + 1) * window)
            at = blocks * window + b * cols
            start = at_window + b * length
            upper[:, b * length : (b + 1) * length] = far[at : at + cols] - stacked_dot(
                late, slice(start, start + window), far_high[rows], far_low[rows]
            )


def local(normals, inv_diag, lag_coupling, fill_mask):
    times, rows = lax.axis_size("tm"), lax.axis_size("row")
    device = lax.axis_index("tm")
    cols, sites = normals.shape[1:]
    blocks, length = inv_diag.shape[1:3]
    window = lag_coupling.shape[2]
    edge = (window - length) // 2
    halo = length + edge
    sides = 1 if rows == 2 else 2
    pairs = times // 2
    f32, bf16 = jnp.float32, jnp.bfloat16
    shape = jax.ShapeDtypeStruct

    def link(source, target):
        return [(s * rows + r, t * rows + r) for s, t in zip(source, target) for r in range(rows)]

    def cross(value, source, target, split=False):
        if sides == 1:
            perm = [(s * rows + r, t * rows + 1 - r) for s, t in zip(source, target) for r in range(2)]
            return lax.ppermute(value, BOTH, perm)
        moved = []
        for side, step in enumerate((1, -1)):
            perm = [
                (s * rows + r, t * rows + r + step)
                for s, t in zip(source, target)
                for r in range(rows)
                if 0 <= r + step < rows
            ]
            moved.append(lax.ppermute(value[side : side + 1] if split else value[None], BOTH, perm))
        return jnp.concatenate(moved)

    tall = blocks * window
    jump = 2
    jumps = rows == 2 and pairs > 5 and blocks == 2
    const, inv_high, inv_low = pl.pallas_call(
        const_kernel,
        out_shape=(
            shape((cols, sites), f32),
            shape((blocks, length, length), bf16), shape((blocks, length, length), bf16),
        ),
        in_specs=[HBM] * 2,
        out_specs=(VMEM,) * 3,
        scratch_shapes=[
            pltpu.VMEM(normals.shape[1:], f32),
            pltpu.VMEM(inv_diag.shape[1:], f32),
            pltpu.SemaphoreType.DMA((1 + blocks,)),
        ],
        compiler_params=PARAMS,
    )(*[pltpu.with_memory_space_constraint(a, pltpu.HBM) for a in (normals, inv_diag)])
    again = pl.pallas_call(
        again_kernel,
        out_shape=shape((cols, sites), f32),
        in_specs=[VMEM],
        out_specs=VMEM,
        compiler_params=PARAMS,
        cost_estimate=pl.CostEstimate(flops=5 * 10**9, bytes_accessed=0, transcendentals=0),
    )(const)
    odd, even = range(1, times, 2), range(0, times, 2)
    first_next = cross(again, odd[-1:], even[-1:])
    first_own = lax.ppermute(const, BOTH, link(odd[-1:], even[-1:]))

    def fused(late, extra, after=()):
        return pl.pallas_call(
            functools.partial(fuse_kernel, (2 * pairs - 4, late)),
            out_shape=(shape((tall, length), bf16), shape((tall, length), bf16), *extra),
            in_specs=[VMEM] * (5 + len(after)),
            out_specs=(VMEM,) * (2 + len(extra)),
            compiler_params=PARAMS,
            cost_estimate=pl.CostEstimate(
                flops=6 * (tall + cols * blocks) * length * length, bytes_accessed=16 * tall * length, transcendentals=0
            ),
        )(fill_mask, const, inv_high, inv_low, lag_coupling, *after)

    near_high, near_low, near = fused(False, (shape((tall + blocks * cols, length), f32),))
    edges = pl.pallas_call(
        functools.partial(edge_kernel, sides, blocks, cols),
        out_shape=shape((sides, window + cols, edge), f32),
        in_specs=[VMEM],
        out_specs=VMEM,
        compiler_params=PARAMS,
    )(near)
    near = pl.pallas_call(
        lambda _own, _edges, own: None,
        out_shape=shape(near.shape, f32),
        in_specs=[VMEM] * 2,
        out_specs=VMEM,
        input_output_aliases={0: 0},
        compiler_params=PARAMS,
    )(near, edges)
    rim = cross(edges, odd[:-1], even[:-1], True)
    far = lax.ppermute(near, BOTH, link(odd[:-1], even[:-1]))

    blank = jnp.zeros((cols, sites), f32)
    upper, lower = pl.pallas_call(
        functools.partial(top_kernel, pairs - 1, sides),
        out_shape=(shape((cols, sites), f32),) * 2,
        in_specs=[VMEM] * 7,
        out_specs=(VMEM,) * 2,
        scratch_shapes=[pltpu.VMEM((2 * cols, sites + 2 * edge), bf16)],
        input_output_aliases={5: 0, 6: 1},
        compiler_params=PARAMS,
        cost_estimate=pl.CostEstimate(flops=50 * 10**9, bytes_accessed=0, transcendentals=0),
    )(first_next, first_own, const, near_high, near_low, blank, blank)
    far_high, far_low = pl.pallas_call(
        split_kernel,
        out_shape=(shape((tall, length), bf16), shape((tall, length), bf16)),
        in_specs=[VMEM],
        out_specs=(VMEM,) * 2,
        compiler_params=PARAMS,
    )(far)
    packs = (shape((blocks * (sites + cols), length), f32), shape((halo + edge, length), f32)) if jumps else ()

    def pair_matrix(first, jumps, packs, mine):
        return pl.pallas_call(
            functools.partial(pair_kernel, (pairs - 2, first), jumps),
            out_shape=(
                shape((2 * tall, length), bf16), shape((2 * tall, length), bf16), shape((cols, sites), f32), *packs
            ),
            in_specs=[VMEM] * 7,
            out_specs=(VMEM,) * (3 + len(packs)),
            scratch_shapes=[pltpu.VMEM((2 * window, length), f32)],
            compiler_params=PARAMS,
            cost_estimate=pl.CostEstimate(flops=10**9, bytes_accessed=0, transcendentals=0),
        )(far, rim, far_high, far_low, *mine, const)

    early = pair_matrix(True, False, (), fused(True, (), (lower,)))
    high, low, both, *packs = pair_matrix(False, jumps, packs, (near_high, near_low))
    if jumps:
        source, target = [2 * jump - 2, 2 * jump], [2 * jump, 2 * jump + 2]
        own_rows = lax.ppermute(packs[0], BOTH, link(source, target))
        other_rows = cross(packs[1], source, target)
        ship = pl.pallas_call(
            rows_kernel,
            out_shape=(shape((blocks * sites, length), bf16),) * 2 + (shape(other_rows.shape, bf16),) * 2,
            in_specs=[VMEM] * 2,
            out_specs=(VMEM,) * 4,
            compiler_params=PARAMS,
        )(own_rows, other_rows)

    def turn(kernel, given, state, scratch=(), extra=(), flops=0):
        return pl.pallas_call(
            kernel,
            out_shape=tuple(shape(v.shape, v.dtype) for v in state) + tuple(extra),
            in_specs=[VMEM] * (len(given) + len(state)),
            out_specs=(VMEM,) * (len(state) + len(extra)),
            scratch_shapes=list(scratch),
            input_output_aliases={len(given) + i: i for i in range(len(state))},
            compiler_params=PARAMS,
            cost_estimate=pl.CostEstimate(flops=flops, bytes_accessed=0, transcendentals=0) if flops else None,
        )(*given, *state)

    parts = (shape((cols, sites + halo), f32),) * 2
    parts_scratch = [pltpu.VMEM((2 * cols, sites), bf16), pltpu.VMEM((cols, sites), f32)]
    late = jnp.zeros((2 * cols, sites + 2 * halo), bf16)
    mine = pairs - 1
    while mine > 0:
        if jumps and mine == jump:
            source, target = [2 * mine], [2 * mine - 4]
            next_in = cross(to_next, source, target)
            own_in = lax.ppermute(to_own, BOTH, link(source, target))
            break
        source, target = [2 * mine], [2 * mine - 2]
        next_in = cross(lower, source, target)
        own_in = lax.ppermute(lower, BOTH, link(source, target))
        if jumps and mine == jump + 1:
            beside = pl.pallas_call(
                functools.partial(parts_kernel, mine, 2 * window),
                out_shape=parts,
                in_specs=[VMEM] * 6,
                out_specs=(VMEM,) * 2,
                scratch_shapes=parts_scratch,
                compiler_params=PARAMS,
            )(lower, own_rows, *ship)
            source, target = [2 * mine], [2 * mine - 4]
            beside_next = cross(beside[0], source, target)
            beside_own = lax.ppermute(beside[1], BOTH, link(source, target))
        mine -= 1
        if mine == 0:
            break
        here = early if mine == pairs - 2 else (high, low, both)
        late, base = turn(
            functools.partial(rim_kernel, mine, sides),
            (next_in, here[2], *here[:2]),
            (late,),
            extra=[shape((cols, sites), f32)],
        )
        if jumps and mine == jump:
            late, lower, to_next, to_own = turn(
                functools.partial(jump_kernel, mine),
                (own_in, base, high, low, own_rows, *ship),
                (late, lower),
                parts_scratch,
                parts,
            )
        else:
            late, lower = turn(
                functools.partial(chain_kernel, mine),
                (own_in, base, *here[:2]),
                (late, lower),
                flops=50 * 10**9 if jumps and mine == pairs - 3 else 0,
            )
    given = (next_in, own_in, beside_next, beside_own) if jumps else (own_in, next_in)
    late, upper = turn(
        functools.partial(upper_kernel, sides, pairs - 1), (*given, far, far_high, far_low), (late, upper)
    )
    returned = lax.ppermute(upper, BOTH, link(even, odd))
    lower = pl.pallas_call(
        functools.partial(last_kernel, jumps),
        out_shape=shape(lower.shape, f32),
        in_specs=[VMEM] * 5,
        out_specs=VMEM,
        input_output_aliases={4: 0},
        compiler_params=PARAMS,
        cost_estimate=pl.CostEstimate(flops=12 * cols * tall * length, bytes_accessed=8 * tall * length, transcendentals=0),
    )(both, high, low, late, lower)
    return jnp.where(device % 2 == 0, lower, returned)[None]


def solution(mesh):
    placed = (
        P("tm", None, "row"),
        P("tm", "row", None, None),
        P("tm", "row", None, None),
        P("tm", "row", None),
    )
    return jax.shard_map(
        local, mesh=mesh, in_specs=placed, out_specs=P("tm", None, "row"), check_vma=False
    )
```

```python
import functools

import jax
import jax.numpy as jnp
from jax import lax
from jax.experimental import pallas as pl
from jax.experimental.pallas import tpu as pltpu
from jax.sharding import PartitionSpec as P

BOTH = ("tm", "row")
VMEM = pl.BlockSpec(memory_space=pltpu.VMEM)
HBM = pl.BlockSpec(memory_space=pltpu.HBM)
PARAMS = pltpu.CompilerParams(vmem_limit_bytes=32 * 1024 * 1024)


def halves(value):
    high = value.astype(jnp.bfloat16)
    low = (value - high.astype(jnp.float32)).astype(jnp.bfloat16)
    return high, low


def dot(a, b):
    return jnp.dot(a, b, preferred_element_type=jnp.float32)


def stacked_dot(pair, cols, high, low):
    rows = pair.shape[0] // 2
    wide = dot(pair[:, cols], high)
    return wide[:rows] + wide[rows:] + dot(pair[:rows, cols], low)


def triple(high, low, inv_high, inv_low):
    return dot(high, inv_high) + dot(low, inv_high) + dot(high, inv_low)


def put_rim(sides, rim, columns):
    if sides == 1:
        row = lax.axis_index("row")

        @pl.when(row == 0)
        def _():
            rim[0] = columns(True)

        @pl.when(row != 0)
        def _():
            rim[0] = columns(False)
    else:
        rim[0] = columns(True)
        rim[1] = columns(False)


def const_kernel(normals, inv, const, inv_high, inv_low, normals_in, inv_in, sems):
    blocks, length = inv.shape[1], inv.shape[2]
    moves = [pltpu.make_async_copy(normals.at[0], normals_in, sems.at[0])]
    for b in range(blocks):
        moves.append(pltpu.make_async_copy(inv.at[0, b], inv_in.at[b], sems.at[1 + b]))
    for move in moves:
        move.start()
    moves[0].wait()
    for b in range(blocks):
        at = slice(b * length, (b + 1) * length)
        high, low = halves(normals_in[:, at])
        moves[1 + b].wait()
        inv_high[b], inv_low[b] = halves(inv_in[b])
        const[:, at] = triple(high, low, inv_high[b], inv_low[b])


def again_kernel(const, again):
    again[...] = const[...]


def fuse_kernel(late, *refs):
    here = lax.axis_index("tm") == late[0]
    given = refs[:5] + refs[6:] if late[1] else refs
    pl.when(here if late[1] else jnp.logical_not(here))(lambda: make_fused(*given))


def make_fused(mask, const, inv_high, inv_low, lag, near_high, near_low, own=None):
    blocks, window, length = lag.shape[1:]
    edge = (window - length) // 2
    cols = const.shape[0]
    cuts = (0, edge, edge + length, window)
    flags = mask[0].astype(jnp.float32)
    for b in range(blocks):
        at = blocks * window + b * cols
        if own is not None:
            own[at : at + cols] = const[:, b * length : (b + 1) * length]
        for part in range(3):
            lo, hi = cuts[part], cuts[part + 1]
            rows = slice(b * window + lo, b * window + hi)
            high, low = halves(lag[0, b, lo:hi] * flags[b : b + 1, part : part + 1])
            value = triple(high, low, inv_high[b], inv_low[b])
            if own is not None:
                own[rows] = value
            near_high[rows], near_low[rows] = halves(value)


def edge_kernel(sides, blocks, cols, own, rim):
    length, edge = own.shape[1], rim.shape[2]
    window = length + 2 * edge

    def columns(last):
        b = blocks - 1 if last else 0
        cut = slice(length - edge, length) if last else slice(0, edge)
        at = blocks * window + b * cols
        return jnp.concatenate([own[b * window : (b + 1) * window, cut], own[at : at + cols, cut]])

    put_rim(sides, rim, columns)


def split_kernel(far, far_high, far_low):
    far_high[...], far_low[...] = halves(far[: far_high.shape[0]])


def cuts_of(blocks, length, sites, span, last):
    packed, cuts = 0, []
    for b in range(blocks):
        start = span // 2 - length // 2 - b * length
        lo, hi = (start + sites, span) if last else (0, start)
        cuts.append((lo, hi, packed))
        packed += hi - lo
    return cuts


def pair_kernel(first, jump, *refs):
    here = lax.axis_index("tm") == 2 * first[0]
    pl.when(here if first[1] else jnp.logical_not(here))(lambda: make_pair(jump, *refs))


def make_pair(jump, far, rim, far_high, far_low, near_high, near_low, const, high, low, both, *rest):
    cols, sites = const.shape
    length = far.shape[1]
    blocks = sites // length
    window = near_high.shape[0] // blocks
    edge = (window - length) // 2
    span = 2 * window
    tall = blocks * window
    total = rest[-1]
    if rim.shape[0] == 1:
        flag = jnp.minimum(lax.axis_index("row"), 1).astype(jnp.float32)
        left, right = rim[0] * flag, rim[0] * (1 - flag)
    else:
        left, right = rim[0], rim[1]
    left_pair, right_pair = halves(left[:window]), halves(right[:window])
    for b in range(blocks):
        here = slice(b * window, (b + 1) * window)
        column = slice(b * length, (b + 1) * length)

        def part(lo, hi):
            rows = slice(b * window + lo, b * window + hi)
            return near_high[rows], near_low[rows]

        def constant(block):
            if block < 0:
                return left[window:]
            if block == blocks:
                return right[window:]
            return far[tall + block * cols : tall + (block + 1) * cols]

        if b > 0:
            before = slice((b - 1) * window, b * window)
            low_pair = far_high[before, length - edge :], far_low[before, length - edge :]
            low_const = constant(b - 1)[:, length - edge :]
        else:
            low_pair, low_const = left_pair, constant(-1)
        if b + 1 < blocks:
            after = slice((b + 1) * window, (b + 2) * window)
            high_pair = far_high[after, :edge], far_low[after, :edge]
            high_const = constant(b + 1)[:, :edge]
        else:
            high_pair, high_const = right_pair, constant(blocks)
        first = triple(*low_pair, *part(0, edge))
        middle = triple(far_high[here], far_low[here], *part(edge, edge + length))
        last = triple(*high_pair, *part(edge + length, window))
        total[:window] = first
        total[window:] = last
        total[length : length + window] += middle
        high[b * span : (b + 1) * span], low[b * span : (b + 1) * span] = halves(total[...])
        both[:, column] = const[:, column] - (
            triple(*halves(low_const), *part(0, edge))
            + triple(*halves(constant(b)), *part(edge, edge + length))
            + triple(*halves(high_const), *part(edge + length, window))
        )
    if jump:
        own_rows, other_rows = rest[:2]

        def value(start, count):
            rows = pl.ds(start, count)
            return high[rows].astype(jnp.float32) + low[rows].astype(jnp.float32)

        for b in range(blocks):
            own_rows[b * sites : (b + 1) * sites] = value(b * span + window - edge - b * length, sites)
            at = blocks * sites + b * cols
            own_rows[at : at + cols] = both[:, b * length : (b + 1) * length]
        starts = [
            [b * span + at for b, (lo, hi, _) in enumerate(cuts_of(blocks, length, sites, span, last)) for at in range(lo, hi, edge)]
            for last in (True, False)
        ]
        row = lax.axis_index("row")
        for chunk, (on_right, on_left) in enumerate(zip(*starts)):
            start = pl.multiple_of(jnp.where(row == 0, on_right, on_left), edge)
            other_rows[chunk * edge : (chunk + 1) * edge] = value(start, edge)


def keep(ref, start, value):
    cols, width = value.shape
    high, low = halves(value)
    ref[:cols, pl.ds(start, width)] = high
    ref[cols:, pl.ds(start, width)] = low


def load(sides, pick, own, halo, ref):
    sites = own.shape[1]
    keep(ref, halo, own)
    for side in range(sides):
        on_right = 1 - jnp.minimum(lax.axis_index("row"), 1).astype(jnp.int32) if sides == 1 else side
        start = pl.multiple_of((1 - on_right) * (sites - halo), 128)
        keep(ref, pl.multiple_of(on_right * (halo + sites), 128), pick(side, pl.ds(start, halo)))


def plain(next_in):
    return lambda side, cut: next_in[:, cut] if len(next_in.shape) == 2 else next_in[side, :, cut]


def top_kernel(mine, sides, next_in, own_in, const, near_high, near_low, _upper, _lower, upper, lower, mid):
    sites = lower.shape[1]
    length = near_high.shape[1]
    blocks = sites // length
    window = near_high.shape[0] // blocks
    edge = (window - length) // 2

    @pl.when(lax.axis_index("tm") == 2 * mine)
    def _():
        mid[...] = jnp.zeros_like(mid)
        load(sides, plain(next_in), own_in[...], edge, mid)
        upper[...] = own_in[...]
        for b in range(blocks):
            at, rows = slice(b * length, (b + 1) * length), slice(b * window, (b + 1) * window)
            product = stacked_dot(mid, slice(b * length, b * length + window), near_high[rows], near_low[rows])
            lower[:, at] = const[:, at] - product


def step(both, high, low, late, lower):
    blocks = lower.shape[1] // high.shape[1]
    length, span = high.shape[1], high.shape[0] // blocks
    for b in range(blocks):
        at, rows = slice(b * length, (b + 1) * length), slice(b * span, (b + 1) * span)
        lower[:, at] = both[:, at] + stacked_dot(late, slice(b * length, b * length + span), high[rows], low[rows])


def load_rims(sides, next_in, sites, halo, late):
    for side in range(sides):
        on_right = 1 - jnp.minimum(lax.axis_index("row"), 1).astype(jnp.int32) if sides == 1 else side
        start = pl.multiple_of((1 - on_right) * (sites - halo), 128)
        keep(late, pl.multiple_of(on_right * (halo + sites), 128), plain(next_in)(side, pl.ds(start, halo)))


def rim_kernel(mine, sides, next_in, both, high, low, _late, late, base):
    sites, length = base.shape[1], high.shape[1]
    blocks = sites // length
    span = high.shape[0] // blocks
    halo = (late.shape[1] - sites) // 2
    edge = halo - length

    @pl.when(lax.axis_index("tm") == 2 * mine)
    def _():
        load_rims(sides, next_in, sites, halo, late)
        cuts = [cuts_of(blocks, length, sites, span, last) for last in (False, True)]
        for b in range(blocks):
            value = both[:, b * length : (b + 1) * length]
            if sides == 2:
                for lo, hi, _ in (cuts[0][b], cuts[1][b]):
                    rows = slice(b * span + lo, b * span + hi)
                    value += stacked_dot(late, slice(b * length + lo, b * length + hi), high[rows], low[rows])
            else:
                on_left = lax.axis_index("row") != 0
                counts = [cut[b][1] - cut[b][0] for cut in cuts]
                for chunk in range(0, max(counts), edge):
                    starts = [cut[b][0] + chunk if chunk < count else 0 for cut, count in zip(cuts, counts)]
                    start = pl.multiple_of(jnp.where(on_left, starts[0], starts[1]), edge)
                    rows = pl.ds(b * span + start, edge)
                    product = stacked_dot(late, pl.ds(b * length + start, edge), high[rows], low[rows])
                    if chunk >= min(counts):
                        product = jnp.where(on_left == (counts[0] > counts[1]), product, 0.0)
                    value += product
            base[:, b * length : (b + 1) * length] = value


def add_own(own_in, base, high, low, late, lower):
    sites, length = lower.shape[1], high.shape[1]
    blocks = sites // length
    span = high.shape[0] // blocks
    halo = (late.shape[1] - sites) // 2
    keep(late, halo, own_in[...])
    for b in range(blocks):
        at, start = slice(b * length, (b + 1) * length), halo - b * length
        rows = slice(b * span + start, b * span + start + sites)
        lower[:, at] = base[:, at] + stacked_dot(late, slice(halo, halo + sites), high[rows], low[rows])


def chain_kernel(mine, own_in, base, high, low, _late, _lower, late, lower):
    pl.when(lax.axis_index("tm") == 2 * mine)(lambda: add_own(own_in, base, high, low, late, lower))


def rows_kernel(own_rows, other_rows, own_high, own_low, other_high, other_low):
    own_high[...], own_low[...] = halves(own_rows[: own_high.shape[0]])
    other_high[...], other_low[...] = halves(other_rows[...])


def add_parts(lower, own_rows, own_high, own_low, other_high, other_low, to_next, to_own, mid, far_mid, span):
    cols, sites = lower.shape
    length = own_rows.shape[1]
    blocks = sites // length
    halo = to_own.shape[1] - sites
    edge = halo - length
    row = lax.axis_index("row")
    keep(mid, 0, lower[...])
    near = pl.multiple_of(jnp.where(row == 0, sites - halo, 0), edge)
    for b in range(blocks):
        at, rows = slice(b * length, (b + 1) * length), slice(b * sites, (b + 1) * sites)
        const = slice(blocks * sites + b * cols, blocks * sites + (b + 1) * cols)
        to_own[:, at] = own_rows[const] + stacked_dot(mid, slice(0, sites), own_high[rows], own_low[rows])
    to_next[:, :halo] = to_own[:, pl.ds(near, halo)]
    pieces = []
    for rows, from_last, from_first in (
        (slice(0, edge), sites - halo, 0),
        (slice(edge, halo), sites - length, 0),
        (slice(halo, halo + edge), sites - edge, length),
    ):
        source = pl.multiple_of(jnp.where(row == 0, from_last, from_first), edge)
        pieces.append(stacked_dot(mid, pl.ds(source, rows.stop - rows.start), other_high[rows], other_low[rows]))
    far_mid[:, :length] = pieces[0] + jnp.where(row == 0, pieces[1], 0.0)
    far_mid[:, length:] = pieces[2] + jnp.where(row == 0, 0.0, pieces[1])
    to_next[:, halo:] = far_mid[...]
    away = pl.multiple_of(jnp.where(row == 0, 0, sites - halo), edge)
    to_own[:, sites:] = far_mid[:, pl.ds(away, halo)]


def jump_kernel(mine, own_in, base, high, low, *rest):
    ship, (_late, _lower, late, lower, to_next, to_own, to_last, *scratch) = rest[:-9], rest[-9:]

    @pl.when(lax.axis_index("tm") == 2 * mine)
    def _():
        add_own(own_in, base, high, low, late, lower)
        add_parts(lower, *ship, to_next, to_own, *scratch, high.shape[0] * high.shape[1] // own_in.shape[1])
        to_last[...] = to_next[...]

    @pl.when(lax.axis_index("tm") != 2 * mine)
    def _():
        for part in (to_next, to_own, to_last):
            part[...] = jnp.zeros_like(part)


def parts_kernel(mine, span, lower, *rest):
    ship, parts = rest[:-4], rest[-4:]

    @pl.when(lax.axis_index("tm") == 2 * mine)
    def _():
        add_parts(lower, *ship, *parts, span)

    @pl.when(lax.axis_index("tm") != 2 * mine)
    def _():
        for part in parts[:2]:
            part[...] = jnp.zeros_like(part)


def last_kernel(jumps, both, high, low, late, _lower, lower):
    device = lax.axis_index("tm")
    pl.when((device == 0) | (device == 2) if jumps else device == 0)(lambda: step(both, high, low, late, lower))


def upper_kernel(sides, top, *rest):
    far, far_high, far_low, _late, _upper, late, upper = rest[-7:]
    cols, sites = upper.shape
    length = far.shape[1]
    blocks = sites // length
    window = far_high.shape[0] // blocks
    halo = (late.shape[1] - sites) // 2
    at_window = halo - (window - length) // 2
    messages = rest[:-7]

    if len(messages) == 2:

        @pl.when(lax.axis_index("tm") == 0)
        def _():
            load(sides, plain(messages[1]), messages[0][...], halo, late)

    sums = ((messages[0], messages[2], messages[1]), messages[3:]) if len(messages) > 2 else ()
    for mine, (*next_in, own_in) in enumerate(sums):

        @pl.when(lax.axis_index("tm") == 2 * mine)
        def _():
            from_next = next_in[0][...] + next_in[1][...] if len(next_in) == 2 else next_in[0][...]
            own = own_in[:, :sites] + from_next[:, halo:]
            near = own_in[:, sites:] + from_next[:, :halo]
            load(sides, lambda side, cut: near, own, halo, late)

    @pl.when(lax.axis_index("tm") != 2 * top)
    def _():
        for b in range(blocks):
            rows = slice(b * window, (b + 1) * window)
            at = blocks * window + b * cols
            start = at_window + b * length
            upper[:, b * length : (b + 1) * length] = far[at : at + cols] - stacked_dot(
                late, slice(start, start + window), far_high[rows], far_low[rows]
            )


def local(normals, inv_diag, lag_coupling, fill_mask):
    times, rows = lax.axis_size("tm"), lax.axis_size("row")
    device = lax.axis_index("tm")
    cols, sites = normals.shape[1:]
    blocks, length = inv_diag.shape[1:3]
    window = lag_coupling.shape[2]
    edge = (window - length) // 2
    halo = length + edge
    sides = 1 if rows == 2 else 2
    pairs = times // 2
    f32, bf16 = jnp.float32, jnp.bfloat16
    shape = jax.ShapeDtypeStruct

    def link(source, target):
        return [(s * rows + r, t * rows + r) for s, t in zip(source, target) for r in range(rows)]

    def cross(value, source, target, split=False):
        if sides == 1:
            perm = [(s * rows + r, t * rows + 1 - r) for s, t in zip(source, target) for r in range(2)]
            return lax.ppermute(value, BOTH, perm)
        moved = []
        for side, step in enumerate((1, -1)):
            perm = [
                (s * rows + r, t * rows + r + step)
                for s, t in zip(source, target)
                for r in range(rows)
                if 0 <= r + step < rows
            ]
            moved.append(lax.ppermute(value[side : side + 1] if split else value[None], BOTH, perm))
        return jnp.concatenate(moved)

    tall = blocks * window
    jump = 2
    jumps = rows == 2 and pairs > 5 and blocks == 2
    const, inv_high, inv_low = pl.pallas_call(
        const_kernel,
        out_shape=(
            shape((cols, sites), f32),
            shape((blocks, length, length), bf16), shape((blocks, length, length), bf16),
        ),
        in_specs=[HBM] * 2,
        out_specs=(VMEM,) * 3,
        scratch_shapes=[
            pltpu.VMEM(normals.shape[1:], f32),
            pltpu.VMEM(inv_diag.shape[1:], f32),
            pltpu.SemaphoreType.DMA((1 + blocks,)),
        ],
        compiler_params=PARAMS,
    )(*[pltpu.with_memory_space_constraint(a, pltpu.HBM) for a in (normals, inv_diag)])
    again = pl.pallas_call(
        again_kernel,
        out_shape=shape((cols, sites), f32),
        in_specs=[VMEM],
        out_specs=VMEM,
        compiler_params=PARAMS,
        cost_estimate=pl.CostEstimate(flops=5 * 10**9, bytes_accessed=0, transcendentals=0),
    )(const)
    odd, even = range(1, times, 2), range(0, times, 2)
    first_next = cross(again, odd[-1:], even[-1:])
    first_own = lax.ppermute(const, BOTH, link(odd[-1:], even[-1:]))

    def fused(late, extra, after=()):
        return pl.pallas_call(
            functools.partial(fuse_kernel, (2 * pairs - 4, late)),
            out_shape=(shape((tall, length), bf16), shape((tall, length), bf16), *extra),
            in_specs=[VMEM] * (5 + len(after)),
            out_specs=(VMEM,) * (2 + len(extra)),
            compiler_params=PARAMS,
            cost_estimate=pl.CostEstimate(
                flops=6 * (tall + cols * blocks) * length * length, bytes_accessed=16 * tall * length, transcendentals=0
            ),
        )(fill_mask, const, inv_high, inv_low, lag_coupling, *after)

    near_high, near_low, near = fused(False, (shape((tall + blocks * cols, length), f32),))
    edges = pl.pallas_call(
        functools.partial(edge_kernel, sides, blocks, cols),
        out_shape=shape((sides, window + cols, edge), f32),
        in_specs=[VMEM],
        out_specs=VMEM,
        compiler_params=PARAMS,
    )(near)
    near = pl.pallas_call(
        lambda _own, _edges, own: None,
        out_shape=shape(near.shape, f32),
        in_specs=[VMEM] * 2,
        out_specs=VMEM,
        input_output_aliases={0: 0},
        compiler_params=PARAMS,
    )(near, edges)
    rim = cross(edges, odd[:-1], even[:-1], True)
    far = lax.ppermute(near, BOTH, link(odd[:-1], even[:-1]))

    blank = jnp.zeros((cols, sites), f32)
    upper, lower = pl.pallas_call(
        functools.partial(top_kernel, pairs - 1, sides),
        out_shape=(shape((cols, sites), f32),) * 2,
        in_specs=[VMEM] * 7,
        out_specs=(VMEM,) * 2,
        scratch_shapes=[pltpu.VMEM((2 * cols, sites + 2 * edge), bf16)],
        input_output_aliases={5: 0, 6: 1},
        compiler_params=PARAMS,
        cost_estimate=pl.CostEstimate(flops=50 * 10**9, bytes_accessed=0, transcendentals=0),
    )(first_next, first_own, const, near_high, near_low, blank, blank)
    far_high, far_low = pl.pallas_call(
        split_kernel,
        out_shape=(shape((tall, length), bf16), shape((tall, length), bf16)),
        in_specs=[VMEM],
        out_specs=(VMEM,) * 2,
        compiler_params=PARAMS,
    )(far)
    packs = (shape((blocks * (sites + cols), length), f32), shape((halo + edge, length), f32)) if jumps else ()

    def pair_matrix(first, jumps, packs, mine):
        return pl.pallas_call(
            functools.partial(pair_kernel, (pairs - 2, first), jumps),
            out_shape=(
                shape((2 * tall, length), bf16), shape((2 * tall, length), bf16), shape((cols, sites), f32), *packs
            ),
            in_specs=[VMEM] * 7,
            out_specs=(VMEM,) * (3 + len(packs)),
            scratch_shapes=[pltpu.VMEM((2 * window, length), f32)],
            compiler_params=PARAMS,
            cost_estimate=pl.CostEstimate(flops=10**9, bytes_accessed=0, transcendentals=0),
        )(far, rim, far_high, far_low, *mine, const)

    early = pair_matrix(True, False, (), fused(True, (), (lower,)))
    high, low, both, *packs = pair_matrix(False, jumps, packs, (near_high, near_low))
    if jumps:
        source, target = [2 * jump - 2, 2 * jump], [2 * jump, 2 * jump + 2]
        own_rows = lax.ppermute(packs[0], BOTH, link(source, target))
        other_rows = cross(packs[1], source, target)
        ship = pl.pallas_call(
            rows_kernel,
            out_shape=(shape((blocks * sites, length), bf16),) * 2 + (shape(other_rows.shape, bf16),) * 2,
            in_specs=[VMEM] * 2,
            out_specs=(VMEM,) * 4,
            compiler_params=PARAMS,
        )(own_rows, other_rows)

    def turn(kernel, given, state, scratch=(), extra=(), flops=0):
        return pl.pallas_call(
            kernel,
            out_shape=tuple(shape(v.shape, v.dtype) for v in state) + tuple(extra),
            in_specs=[VMEM] * (len(given) + len(state)),
            out_specs=(VMEM,) * (len(state) + len(extra)),
            scratch_shapes=list(scratch),
            input_output_aliases={len(given) + i: i for i in range(len(state))},
            compiler_params=PARAMS,
            cost_estimate=pl.CostEstimate(flops=flops, bytes_accessed=0, transcendentals=0) if flops else None,
        )(*given, *state)

    parts = (shape((cols, sites + halo), f32),) * 2
    parts_scratch = [pltpu.VMEM((2 * cols, sites), bf16), pltpu.VMEM((cols, sites), f32)]
    late = jnp.zeros((2 * cols, sites + 2 * halo), bf16)
    mine = pairs - 1
    while mine > 0:
        if jumps and mine == jump:
            source, target = [2 * mine], [2 * mine - 4]
            first_in = lax.ppermute(to_next, BOTH, [(2 * source[0] + 1, 2 * target[0])])
            own_in = lax.ppermute(to_own, BOTH, link(source, target))
            next_in = lax.ppermute(to_last, BOTH, [(2 * source[0], 2 * target[0] + 1)])
            break
        source, target = [2 * mine], [2 * mine - 2]
        next_in = cross(lower, source, target)
        own_in = lax.ppermute(lower, BOTH, link(source, target))
        if jumps and mine == jump + 1:
            beside = pl.pallas_call(
                functools.partial(parts_kernel, mine, 2 * window),
                out_shape=parts,
                in_specs=[VMEM] * 6,
                out_specs=(VMEM,) * 2,
                scratch_shapes=parts_scratch,
                compiler_params=PARAMS,
            )(lower, own_rows, *ship)
            source, target = [2 * mine], [2 * mine - 4]
            beside_next = cross(beside[0], source, target)
            beside_own = lax.ppermute(beside[1], BOTH, link(source, target))
        mine -= 1
        if mine == 0:
            break
        here = early if mine == pairs - 2 else (high, low, both)
        late, base = turn(
            functools.partial(rim_kernel, mine, sides),
            (next_in, here[2], *here[:2]),
            (late,),
            extra=[shape((cols, sites), f32)],
        )
        if jumps and mine == jump:
            late, lower, to_next, to_own, to_last = turn(
                functools.partial(jump_kernel, mine),
                (own_in, base, high, low, own_rows, *ship),
                (late, lower),
                parts_scratch,
                parts + parts[:1],
            )
        else:
            late, lower = turn(
                functools.partial(chain_kernel, mine),
                (own_in, base, *here[:2]),
                (late, lower),
                flops=50 * 10**9 if jumps and mine == pairs - 3 else 0,
            )
    given = (first_in, own_in, next_in, beside_next, beside_own) if jumps else (own_in, next_in)
    late, upper = turn(
        functools.partial(upper_kernel, sides, pairs - 1), (*given, far, far_high, far_low), (late, upper)
    )
    returned = lax.ppermute(upper, BOTH, link(even, odd))
    lower = pl.pallas_call(
        functools.partial(last_kernel, jumps),
        out_shape=shape(lower.shape, f32),
        in_specs=[VMEM] * 5,
        out_specs=VMEM,
        input_output_aliases={4: 0},
        compiler_params=PARAMS,
        cost_estimate=pl.CostEstimate(flops=12 * cols * tall * length, bytes_accessed=8 * tall * length, transcendentals=0),
    )(both, high, low, late, lower)
    return jnp.where(device % 2 == 0, lower, returned)[None]


def solution(mesh):
    placed = (
        P("tm", None, "row"),
        P("tm", "row", None, None),
        P("tm", "row", None, None),
        P("tm", "row", None),
    )
    return jax.shard_map(
        local, mesh=mesh, in_specs=placed, out_specs=P("tm", None, "row"), check_vma=False
    )
```

```python
import functools

import jax
import jax.numpy as jnp
from jax import lax
from jax.experimental import pallas as pl
from jax.experimental.pallas import tpu as pltpu
from jax.sharding import PartitionSpec as P

BOTH = ("tm", "row")
VMEM = pl.BlockSpec(memory_space=pltpu.VMEM)
HBM = pl.BlockSpec(memory_space=pltpu.HBM)
PARAMS = pltpu.CompilerParams(vmem_limit_bytes=32 * 1024 * 1024)


def halves(value):
    high = value.astype(jnp.bfloat16)
    low = (value - high.astype(jnp.float32)).astype(jnp.bfloat16)
    return high, low


def dot(a, b):
    return jnp.dot(a, b, preferred_element_type=jnp.float32)


def stacked_dot(pair, cols, high, low):
    rows = pair.shape[0] // 2
    wide = dot(pair[:, cols], high)
    return wide[:rows] + wide[rows:] + dot(pair[:rows, cols], low)


def triple(high, low, inv_high, inv_low):
    return dot(high, inv_high) + dot(low, inv_high) + dot(high, inv_low)


def put_rim(sides, rim, columns):
    if sides == 1:
        row = lax.axis_index("row")

        @pl.when(row == 0)
        def _():
            rim[0] = columns(True)

        @pl.when(row != 0)
        def _():
            rim[0] = columns(False)
    else:
        rim[0] = columns(True)
        rim[1] = columns(False)


def const_kernel(normals, inv, const, inv_high, inv_low, normals_in, inv_in, sems):
    blocks, length = inv.shape[1], inv.shape[2]
    moves = [pltpu.make_async_copy(normals.at[0], normals_in, sems.at[0])]
    for b in range(blocks):
        moves.append(pltpu.make_async_copy(inv.at[0, b], inv_in.at[b], sems.at[1 + b]))
    for move in moves:
        move.start()
    moves[0].wait()
    for b in range(blocks):
        at = slice(b * length, (b + 1) * length)
        high, low = halves(normals_in[:, at])
        moves[1 + b].wait()
        inv_high[b], inv_low[b] = halves(inv_in[b])
        const[:, at] = triple(high, low, inv_high[b], inv_low[b])


def copy_kernel(const, _after, copy):
    copy[...] = const[...]


def rim_of_kernel(sides, const, rim):
    edge, sites = rim.shape[2], const.shape[1]
    put_rim(sides, rim, lambda last: const[:, sites - edge :] if last else const[:, :edge])


def fuse_kernel(late, *refs):
    here = lax.axis_index("tm") == late[0]
    given = refs[:5] + refs[6:] if late[1] else refs
    pl.when(here if late[1] else jnp.logical_not(here))(lambda: make_fused(*given))


def make_fused(mask, const, inv_high, inv_low, lag, near_high, near_low, own=None):
    blocks, window, length = lag.shape[1:]
    edge = (window - length) // 2
    cols = const.shape[0]
    cuts = (0, edge, edge + length, window)
    flags = mask[0].astype(jnp.float32)
    for b in range(blocks):
        at = blocks * window + b * cols
        if own is not None:
            own[at : at + cols] = const[:, b * length : (b + 1) * length]
        for part in range(3):
            lo, hi = cuts[part], cuts[part + 1]
            rows = slice(b * window + lo, b * window + hi)
            high, low = halves(lag[0, b, lo:hi] * flags[b : b + 1, part : part + 1])
            value = triple(high, low, inv_high[b], inv_low[b])
            if own is not None:
                own[rows] = value
            near_high[rows], near_low[rows] = halves(value)


def edge_kernel(sides, blocks, cols, own, rim):
    length, edge = own.shape[1], rim.shape[2]
    window = length + 2 * edge

    def columns(last):
        b = blocks - 1 if last else 0
        cut = slice(length - edge, length) if last else slice(0, edge)
        at = blocks * window + b * cols
        return jnp.concatenate([own[b * window : (b + 1) * window, cut], own[at : at + cols, cut]])

    put_rim(sides, rim, columns)


def split_kernel(far, far_high, far_low):
    far_high[...], far_low[...] = halves(far[: far_high.shape[0]])


def cuts_of(blocks, length, sites, span, last):
    packed, cuts = 0, []
    for b in range(blocks):
        start = span // 2 - length // 2 - b * length
        lo, hi = (start + sites, span) if last else (0, start)
        cuts.append((lo, hi, packed))
        packed += hi - lo
    return cuts


def pair_kernel(first, jump, *refs):
    here = lax.axis_index("tm") == 2 * first[0]
    pl.when(here if first[1] else jnp.logical_not(here))(lambda: make_pair(jump, *refs))


def make_pair(jump, far, rim, far_high, far_low, near_high, near_low, const, high, low, both, *rest):
    cols, sites = const.shape
    length = far.shape[1]
    blocks = sites // length
    window = near_high.shape[0] // blocks
    edge = (window - length) // 2
    span = 2 * window
    tall = blocks * window
    total = rest[-1]
    if rim.shape[0] == 1:
        flag = jnp.minimum(lax.axis_index("row"), 1).astype(jnp.float32)
        left, right = rim[0] * flag, rim[0] * (1 - flag)
    else:
        left, right = rim[0], rim[1]
    left_pair, right_pair = halves(left[:window]), halves(right[:window])
    for b in range(blocks):
        here = slice(b * window, (b + 1) * window)
        column = slice(b * length, (b + 1) * length)

        def part(lo, hi):
            rows = slice(b * window + lo, b * window + hi)
            return near_high[rows], near_low[rows]

        def constant(block):
            if block < 0:
                return left[window:]
            if block == blocks:
                return right[window:]
            return far[tall + block * cols : tall + (block + 1) * cols]

        if b > 0:
            before = slice((b - 1) * window, b * window)
            low_pair = far_high[before, length - edge :], far_low[before, length - edge :]
            low_const = constant(b - 1)[:, length - edge :]
        else:
            low_pair, low_const = left_pair, constant(-1)
        if b + 1 < blocks:
            after = slice((b + 1) * window, (b + 2) * window)
            high_pair = far_high[after, :edge], far_low[after, :edge]
            high_const = constant(b + 1)[:, :edge]
        else:
            high_pair, high_const = right_pair, constant(blocks)
        first = triple(*low_pair, *part(0, edge))
        middle = triple(far_high[here], far_low[here], *part(edge, edge + length))
        last = triple(*high_pair, *part(edge + length, window))
        total[:window] = first
        total[window:] = last
        total[length : length + window] += middle
        high[b * span : (b + 1) * span], low[b * span : (b + 1) * span] = halves(total[...])
        both[:, column] = const[:, column] - (
            triple(*halves(low_const), *part(0, edge))
            + triple(*halves(constant(b)), *part(edge, edge + length))
            + triple(*halves(high_const), *part(edge + length, window))
        )
    if jump:
        own_rows, other_rows = rest[:2]

        def value(start, count):
            rows = pl.ds(start, count)
            return high[rows].astype(jnp.float32) + low[rows].astype(jnp.float32)

        for b in range(blocks):
            own_rows[b * sites : (b + 1) * sites] = value(b * span + window - edge - b * length, sites)
            at = blocks * sites + b * cols
            own_rows[at : at + cols] = both[:, b * length : (b + 1) * length]
        starts = [
            [b * span + at for b, (lo, hi, _) in enumerate(cuts_of(blocks, length, sites, span, last)) for at in range(lo, hi, edge)]
            for last in (True, False)
        ]
        row = lax.axis_index("row")
        for chunk, (on_right, on_left) in enumerate(zip(*starts)):
            start = pl.multiple_of(jnp.where(row == 0, on_right, on_left), edge)
            other_rows[chunk * edge : (chunk + 1) * edge] = value(start, edge)


def keep(ref, start, value):
    cols, width = value.shape
    high, low = halves(value)
    ref[:cols, pl.ds(start, width)] = high
    ref[cols:, pl.ds(start, width)] = low


def load(sides, pick, own, halo, ref):
    sites = own.shape[1]
    keep(ref, halo, own)
    for side in range(sides):
        on_right = 1 - jnp.minimum(lax.axis_index("row"), 1).astype(jnp.int32) if sides == 1 else side
        start = pl.multiple_of((1 - on_right) * (sites - halo), 128)
        keep(ref, pl.multiple_of(on_right * (halo + sites), 128), pick(side, pl.ds(start, halo)))


def plain(next_in):
    return lambda side, cut: next_in[:, cut] if len(next_in.shape) == 2 else next_in[side, :, cut]


def top_kernel(mine, sides, next_in, own_in, const, near_high, near_low, _upper, _lower, upper, lower, mid):
    sites = lower.shape[1]
    length = near_high.shape[1]
    blocks = sites // length
    window = near_high.shape[0] // blocks
    edge = (window - length) // 2

    @pl.when(lax.axis_index("tm") == 2 * mine)
    def _():
        mid[...] = jnp.zeros_like(mid)
        load(sides, lambda side, cut: next_in[side], own_in[...], edge, mid)
        upper[...] = own_in[...]
        for b in range(blocks):
            at, rows = slice(b * length, (b + 1) * length), slice(b * window, (b + 1) * window)
            product = stacked_dot(mid, slice(b * length, b * length + window), near_high[rows], near_low[rows])
            lower[:, at] = const[:, at] - product


def step(both, high, low, late, lower):
    blocks = lower.shape[1] // high.shape[1]
    length, span = high.shape[1], high.shape[0] // blocks
    for b in range(blocks):
        at, rows = slice(b * length, (b + 1) * length), slice(b * span, (b + 1) * span)
        lower[:, at] = both[:, at] + stacked_dot(late, slice(b * length, b * length + span), high[rows], low[rows])


def load_rims(sides, next_in, sites, halo, late):
    for side in range(sides):
        on_right = 1 - jnp.minimum(lax.axis_index("row"), 1).astype(jnp.int32) if sides == 1 else side
        start = pl.multiple_of((1 - on_right) * (sites - halo), 128)
        keep(late, pl.multiple_of(on_right * (halo + sites), 128), plain(next_in)(side, pl.ds(start, halo)))


def rim_kernel(mine, sides, next_in, both, high, low, _late, late, base):
    sites, length = base.shape[1], high.shape[1]
    blocks = sites // length
    span = high.shape[0] // blocks
    halo = (late.shape[1] - sites) // 2
    edge = halo - length

    @pl.when(lax.axis_index("tm") == 2 * mine)
    def _():
        load_rims(sides, next_in, sites, halo, late)
        cuts = [cuts_of(blocks, length, sites, span, last) for last in (False, True)]
        for b in range(blocks):
            value = both[:, b * length : (b + 1) * length]
            if sides == 2:
                for lo, hi, _ in (cuts[0][b], cuts[1][b]):
                    rows = slice(b * span + lo, b * span + hi)
                    value += stacked_dot(late, slice(b * length + lo, b * length + hi), high[rows], low[rows])
            else:
                on_left = lax.axis_index("row") != 0
                counts = [cut[b][1] - cut[b][0] for cut in cuts]
                for chunk in range(0, max(counts), edge):
                    starts = [cut[b][0] + chunk if chunk < count else 0 for cut, count in zip(cuts, counts)]
                    start = pl.multiple_of(jnp.where(on_left, starts[0], starts[1]), edge)
                    rows = pl.ds(b * span + start, edge)
                    product = stacked_dot(late, pl.ds(b * length + start, edge), high[rows], low[rows])
                    if chunk >= min(counts):
                        product = jnp.where(on_left == (counts[0] > counts[1]), product, 0.0)
                    value += product
            base[:, b * length : (b + 1) * length] = value


def add_own(own_in, base, high, low, late, lower):
    sites, length = lower.shape[1], high.shape[1]
    blocks = sites // length
    span = high.shape[0] // blocks
    halo = (late.shape[1] - sites) // 2
    keep(late, halo, own_in[...])
    for b in range(blocks):
        at, start = slice(b * length, (b + 1) * length), halo - b * length
        rows = slice(b * span + start, b * span + start + sites)
        lower[:, at] = base[:, at] + stacked_dot(late, slice(halo, halo + sites), high[rows], low[rows])


def chain_kernel(mine, own_in, base, high, low, _late, _lower, late, lower):
    pl.when(lax.axis_index("tm") == 2 * mine)(lambda: add_own(own_in, base, high, low, late, lower))


def rows_kernel(own_rows, other_rows, own_high, own_low, other_high, other_low):
    own_high[...], own_low[...] = halves(own_rows[: own_high.shape[0]])
    other_high[...], other_low[...] = halves(other_rows[...])


def add_parts(lower, own_rows, own_high, own_low, other_high, other_low, to_next, to_own, mid, far_mid, span):
    cols, sites = lower.shape
    length = own_rows.shape[1]
    blocks = sites // length
    halo = to_own.shape[1] - sites
    edge = halo - length
    row = lax.axis_index("row")
    keep(mid, 0, lower[...])
    near = pl.multiple_of(jnp.where(row == 0, sites - halo, 0), edge)
    for b in range(blocks):
        at, rows = slice(b * length, (b + 1) * length), slice(b * sites, (b + 1) * sites)
        const = slice(blocks * sites + b * cols, blocks * sites + (b + 1) * cols)
        to_own[:, at] = own_rows[const] + stacked_dot(mid, slice(0, sites), own_high[rows], own_low[rows])
    to_next[:, :halo] = to_own[:, pl.ds(near, halo)]
    pieces = []
    for rows, from_last, from_first in (
        (slice(0, edge), sites - halo, 0),
        (slice(edge, halo), sites - length, 0),
        (slice(halo, halo + edge), sites - edge, length),
    ):
        source = pl.multiple_of(jnp.where(row == 0, from_last, from_first), edge)
        pieces.append(stacked_dot(mid, pl.ds(source, rows.stop - rows.start), other_high[rows], other_low[rows]))
    far_mid[:, :length] = pieces[0] + jnp.where(row == 0, pieces[1], 0.0)
    far_mid[:, length:] = pieces[2] + jnp.where(row == 0, 0.0, pieces[1])
    to_next[:, halo:] = far_mid[...]
    away = pl.multiple_of(jnp.where(row == 0, 0, sites - halo), edge)
    to_own[:, sites:] = far_mid[:, pl.ds(away, halo)]


def jump_kernel(mine, own_in, base, high, low, *rest):
    ship, (_late, _lower, late, lower, to_next, to_own, to_last, *scratch) = rest[:-9], rest[-9:]

    @pl.when(lax.axis_index("tm") == 2 * mine)
    def _():
        add_own(own_in, base, high, low, late, lower)
        add_parts(lower, *ship, to_next, to_own, *scratch, high.shape[0] * high.shape[1] // own_in.shape[1])
        to_last[...] = to_next[...]

    @pl.when(lax.axis_index("tm") != 2 * mine)
    def _():
        for part in (to_next, to_own, to_last):
            part[...] = jnp.zeros_like(part)


def parts_kernel(mine, span, lower, *rest):
    ship, parts = rest[:-4], rest[-4:]

    @pl.when(lax.axis_index("tm") == 2 * mine)
    def _():
        add_parts(lower, *ship, *parts, span)

    @pl.when(lax.axis_index("tm") != 2 * mine)
    def _():
        for part in parts[:2]:
            part[...] = jnp.zeros_like(part)


def last_kernel(jumps, both, high, low, late, _lower, lower):
    device = lax.axis_index("tm")
    pl.when((device == 0) | (device == 2) if jumps else device == 0)(lambda: step(both, high, low, late, lower))


def upper_kernel(sides, top, *rest):
    far, far_high, far_low, _late, _upper, late, upper = rest[-7:]
    cols, sites = upper.shape
    length = far.shape[1]
    blocks = sites // length
    window = far_high.shape[0] // blocks
    halo = (late.shape[1] - sites) // 2
    at_window = halo - (window - length) // 2
    messages = rest[:-7]

    if len(messages) == 2:

        @pl.when(lax.axis_index("tm") == 0)
        def _():
            load(sides, plain(messages[1]), messages[0][...], halo, late)

    sums = ((messages[0], messages[2], messages[1]), messages[3:]) if len(messages) > 2 else ()
    for mine, (*next_in, own_in) in enumerate(sums):

        @pl.when(lax.axis_index("tm") == 2 * mine)
        def _():
            from_next = next_in[0][...] + next_in[1][...] if len(next_in) == 2 else next_in[0][...]
            own = own_in[:, :sites] + from_next[:, halo:]
            near = own_in[:, sites:] + from_next[:, :halo]
            load(sides, lambda side, cut: near, own, halo, late)

    @pl.when(lax.axis_index("tm") != 2 * top)
    def _():
        for b in range(blocks):
            rows = slice(b * window, (b + 1) * window)
            at = blocks * window + b * cols
            start = at_window + b * length
            upper[:, b * length : (b + 1) * length] = far[at : at + cols] - stacked_dot(
                late, slice(start, start + window), far_high[rows], far_low[rows]
            )


def local(normals, inv_diag, lag_coupling, fill_mask):
    times, rows = lax.axis_size("tm"), lax.axis_size("row")
    device = lax.axis_index("tm")
    cols, sites = normals.shape[1:]
    blocks, length = inv_diag.shape[1:3]
    window = lag_coupling.shape[2]
    edge = (window - length) // 2
    halo = length + edge
    sides = 1 if rows == 2 else 2
    pairs = times // 2
    f32, bf16 = jnp.float32, jnp.bfloat16
    shape = jax.ShapeDtypeStruct

    def link(source, target):
        return [(s * rows + r, t * rows + r) for s, t in zip(source, target) for r in range(rows)]

    def cross(value, source, target, split=False):
        if sides == 1:
            perm = [(s * rows + r, t * rows + 1 - r) for s, t in zip(source, target) for r in range(2)]
            return lax.ppermute(value, BOTH, perm)
        moved = []
        for side, step in enumerate((1, -1)):
            perm = [
                (s * rows + r, t * rows + r + step)
                for s, t in zip(source, target)
                for r in range(rows)
                if 0 <= r + step < rows
            ]
            moved.append(lax.ppermute(value[side : side + 1] if split else value[None], BOTH, perm))
        return jnp.concatenate(moved)

    tall = blocks * window
    jump = 2
    jumps = rows == 2 and pairs > 5 and blocks == 2
    const, inv_high, inv_low = pl.pallas_call(
        const_kernel,
        out_shape=(
            shape((cols, sites), f32),
            shape((blocks, length, length), bf16), shape((blocks, length, length), bf16),
        ),
        in_specs=[HBM] * 2,
        out_specs=(VMEM,) * 3,
        scratch_shapes=[
            pltpu.VMEM(normals.shape[1:], f32),
            pltpu.VMEM(inv_diag.shape[1:], f32),
            pltpu.SemaphoreType.DMA((1 + blocks,)),
        ],
        compiler_params=PARAMS,
    )(*[pltpu.with_memory_space_constraint(a, pltpu.HBM) for a in (normals, inv_diag)])
    const_rim = pl.pallas_call(
        functools.partial(rim_of_kernel, sides),
        out_shape=shape((sides, cols, edge), f32),
        in_specs=[VMEM],
        out_specs=VMEM,
        compiler_params=PARAMS,
        cost_estimate=pl.CostEstimate(flops=5 * 10**9, bytes_accessed=0, transcendentals=0),
    )(const)
    again = pl.pallas_call(
        copy_kernel,
        out_shape=shape((cols, sites), f32),
        in_specs=[VMEM] * 2,
        out_specs=VMEM,
        compiler_params=PARAMS,
    )(const, const_rim)
    odd, even = range(1, times, 2), range(0, times, 2)
    first_next = cross(const_rim, odd[-1:], even[-1:], True)
    first_own = lax.ppermute(again, BOTH, link(odd[-1:], even[-1:]))

    def fused(late, extra, after=()):
        return pl.pallas_call(
            functools.partial(fuse_kernel, (2 * pairs - 4, late)),
            out_shape=(shape((tall, length), bf16), shape((tall, length), bf16), *extra),
            in_specs=[VMEM] * (5 + len(after)),
            out_specs=(VMEM,) * (2 + len(extra)),
            compiler_params=PARAMS,
            cost_estimate=pl.CostEstimate(
                flops=(6 if late else 150) * (tall + cols * blocks) * length * length, bytes_accessed=0, transcendentals=0
            ),
        )(fill_mask, const, inv_high, inv_low, lag_coupling, *after)

    near_high, near_low, near = fused(False, (shape((tall + blocks * cols, length), f32),))
    edges = pl.pallas_call(
        functools.partial(edge_kernel, sides, blocks, cols),
        out_shape=shape((sides, window + cols, edge), f32),
        in_specs=[VMEM],
        out_specs=VMEM,
        compiler_params=PARAMS,
    )(near)
    near = pl.pallas_call(
        lambda _own, _edges, own: None,
        out_shape=shape(near.shape, f32),
        in_specs=[VMEM] * 2,
        out_specs=VMEM,
        input_output_aliases={0: 0},
        compiler_params=PARAMS,
    )(near, edges)
    rim = cross(edges, odd[:-1], even[:-1], True)
    far = lax.ppermute(near, BOTH, link(odd[:-1], even[:-1]))

    blank = jnp.zeros((cols, sites), f32)
    upper, lower = pl.pallas_call(
        functools.partial(top_kernel, pairs - 1, sides),
        out_shape=(shape((cols, sites), f32),) * 2,
        in_specs=[VMEM] * 7,
        out_specs=(VMEM,) * 2,
        scratch_shapes=[pltpu.VMEM((2 * cols, sites + 2 * edge), bf16)],
        input_output_aliases={5: 0, 6: 1},
        compiler_params=PARAMS,
        cost_estimate=pl.CostEstimate(flops=50 * 10**9, bytes_accessed=0, transcendentals=0),
    )(first_next, first_own, const, near_high, near_low, blank, blank)
    far_high, far_low = pl.pallas_call(
        split_kernel,
        out_shape=(shape((tall, length), bf16), shape((tall, length), bf16)),
        in_specs=[VMEM],
        out_specs=(VMEM,) * 2,
        compiler_params=PARAMS,
    )(far)
    packs = (shape((blocks * (sites + cols), length), f32), shape((halo + edge, length), f32)) if jumps else ()

    def pair_matrix(first, jumps, packs, mine):
        return pl.pallas_call(
            functools.partial(pair_kernel, (pairs - 2, first), jumps),
            out_shape=(
                shape((2 * tall, length), bf16), shape((2 * tall, length), bf16), shape((cols, sites), f32), *packs
            ),
            in_specs=[VMEM] * 7,
            out_specs=(VMEM,) * (3 + len(packs)),
            scratch_shapes=[pltpu.VMEM((2 * window, length), f32)],
            compiler_params=PARAMS,
            cost_estimate=pl.CostEstimate(flops=10**9, bytes_accessed=0, transcendentals=0),
        )(far, rim, far_high, far_low, *mine, const)

    early = pair_matrix(True, False, (), fused(True, (), (lower,)))
    high, low, both, *packs = pair_matrix(False, jumps, packs, (near_high, near_low))
    if jumps:
        source, target = [2 * jump - 2, 2 * jump], [2 * jump, 2 * jump + 2]
        own_rows = lax.ppermute(packs[0], BOTH, link(source, target))
        other_rows = cross(packs[1], source, target)
        ship = pl.pallas_call(
            rows_kernel,
            out_shape=(shape((blocks * sites, length), bf16),) * 2 + (shape(other_rows.shape, bf16),) * 2,
            in_specs=[VMEM] * 2,
            out_specs=(VMEM,) * 4,
            compiler_params=PARAMS,
        )(own_rows, other_rows)

    def turn(kernel, given, state, scratch=(), extra=(), flops=0):
        return pl.pallas_call(
            kernel,
            out_shape=tuple(shape(v.shape, v.dtype) for v in state) + tuple(extra),
            in_specs=[VMEM] * (len(given) + len(state)),
            out_specs=(VMEM,) * (len(state) + len(extra)),
            scratch_shapes=list(scratch),
            input_output_aliases={len(given) + i: i for i in range(len(state))},
            compiler_params=PARAMS,
            cost_estimate=pl.CostEstimate(flops=flops, bytes_accessed=0, transcendentals=0) if flops else None,
        )(*given, *state)

    parts = (shape((cols, sites + halo), f32),) * 2
    parts_scratch = [pltpu.VMEM((2 * cols, sites), bf16), pltpu.VMEM((cols, sites), f32)]
    late = jnp.zeros((2 * cols, sites + 2 * halo), bf16)
    mine = pairs - 1
    while mine > 0:
        if jumps and mine == jump:
            source, target = [2 * mine], [2 * mine - 4]
            first_in = lax.ppermute(to_next, BOTH, [(2 * source[0] + 1, 2 * target[0])])
            own_in = lax.ppermute(to_own, BOTH, link(source, target))
            next_in = lax.ppermute(to_last, BOTH, [(2 * source[0], 2 * target[0] + 1)])
            break
        source, target = [2 * mine], [2 * mine - 2]
        next_in = cross(lower, source, target)
        own_in = lax.ppermute(lower, BOTH, link(source, target))
        if jumps and mine == jump + 1:
            beside = pl.pallas_call(
                functools.partial(parts_kernel, mine, 2 * window),
                out_shape=parts,
                in_specs=[VMEM] * 6,
                out_specs=(VMEM,) * 2,
                scratch_shapes=parts_scratch,
                compiler_params=PARAMS,
            )(lower, own_rows, *ship)
            source, target = [2 * mine], [2 * mine - 4]
            beside_next = cross(beside[0], source, target)
            beside_own = lax.ppermute(beside[1], BOTH, link(source, target))
        mine -= 1
        if mine == 0:
            break
        here = early if mine == pairs - 2 else (high, low, both)
        late, base = turn(
            functools.partial(rim_kernel, mine, sides),
            (next_in, here[2], *here[:2]),
            (late,),
            extra=[shape((cols, sites), f32)],
        )
        if jumps and mine == jump:
            late, lower, to_next, to_own, to_last = turn(
                functools.partial(jump_kernel, mine),
                (own_in, base, high, low, own_rows, *ship),
                (late, lower),
                parts_scratch,
                parts + parts[:1],
            )
        else:
            late, lower = turn(
                functools.partial(chain_kernel, mine),
                (own_in, base, *here[:2]),
                (late, lower),
                flops=50 * 10**9 if jumps and mine == pairs - 3 else 0,
            )
    given = (first_in, own_in, next_in, beside_next, beside_own) if jumps else (own_in, next_in)
    late, upper = turn(
        functools.partial(upper_kernel, sides, pairs - 1), (*given, far, far_high, far_low), (late, upper)
    )
    returned = lax.ppermute(upper, BOTH, link(even, odd))
    lower = pl.pallas_call(
        functools.partial(last_kernel, jumps),
        out_shape=shape(lower.shape, f32),
        in_specs=[VMEM] * 5,
        out_specs=VMEM,
        input_output_aliases={4: 0},
        compiler_params=PARAMS,
        cost_estimate=pl.CostEstimate(flops=12 * cols * tall * length, bytes_accessed=8 * tall * length, transcendentals=0),
    )(both, high, low, late, lower)
    return jnp.where(device % 2 == 0, lower, returned)[None]


def solution(mesh):
    placed = (
        P("tm", None, "row"),
        P("tm", "row", None, None),
        P("tm", "row", None, None),
        P("tm", "row", None),
    )
    return jax.shard_map(
        local, mesh=mesh, in_specs=placed, out_specs=P("tm", None, "row"), check_vma=False
    )
```

```python
import functools

import jax
import jax.numpy as jnp
from jax import lax
from jax.experimental import pallas as pl
from jax.experimental.pallas import tpu as pltpu
from jax.sharding import PartitionSpec as P

BOTH = ("tm", "row")
VMEM = pl.BlockSpec(memory_space=pltpu.VMEM)
HBM = pl.BlockSpec(memory_space=pltpu.HBM)
PARAMS = pltpu.CompilerParams(vmem_limit_bytes=32 * 1024 * 1024)


def halves(value):
    high = value.astype(jnp.bfloat16)
    low = (value - high.astype(jnp.float32)).astype(jnp.bfloat16)
    return high, low


def dot(a, b):
    return jnp.dot(a, b, preferred_element_type=jnp.float32)


def stacked_dot(pair, cols, high, low):
    rows = pair.shape[0] // 2
    wide = dot(pair[:, cols], high)
    return wide[:rows] + wide[rows:] + dot(pair[:rows, cols], low)


def triple(high, low, inv_high, inv_low):
    return dot(high, inv_high) + dot(low, inv_high) + dot(high, inv_low)


def put_rim(sides, rim, columns):
    if sides == 1:
        row = lax.axis_index("row")

        @pl.when(row == 0)
        def _():
            rim[0] = columns(True)

        @pl.when(row != 0)
        def _():
            rim[0] = columns(False)
    else:
        rim[0] = columns(True)
        rim[1] = columns(False)


def const_kernel(which, normals, inv, *refs):
    device = lax.axis_index("tm")
    late = device == which[1]
    odd = device % 2 == 1
    active = {"odd": odd, "even": jnp.logical_not(odd | late), "late": late}[which[0]]
    pl.when(active)(lambda: make_const(normals, inv, *refs[-6:]))


def make_const(normals, inv, const, inv_high, inv_low, normals_in, inv_in, sems):
    blocks, length = inv.shape[1], inv.shape[2]
    moves = [pltpu.make_async_copy(normals.at[0], normals_in, sems.at[0])]
    for b in range(blocks):
        moves.append(pltpu.make_async_copy(inv.at[0, b], inv_in.at[b], sems.at[1 + b]))
    for move in moves:
        move.start()
    moves[0].wait()
    for b in range(blocks):
        at = slice(b * length, (b + 1) * length)
        high, low = halves(normals_in[:, at])
        moves[1 + b].wait()
        inv_high[b], inv_low[b] = halves(inv_in[b])
        const[:, at] = triple(high, low, inv_high[b], inv_low[b])


def copy_kernel(const, _after, copy):
    copy[...] = const[...]


def rim_of_kernel(sides, const, rim):
    edge, sites = rim.shape[2], const.shape[1]
    put_rim(sides, rim, lambda last: const[:, sites - edge :] if last else const[:, :edge])


def fuse_kernel(late, *refs):
    here = lax.axis_index("tm") == late[0]
    pl.when(here if late[1] else jnp.logical_not(here))(lambda: make_fused(*refs))


def make_fused(mask, const, inv_high, inv_low, lag, near_high, near_low, own=None):
    blocks, window, length = lag.shape[1:]
    edge = (window - length) // 2
    cols = const.shape[0]
    cuts = (0, edge, edge + length, window)
    flags = mask[0].astype(jnp.float32)
    for b in range(blocks):
        at = blocks * window + b * cols
        if own is not None:
            own[at : at + cols] = const[:, b * length : (b + 1) * length]
        for part in range(3):
            lo, hi = cuts[part], cuts[part + 1]
            rows = slice(b * window + lo, b * window + hi)
            high, low = halves(lag[0, b, lo:hi] * flags[b : b + 1, part : part + 1])
            value = triple(high, low, inv_high[b], inv_low[b])
            if own is not None:
                own[rows] = value
            near_high[rows], near_low[rows] = halves(value)


def edge_kernel(sides, blocks, cols, own, rim):
    length, edge = own.shape[1], rim.shape[2]
    window = length + 2 * edge

    def columns(last):
        b = blocks - 1 if last else 0
        cut = slice(length - edge, length) if last else slice(0, edge)
        at = blocks * window + b * cols
        return jnp.concatenate([own[b * window : (b + 1) * window, cut], own[at : at + cols, cut]])

    put_rim(sides, rim, columns)


def split_kernel(far, far_high, far_low):
    far_high[...], far_low[...] = halves(far[: far_high.shape[0]])


def cuts_of(blocks, length, sites, span, last):
    packed, cuts = 0, []
    for b in range(blocks):
        start = span // 2 - length // 2 - b * length
        lo, hi = (start + sites, span) if last else (0, start)
        cuts.append((lo, hi, packed))
        packed += hi - lo
    return cuts


def pair_kernel(first, jump, *refs):
    here = lax.axis_index("tm") == 2 * first[0]
    pl.when(here if first[1] else jnp.logical_not(here))(lambda: make_pair(jump, *refs))


def make_pair(jump, far, rim, far_high, far_low, near_high, near_low, const, high, low, both, *rest):
    cols, sites = const.shape
    length = far.shape[1]
    blocks = sites // length
    window = near_high.shape[0] // blocks
    edge = (window - length) // 2
    span = 2 * window
    tall = blocks * window
    total = rest[-1]
    if rim.shape[0] == 1:
        flag = jnp.minimum(lax.axis_index("row"), 1).astype(jnp.float32)
        left, right = rim[0] * flag, rim[0] * (1 - flag)
    else:
        left, right = rim[0], rim[1]
    left_pair, right_pair = halves(left[:window]), halves(right[:window])
    for b in range(blocks):
        here = slice(b * window, (b + 1) * window)
        column = slice(b * length, (b + 1) * length)

        def part(lo, hi):
            rows = slice(b * window + lo, b * window + hi)
            return near_high[rows], near_low[rows]

        def constant(block):
            if block < 0:
                return left[window:]
            if block == blocks:
                return right[window:]
            return far[tall + block * cols : tall + (block + 1) * cols]

        if b > 0:
            before = slice((b - 1) * window, b * window)
            low_pair = far_high[before, length - edge :], far_low[before, length - edge :]
            low_const = constant(b - 1)[:, length - edge :]
        else:
            low_pair, low_const = left_pair, constant(-1)
        if b + 1 < blocks:
            after = slice((b + 1) * window, (b + 2) * window)
            high_pair = far_high[after, :edge], far_low[after, :edge]
            high_const = constant(b + 1)[:, :edge]
        else:
            high_pair, high_const = right_pair, constant(blocks)
        first = triple(*low_pair, *part(0, edge))
        middle = triple(far_high[here], far_low[here], *part(edge, edge + length))
        last = triple(*high_pair, *part(edge + length, window))
        total[:window] = first
        total[window:] = last
        total[length : length + window] += middle
        high[b * span : (b + 1) * span], low[b * span : (b + 1) * span] = halves(total[...])
        both[:, column] = const[:, column] - (
            triple(*halves(low_const), *part(0, edge))
            + triple(*halves(constant(b)), *part(edge, edge + length))
            + triple(*halves(high_const), *part(edge + length, window))
        )
    if jump:
        own_rows, other_rows = rest[:2]

        def value(start, count):
            rows = pl.ds(start, count)
            return high[rows].astype(jnp.float32) + low[rows].astype(jnp.float32)

        for b in range(blocks):
            own_rows[b * sites : (b + 1) * sites] = value(b * span + window - edge - b * length, sites)
            at = blocks * sites + b * cols
            own_rows[at : at + cols] = both[:, b * length : (b + 1) * length]
        starts = [
            [b * span + at for b, (lo, hi, _) in enumerate(cuts_of(blocks, length, sites, span, last)) for at in range(lo, hi, edge)]
            for last in (True, False)
        ]
        row = lax.axis_index("row")
        for chunk, (on_right, on_left) in enumerate(zip(*starts)):
            start = pl.multiple_of(jnp.where(row == 0, on_right, on_left), edge)
            other_rows[chunk * edge : (chunk + 1) * edge] = value(start, edge)


def keep(ref, start, value):
    cols, width = value.shape
    high, low = halves(value)
    ref[:cols, pl.ds(start, width)] = high
    ref[cols:, pl.ds(start, width)] = low


def load(sides, pick, own, halo, ref):
    sites = own.shape[1]
    keep(ref, halo, own)
    for side in range(sides):
        on_right = 1 - jnp.minimum(lax.axis_index("row"), 1).astype(jnp.int32) if sides == 1 else side
        start = pl.multiple_of((1 - on_right) * (sites - halo), 128)
        keep(ref, pl.multiple_of(on_right * (halo + sites), 128), pick(side, pl.ds(start, halo)))


def plain(next_in):
    return lambda side, cut: next_in[:, cut] if len(next_in.shape) == 2 else next_in[side, :, cut]


def top_kernel(mine, sides, next_in, own_in, const, near_high, near_low, _upper, _lower, upper, lower, mid):
    sites = lower.shape[1]
    length = near_high.shape[1]
    blocks = sites // length
    window = near_high.shape[0] // blocks
    edge = (window - length) // 2

    @pl.when(lax.axis_index("tm") == 2 * mine)
    def _():
        mid[...] = jnp.zeros_like(mid)
        load(sides, lambda side, cut: next_in[side], own_in[...], edge, mid)
        upper[...] = own_in[...]
        for b in range(blocks):
            at, rows = slice(b * length, (b + 1) * length), slice(b * window, (b + 1) * window)
            product = stacked_dot(mid, slice(b * length, b * length + window), near_high[rows], near_low[rows])
            lower[:, at] = const[:, at] - product


def step(both, high, low, late, lower):
    blocks = lower.shape[1] // high.shape[1]
    length, span = high.shape[1], high.shape[0] // blocks
    for b in range(blocks):
        at, rows = slice(b * length, (b + 1) * length), slice(b * span, (b + 1) * span)
        lower[:, at] = both[:, at] + stacked_dot(late, slice(b * length, b * length + span), high[rows], low[rows])


def load_rims(sides, next_in, sites, halo, late):
    for side in range(sides):
        on_right = 1 - jnp.minimum(lax.axis_index("row"), 1).astype(jnp.int32) if sides == 1 else side
        start = pl.multiple_of((1 - on_right) * (sites - halo), 128)
        keep(late, pl.multiple_of(on_right * (halo + sites), 128), plain(next_in)(side, pl.ds(start, halo)))


def rim_kernel(mine, sides, next_in, both, high, low, _late, late, base):
    sites, length = base.shape[1], high.shape[1]
    blocks = sites // length
    span = high.shape[0] // blocks
    halo = (late.shape[1] - sites) // 2
    edge = halo - length

    @pl.when(lax.axis_index("tm") == 2 * mine)
    def _():
        load_rims(sides, next_in, sites, halo, late)
        cuts = [cuts_of(blocks, length, sites, span, last) for last in (False, True)]
        for b in range(blocks):
            value = both[:, b * length : (b + 1) * length]
            if sides == 2:
                for lo, hi, _ in (cuts[0][b], cuts[1][b]):
                    rows = slice(b * span + lo, b * span + hi)
                    value += stacked_dot(late, slice(b * length + lo, b * length + hi), high[rows], low[rows])
            else:
                on_left = lax.axis_index("row") != 0
                counts = [cut[b][1] - cut[b][0] for cut in cuts]
                for chunk in range(0, max(counts), edge):
                    starts = [cut[b][0] + chunk if chunk < count else 0 for cut, count in zip(cuts, counts)]
                    start = pl.multiple_of(jnp.where(on_left, starts[0], starts[1]), edge)
                    rows = pl.ds(b * span + start, edge)
                    product = stacked_dot(late, pl.ds(b * length + start, edge), high[rows], low[rows])
                    if chunk >= min(counts):
                        product = jnp.where(on_left == (counts[0] > counts[1]), product, 0.0)
                    value += product
            base[:, b * length : (b + 1) * length] = value


def add_own(own_in, base, high, low, late, lower):
    sites, length = lower.shape[1], high.shape[1]
    blocks = sites // length
    span = high.shape[0] // blocks
    halo = (late.shape[1] - sites) // 2
    keep(late, halo, own_in[...])
    for b in range(blocks):
        at, start = slice(b * length, (b + 1) * length), halo - b * length
        rows = slice(b * span + start, b * span + start + sites)
        lower[:, at] = base[:, at] + stacked_dot(late, slice(halo, halo + sites), high[rows], low[rows])


def chain_kernel(mine, own_in, base, high, low, _late, _lower, late, lower):
    pl.when(lax.axis_index("tm") == 2 * mine)(lambda: add_own(own_in, base, high, low, late, lower))


def rows_kernel(own_rows, other_rows, own_high, own_low, other_high, other_low):
    own_high[...], own_low[...] = halves(own_rows[: own_high.shape[0]])
    other_high[...], other_low[...] = halves(other_rows[...])


def add_parts(lower, own_rows, own_high, own_low, other_high, other_low, to_next, to_own, mid, far_mid, span):
    cols, sites = lower.shape
    length = own_rows.shape[1]
    blocks = sites // length
    halo = to_own.shape[1] - sites
    edge = halo - length
    row = lax.axis_index("row")
    keep(mid, 0, lower[...])
    near = pl.multiple_of(jnp.where(row == 0, sites - halo, 0), edge)
    for b in range(blocks):
        at, rows = slice(b * length, (b + 1) * length), slice(b * sites, (b + 1) * sites)
        const = slice(blocks * sites + b * cols, blocks * sites + (b + 1) * cols)
        to_own[:, at] = own_rows[const] + stacked_dot(mid, slice(0, sites), own_high[rows], own_low[rows])
    to_next[:, :halo] = to_own[:, pl.ds(near, halo)]
    pieces = []
    for rows, from_last, from_first in (
        (slice(0, edge), sites - halo, 0),
        (slice(edge, halo), sites - length, 0),
        (slice(halo, halo + edge), sites - edge, length),
    ):
        source = pl.multiple_of(jnp.where(row == 0, from_last, from_first), edge)
        pieces.append(stacked_dot(mid, pl.ds(source, rows.stop - rows.start), other_high[rows], other_low[rows]))
    far_mid[:, :length] = pieces[0] + jnp.where(row == 0, pieces[1], 0.0)
    far_mid[:, length:] = pieces[2] + jnp.where(row == 0, 0.0, pieces[1])
    to_next[:, halo:] = far_mid[...]
    away = pl.multiple_of(jnp.where(row == 0, 0, sites - halo), edge)
    to_own[:, sites:] = far_mid[:, pl.ds(away, halo)]


def jump_kernel(mine, own_in, base, high, low, *rest):
    ship, (_late, _lower, late, lower, to_next, to_own, to_last, *scratch) = rest[:-9], rest[-9:]

    @pl.when(lax.axis_index("tm") == 2 * mine)
    def _():
        add_own(own_in, base, high, low, late, lower)
        add_parts(lower, *ship, to_next, to_own, *scratch, high.shape[0] * high.shape[1] // own_in.shape[1])
        to_last[...] = to_next[...]

    @pl.when(lax.axis_index("tm") != 2 * mine)
    def _():
        for part in (to_next, to_own, to_last):
            part[...] = jnp.zeros_like(part)


def parts_kernel(mine, span, lower, *rest):
    ship, parts = rest[:-4], rest[-4:]

    @pl.when(lax.axis_index("tm") == 2 * mine)
    def _():
        add_parts(lower, *ship, *parts, span)

    @pl.when(lax.axis_index("tm") != 2 * mine)
    def _():
        for part in parts[:2]:
            part[...] = jnp.zeros_like(part)


def last_kernel(jumps, both, high, low, late, _lower, lower):
    device = lax.axis_index("tm")
    pl.when((device == 0) | (device == 2) if jumps else device == 0)(lambda: step(both, high, low, late, lower))


def upper_kernel(sides, top, *rest):
    far, far_high, far_low, _late, _upper, late, upper = rest[-7:]
    cols, sites = upper.shape
    length = far.shape[1]
    blocks = sites // length
    window = far_high.shape[0] // blocks
    halo = (late.shape[1] - sites) // 2
    at_window = halo - (window - length) // 2
    messages = rest[:-7]

    if len(messages) == 2:

        @pl.when(lax.axis_index("tm") == 0)
        def _():
            load(sides, plain(messages[1]), messages[0][...], halo, late)

    sums = ((messages[0], messages[2], messages[1]), messages[3:]) if len(messages) > 2 else ()
    for mine, (*next_in, own_in) in enumerate(sums):

        @pl.when(lax.axis_index("tm") == 2 * mine)
        def _():
            from_next = next_in[0][...] + next_in[1][...] if len(next_in) == 2 else next_in[0][...]
            own = own_in[:, :sites] + from_next[:, halo:]
            near = own_in[:, sites:] + from_next[:, :halo]
            load(sides, lambda side, cut: near, own, halo, late)

    @pl.when(lax.axis_index("tm") != 2 * top)
    def _():
        for b in range(blocks):
            rows = slice(b * window, (b + 1) * window)
            at = blocks * window + b * cols
            start = at_window + b * length
            upper[:, b * length : (b + 1) * length] = far[at : at + cols] - stacked_dot(
                late, slice(start, start + window), far_high[rows], far_low[rows]
            )


def local(normals, inv_diag, lag_coupling, fill_mask):
    times, rows = lax.axis_size("tm"), lax.axis_size("row")
    device = lax.axis_index("tm")
    cols, sites = normals.shape[1:]
    blocks, length = inv_diag.shape[1:3]
    window = lag_coupling.shape[2]
    edge = (window - length) // 2
    halo = length + edge
    sides = 1 if rows == 2 else 2
    pairs = times // 2
    f32, bf16 = jnp.float32, jnp.bfloat16
    shape = jax.ShapeDtypeStruct

    def link(source, target):
        return [(s * rows + r, t * rows + r) for s, t in zip(source, target) for r in range(rows)]

    def cross(value, source, target, split=False):
        if sides == 1:
            perm = [(s * rows + r, t * rows + 1 - r) for s, t in zip(source, target) for r in range(2)]
            return lax.ppermute(value, BOTH, perm)
        moved = []
        for side, step in enumerate((1, -1)):
            perm = [
                (s * rows + r, t * rows + r + step)
                for s, t in zip(source, target)
                for r in range(rows)
                if 0 <= r + step < rows
            ]
            moved.append(lax.ppermute(value[side : side + 1] if split else value[None], BOTH, perm))
        return jnp.concatenate(moved)

    tall = blocks * window
    jump = 2
    jumps = rows == 2 and pairs > 5 and blocks == 2

    def consts(which, alias=(), after=()):
        return pl.pallas_call(
            functools.partial(const_kernel, (which, 2 * pairs - 4)),
            out_shape=(
                shape((cols, sites), f32),
                shape((blocks, length, length), bf16), shape((blocks, length, length), bf16),
            ),
            in_specs=[HBM] * 2 + [VMEM] * (len(alias) + len(after)),
            out_specs=(VMEM,) * 3,
            scratch_shapes=[
                pltpu.VMEM(normals.shape[1:], f32),
                pltpu.VMEM(inv_diag.shape[1:], f32),
                pltpu.SemaphoreType.DMA((1 + blocks,)),
            ],
            input_output_aliases={2 + i: i for i in range(len(alias))},
            compiler_params=PARAMS,
            cost_estimate=pl.CostEstimate(flops=10**9 if which == "late" else 0, bytes_accessed=0, transcendentals=0),
        )(*[pltpu.with_memory_space_constraint(a, pltpu.HBM) for a in (normals, inv_diag)], *alias, *after)

    odd_parts = consts("odd")
    const = odd_parts[0]
    const_rim = pl.pallas_call(
        functools.partial(rim_of_kernel, sides),
        out_shape=shape((sides, cols, edge), f32),
        in_specs=[VMEM],
        out_specs=VMEM,
        compiler_params=PARAMS,
        cost_estimate=pl.CostEstimate(flops=5 * 10**9, bytes_accessed=0, transcendentals=0),
    )(const)
    again = pl.pallas_call(
        copy_kernel,
        out_shape=shape((cols, sites), f32),
        in_specs=[VMEM] * 2,
        out_specs=VMEM,
        compiler_params=PARAMS,
    )(const, const_rim)
    odd, even = range(1, times, 2), range(0, times, 2)
    first_next = cross(const_rim, odd[-1:], even[-1:], True)
    first_own = lax.ppermute(again, BOTH, link(odd[-1:], even[-1:]))

    const, inv_high, inv_low = consts("even", odd_parts, (const_rim, again))

    def fused(late, extra, const, inv_high, inv_low):
        return pl.pallas_call(
            functools.partial(fuse_kernel, (2 * pairs - 4, late)),
            out_shape=(shape((tall, length), bf16), shape((tall, length), bf16), *extra),
            in_specs=[VMEM] * 5,
            out_specs=(VMEM,) * (2 + len(extra)),
            compiler_params=PARAMS,
            cost_estimate=pl.CostEstimate(
                flops=(6 if late else 150) * (tall + cols * blocks) * length * length, bytes_accessed=0, transcendentals=0
            ),
        )(fill_mask, const, inv_high, inv_low, lag_coupling)

    near_high, near_low, near = fused(False, (shape((tall + blocks * cols, length), f32),), const, inv_high, inv_low)
    edges = pl.pallas_call(
        functools.partial(edge_kernel, sides, blocks, cols),
        out_shape=shape((sides, window + cols, edge), f32),
        in_specs=[VMEM],
        out_specs=VMEM,
        compiler_params=PARAMS,
    )(near)
    near = pl.pallas_call(
        lambda _own, _edges, own: None,
        out_shape=shape(near.shape, f32),
        in_specs=[VMEM] * 2,
        out_specs=VMEM,
        input_output_aliases={0: 0},
        compiler_params=PARAMS,
    )(near, edges)
    rim = cross(edges, odd[:-1], even[:-1], True)
    far = lax.ppermute(near, BOTH, link(odd[:-1], even[:-1]))

    blank = jnp.zeros((cols, sites), f32)
    upper, lower = pl.pallas_call(
        functools.partial(top_kernel, pairs - 1, sides),
        out_shape=(shape((cols, sites), f32),) * 2,
        in_specs=[VMEM] * 7,
        out_specs=(VMEM,) * 2,
        scratch_shapes=[pltpu.VMEM((2 * cols, sites + 2 * edge), bf16)],
        input_output_aliases={5: 0, 6: 1},
        compiler_params=PARAMS,
        cost_estimate=pl.CostEstimate(flops=50 * 10**9, bytes_accessed=0, transcendentals=0),
    )(first_next, first_own, const, near_high, near_low, blank, blank)
    far_high, far_low = pl.pallas_call(
        split_kernel,
        out_shape=(shape((tall, length), bf16), shape((tall, length), bf16)),
        in_specs=[VMEM],
        out_specs=(VMEM,) * 2,
        compiler_params=PARAMS,
    )(far)
    packs = (shape((blocks * (sites + cols), length), f32), shape((halo + edge, length), f32)) if jumps else ()

    def pair_matrix(first, jumps, packs, mine, const):
        return pl.pallas_call(
            functools.partial(pair_kernel, (pairs - 2, first), jumps),
            out_shape=(
                shape((2 * tall, length), bf16), shape((2 * tall, length), bf16), shape((cols, sites), f32), *packs
            ),
            in_specs=[VMEM] * 7,
            out_specs=(VMEM,) * (3 + len(packs)),
            scratch_shapes=[pltpu.VMEM((2 * window, length), f32)],
            compiler_params=PARAMS,
            cost_estimate=pl.CostEstimate(flops=10**9, bytes_accessed=0, transcendentals=0),
        )(far, rim, far_high, far_low, *mine, const)

    late_parts = consts("late", (), (lower,))
    early = pair_matrix(True, False, (), fused(True, (), *late_parts), late_parts[0])
    high, low, both, *packs = pair_matrix(False, jumps, packs, (near_high, near_low), const)
    if jumps:
        source, target = [2 * jump - 2, 2 * jump], [2 * jump, 2 * jump + 2]
        own_rows = lax.ppermute(packs[0], BOTH, link(source, target))
        other_rows = cross(packs[1], source, target)
        ship = pl.pallas_call(
            rows_kernel,
            out_shape=(shape((blocks * sites, length), bf16),) * 2 + (shape(other_rows.shape, bf16),) * 2,
            in_specs=[VMEM] * 2,
            out_specs=(VMEM,) * 4,
            compiler_params=PARAMS,
        )(own_rows, other_rows)

    def turn(kernel, given, state, scratch=(), extra=(), flops=0):
        return pl.pallas_call(
            kernel,
            out_shape=tuple(shape(v.shape, v.dtype) for v in state) + tuple(extra),
            in_specs=[VMEM] * (len(given) + len(state)),
            out_specs=(VMEM,) * (len(state) + len(extra)),
            scratch_shapes=list(scratch),
            input_output_aliases={len(given) + i: i for i in range(len(state))},
            compiler_params=PARAMS,
            cost_estimate=pl.CostEstimate(flops=flops, bytes_accessed=0, transcendentals=0) if flops else None,
        )(*given, *state)

    parts = (shape((cols, sites + halo), f32),) * 2
    parts_scratch = [pltpu.VMEM((2 * cols, sites), bf16), pltpu.VMEM((cols, sites), f32)]
    late = jnp.zeros((2 * cols, sites + 2 * halo), bf16)
    mine = pairs - 1
    while mine > 0:
        if jumps and mine == jump:
            source, target = [2 * mine], [2 * mine - 4]
            first_in = lax.ppermute(to_next, BOTH, [(2 * source[0] + 1, 2 * target[0])])
            own_in = lax.ppermute(to_own, BOTH, link(source, target))
            next_in = lax.ppermute(to_last, BOTH, [(2 * source[0], 2 * target[0] + 1)])
            break
        source, target = [2 * mine], [2 * mine - 2]
        next_in = cross(lower, source, target)
        own_in = lax.ppermute(lower, BOTH, link(source, target))
        if jumps and mine == jump + 1:
            beside = pl.pallas_call(
                functools.partial(parts_kernel, mine, 2 * window),
                out_shape=parts,
                in_specs=[VMEM] * 6,
                out_specs=(VMEM,) * 2,
                scratch_shapes=parts_scratch,
                compiler_params=PARAMS,
            )(lower, own_rows, *ship)
            source, target = [2 * mine], [2 * mine - 4]
            beside_next = cross(beside[0], source, target)
            beside_own = lax.ppermute(beside[1], BOTH, link(source, target))
        mine -= 1
        if mine == 0:
            break
        here = early if mine == pairs - 2 else (high, low, both)
        late, base = turn(
            functools.partial(rim_kernel, mine, sides),
            (next_in, here[2], *here[:2]),
            (late,),
            extra=[shape((cols, sites), f32)],
        )
        if jumps and mine == jump:
            late, lower, to_next, to_own, to_last = turn(
                functools.partial(jump_kernel, mine),
                (own_in, base, high, low, own_rows, *ship),
                (late, lower),
                parts_scratch,
                parts + parts[:1],
            )
        else:
            late, lower = turn(
                functools.partial(chain_kernel, mine),
                (own_in, base, *here[:2]),
                (late, lower),
                flops=50 * 10**9 if jumps and mine == pairs - 3 else 0,
            )
    given = (first_in, own_in, next_in, beside_next, beside_own) if jumps else (own_in, next_in)
    late, upper = turn(
        functools.partial(upper_kernel, sides, pairs - 1), (*given, far, far_high, far_low), (late, upper)
    )
    returned = lax.ppermute(upper, BOTH, link(even, odd))
    lower = pl.pallas_call(
        functools.partial(last_kernel, jumps),
        out_shape=shape(lower.shape, f32),
        in_specs=[VMEM] * 5,
        out_specs=VMEM,
        input_output_aliases={4: 0},
        compiler_params=PARAMS,
        cost_estimate=pl.CostEstimate(flops=12 * cols * tall * length, bytes_accessed=8 * tall * length, transcendentals=0),
    )(both, high, low, late, lower)
    return jnp.where(device % 2 == 0, lower, returned)[None]


def solution(mesh):
    placed = (
        P("tm", None, "row"),
        P("tm", "row", None, None),
        P("tm", "row", None, None),
        P("tm", "row", None),
    )
    return jax.shard_map(
        local, mesh=mesh, in_specs=placed, out_specs=P("tm", None, "row"), check_vma=False
    )
```

```python
import functools

import jax
import jax.numpy as jnp
from jax import lax
from jax.experimental import pallas as pl
from jax.experimental.pallas import tpu as pltpu
from jax.sharding import PartitionSpec as P

BOTH = ("tm", "row")
VMEM = pl.BlockSpec(memory_space=pltpu.VMEM)
HBM = pl.BlockSpec(memory_space=pltpu.HBM)
PARAMS = pltpu.CompilerParams(vmem_limit_bytes=32 * 1024 * 1024)


def halves(value):
    high = value.astype(jnp.bfloat16)
    low = (value - high.astype(jnp.float32)).astype(jnp.bfloat16)
    return high, low


def dot(a, b):
    return jnp.dot(a, b, preferred_element_type=jnp.float32)


def stacked_dot(pair, cols, high, low):
    rows = pair.shape[0] // 2
    wide = dot(pair[:, cols], high)
    return wide[:rows] + wide[rows:] + dot(pair[:rows, cols], low)


def triple(high, low, inv_high, inv_low):
    return dot(high, inv_high) + dot(low, inv_high) + dot(high, inv_low)


def put_rim(sides, rim, columns):
    if sides == 1:
        row = lax.axis_index("row")

        @pl.when(row == 0)
        def _():
            rim[0] = columns(True)

        @pl.when(row != 0)
        def _():
            rim[0] = columns(False)
    else:
        rim[0] = columns(True)
        rim[1] = columns(False)


def const_kernel(which, normals, inv, *refs):
    device = lax.axis_index("tm")
    late = device == which[1]
    odd = device % 2 == 1
    active = {"odd": odd, "even": jnp.logical_not(odd | late), "late": late}[which[0]]
    pl.when(active)(lambda: make_const(normals, inv, *refs[-6:]))


def make_const(normals, inv, const, inv_high, inv_low, normals_in, inv_in, sems):
    blocks, length = inv.shape[1], inv.shape[2]
    moves = [pltpu.make_async_copy(normals.at[0], normals_in, sems.at[0])]
    for b in range(blocks):
        moves.append(pltpu.make_async_copy(inv.at[0, b], inv_in.at[b], sems.at[1 + b]))
    for move in moves:
        move.start()
    moves[0].wait()
    for b in range(blocks):
        at = slice(b * length, (b + 1) * length)
        high, low = halves(normals_in[:, at])
        moves[1 + b].wait()
        inv_high[b], inv_low[b] = halves(inv_in[b])
        const[:, at] = triple(high, low, inv_high[b], inv_low[b])


def copy_kernel(const, _after, copy):
    copy[...] = const[...]


def rim_of_kernel(sides, const, rim):
    edge, sites = rim.shape[2], const.shape[1]
    put_rim(sides, rim, lambda last: const[:, sites - edge :] if last else const[:, :edge])


def fuse_kernel(late, *refs):
    here = lax.axis_index("tm") == late[0]
    pl.when(here if late[1] else jnp.logical_not(here))(lambda: make_fused(*refs))


def make_fused(mask, const, inv_high, inv_low, lag, near_high, near_low, own=None):
    blocks, window, length = lag.shape[1:]
    edge = (window - length) // 2
    cols = const.shape[0]
    cuts = (0, edge, edge + length, window)
    flags = mask[0].astype(jnp.float32)
    for b in range(blocks):
        at = blocks * window + b * cols
        if own is not None:
            own[at : at + cols] = const[:, b * length : (b + 1) * length]
        for part in range(3):
            lo, hi = cuts[part], cuts[part + 1]
            rows = slice(b * window + lo, b * window + hi)
            high, low = halves(lag[0, b, lo:hi] * flags[b : b + 1, part : part + 1])
            value = triple(high, low, inv_high[b], inv_low[b])
            if own is not None:
                own[rows] = value
            near_high[rows], near_low[rows] = halves(value)


def edge_kernel(sides, blocks, cols, own, rim):
    length, edge = own.shape[1], rim.shape[2]
    window = length + 2 * edge

    def columns(last):
        b = blocks - 1 if last else 0
        cut = slice(length - edge, length) if last else slice(0, edge)
        at = blocks * window + b * cols
        return jnp.concatenate([own[b * window : (b + 1) * window, cut], own[at : at + cols, cut]])

    put_rim(sides, rim, columns)


def merge_kernel(apart, far_in, rim_in, _far, _rim, _far_high, _far_low, far, rim, far_high, far_low):
    @pl.when(lax.axis_index("tm") == apart)
    def _():
        far[...] = far_in[...]
        rim[...] = rim_in[...]
        far_high[...], far_low[...] = halves(far_in[: far_high.shape[0]])


def pass_kernel(source, near_in, edges_in, _after, near, edges):
    @pl.when(lax.axis_index("tm") == source)
    def _():
        near[...] = near_in[...]
        edges[...] = edges_in[...]


def split_kernel(far, far_high, far_low):
    far_high[...], far_low[...] = halves(far[: far_high.shape[0]])


def cuts_of(blocks, length, sites, span, last):
    packed, cuts = 0, []
    for b in range(blocks):
        start = span // 2 - length // 2 - b * length
        lo, hi = (start + sites, span) if last else (0, start)
        cuts.append((lo, hi, packed))
        packed += hi - lo
    return cuts


def pair_kernel(first, jump, *refs):
    here = lax.axis_index("tm") == 2 * first[0]
    pl.when(here if first[1] else jnp.logical_not(here))(lambda: make_pair(jump, *refs))


def make_pair(jump, far, rim, far_high, far_low, near_high, near_low, const, high, low, both, *rest):
    cols, sites = const.shape
    length = far.shape[1]
    blocks = sites // length
    window = near_high.shape[0] // blocks
    edge = (window - length) // 2
    span = 2 * window
    tall = blocks * window
    total = rest[-1]
    if rim.shape[0] == 1:
        flag = jnp.minimum(lax.axis_index("row"), 1).astype(jnp.float32)
        left, right = rim[0] * flag, rim[0] * (1 - flag)
    else:
        left, right = rim[0], rim[1]
    left_pair, right_pair = halves(left[:window]), halves(right[:window])
    for b in range(blocks):
        here = slice(b * window, (b + 1) * window)
        column = slice(b * length, (b + 1) * length)

        def part(lo, hi):
            rows = slice(b * window + lo, b * window + hi)
            return near_high[rows], near_low[rows]

        def constant(block):
            if block < 0:
                return left[window:]
            if block == blocks:
                return right[window:]
            return far[tall + block * cols : tall + (block + 1) * cols]

        if b > 0:
            before = slice((b - 1) * window, b * window)
            low_pair = far_high[before, length - edge :], far_low[before, length - edge :]
            low_const = constant(b - 1)[:, length - edge :]
        else:
            low_pair, low_const = left_pair, constant(-1)
        if b + 1 < blocks:
            after = slice((b + 1) * window, (b + 2) * window)
            high_pair = far_high[after, :edge], far_low[after, :edge]
            high_const = constant(b + 1)[:, :edge]
        else:
            high_pair, high_const = right_pair, constant(blocks)
        first = triple(*low_pair, *part(0, edge))
        middle = triple(far_high[here], far_low[here], *part(edge, edge + length))
        last = triple(*high_pair, *part(edge + length, window))
        total[:window] = first
        total[window:] = last
        total[length : length + window] += middle
        high[b * span : (b + 1) * span], low[b * span : (b + 1) * span] = halves(total[...])
        both[:, column] = const[:, column] - (
            triple(*halves(low_const), *part(0, edge))
            + triple(*halves(constant(b)), *part(edge, edge + length))
            + triple(*halves(high_const), *part(edge + length, window))
        )
    if jump:
        own_rows, other_rows = rest[:2]

        def value(start, count):
            rows = pl.ds(start, count)
            return high[rows].astype(jnp.float32) + low[rows].astype(jnp.float32)

        for b in range(blocks):
            own_rows[b * sites : (b + 1) * sites] = value(b * span + window - edge - b * length, sites)
            at = blocks * sites + b * cols
            own_rows[at : at + cols] = both[:, b * length : (b + 1) * length]
        starts = [
            [b * span + at for b, (lo, hi, _) in enumerate(cuts_of(blocks, length, sites, span, last)) for at in range(lo, hi, edge)]
            for last in (True, False)
        ]
        row = lax.axis_index("row")
        for chunk, (on_right, on_left) in enumerate(zip(*starts)):
            start = pl.multiple_of(jnp.where(row == 0, on_right, on_left), edge)
            other_rows[chunk * edge : (chunk + 1) * edge] = value(start, edge)


def keep(ref, start, value):
    cols, width = value.shape
    high, low = halves(value)
    ref[:cols, pl.ds(start, width)] = high
    ref[cols:, pl.ds(start, width)] = low


def load(sides, pick, own, halo, ref):
    sites = own.shape[1]
    keep(ref, halo, own)
    for side in range(sides):
        on_right = 1 - jnp.minimum(lax.axis_index("row"), 1).astype(jnp.int32) if sides == 1 else side
        start = pl.multiple_of((1 - on_right) * (sites - halo), 128)
        keep(ref, pl.multiple_of(on_right * (halo + sites), 128), pick(side, pl.ds(start, halo)))


def plain(next_in):
    return lambda side, cut: next_in[:, cut] if len(next_in.shape) == 2 else next_in[side, :, cut]


def top_kernel(mine, sides, next_in, own_in, const, near_high, near_low, _upper, _lower, upper, lower, mid):
    sites = lower.shape[1]
    length = near_high.shape[1]
    blocks = sites // length
    window = near_high.shape[0] // blocks
    edge = (window - length) // 2

    @pl.when(lax.axis_index("tm") == 2 * mine)
    def _():
        mid[...] = jnp.zeros_like(mid)
        load(sides, lambda side, cut: next_in[side], own_in[...], edge, mid)
        upper[...] = own_in[...]
        for b in range(blocks):
            at, rows = slice(b * length, (b + 1) * length), slice(b * window, (b + 1) * window)
            product = stacked_dot(mid, slice(b * length, b * length + window), near_high[rows], near_low[rows])
            lower[:, at] = const[:, at] - product


def step(both, high, low, late, lower):
    blocks = lower.shape[1] // high.shape[1]
    length, span = high.shape[1], high.shape[0] // blocks
    for b in range(blocks):
        at, rows = slice(b * length, (b + 1) * length), slice(b * span, (b + 1) * span)
        lower[:, at] = both[:, at] + stacked_dot(late, slice(b * length, b * length + span), high[rows], low[rows])


def load_rims(sides, next_in, sites, halo, late):
    for side in range(sides):
        on_right = 1 - jnp.minimum(lax.axis_index("row"), 1).astype(jnp.int32) if sides == 1 else side
        start = pl.multiple_of((1 - on_right) * (sites - halo), 128)
        keep(late, pl.multiple_of(on_right * (halo + sites), 128), plain(next_in)(side, pl.ds(start, halo)))


def rim_kernel(mine, sides, next_in, both, high, low, _late, late, base):
    sites, length = base.shape[1], high.shape[1]
    blocks = sites // length
    span = high.shape[0] // blocks
    halo = (late.shape[1] - sites) // 2
    edge = halo - length

    @pl.when(lax.axis_index("tm") == 2 * mine)
    def _():
        load_rims(sides, next_in, sites, halo, late)
        cuts = [cuts_of(blocks, length, sites, span, last) for last in (False, True)]
        for b in range(blocks):
            value = both[:, b * length : (b + 1) * length]
            if sides == 2:
                for lo, hi, _ in (cuts[0][b], cuts[1][b]):
                    rows = slice(b * span + lo, b * span + hi)
                    value += stacked_dot(late, slice(b * length + lo, b * length + hi), high[rows], low[rows])
            else:
                on_left = lax.axis_index("row") != 0
                counts = [cut[b][1] - cut[b][0] for cut in cuts]
                for chunk in range(0, max(counts), edge):
                    starts = [cut[b][0] + chunk if chunk < count else 0 for cut, count in zip(cuts, counts)]
                    start = pl.multiple_of(jnp.where(on_left, starts[0], starts[1]), edge)
                    rows = pl.ds(b * span + start, edge)
                    product = stacked_dot(late, pl.ds(b * length + start, edge), high[rows], low[rows])
                    if chunk >= min(counts):
                        product = jnp.where(on_left == (counts[0] > counts[1]), product, 0.0)
                    value += product
            base[:, b * length : (b + 1) * length] = value


def add_own(own_in, base, high, low, late, lower):
    sites, length = lower.shape[1], high.shape[1]
    blocks = sites // length
    span = high.shape[0] // blocks
    halo = (late.shape[1] - sites) // 2
    keep(late, halo, own_in[...])
    for b in range(blocks):
        at, start = slice(b * length, (b + 1) * length), halo - b * length
        rows = slice(b * span + start, b * span + start + sites)
        lower[:, at] = base[:, at] + stacked_dot(late, slice(halo, halo + sites), high[rows], low[rows])


def chain_kernel(mine, own_in, base, high, low, _late, _lower, late, lower):
    pl.when(lax.axis_index("tm") == 2 * mine)(lambda: add_own(own_in, base, high, low, late, lower))


def rows_kernel(own_rows, other_rows, own_high, own_low, other_high, other_low):
    own_high[...], own_low[...] = halves(own_rows[: own_high.shape[0]])
    other_high[...], other_low[...] = halves(other_rows[...])


def add_parts(lower, own_rows, own_high, own_low, other_high, other_low, to_next, to_own, mid, far_mid, span):
    cols, sites = lower.shape
    length = own_rows.shape[1]
    blocks = sites // length
    halo = to_own.shape[1] - sites
    edge = halo - length
    row = lax.axis_index("row")
    keep(mid, 0, lower[...])
    near = pl.multiple_of(jnp.where(row == 0, sites - halo, 0), edge)
    for b in range(blocks):
        at, rows = slice(b * length, (b + 1) * length), slice(b * sites, (b + 1) * sites)
        const = slice(blocks * sites + b * cols, blocks * sites + (b + 1) * cols)
        to_own[:, at] = own_rows[const] + stacked_dot(mid, slice(0, sites), own_high[rows], own_low[rows])
    to_next[:, :halo] = to_own[:, pl.ds(near, halo)]
    pieces = []
    for rows, from_last, from_first in (
        (slice(0, edge), sites - halo, 0),
        (slice(edge, halo), sites - length, 0),
        (slice(halo, halo + edge), sites - edge, length),
    ):
        source = pl.multiple_of(jnp.where(row == 0, from_last, from_first), edge)
        pieces.append(stacked_dot(mid, pl.ds(source, rows.stop - rows.start), other_high[rows], other_low[rows]))
    far_mid[:, :length] = pieces[0] + jnp.where(row == 0, pieces[1], 0.0)
    far_mid[:, length:] = pieces[2] + jnp.where(row == 0, 0.0, pieces[1])
    to_next[:, halo:] = far_mid[...]
    away = pl.multiple_of(jnp.where(row == 0, 0, sites - halo), edge)
    to_own[:, sites:] = far_mid[:, pl.ds(away, halo)]


def jump_kernel(mine, own_in, base, high, low, *rest):
    ship, (_late, _lower, late, lower, to_next, to_own, to_last, *scratch) = rest[:-9], rest[-9:]

    @pl.when(lax.axis_index("tm") == 2 * mine)
    def _():
        add_own(own_in, base, high, low, late, lower)
        add_parts(lower, *ship, to_next, to_own, *scratch, high.shape[0] * high.shape[1] // own_in.shape[1])
        to_last[...] = to_next[...]

    @pl.when(lax.axis_index("tm") != 2 * mine)
    def _():
        for part in (to_next, to_own, to_last):
            part[...] = jnp.zeros_like(part)


def parts_kernel(mine, span, lower, *rest):
    ship, parts = rest[:-4], rest[-4:]

    @pl.when(lax.axis_index("tm") == 2 * mine)
    def _():
        add_parts(lower, *ship, *parts, span)

    @pl.when(lax.axis_index("tm") != 2 * mine)
    def _():
        for part in parts[:2]:
            part[...] = jnp.zeros_like(part)


def last_kernel(jumps, both, high, low, late, _lower, lower):
    device = lax.axis_index("tm")
    pl.when((device == 0) | (device == 2) if jumps else device == 0)(lambda: step(both, high, low, late, lower))


def upper_kernel(sides, top, *rest):
    far, far_high, far_low, _late, _upper, late, upper = rest[-7:]
    cols, sites = upper.shape
    length = far.shape[1]
    blocks = sites // length
    window = far_high.shape[0] // blocks
    halo = (late.shape[1] - sites) // 2
    at_window = halo - (window - length) // 2
    messages = rest[:-7]

    if len(messages) == 2:

        @pl.when(lax.axis_index("tm") == 0)
        def _():
            load(sides, plain(messages[1]), messages[0][...], halo, late)

    sums = ((messages[0], messages[2], messages[1]), messages[3:]) if len(messages) > 2 else ()
    for mine, (*next_in, own_in) in enumerate(sums):

        @pl.when(lax.axis_index("tm") == 2 * mine)
        def _():
            from_next = next_in[0][...] + next_in[1][...] if len(next_in) == 2 else next_in[0][...]
            own = own_in[:, :sites] + from_next[:, halo:]
            near = own_in[:, sites:] + from_next[:, :halo]
            load(sides, lambda side, cut: near, own, halo, late)

    @pl.when(lax.axis_index("tm") != 2 * top)
    def _():
        for b in range(blocks):
            rows = slice(b * window, (b + 1) * window)
            at = blocks * window + b * cols
            start = at_window + b * length
            upper[:, b * length : (b + 1) * length] = far[at : at + cols] - stacked_dot(
                late, slice(start, start + window), far_high[rows], far_low[rows]
            )


def local(normals, inv_diag, lag_coupling, fill_mask):
    times, rows = lax.axis_size("tm"), lax.axis_size("row")
    device = lax.axis_index("tm")
    cols, sites = normals.shape[1:]
    blocks, length = inv_diag.shape[1:3]
    window = lag_coupling.shape[2]
    edge = (window - length) // 2
    halo = length + edge
    sides = 1 if rows == 2 else 2
    pairs = times // 2
    f32, bf16 = jnp.float32, jnp.bfloat16
    shape = jax.ShapeDtypeStruct

    def link(source, target):
        return [(s * rows + r, t * rows + r) for s, t in zip(source, target) for r in range(rows)]

    def cross(value, source, target, split=False):
        if sides == 1:
            perm = [(s * rows + r, t * rows + 1 - r) for s, t in zip(source, target) for r in range(2)]
            return lax.ppermute(value, BOTH, perm)
        moved = []
        for side, step in enumerate((1, -1)):
            perm = [
                (s * rows + r, t * rows + r + step)
                for s, t in zip(source, target)
                for r in range(rows)
                if 0 <= r + step < rows
            ]
            moved.append(lax.ppermute(value[side : side + 1] if split else value[None], BOTH, perm))
        return jnp.concatenate(moved)

    tall = blocks * window
    jump = 2
    jumps = rows == 2 and pairs > 5 and blocks == 2

    def consts(which, alias=(), after=()):
        return pl.pallas_call(
            functools.partial(const_kernel, (which, 2 * pairs - 4)),
            out_shape=(
                shape((cols, sites), f32),
                shape((blocks, length, length), bf16), shape((blocks, length, length), bf16),
            ),
            in_specs=[HBM] * 2 + [VMEM] * (len(alias) + len(after)),
            out_specs=(VMEM,) * 3,
            scratch_shapes=[
                pltpu.VMEM(normals.shape[1:], f32),
                pltpu.VMEM(inv_diag.shape[1:], f32),
                pltpu.SemaphoreType.DMA((1 + blocks,)),
            ],
            input_output_aliases={2 + i: i for i in range(len(alias))},
            compiler_params=PARAMS,
            cost_estimate=pl.CostEstimate(flops=10**9 if which == "late" else 0, bytes_accessed=0, transcendentals=0),
        )(*[pltpu.with_memory_space_constraint(a, pltpu.HBM) for a in (normals, inv_diag)], *alias, *after)

    odd_parts = consts("odd")
    const = odd_parts[0]
    const_rim = pl.pallas_call(
        functools.partial(rim_of_kernel, sides),
        out_shape=shape((sides, cols, edge), f32),
        in_specs=[VMEM],
        out_specs=VMEM,
        compiler_params=PARAMS,
        cost_estimate=pl.CostEstimate(flops=5 * 10**9, bytes_accessed=0, transcendentals=0),
    )(const)
    again = pl.pallas_call(
        copy_kernel,
        out_shape=shape((cols, sites), f32),
        in_specs=[VMEM] * 2,
        out_specs=VMEM,
        compiler_params=PARAMS,
    )(const, const_rim)
    odd, even = range(1, times, 2), range(0, times, 2)
    first_next = cross(const_rim, odd[-1:], even[-1:], True)
    first_own = lax.ppermute(again, BOTH, link(odd[-1:], even[-1:]))

    const, inv_high, inv_low = consts("even", odd_parts, (const_rim, again))

    def fused(late, extra, const, inv_high, inv_low):
        return pl.pallas_call(
            functools.partial(fuse_kernel, (2 * pairs - 4, late)),
            out_shape=(shape((tall, length), bf16), shape((tall, length), bf16), *extra),
            in_specs=[VMEM] * 5,
            out_specs=(VMEM,) * (2 + len(extra)),
            compiler_params=PARAMS,
            cost_estimate=pl.CostEstimate(
                flops=(6 if late else 150) * (tall + cols * blocks) * length * length, bytes_accessed=0, transcendentals=0
            ),
        )(fill_mask, const, inv_high, inv_low, lag_coupling)

    near_high, near_low, near = fused(False, (shape((tall + blocks * cols, length), f32),), const, inv_high, inv_low)
    edges = pl.pallas_call(
        functools.partial(edge_kernel, sides, blocks, cols),
        out_shape=shape((sides, window + cols, edge), f32),
        in_specs=[VMEM],
        out_specs=VMEM,
        compiler_params=PARAMS,
    )(near)
    near = pl.pallas_call(
        lambda _own, _edges, own: None,
        out_shape=shape(near.shape, f32),
        in_specs=[VMEM] * 2,
        out_specs=VMEM,
        input_output_aliases={0: 0},
        compiler_params=PARAMS,
    )(near, edges)
    apart = 2 * pairs - 6 if pairs > 3 else None
    first_odd = [t for t in odd[:-1] if t - 1 != apart]
    first_even = [t for t in even[:-1] if t != apart]
    rim = cross(edges, first_odd, first_even, True)
    far = lax.ppermute(near, BOTH, link(first_odd, first_even))

    blank = jnp.zeros((cols, sites), f32)
    upper, lower = pl.pallas_call(
        functools.partial(top_kernel, pairs - 1, sides),
        out_shape=(shape((cols, sites), f32),) * 2,
        in_specs=[VMEM] * 7,
        out_specs=(VMEM,) * 2,
        scratch_shapes=[pltpu.VMEM((2 * cols, sites + 2 * edge), bf16)],
        input_output_aliases={5: 0, 6: 1},
        compiler_params=PARAMS,
        cost_estimate=pl.CostEstimate(flops=50 * 10**9, bytes_accessed=0, transcendentals=0),
    )(first_next, first_own, const, near_high, near_low, blank, blank)
    far_high, far_low = pl.pallas_call(
        split_kernel,
        out_shape=(shape((tall, length), bf16), shape((tall, length), bf16)),
        in_specs=[VMEM],
        out_specs=(VMEM,) * 2,
        compiler_params=PARAMS,
    )(far)
    packs = (shape((blocks * (sites + cols), length), f32), shape((halo + edge, length), f32)) if jumps else ()

    def pair_matrix(first, jumps, packs, mine, const):
        return pl.pallas_call(
            functools.partial(pair_kernel, (pairs - 2, first), jumps),
            out_shape=(
                shape((2 * tall, length), bf16), shape((2 * tall, length), bf16), shape((cols, sites), f32), *packs
            ),
            in_specs=[VMEM] * 7,
            out_specs=(VMEM,) * (3 + len(packs)),
            scratch_shapes=[pltpu.VMEM((2 * window, length), f32)],
            compiler_params=PARAMS,
            cost_estimate=pl.CostEstimate(flops=50 * 10**9 if first else 10**9, bytes_accessed=0, transcendentals=0),
        )(far, rim, far_high, far_low, *mine, const)

    late_parts = consts("late", (), (lower,))
    early = pair_matrix(True, False, (), fused(True, (), *late_parts), late_parts[0])
    if apart is not None:
        given = (near, edges, lower)
        near, edges = pl.pallas_call(
            functools.partial(pass_kernel, apart + 1),
            out_shape=(shape(near.shape, f32), shape(edges.shape, f32)),
            in_specs=[VMEM] * 3,
            out_specs=(VMEM,) * 2,
            compiler_params=PARAMS,
        )(*given)
        far_in = lax.ppermute(near, BOTH, link([apart + 1], [apart]))
        rim_in = cross(edges, [apart + 1], [apart], True)
        merged = (far, rim, far_high, far_low)
        far, rim, far_high, far_low = pl.pallas_call(
            functools.partial(merge_kernel, apart),
            out_shape=tuple(shape(v.shape, v.dtype) for v in merged),
            in_specs=[VMEM] * 6,
            out_specs=(VMEM,) * 4,
            input_output_aliases={2 + i: i for i in range(4)},
            compiler_params=PARAMS,
        )(far_in, rim_in, *merged)
    high, low, both, *packs = pair_matrix(False, jumps, packs, (near_high, near_low), const)
    if jumps:
        source, target = [2 * jump - 2, 2 * jump], [2 * jump, 2 * jump + 2]
        own_rows = lax.ppermute(packs[0], BOTH, link(source, target))
        other_rows = cross(packs[1], source, target)
        ship = pl.pallas_call(
            rows_kernel,
            out_shape=(shape((blocks * sites, length), bf16),) * 2 + (shape(other_rows.shape, bf16),) * 2,
            in_specs=[VMEM] * 2,
            out_specs=(VMEM,) * 4,
            compiler_params=PARAMS,
        )(own_rows, other_rows)

    def turn(kernel, given, state, scratch=(), extra=(), flops=0):
        return pl.pallas_call(
            kernel,
            out_shape=tuple(shape(v.shape, v.dtype) for v in state) + tuple(extra),
            in_specs=[VMEM] * (len(given) + len(state)),
            out_specs=(VMEM,) * (len(state) + len(extra)),
            scratch_shapes=list(scratch),
            input_output_aliases={len(given) + i: i for i in range(len(state))},
            compiler_params=PARAMS,
            cost_estimate=pl.CostEstimate(flops=flops, bytes_accessed=0, transcendentals=0) if flops else None,
        )(*given, *state)

    parts = (shape((cols, sites + halo), f32),) * 2
    parts_scratch = [pltpu.VMEM((2 * cols, sites), bf16), pltpu.VMEM((cols, sites), f32)]
    late = jnp.zeros((2 * cols, sites + 2 * halo), bf16)
    mine = pairs - 1
    while mine > 0:
        if jumps and mine == jump:
            source, target = [2 * mine], [2 * mine - 4]
            first_in = lax.ppermute(to_next, BOTH, [(2 * source[0] + 1, 2 * target[0])])
            own_in = lax.ppermute(to_own, BOTH, link(source, target))
            next_in = lax.ppermute(to_last, BOTH, [(2 * source[0], 2 * target[0] + 1)])
            break
        source, target = [2 * mine], [2 * mine - 2]
        next_in = cross(lower, source, target)
        own_in = lax.ppermute(lower, BOTH, link(source, target))
        if jumps and mine == jump + 1:
            beside = pl.pallas_call(
                functools.partial(parts_kernel, mine, 2 * window),
                out_shape=parts,
                in_specs=[VMEM] * 6,
                out_specs=(VMEM,) * 2,
                scratch_shapes=parts_scratch,
                compiler_params=PARAMS,
            )(lower, own_rows, *ship)
            source, target = [2 * mine], [2 * mine - 4]
            beside_next = cross(beside[0], source, target)
            beside_own = lax.ppermute(beside[1], BOTH, link(source, target))
        mine -= 1
        if mine == 0:
            break
        here = early if mine == pairs - 2 else (high, low, both)
        late, base = turn(
            functools.partial(rim_kernel, mine, sides),
            (next_in, here[2], *here[:2]),
            (late,),
            extra=[shape((cols, sites), f32)],
        )
        if jumps and mine == jump:
            late, lower, to_next, to_own, to_last = turn(
                functools.partial(jump_kernel, mine),
                (own_in, base, high, low, own_rows, *ship),
                (late, lower),
                parts_scratch,
                parts + parts[:1],
            )
        else:
            late, lower = turn(
                functools.partial(chain_kernel, mine),
                (own_in, base, *here[:2]),
                (late, lower),
                flops=50 * 10**9 if jumps and mine == pairs - 3 else 0,
            )
    given = (first_in, own_in, next_in, beside_next, beside_own) if jumps else (own_in, next_in)
    late, upper = turn(
        functools.partial(upper_kernel, sides, pairs - 1), (*given, far, far_high, far_low), (late, upper)
    )
    returned = lax.ppermute(upper, BOTH, link(even, odd))
    lower = pl.pallas_call(
        functools.partial(last_kernel, jumps),
        out_shape=shape(lower.shape, f32),
        in_specs=[VMEM] * 5,
        out_specs=VMEM,
        input_output_aliases={4: 0},
        compiler_params=PARAMS,
        cost_estimate=pl.CostEstimate(flops=12 * cols * tall * length, bytes_accessed=8 * tall * length, transcendentals=0),
    )(both, high, low, late, lower)
    return jnp.where(device % 2 == 0, lower, returned)[None]


def solution(mesh):
    placed = (
        P("tm", None, "row"),
        P("tm", "row", None, None),
        P("tm", "row", None, None),
        P("tm", "row", None),
    )
    return jax.shard_map(
        local, mesh=mesh, in_specs=placed, out_specs=P("tm", None, "row"), check_vma=False
    )
```

```python
import functools

import jax
import jax.numpy as jnp
from jax import lax
from jax.experimental import pallas as pl
from jax.experimental.pallas import tpu as pltpu
from jax.sharding import PartitionSpec as P

BOTH = ("tm", "row")
VMEM = pl.BlockSpec(memory_space=pltpu.VMEM)
HBM = pl.BlockSpec(memory_space=pltpu.HBM)
PARAMS = pltpu.CompilerParams(vmem_limit_bytes=32 * 1024 * 1024)


def halves(value):
    high = value.astype(jnp.bfloat16)
    low = (value - high.astype(jnp.float32)).astype(jnp.bfloat16)
    return high, low


def dot(a, b):
    return jnp.dot(a, b, preferred_element_type=jnp.float32)


def stacked_dot(pair, cols, high, low):
    rows = pair.shape[0] // 2
    wide = dot(pair[:, cols], high)
    return wide[:rows] + wide[rows:] + dot(pair[:rows, cols], low)


def triple(high, low, inv_high, inv_low):
    return dot(high, inv_high) + dot(low, inv_high) + dot(high, inv_low)


def put_rim(sides, rim, columns):
    if sides == 1:
        row = lax.axis_index("row")

        @pl.when(row == 0)
        def _():
            rim[0] = columns(True)

        @pl.when(row != 0)
        def _():
            rim[0] = columns(False)
    else:
        rim[0] = columns(True)
        rim[1] = columns(False)


def const_kernel(normals, inv, const, inv_high, inv_low, normals_in, inv_in, sems):
    blocks, length = inv.shape[1], inv.shape[2]
    moves = [pltpu.make_async_copy(normals.at[0], normals_in, sems.at[0])]
    for b in range(blocks):
        moves.append(pltpu.make_async_copy(inv.at[0, b], inv_in.at[b], sems.at[1 + b]))
    for move in moves:
        move.start()
    moves[0].wait()
    for b in range(blocks):
        at = slice(b * length, (b + 1) * length)
        high, low = halves(normals_in[:, at])
        moves[1 + b].wait()
        inv_high[b], inv_low[b] = halves(inv_in[b])
        const[:, at] = triple(high, low, inv_high[b], inv_low[b])


def again_kernel(const, again):
    again[...] = const[...]


def fuse_kernel(late, *refs):
    here = lax.axis_index("tm") == late[0]
    given = refs[:5] + refs[6:] if late[1] else refs
    pl.when(here if late[1] else jnp.logical_not(here))(lambda: make_fused(*given))


def make_fused(mask, const, inv_high, inv_low, lag, near_high, near_low, own=None):
    blocks, window, length = lag.shape[1:]
    edge = (window - length) // 2
    cols = const.shape[0]
    cuts = (0, edge, edge + length, window)
    flags = mask[0].astype(jnp.float32)
    for b in range(blocks):
        at = blocks * window + b * cols
        if own is not None:
            own[at : at + cols] = const[:, b * length : (b + 1) * length]
        for part in range(3):
            lo, hi = cuts[part], cuts[part + 1]
            rows = slice(b * window + lo, b * window + hi)
            high, low = halves(lag[0, b, lo:hi] * flags[b : b + 1, part : part + 1])
            value = triple(high, low, inv_high[b], inv_low[b])
            if own is not None:
                own[rows] = value
            near_high[rows], near_low[rows] = halves(value)


def edge_kernel(sides, blocks, cols, own, rim):
    length, edge = own.shape[1], rim.shape[2]
    window = length + 2 * edge

    def columns(last):
        b = blocks - 1 if last else 0
        cut = slice(length - edge, length) if last else slice(0, edge)
        at = blocks * window + b * cols
        return jnp.concatenate([own[b * window : (b + 1) * window, cut], own[at : at + cols, cut]])

    put_rim(sides, rim, columns)


def split_kernel(far, far_high, far_low):
    far_high[...], far_low[...] = halves(far[: far_high.shape[0]])


def cuts_of(blocks, length, sites, span, last):
    packed, cuts = 0, []
    for b in range(blocks):
        start = span // 2 - length // 2 - b * length
        lo, hi = (start + sites, span) if last else (0, start)
        cuts.append((lo, hi, packed))
        packed += hi - lo
    return cuts


def pair_kernel(first, jump, *refs):
    here = lax.axis_index("tm") == 2 * first[0]
    pl.when(here if first[1] else jnp.logical_not(here))(lambda: make_pair(jump, *refs))


def make_pair(jump, far, rim, far_high, far_low, near_high, near_low, const, high, low, both, *rest):
    cols, sites = const.shape
    length = far.shape[1]
    blocks = sites // length
    window = near_high.shape[0] // blocks
    edge = (window - length) // 2
    span = 2 * window
    tall = blocks * window
    total = rest[-1]
    if rim.shape[0] == 1:
        flag = jnp.minimum(lax.axis_index("row"), 1).astype(jnp.float32)
        left, right = rim[0] * flag, rim[0] * (1 - flag)
    else:
        left, right = rim[0], rim[1]
    left_pair, right_pair = halves(left[:window]), halves(right[:window])
    for b in range(blocks):
        here = slice(b * window, (b + 1) * window)
        column = slice(b * length, (b + 1) * length)

        def part(lo, hi):
            rows = slice(b * window + lo, b * window + hi)
            return near_high[rows], near_low[rows]

        def constant(block):
            if block < 0:
                return left[window:]
            if block == blocks:
                return right[window:]
            return far[tall + block * cols : tall + (block + 1) * cols]

        if b > 0:
            before = slice((b - 1) * window, b * window)
            low_pair = far_high[before, length - edge :], far_low[before, length - edge :]
            low_const = constant(b - 1)[:, length - edge :]
        else:
            low_pair, low_const = left_pair, constant(-1)
        if b + 1 < blocks:
            after = slice((b + 1) * window, (b + 2) * window)
            high_pair = far_high[after, :edge], far_low[after, :edge]
            high_const = constant(b + 1)[:, :edge]
        else:
            high_pair, high_const = right_pair, constant(blocks)
        first = triple(*low_pair, *part(0, edge))
        middle = triple(far_high[here], far_low[here], *part(edge, edge + length))
        last = triple(*high_pair, *part(edge + length, window))
        total[:window] = first
        total[window:] = last
        total[length : length + window] += middle
        high[b * span : (b + 1) * span], low[b * span : (b + 1) * span] = halves(total[...])
        both[:, column] = const[:, column] - (
            triple(*halves(low_const), *part(0, edge))
            + triple(*halves(constant(b)), *part(edge, edge + length))
            + triple(*halves(high_const), *part(edge + length, window))
        )
    if jump:
        own_rows, other_rows = rest[:2]

        def value(start, count):
            rows = pl.ds(start, count)
            return high[rows].astype(jnp.float32) + low[rows].astype(jnp.float32)

        for b in range(blocks):
            own_rows[b * sites : (b + 1) * sites] = value(b * span + window - edge - b * length, sites)
            at = blocks * sites + b * cols
            own_rows[at : at + cols] = both[:, b * length : (b + 1) * length]
        starts = [
            [b * span + at for b, (lo, hi, _) in enumerate(cuts_of(blocks, length, sites, span, last)) for at in range(lo, hi, edge)]
            for last in (True, False)
        ]
        row = lax.axis_index("row")
        for chunk, (on_right, on_left) in enumerate(zip(*starts)):
            start = pl.multiple_of(jnp.where(row == 0, on_right, on_left), edge)
            other_rows[chunk * edge : (chunk + 1) * edge] = value(start, edge)


def keep(ref, start, value):
    cols, width = value.shape
    high, low = halves(value)
    ref[:cols, pl.ds(start, width)] = high
    ref[cols:, pl.ds(start, width)] = low


def load(sides, pick, own, halo, ref):
    sites = own.shape[1]
    keep(ref, halo, own)
    for side in range(sides):
        on_right = 1 - jnp.minimum(lax.axis_index("row"), 1).astype(jnp.int32) if sides == 1 else side
        start = pl.multiple_of((1 - on_right) * (sites - halo), 128)
        keep(ref, pl.multiple_of(on_right * (halo + sites), 128), pick(side, pl.ds(start, halo)))


def plain(next_in):
    return lambda side, cut: next_in[:, cut] if len(next_in.shape) == 2 else next_in[side, :, cut]


def top_kernel(mine, sides, next_in, own_in, const, near_high, near_low, _upper, _lower, upper, lower, *rest):
    mid = rest[-1]
    sites = lower.shape[1]
    length = near_high.shape[1]
    blocks = sites // length
    window = near_high.shape[0] // blocks
    edge = (window - length) // 2

    @pl.when(lax.axis_index("tm") == 2 * mine)
    def _():
        mid[...] = jnp.zeros_like(mid)
        load(sides, plain(next_in), own_in[...], edge, mid)
        upper[...] = own_in[...]
        for b in range(blocks):
            at, rows = slice(b * length, (b + 1) * length), slice(b * window, (b + 1) * window)
            product = stacked_dot(mid, slice(b * length, b * length + window), near_high[rows], near_low[rows])
            lower[:, at] = const[:, at] - product
        if len(rest) > 1:
            halo = rest[0].shape[1]
            start = pl.multiple_of(jnp.where(lax.axis_index("row") == 0, sites - halo, 0), 128)
            rest[0][...] = lower[:, pl.ds(start, halo)]


def step(both, high, low, late, lower):
    blocks = lower.shape[1] // high.shape[1]
    length, span = high.shape[1], high.shape[0] // blocks
    for b in range(blocks):
        at, rows = slice(b * length, (b + 1) * length), slice(b * span, (b + 1) * span)
        lower[:, at] = both[:, at] + stacked_dot(late, slice(b * length, b * length + span), high[rows], low[rows])


def load_rims(sides, next_in, sites, halo, late):
    for side in range(sides):
        on_right = 1 - jnp.minimum(lax.axis_index("row"), 1).astype(jnp.int32) if sides == 1 else side
        if next_in.shape[-1] == halo:
            value = next_in[...]
        else:
            value = plain(next_in)(side, pl.ds(pl.multiple_of((1 - on_right) * (sites - halo), 128), halo))
        keep(late, pl.multiple_of(on_right * (halo + sites), 128), value)


def rim_kernel(mine, sides, next_in, both, high, low, _late, late, base):
    sites, length = base.shape[1], high.shape[1]
    blocks = sites // length
    span = high.shape[0] // blocks
    halo = (late.shape[1] - sites) // 2
    edge = halo - length

    @pl.when(lax.axis_index("tm") == 2 * mine)
    def _():
        load_rims(sides, next_in, sites, halo, late)
        cuts = [cuts_of(blocks, length, sites, span, last) for last in (False, True)]
        for b in range(blocks):
            value = both[:, b * length : (b + 1) * length]
            if sides == 2:
                for lo, hi, _ in (cuts[0][b], cuts[1][b]):
                    rows = slice(b * span + lo, b * span + hi)
                    value += stacked_dot(late, slice(b * length + lo, b * length + hi), high[rows], low[rows])
            else:
                on_left = lax.axis_index("row") != 0
                counts = [cut[b][1] - cut[b][0] for cut in cuts]
                for chunk in range(0, max(counts), edge):
                    starts = [cut[b][0] + chunk if chunk < count else 0 for cut, count in zip(cuts, counts)]
                    start = pl.multiple_of(jnp.where(on_left, starts[0], starts[1]), edge)
                    rows = pl.ds(b * span + start, edge)
                    product = stacked_dot(late, pl.ds(b * length + start, edge), high[rows], low[rows])
                    if chunk >= min(counts):
                        product = jnp.where(on_left == (counts[0] > counts[1]), product, 0.0)
                    value += product
            base[:, b * length : (b + 1) * length] = value


def add_own(own_in, base, high, low, late, lower):
    sites, length = lower.shape[1], high.shape[1]
    blocks = sites // length
    span = high.shape[0] // blocks
    halo = (late.shape[1] - sites) // 2
    keep(late, halo, own_in[...])
    for b in range(blocks):
        at, start = slice(b * length, (b + 1) * length), halo - b * length
        rows = slice(b * span + start, b * span + start + sites)
        lower[:, at] = base[:, at] + stacked_dot(late, slice(halo, halo + sites), high[rows], low[rows])


def chain_kernel(mine, own_in, base, high, low, _late, _lower, late, lower, near=None):
    @pl.when(lax.axis_index("tm") == 2 * mine)
    def _():
        add_own(own_in, base, high, low, late, lower)
        if near is not None:
            sites, halo = lower.shape[1], near.shape[1]
            start = pl.multiple_of(jnp.where(lax.axis_index("row") == 0, sites - halo, 0), 128)
            near[...] = lower[:, pl.ds(start, halo)]


def rows_kernel(own_rows, other_rows, own_high, own_low, other_high, other_low):
    own_high[...], own_low[...] = halves(own_rows[: own_high.shape[0]])
    other_high[...], other_low[...] = halves(other_rows[...])


def add_parts(lower, own_rows, own_high, own_low, other_high, other_low, to_next, to_own, mid, far_mid, span):
    cols, sites = lower.shape
    length = own_rows.shape[1]
    blocks = sites // length
    halo = to_own.shape[1] - sites
    edge = halo - length
    row = lax.axis_index("row")
    keep(mid, 0, lower[...])
    near = pl.multiple_of(jnp.where(row == 0, sites - halo, 0), edge)
    for b in range(blocks):
        at, rows = slice(b * length, (b + 1) * length), slice(b * sites, (b + 1) * sites)
        const = slice(blocks * sites + b * cols, blocks * sites + (b + 1) * cols)
        to_own[:, at] = own_rows[const] + stacked_dot(mid, slice(0, sites), own_high[rows], own_low[rows])
    to_next[:, :halo] = to_own[:, pl.ds(near, halo)]
    pieces = []
    for rows, from_last, from_first in (
        (slice(0, edge), sites - halo, 0),
        (slice(edge, halo), sites - length, 0),
        (slice(halo, halo + edge), sites - edge, length),
    ):
        source = pl.multiple_of(jnp.where(row == 0, from_last, from_first), edge)
        pieces.append(stacked_dot(mid, pl.ds(source, rows.stop - rows.start), other_high[rows], other_low[rows]))
    far_mid[:, :length] = pieces[0] + jnp.where(row == 0, pieces[1], 0.0)
    far_mid[:, length:] = pieces[2] + jnp.where(row == 0, 0.0, pieces[1])
    to_next[:, halo:] = far_mid[...]
    away = pl.multiple_of(jnp.where(row == 0, 0, sites - halo), edge)
    to_own[:, sites:] = far_mid[:, pl.ds(away, halo)]


def jump_kernel(mine, own_in, base, high, low, *rest):
    ship, (_late, _lower, late, lower, to_next, to_own, to_last, *scratch) = rest[:-9], rest[-9:]

    @pl.when(lax.axis_index("tm") == 2 * mine)
    def _():
        add_own(own_in, base, high, low, late, lower)
        add_parts(lower, *ship, to_next, to_own, *scratch, high.shape[0] * high.shape[1] // own_in.shape[1])
        to_last[...] = to_next[...]

    @pl.when(lax.axis_index("tm") != 2 * mine)
    def _():
        for part in (to_next, to_own, to_last):
            part[...] = jnp.zeros_like(part)


def parts_kernel(mine, span, lower, *rest):
    ship, parts = rest[:-4], rest[-4:]

    @pl.when(lax.axis_index("tm") == 2 * mine)
    def _():
        add_parts(lower, *ship, *parts, span)

    @pl.when(lax.axis_index("tm") != 2 * mine)
    def _():
        for part in parts[:2]:
            part[...] = jnp.zeros_like(part)


def last_kernel(jumps, both, high, low, late, _lower, lower):
    device = lax.axis_index("tm")
    pl.when((device == 0) | (device == 2) if jumps else device == 0)(lambda: step(both, high, low, late, lower))


def upper_kernel(sides, top, *rest):
    far, far_high, far_low, _late, _upper, late, upper = rest[-7:]
    cols, sites = upper.shape
    length = far.shape[1]
    blocks = sites // length
    window = far_high.shape[0] // blocks
    halo = (late.shape[1] - sites) // 2
    at_window = halo - (window - length) // 2
    messages = rest[:-7]

    if len(messages) == 2:

        @pl.when(lax.axis_index("tm") == 0)
        def _():
            load(sides, plain(messages[1]), messages[0][...], halo, late)

    sums = ((messages[0], messages[2], messages[1]), messages[3:]) if len(messages) > 2 else ()
    for mine, (*next_in, own_in) in enumerate(sums):

        @pl.when(lax.axis_index("tm") == 2 * mine)
        def _():
            from_next = next_in[0][...] + next_in[1][...] if len(next_in) == 2 else next_in[0][...]
            own = own_in[:, :sites] + from_next[:, halo:]
            near = own_in[:, sites:] + from_next[:, :halo]
            load(sides, lambda side, cut: near, own, halo, late)

    @pl.when(lax.axis_index("tm") != 2 * top)
    def _():
        for b in range(blocks):
            rows = slice(b * window, (b + 1) * window)
            at = blocks * window + b * cols
            start = at_window + b * length
            upper[:, b * length : (b + 1) * length] = far[at : at + cols] - stacked_dot(
                late, slice(start, start + window), far_high[rows], far_low[rows]
            )


def local(normals, inv_diag, lag_coupling, fill_mask):
    times, rows = lax.axis_size("tm"), lax.axis_size("row")
    device = lax.axis_index("tm")
    cols, sites = normals.shape[1:]
    blocks, length = inv_diag.shape[1:3]
    window = lag_coupling.shape[2]
    edge = (window - length) // 2
    halo = length + edge
    sides = 1 if rows == 2 else 2
    pairs = times // 2
    f32, bf16 = jnp.float32, jnp.bfloat16
    shape = jax.ShapeDtypeStruct

    def link(source, target):
        return [(s * rows + r, t * rows + r) for s, t in zip(source, target) for r in range(rows)]

    def cross(value, source, target, split=False):
        if sides == 1:
            perm = [(s * rows + r, t * rows + 1 - r) for s, t in zip(source, target) for r in range(2)]
            return lax.ppermute(value, BOTH, perm)
        moved = []
        for side, step in enumerate((1, -1)):
            perm = [
                (s * rows + r, t * rows + r + step)
                for s, t in zip(source, target)
                for r in range(rows)
                if 0 <= r + step < rows
            ]
            moved.append(lax.ppermute(value[side : side + 1] if split else value[None], BOTH, perm))
        return jnp.concatenate(moved)

    tall = blocks * window
    jump = 2
    jumps = rows == 2 and pairs > 5 and blocks == 2
    const, inv_high, inv_low = pl.pallas_call(
        const_kernel,
        out_shape=(
            shape((cols, sites), f32),
            shape((blocks, length, length), bf16), shape((blocks, length, length), bf16),
        ),
        in_specs=[HBM] * 2,
        out_specs=(VMEM,) * 3,
        scratch_shapes=[
            pltpu.VMEM(normals.shape[1:], f32),
            pltpu.VMEM(inv_diag.shape[1:], f32),
            pltpu.SemaphoreType.DMA((1 + blocks,)),
        ],
        compiler_params=PARAMS,
    )(*[pltpu.with_memory_space_constraint(a, pltpu.HBM) for a in (normals, inv_diag)])
    again = pl.pallas_call(
        again_kernel,
        out_shape=shape((cols, sites), f32),
        in_specs=[VMEM],
        out_specs=VMEM,
        compiler_params=PARAMS,
        cost_estimate=pl.CostEstimate(flops=5 * 10**9, bytes_accessed=0, transcendentals=0),
    )(const)
    odd, even = range(1, times, 2), range(0, times, 2)
    first_next = cross(again, odd[-1:], even[-1:])
    first_own = lax.ppermute(const, BOTH, link(odd[-1:], even[-1:]))

    def fused(late, extra, after=()):
        return pl.pallas_call(
            functools.partial(fuse_kernel, (2 * pairs - 4, late)),
            out_shape=(shape((tall, length), bf16), shape((tall, length), bf16), *extra),
            in_specs=[VMEM] * (5 + len(after)),
            out_specs=(VMEM,) * (2 + len(extra)),
            compiler_params=PARAMS,
            cost_estimate=pl.CostEstimate(
                flops=6 * (tall + cols * blocks) * length * length, bytes_accessed=16 * tall * length, transcendentals=0
            ),
        )(fill_mask, const, inv_high, inv_low, lag_coupling, *after)

    near_high, near_low, near = fused(False, (shape((tall + blocks * cols, length), f32),))
    edges = pl.pallas_call(
        functools.partial(edge_kernel, sides, blocks, cols),
        out_shape=shape((sides, window + cols, edge), f32),
        in_specs=[VMEM],
        out_specs=VMEM,
        compiler_params=PARAMS,
    )(near)
    near = pl.pallas_call(
        lambda _own, _edges, own: None,
        out_shape=shape(near.shape, f32),
        in_specs=[VMEM] * 2,
        out_specs=VMEM,
        input_output_aliases={0: 0},
        compiler_params=PARAMS,
    )(near, edges)
    rim = cross(edges, odd[:-1], even[:-1], True)
    far = lax.ppermute(near, BOTH, link(odd[:-1], even[:-1]))

    blank = jnp.zeros((cols, sites), f32)
    near_shape = (shape((cols, halo), f32),) if sides == 1 else ()
    upper, lower, *near = pl.pallas_call(
        functools.partial(top_kernel, pairs - 1, sides),
        out_shape=(shape((cols, sites), f32),) * 2 + near_shape,
        in_specs=[VMEM] * 7,
        out_specs=(VMEM,) * (2 + len(near_shape)),
        scratch_shapes=[pltpu.VMEM((2 * cols, sites + 2 * edge), bf16)],
        input_output_aliases={5: 0, 6: 1},
        compiler_params=PARAMS,
        cost_estimate=pl.CostEstimate(flops=50 * 10**9, bytes_accessed=0, transcendentals=0),
    )(first_next, first_own, const, near_high, near_low, blank, blank)
    far_high, far_low = pl.pallas_call(
        split_kernel,
        out_shape=(shape((tall, length), bf16), shape((tall, length), bf16)),
        in_specs=[VMEM],
        out_specs=(VMEM,) * 2,
        compiler_params=PARAMS,
    )(far)
    packs = (shape((blocks * (sites + cols), length), f32), shape((halo + edge, length), f32)) if jumps else ()

    def pair_matrix(first, jumps, packs, mine):
        return pl.pallas_call(
            functools.partial(pair_kernel, (pairs - 2, first), jumps),
            out_shape=(
                shape((2 * tall, length), bf16), shape((2 * tall, length), bf16), shape((cols, sites), f32), *packs
            ),
            in_specs=[VMEM] * 7,
            out_specs=(VMEM,) * (3 + len(packs)),
            scratch_shapes=[pltpu.VMEM((2 * window, length), f32)],
            compiler_params=PARAMS,
            cost_estimate=pl.CostEstimate(flops=10**9, bytes_accessed=0, transcendentals=0),
        )(far, rim, far_high, far_low, *mine, const)

    early = pair_matrix(True, False, (), fused(True, (), (lower,)))
    high, low, both, *packs = pair_matrix(False, jumps, packs, (near_high, near_low))
    if jumps:
        source, target = [2 * jump - 2, 2 * jump], [2 * jump, 2 * jump + 2]
        own_rows = lax.ppermute(packs[0], BOTH, link(source, target))
        other_rows = cross(packs[1], source, target)
        ship = pl.pallas_call(
            rows_kernel,
            out_shape=(shape((blocks * sites, length), bf16),) * 2 + (shape(other_rows.shape, bf16),) * 2,
            in_specs=[VMEM] * 2,
            out_specs=(VMEM,) * 4,
            compiler_params=PARAMS,
        )(own_rows, other_rows)

    def turn(kernel, given, state, scratch=(), extra=(), flops=0):
        return pl.pallas_call(
            kernel,
            out_shape=tuple(shape(v.shape, v.dtype) for v in state) + tuple(extra),
            in_specs=[VMEM] * (len(given) + len(state)),
            out_specs=(VMEM,) * (len(state) + len(extra)),
            scratch_shapes=list(scratch),
            input_output_aliases={len(given) + i: i for i in range(len(state))},
            compiler_params=PARAMS,
            cost_estimate=pl.CostEstimate(flops=flops, bytes_accessed=0, transcendentals=0) if flops else None,
        )(*given, *state)

    parts = (shape((cols, sites + halo), f32),) * 2
    parts_scratch = [pltpu.VMEM((2 * cols, sites), bf16), pltpu.VMEM((cols, sites), f32)]
    late = jnp.zeros((2 * cols, sites + 2 * halo), bf16)
    mine = pairs - 1
    while mine > 0:
        if jumps and mine == jump:
            source, target = [2 * mine], [2 * mine - 4]
            first_in = lax.ppermute(to_next, BOTH, [(2 * source[0] + 1, 2 * target[0])])
            own_in = lax.ppermute(to_own, BOTH, link(source, target))
            next_in = lax.ppermute(to_last, BOTH, [(2 * source[0], 2 * target[0] + 1)])
            break
        source, target = [2 * mine], [2 * mine - 2]
        next_in = cross(near[0] if near else lower, source, target)
        own_in = lax.ppermute(lower, BOTH, link(source, target))
        if jumps and mine == jump + 1:
            beside = pl.pallas_call(
                functools.partial(parts_kernel, mine, 2 * window),
                out_shape=parts,
                in_specs=[VMEM] * 6,
                out_specs=(VMEM,) * 2,
                scratch_shapes=parts_scratch,
                compiler_params=PARAMS,
            )(lower, own_rows, *ship)
            source, target = [2 * mine], [2 * mine - 4]
            beside_next = cross(beside[0], source, target)
            beside_own = lax.ppermute(beside[1], BOTH, link(source, target))
        mine -= 1
        if mine == 0:
            break
        here = early if mine == pairs - 2 else (high, low, both)
        late, base = turn(
            functools.partial(rim_kernel, mine, sides),
            (next_in, here[2], *here[:2]),
            (late,),
            extra=[shape((cols, sites), f32)],
        )
        if jumps and mine == jump:
            late, lower, to_next, to_own, to_last = turn(
                functools.partial(jump_kernel, mine),
                (own_in, base, high, low, own_rows, *ship),
                (late, lower),
                parts_scratch,
                parts + parts[:1],
            )
        else:
            late, lower, *near = turn(
                functools.partial(chain_kernel, mine),
                (own_in, base, *here[:2]),
                (late, lower),
                extra=[shape((cols, halo), f32)] if sides == 1 and mine == pairs - 2 else [],
                flops=50 * 10**9 if jumps and mine == pairs - 3 else 0,
            )
    given = (first_in, own_in, next_in, beside_next, beside_own) if jumps else (own_in, next_in)
    late, upper = turn(
        functools.partial(upper_kernel, sides, pairs - 1), (*given, far, far_high, far_low), (late, upper)
    )
    returned = lax.ppermute(upper, BOTH, link(even, odd))
    lower = pl.pallas_call(
        functools.partial(last_kernel, jumps),
        out_shape=shape(lower.shape, f32),
        in_specs=[VMEM] * 5,
        out_specs=VMEM,
        input_output_aliases={4: 0},
        compiler_params=PARAMS,
        cost_estimate=pl.CostEstimate(flops=12 * cols * tall * length, bytes_accessed=8 * tall * length, transcendentals=0),
    )(both, high, low, late, lower)
    return jnp.where(device % 2 == 0, lower, returned)[None]


def solution(mesh):
    placed = (
        P("tm", None, "row"),
        P("tm", "row", None, None),
        P("tm", "row", None, None),
        P("tm", "row", None),
    )
    return jax.shard_map(
        local, mesh=mesh, in_specs=placed, out_specs=P("tm", None, "row"), check_vma=False
    )
```

```python
import functools

import jax
import jax.numpy as jnp
from jax import lax
from jax.experimental import pallas as pl
from jax.experimental.pallas import tpu as pltpu
from jax.sharding import PartitionSpec as P

BOTH = ("tm", "row")
VMEM = pl.BlockSpec(memory_space=pltpu.VMEM)
HBM = pl.BlockSpec(memory_space=pltpu.HBM)
PARAMS = pltpu.CompilerParams(vmem_limit_bytes=32 * 1024 * 1024)


def halves(value):
    high = value.astype(jnp.bfloat16)
    low = (value - high.astype(jnp.float32)).astype(jnp.bfloat16)
    return high, low


def dot(a, b):
    return jnp.dot(a, b, preferred_element_type=jnp.float32)


def stacked_dot(pair, cols, high, low):
    rows = pair.shape[0] // 2
    wide = dot(pair[:, cols], high)
    return wide[:rows] + wide[rows:] + dot(pair[:rows, cols], low)


def triple(high, low, inv_high, inv_low):
    return dot(high, inv_high) + dot(low, inv_high) + dot(high, inv_low)


def put_rim(sides, rim, columns):
    if sides == 1:
        row = lax.axis_index("row")

        @pl.when(row == 0)
        def _():
            rim[0] = columns(True)

        @pl.when(row != 0)
        def _():
            rim[0] = columns(False)
    else:
        rim[0] = columns(True)
        rim[1] = columns(False)


def const_kernel(normals, inv, const, inv_high, inv_low, normals_in, inv_in, sems):
    blocks, length = inv.shape[1], inv.shape[2]
    moves = [pltpu.make_async_copy(normals.at[0], normals_in, sems.at[0])]
    for b in range(blocks):
        moves.append(pltpu.make_async_copy(inv.at[0, b], inv_in.at[b], sems.at[1 + b]))
    for move in moves:
        move.start()
    moves[0].wait()
    for b in range(blocks):
        at = slice(b * length, (b + 1) * length)
        high, low = halves(normals_in[:, at])
        moves[1 + b].wait()
        inv_high[b], inv_low[b] = halves(inv_in[b])
        const[:, at] = triple(high, low, inv_high[b], inv_low[b])


def copy_kernel(const, _after, copy):
    copy[...] = const[...]


def rim_of_kernel(sides, const, rim):
    edge, sites = rim.shape[2], const.shape[1]
    put_rim(sides, rim, lambda last: const[:, sites - edge :] if last else const[:, :edge])


def fuse_kernel(late, *refs):
    here = lax.axis_index("tm") == late[0]
    given = refs[:5] + refs[6:] if late[1] else refs
    pl.when(here if late[1] else jnp.logical_not(here))(lambda: make_fused(*given))


def make_fused(mask, const, inv_high, inv_low, lag, near_high, near_low, own=None):
    blocks, window, length = lag.shape[1:]
    edge = (window - length) // 2
    cols = const.shape[0]
    cuts = (0, edge, edge + length, window)
    flags = mask[0].astype(jnp.float32)
    for b in range(blocks):
        at = blocks * window + b * cols
        if own is not None:
            own[at : at + cols] = const[:, b * length : (b + 1) * length]
        for part in range(3):
            lo, hi = cuts[part], cuts[part + 1]
            rows = slice(b * window + lo, b * window + hi)
            high, low = halves(lag[0, b, lo:hi] * flags[b : b + 1, part : part + 1])
            value = triple(high, low, inv_high[b], inv_low[b])
            if own is not None:
                own[rows] = value
            near_high[rows], near_low[rows] = halves(value)


def edge_kernel(sides, blocks, cols, own, rim):
    length, edge = own.shape[1], rim.shape[2]
    window = length + 2 * edge

    def columns(last):
        b = blocks - 1 if last else 0
        cut = slice(length - edge, length) if last else slice(0, edge)
        at = blocks * window + b * cols
        return jnp.concatenate([own[b * window : (b + 1) * window, cut], own[at : at + cols, cut]])

    put_rim(sides, rim, columns)


def split_kernel(far, far_high, far_low):
    far_high[...], far_low[...] = halves(far[: far_high.shape[0]])


def cuts_of(blocks, length, sites, span, last):
    packed, cuts = 0, []
    for b in range(blocks):
        start = span // 2 - length // 2 - b * length
        lo, hi = (start + sites, span) if last else (0, start)
        cuts.append((lo, hi, packed))
        packed += hi - lo
    return cuts


def pair_kernel(first, jump, *refs):
    here = lax.axis_index("tm") == 2 * first[0]
    pl.when(here if first[1] else jnp.logical_not(here))(lambda: make_pair(jump, *refs))


def make_pair(jump, far, rim, far_high, far_low, near_high, near_low, const, high, low, both, *rest):
    cols, sites = const.shape
    length = far.shape[1]
    blocks = sites // length
    window = near_high.shape[0] // blocks
    edge = (window - length) // 2
    span = 2 * window
    tall = blocks * window
    total = rest[-1]
    if rim.shape[0] == 1:
        flag = jnp.minimum(lax.axis_index("row"), 1).astype(jnp.float32)
        left, right = rim[0] * flag, rim[0] * (1 - flag)
    else:
        left, right = rim[0], rim[1]
    left_pair, right_pair = halves(left[:window]), halves(right[:window])
    for b in range(blocks):
        here = slice(b * window, (b + 1) * window)
        column = slice(b * length, (b + 1) * length)

        def part(lo, hi):
            rows = slice(b * window + lo, b * window + hi)
            return near_high[rows], near_low[rows]

        def constant(block):
            if block < 0:
                return left[window:]
            if block == blocks:
                return right[window:]
            return far[tall + block * cols : tall + (block + 1) * cols]

        if b > 0:
            before = slice((b - 1) * window, b * window)
            low_pair = far_high[before, length - edge :], far_low[before, length - edge :]
            low_const = constant(b - 1)[:, length - edge :]
        else:
            low_pair, low_const = left_pair, constant(-1)
        if b + 1 < blocks:
            after = slice((b + 1) * window, (b + 2) * window)
            high_pair = far_high[after, :edge], far_low[after, :edge]
            high_const = constant(b + 1)[:, :edge]
        else:
            high_pair, high_const = right_pair, constant(blocks)
        first = triple(*low_pair, *part(0, edge))
        middle = triple(far_high[here], far_low[here], *part(edge, edge + length))
        last = triple(*high_pair, *part(edge + length, window))
        total[:window] = first
        total[window:] = last
        total[length : length + window] += middle
        high[b * span : (b + 1) * span], low[b * span : (b + 1) * span] = halves(total[...])
        both[:, column] = const[:, column] - (
            triple(*halves(low_const), *part(0, edge))
            + triple(*halves(constant(b)), *part(edge, edge + length))
            + triple(*halves(high_const), *part(edge + length, window))
        )
    if jump:
        own_rows, other_rows = rest[:2]

        def value(start, count):
            rows = pl.ds(start, count)
            return high[rows].astype(jnp.float32) + low[rows].astype(jnp.float32)

        for b in range(blocks):
            own_rows[b * sites : (b + 1) * sites] = value(b * span + window - edge - b * length, sites)
            at = blocks * sites + b * cols
            own_rows[at : at + cols] = both[:, b * length : (b + 1) * length]
        starts = [
            [b * span + at for b, (lo, hi, _) in enumerate(cuts_of(blocks, length, sites, span, last)) for at in range(lo, hi, edge)]
            for last in (True, False)
        ]
        row = lax.axis_index("row")
        for chunk, (on_right, on_left) in enumerate(zip(*starts)):
            start = pl.multiple_of(jnp.where(row == 0, on_right, on_left), edge)
            other_rows[chunk * edge : (chunk + 1) * edge] = value(start, edge)


def keep(ref, start, value):
    cols, width = value.shape
    high, low = halves(value)
    ref[:cols, pl.ds(start, width)] = high
    ref[cols:, pl.ds(start, width)] = low


def load(sides, pick, own, halo, ref):
    sites = own.shape[1]
    keep(ref, halo, own)
    for side in range(sides):
        on_right = 1 - jnp.minimum(lax.axis_index("row"), 1).astype(jnp.int32) if sides == 1 else side
        start = pl.multiple_of((1 - on_right) * (sites - halo), 128)
        keep(ref, pl.multiple_of(on_right * (halo + sites), 128), pick(side, pl.ds(start, halo)))


def plain(next_in):
    return lambda side, cut: next_in[:, cut] if len(next_in.shape) == 2 else next_in[side, :, cut]


def top_kernel(mine, sides, next_in, own_in, const, near_high, near_low, _upper, _lower, upper, lower, *rest):
    mid = rest[-1]
    sites = lower.shape[1]
    length = near_high.shape[1]
    blocks = sites // length
    window = near_high.shape[0] // blocks
    edge = (window - length) // 2

    @pl.when(lax.axis_index("tm") == 2 * mine)
    def _():
        mid[...] = jnp.zeros_like(mid)
        load(sides, lambda side, cut: next_in[side], own_in[...], edge, mid)
        upper[...] = own_in[...]
        for b in range(blocks):
            at, rows = slice(b * length, (b + 1) * length), slice(b * window, (b + 1) * window)
            product = stacked_dot(mid, slice(b * length, b * length + window), near_high[rows], near_low[rows])
            lower[:, at] = const[:, at] - product
        if len(rest) > 1:
            halo = rest[0].shape[1]
            start = pl.multiple_of(jnp.where(lax.axis_index("row") == 0, sites - halo, 0), 128)
            rest[0][...] = lower[:, pl.ds(start, halo)]


def step(both, high, low, late, lower):
    blocks = lower.shape[1] // high.shape[1]
    length, span = high.shape[1], high.shape[0] // blocks
    for b in range(blocks):
        at, rows = slice(b * length, (b + 1) * length), slice(b * span, (b + 1) * span)
        lower[:, at] = both[:, at] + stacked_dot(late, slice(b * length, b * length + span), high[rows], low[rows])


def load_rims(sides, next_in, sites, halo, late):
    for side in range(sides):
        on_right = 1 - jnp.minimum(lax.axis_index("row"), 1).astype(jnp.int32) if sides == 1 else side
        if next_in.shape[-1] == halo:
            value = next_in[...]
        else:
            value = plain(next_in)(side, pl.ds(pl.multiple_of((1 - on_right) * (sites - halo), 128), halo))
        keep(late, pl.multiple_of(on_right * (halo + sites), 128), value)


def rim_kernel(mine, sides, next_in, both, high, low, _late, late, base):
    sites, length = base.shape[1], high.shape[1]
    blocks = sites // length
    span = high.shape[0] // blocks
    halo = (late.shape[1] - sites) // 2
    edge = halo - length

    @pl.when(lax.axis_index("tm") == 2 * mine)
    def _():
        load_rims(sides, next_in, sites, halo, late)
        cuts = [cuts_of(blocks, length, sites, span, last) for last in (False, True)]
        for b in range(blocks):
            value = both[:, b * length : (b + 1) * length]
            if sides == 2:
                for lo, hi, _ in (cuts[0][b], cuts[1][b]):
                    rows = slice(b * span + lo, b * span + hi)
                    value += stacked_dot(late, slice(b * length + lo, b * length + hi), high[rows], low[rows])
            else:
                on_left = lax.axis_index("row") != 0
                counts = [cut[b][1] - cut[b][0] for cut in cuts]
                for chunk in range(0, max(counts), edge):
                    starts = [cut[b][0] + chunk if chunk < count else 0 for cut, count in zip(cuts, counts)]
                    start = pl.multiple_of(jnp.where(on_left, starts[0], starts[1]), edge)
                    rows = pl.ds(b * span + start, edge)
                    product = stacked_dot(late, pl.ds(b * length + start, edge), high[rows], low[rows])
                    if chunk >= min(counts):
                        product = jnp.where(on_left == (counts[0] > counts[1]), product, 0.0)
                    value += product
            base[:, b * length : (b + 1) * length] = value


def add_own(own_in, base, high, low, late, lower):
    sites, length = lower.shape[1], high.shape[1]
    blocks = sites // length
    span = high.shape[0] // blocks
    halo = (late.shape[1] - sites) // 2
    keep(late, halo, own_in[...])
    for b in range(blocks):
        at, start = slice(b * length, (b + 1) * length), halo - b * length
        rows = slice(b * span + start, b * span + start + sites)
        lower[:, at] = base[:, at] + stacked_dot(late, slice(halo, halo + sites), high[rows], low[rows])


def chain_kernel(mine, own_in, base, high, low, _late, _lower, late, lower, near=None):
    @pl.when(lax.axis_index("tm") == 2 * mine)
    def _():
        add_own(own_in, base, high, low, late, lower)
        if near is not None:
            sites, halo = lower.shape[1], near.shape[1]
            start = pl.multiple_of(jnp.where(lax.axis_index("row") == 0, sites - halo, 0), 128)
            near[...] = lower[:, pl.ds(start, halo)]


def rows_kernel(own_rows, other_rows, own_high, own_low, other_high, other_low):
    own_high[...], own_low[...] = halves(own_rows[: own_high.shape[0]])
    other_high[...], other_low[...] = halves(other_rows[...])


def add_parts(lower, own_rows, own_high, own_low, other_high, other_low, to_next, to_own, mid, far_mid, span):
    cols, sites = lower.shape
    length = own_rows.shape[1]
    blocks = sites // length
    halo = to_own.shape[1] - sites
    edge = halo - length
    row = lax.axis_index("row")
    keep(mid, 0, lower[...])
    near = pl.multiple_of(jnp.where(row == 0, sites - halo, 0), edge)
    for b in range(blocks):
        at, rows = slice(b * length, (b + 1) * length), slice(b * sites, (b + 1) * sites)
        const = slice(blocks * sites + b * cols, blocks * sites + (b + 1) * cols)
        to_own[:, at] = own_rows[const] + stacked_dot(mid, slice(0, sites), own_high[rows], own_low[rows])
    to_next[:, :halo] = to_own[:, pl.ds(near, halo)]
    pieces = []
    for rows, from_last, from_first in (
        (slice(0, edge), sites - halo, 0),
        (slice(edge, halo), sites - length, 0),
        (slice(halo, halo + edge), sites - edge, length),
    ):
        source = pl.multiple_of(jnp.where(row == 0, from_last, from_first), edge)
        pieces.append(stacked_dot(mid, pl.ds(source, rows.stop - rows.start), other_high[rows], other_low[rows]))
    far_mid[:, :length] = pieces[0] + jnp.where(row == 0, pieces[1], 0.0)
    far_mid[:, length:] = pieces[2] + jnp.where(row == 0, 0.0, pieces[1])
    to_next[:, halo:] = far_mid[...]
    away = pl.multiple_of(jnp.where(row == 0, 0, sites - halo), edge)
    to_own[:, sites:] = far_mid[:, pl.ds(away, halo)]


def jump_kernel(mine, own_in, base, high, low, *rest):
    ship, (_late, _lower, late, lower, to_next, to_own, to_last, *scratch) = rest[:-9], rest[-9:]

    @pl.when(lax.axis_index("tm") == 2 * mine)
    def _():
        add_own(own_in, base, high, low, late, lower)
        add_parts(lower, *ship, to_next, to_own, *scratch, high.shape[0] * high.shape[1] // own_in.shape[1])
        to_last[...] = to_next[...]

    @pl.when(lax.axis_index("tm") != 2 * mine)
    def _():
        for part in (to_next, to_own, to_last):
            part[...] = jnp.zeros_like(part)


def parts_kernel(mine, span, lower, *rest):
    ship, parts = rest[:-4], rest[-4:]

    @pl.when(lax.axis_index("tm") == 2 * mine)
    def _():
        add_parts(lower, *ship, *parts, span)

    @pl.when(lax.axis_index("tm") != 2 * mine)
    def _():
        for part in parts[:2]:
            part[...] = jnp.zeros_like(part)


def last_kernel(jumps, both, high, low, late, _lower, lower):
    device = lax.axis_index("tm")
    pl.when((device == 0) | (device == 2) if jumps else device == 0)(lambda: step(both, high, low, late, lower))


def upper_kernel(sides, top, *rest):
    far, far_high, far_low, _late, _upper, late, upper = rest[-7:]
    cols, sites = upper.shape
    length = far.shape[1]
    blocks = sites // length
    window = far_high.shape[0] // blocks
    halo = (late.shape[1] - sites) // 2
    at_window = halo - (window - length) // 2
    messages = rest[:-7]

    if len(messages) == 2:

        @pl.when(lax.axis_index("tm") == 0)
        def _():
            load(sides, plain(messages[1]), messages[0][...], halo, late)

    sums = ((messages[0], messages[2], messages[1]), messages[3:]) if len(messages) > 2 else ()
    for mine, (*next_in, own_in) in enumerate(sums):

        @pl.when(lax.axis_index("tm") == 2 * mine)
        def _():
            from_next = next_in[0][...] + next_in[1][...] if len(next_in) == 2 else next_in[0][...]
            own = own_in[:, :sites] + from_next[:, halo:]
            near = own_in[:, sites:] + from_next[:, :halo]
            load(sides, lambda side, cut: near, own, halo, late)

    @pl.when(lax.axis_index("tm") != 2 * top)
    def _():
        for b in range(blocks):
            rows = slice(b * window, (b + 1) * window)
            at = blocks * window + b * cols
            start = at_window + b * length
            upper[:, b * length : (b + 1) * length] = far[at : at + cols] - stacked_dot(
                late, slice(start, start + window), far_high[rows], far_low[rows]
            )


def local(normals, inv_diag, lag_coupling, fill_mask):
    times, rows = lax.axis_size("tm"), lax.axis_size("row")
    device = lax.axis_index("tm")
    cols, sites = normals.shape[1:]
    blocks, length = inv_diag.shape[1:3]
    window = lag_coupling.shape[2]
    edge = (window - length) // 2
    halo = length + edge
    sides = 1 if rows == 2 else 2
    pairs = times // 2
    f32, bf16 = jnp.float32, jnp.bfloat16
    shape = jax.ShapeDtypeStruct

    def link(source, target):
        return [(s * rows + r, t * rows + r) for s, t in zip(source, target) for r in range(rows)]

    def cross(value, source, target, split=False):
        if sides == 1:
            perm = [(s * rows + r, t * rows + 1 - r) for s, t in zip(source, target) for r in range(2)]
            return lax.ppermute(value, BOTH, perm)
        moved = []
        for side, step in enumerate((1, -1)):
            perm = [
                (s * rows + r, t * rows + r + step)
                for s, t in zip(source, target)
                for r in range(rows)
                if 0 <= r + step < rows
            ]
            moved.append(lax.ppermute(value[side : side + 1] if split else value[None], BOTH, perm))
        return jnp.concatenate(moved)

    tall = blocks * window
    jump = 2
    jumps = rows == 2 and pairs > 5 and blocks == 2
    const, inv_high, inv_low = pl.pallas_call(
        const_kernel,
        out_shape=(
            shape((cols, sites), f32),
            shape((blocks, length, length), bf16), shape((blocks, length, length), bf16),
        ),
        in_specs=[HBM] * 2,
        out_specs=(VMEM,) * 3,
        scratch_shapes=[
            pltpu.VMEM(normals.shape[1:], f32),
            pltpu.VMEM(inv_diag.shape[1:], f32),
            pltpu.SemaphoreType.DMA((1 + blocks,)),
        ],
        compiler_params=PARAMS,
    )(*[pltpu.with_memory_space_constraint(a, pltpu.HBM) for a in (normals, inv_diag)])
    const_rim = pl.pallas_call(
        functools.partial(rim_of_kernel, sides),
        out_shape=shape((sides, cols, edge), f32),
        in_specs=[VMEM],
        out_specs=VMEM,
        compiler_params=PARAMS,
        cost_estimate=pl.CostEstimate(flops=5 * 10**9, bytes_accessed=0, transcendentals=0),
    )(const)
    again = pl.pallas_call(
        copy_kernel,
        out_shape=shape((cols, sites), f32),
        in_specs=[VMEM] * 2,
        out_specs=VMEM,
        compiler_params=PARAMS,
    )(const, const_rim)
    odd, even = range(1, times, 2), range(0, times, 2)
    first_next = cross(const_rim, odd[-1:], even[-1:], True)
    first_own = lax.ppermute(again, BOTH, link(odd[-1:], even[-1:]))

    def fused(late, extra, after=()):
        return pl.pallas_call(
            functools.partial(fuse_kernel, (2 * pairs - 4, late)),
            out_shape=(shape((tall, length), bf16), shape((tall, length), bf16), *extra),
            in_specs=[VMEM] * (5 + len(after)),
            out_specs=(VMEM,) * (2 + len(extra)),
            compiler_params=PARAMS,
            cost_estimate=pl.CostEstimate(
                flops=(6 if late else 150) * (tall + cols * blocks) * length * length, bytes_accessed=0, transcendentals=0
            ),
        )(fill_mask, const, inv_high, inv_low, lag_coupling, *after)

    near_high, near_low, near = fused(False, (shape((tall + blocks * cols, length), f32),))
    edges = pl.pallas_call(
        functools.partial(edge_kernel, sides, blocks, cols),
        out_shape=shape((sides, window + cols, edge), f32),
        in_specs=[VMEM],
        out_specs=VMEM,
        compiler_params=PARAMS,
    )(near)
    near = pl.pallas_call(
        lambda _own, _edges, own: None,
        out_shape=shape(near.shape, f32),
        in_specs=[VMEM] * 2,
        out_specs=VMEM,
        input_output_aliases={0: 0},
        compiler_params=PARAMS,
    )(near, edges)
    rim = cross(edges, odd[:-1], even[:-1], True)
    far = lax.ppermute(near, BOTH, link(odd[:-1], even[:-1]))

    blank = jnp.zeros((cols, sites), f32)
    near_shape = (shape((cols, halo), f32),) if sides == 1 else ()
    upper, lower, *near = pl.pallas_call(
        functools.partial(top_kernel, pairs - 1, sides),
        out_shape=(shape((cols, sites), f32),) * 2 + near_shape,
        in_specs=[VMEM] * 7,
        out_specs=(VMEM,) * (2 + len(near_shape)),
        scratch_shapes=[pltpu.VMEM((2 * cols, sites + 2 * edge), bf16)],
        input_output_aliases={5: 0, 6: 1},
        compiler_params=PARAMS,
        cost_estimate=pl.CostEstimate(flops=50 * 10**9, bytes_accessed=0, transcendentals=0),
    )(first_next, first_own, const, near_high, near_low, blank, blank)
    far_high, far_low = pl.pallas_call(
        split_kernel,
        out_shape=(shape((tall, length), bf16), shape((tall, length), bf16)),
        in_specs=[VMEM],
        out_specs=(VMEM,) * 2,
        compiler_params=PARAMS,
    )(far)
    packs = (shape((blocks * (sites + cols), length), f32), shape((halo + edge, length), f32)) if jumps else ()

    def pair_matrix(first, jumps, packs, mine):
        return pl.pallas_call(
            functools.partial(pair_kernel, (pairs - 2, first), jumps),
            out_shape=(
                shape((2 * tall, length), bf16), shape((2 * tall, length), bf16), shape((cols, sites), f32), *packs
            ),
            in_specs=[VMEM] * 7,
            out_specs=(VMEM,) * (3 + len(packs)),
            scratch_shapes=[pltpu.VMEM((2 * window, length), f32)],
            compiler_params=PARAMS,
            cost_estimate=pl.CostEstimate(flops=10**9, bytes_accessed=0, transcendentals=0),
        )(far, rim, far_high, far_low, *mine, const)

    early = pair_matrix(True, False, (), fused(True, (), (lower,)))
    high, low, both, *packs = pair_matrix(False, jumps, packs, (near_high, near_low))
    if jumps:
        source, target = [2 * jump - 2, 2 * jump], [2 * jump, 2 * jump + 2]
        own_rows = lax.ppermute(packs[0], BOTH, link(source, target))
        other_rows = cross(packs[1], source, target)
        ship = pl.pallas_call(
            rows_kernel,
            out_shape=(shape((blocks * sites, length), bf16),) * 2 + (shape(other_rows.shape, bf16),) * 2,
            in_specs=[VMEM] * 2,
            out_specs=(VMEM,) * 4,
            compiler_params=PARAMS,
        )(own_rows, other_rows)

    def turn(kernel, given, state, scratch=(), extra=(), flops=0):
        return pl.pallas_call(
            kernel,
            out_shape=tuple(shape(v.shape, v.dtype) for v in state) + tuple(extra),
            in_specs=[VMEM] * (len(given) + len(state)),
            out_specs=(VMEM,) * (len(state) + len(extra)),
            scratch_shapes=list(scratch),
            input_output_aliases={len(given) + i: i for i in range(len(state))},
            compiler_params=PARAMS,
            cost_estimate=pl.CostEstimate(flops=flops, bytes_accessed=0, transcendentals=0) if flops else None,
        )(*given, *state)

    parts = (shape((cols, sites + halo), f32),) * 2
    parts_scratch = [pltpu.VMEM((2 * cols, sites), bf16), pltpu.VMEM((cols, sites), f32)]
    late = jnp.zeros((2 * cols, sites + 2 * halo), bf16)
    mine = pairs - 1
    while mine > 0:
        if jumps and mine == jump:
            source, target = [2 * mine], [2 * mine - 4]
            first_in = lax.ppermute(to_next, BOTH, [(2 * source[0] + 1, 2 * target[0])])
            own_in = lax.ppermute(to_own, BOTH, link(source, target))
            next_in = lax.ppermute(to_last, BOTH, [(2 * source[0], 2 * target[0] + 1)])
            break
        source, target = [2 * mine], [2 * mine - 2]
        next_in = cross(near[0] if near else lower, source, target)
        own_in = lax.ppermute(lower, BOTH, link(source, target))
        if jumps and mine == jump + 1:
            beside = pl.pallas_call(
                functools.partial(parts_kernel, mine, 2 * window),
                out_shape=parts,
                in_specs=[VMEM] * 6,
                out_specs=(VMEM,) * 2,
                scratch_shapes=parts_scratch,
                compiler_params=PARAMS,
            )(lower, own_rows, *ship)
            source, target = [2 * mine], [2 * mine - 4]
            beside_next = cross(beside[0], source, target)
            beside_own = lax.ppermute(beside[1], BOTH, link(source, target))
        mine -= 1
        if mine == 0:
            break
        here = early if mine == pairs - 2 else (high, low, both)
        late, base = turn(
            functools.partial(rim_kernel, mine, sides),
            (next_in, here[2], *here[:2]),
            (late,),
            extra=[shape((cols, sites), f32)],
        )
        if jumps and mine == jump:
            late, lower, to_next, to_own, to_last = turn(
                functools.partial(jump_kernel, mine),
                (own_in, base, high, low, own_rows, *ship),
                (late, lower),
                parts_scratch,
                parts + parts[:1],
            )
        else:
            late, lower, *near = turn(
                functools.partial(chain_kernel, mine),
                (own_in, base, *here[:2]),
                (late, lower),
                extra=[shape((cols, halo), f32)] if sides == 1 and mine == pairs - 2 else [],
                flops=50 * 10**9 if jumps and mine == pairs - 3 else 0,
            )
    given = (first_in, own_in, next_in, beside_next, beside_own) if jumps else (own_in, next_in)
    late, upper = turn(
        functools.partial(upper_kernel, sides, pairs - 1), (*given, far, far_high, far_low), (late, upper)
    )
    returned = lax.ppermute(upper, BOTH, link(even, odd))
    lower = pl.pallas_call(
        functools.partial(last_kernel, jumps),
        out_shape=shape(lower.shape, f32),
        in_specs=[VMEM] * 5,
        out_specs=VMEM,
        input_output_aliases={4: 0},
        compiler_params=PARAMS,
        cost_estimate=pl.CostEstimate(flops=12 * cols * tall * length, bytes_accessed=8 * tall * length, transcendentals=0),
    )(both, high, low, late, lower)
    return jnp.where(device % 2 == 0, lower, returned)[None]


def solution(mesh):
    placed = (
        P("tm", None, "row"),
        P("tm", "row", None, None),
        P("tm", "row", None, None),
        P("tm", "row", None),
    )
    return jax.shard_map(
        local, mesh=mesh, in_specs=placed, out_specs=P("tm", None, "row"), check_vma=False
    )
```

```python
import functools

import jax
import jax.numpy as jnp
from jax import lax
from jax.experimental import pallas as pl
from jax.experimental.pallas import tpu as pltpu
from jax.sharding import PartitionSpec as P

BOTH = ("tm", "row")
VMEM = pl.BlockSpec(memory_space=pltpu.VMEM)
HBM = pl.BlockSpec(memory_space=pltpu.HBM)
PARAMS = pltpu.CompilerParams(vmem_limit_bytes=32 * 1024 * 1024)


def halves(value):
    high = value.astype(jnp.bfloat16)
    low = (value - high.astype(jnp.float32)).astype(jnp.bfloat16)
    return high, low


def dot(a, b):
    return jnp.dot(a, b, preferred_element_type=jnp.float32)


def stacked_dot(pair, cols, high, low):
    rows = pair.shape[0] // 2
    wide = dot(pair[:, cols], high)
    return wide[:rows] + wide[rows:] + dot(pair[:rows, cols], low)


def triple(high, low, inv_high, inv_low):
    return dot(high, inv_high) + dot(low, inv_high) + dot(high, inv_low)


def put_rim(sides, rim, columns):
    if sides == 1:
        row = lax.axis_index("row")

        @pl.when(row == 0)
        def _():
            rim[0] = columns(True)

        @pl.when(row != 0)
        def _():
            rim[0] = columns(False)
    else:
        rim[0] = columns(True)
        rim[1] = columns(False)


def const_kernel(normals, inv, const, inv_high, inv_low, normals_in, inv_in, sems):
    blocks, length = inv.shape[1], inv.shape[2]
    moves = [pltpu.make_async_copy(normals.at[0], normals_in, sems.at[0])]
    for b in range(blocks):
        moves.append(pltpu.make_async_copy(inv.at[0, b], inv_in.at[b], sems.at[1 + b]))
    for move in moves:
        move.start()
    moves[0].wait()
    for b in range(blocks):
        at = slice(b * length, (b + 1) * length)
        high, low = halves(normals_in[:, at])
        moves[1 + b].wait()
        inv_high[b], inv_low[b] = halves(inv_in[b])
        const[:, at] = triple(high, low, inv_high[b], inv_low[b])


def again_kernel(const, again):
    again[...] = const[...]


def fuse_kernel(late, *refs):
    here = lax.axis_index("tm") == late[0]
    given = refs[:5] + refs[6:] if late[1] else refs
    pl.when(here if late[1] else jnp.logical_not(here))(lambda: make_fused(*given))


def make_fused(mask, const, inv_high, inv_low, lag, near_high, near_low, own=None):
    blocks, window, length = lag.shape[1:]
    edge = (window - length) // 2
    cols = const.shape[0]
    cuts = (0, edge, edge + length, window)
    flags = mask[0].astype(jnp.float32)
    for b in range(blocks):
        at = blocks * window + b * cols
        if own is not None:
            own[at : at + cols] = const[:, b * length : (b + 1) * length]
        for part in range(3):
            lo, hi = cuts[part], cuts[part + 1]
            rows = slice(b * window + lo, b * window + hi)
            high, low = halves(lag[0, b, lo:hi] * flags[b : b + 1, part : part + 1])
            value = triple(high, low, inv_high[b], inv_low[b])
            if own is not None:
                own[rows] = value
            near_high[rows], near_low[rows] = halves(value)


def edge_kernel(sides, blocks, cols, own, rim):
    length, edge = own.shape[1], rim.shape[2]
    window = length + 2 * edge

    def columns(last):
        b = blocks - 1 if last else 0
        cut = slice(length - edge, length) if last else slice(0, edge)
        at = blocks * window + b * cols
        return jnp.concatenate([own[b * window : (b + 1) * window, cut], own[at : at + cols, cut]])

    put_rim(sides, rim, columns)


def split_kernel(far, far_high, far_low):
    far_high[...], far_low[...] = halves(far[: far_high.shape[0]])


def cuts_of(blocks, length, sites, span, last):
    packed, cuts = 0, []
    for b in range(blocks):
        start = span // 2 - length // 2 - b * length
        lo, hi = (start + sites, span) if last else (0, start)
        cuts.append((lo, hi, packed))
        packed += hi - lo
    return cuts


def pair_kernel(first, jump, *refs):
    here = lax.axis_index("tm") == 2 * first[0]
    pl.when(here if first[1] else jnp.logical_not(here))(lambda: make_pair(jump, *refs))


def make_pair(jump, far, rim, far_high, far_low, near_high, near_low, const, high, low, both, *rest):
    cols, sites = const.shape
    length = far.shape[1]
    blocks = sites // length
    window = near_high.shape[0] // blocks
    edge = (window - length) // 2
    span = 2 * window
    tall = blocks * window
    total = rest[-1]
    if rim.shape[0] == 1:
        flag = jnp.minimum(lax.axis_index("row"), 1).astype(jnp.float32)
        left, right = rim[0] * flag, rim[0] * (1 - flag)
    else:
        left, right = rim[0], rim[1]
    left_pair, right_pair = halves(left[:window]), halves(right[:window])
    for b in range(blocks):
        here = slice(b * window, (b + 1) * window)
        column = slice(b * length, (b + 1) * length)

        def part(lo, hi):
            rows = slice(b * window + lo, b * window + hi)
            return near_high[rows], near_low[rows]

        def constant(block):
            if block < 0:
                return left[window:]
            if block == blocks:
                return right[window:]
            return far[tall + block * cols : tall + (block + 1) * cols]

        if b > 0:
            before = slice((b - 1) * window, b * window)
            low_pair = far_high[before, length - edge :], far_low[before, length - edge :]
            low_const = constant(b - 1)[:, length - edge :]
        else:
            low_pair, low_const = left_pair, constant(-1)
        if b + 1 < blocks:
            after = slice((b + 1) * window, (b + 2) * window)
            high_pair = far_high[after, :edge], far_low[after, :edge]
            high_const = constant(b + 1)[:, :edge]
        else:
            high_pair, high_const = right_pair, constant(blocks)
        first = triple(*low_pair, *part(0, edge))
        middle = triple(far_high[here], far_low[here], *part(edge, edge + length))
        last = triple(*high_pair, *part(edge + length, window))
        total[:window] = first
        total[window:] = last
        total[length : length + window] += middle
        high[b * span : (b + 1) * span], low[b * span : (b + 1) * span] = halves(total[...])
        both[:, column] = const[:, column] - (
            triple(*halves(low_const), *part(0, edge))
            + triple(*halves(constant(b)), *part(edge, edge + length))
            + triple(*halves(high_const), *part(edge + length, window))
        )
    if jump:
        own_rows, other_rows = rest[:2]

        def value(start, count):
            rows = pl.ds(start, count)
            return high[rows].astype(jnp.float32) + low[rows].astype(jnp.float32)

        for b in range(blocks):
            own_rows[b * sites : (b + 1) * sites] = value(b * span + window - edge - b * length, sites)
            at = blocks * sites + b * cols
            own_rows[at : at + cols] = both[:, b * length : (b + 1) * length]
        starts = [
            [b * span + at for b, (lo, hi, _) in enumerate(cuts_of(blocks, length, sites, span, last)) for at in range(lo, hi, edge)]
            for last in (True, False)
        ]
        row = lax.axis_index("row")
        for chunk, (on_right, on_left) in enumerate(zip(*starts)):
            start = pl.multiple_of(jnp.where(row == 0, on_right, on_left), edge)
            other_rows[chunk * edge : (chunk + 1) * edge] = value(start, edge)


def keep(ref, start, value):
    cols, width = value.shape
    high, low = halves(value)
    ref[:cols, pl.ds(start, width)] = high
    ref[cols:, pl.ds(start, width)] = low


def load(sides, pick, own, halo, ref):
    sites = own.shape[1]
    keep(ref, halo, own)
    for side in range(sides):
        on_right = 1 - jnp.minimum(lax.axis_index("row"), 1).astype(jnp.int32) if sides == 1 else side
        start = pl.multiple_of((1 - on_right) * (sites - halo), 128)
        keep(ref, pl.multiple_of(on_right * (halo + sites), 128), pick(side, pl.ds(start, halo)))


def plain(next_in):
    return lambda side, cut: next_in[:, cut] if len(next_in.shape) == 2 else next_in[side, :, cut]


def top_kernel(mine, sides, next_in, own_in, const, near_high, near_low, _upper, _lower, upper, lower, *rest):
    mid = rest[-1]
    sites = lower.shape[1]
    length = near_high.shape[1]
    blocks = sites // length
    window = near_high.shape[0] // blocks
    edge = (window - length) // 2

    @pl.when(lax.axis_index("tm") == 2 * mine)
    def _():
        mid[...] = jnp.zeros_like(mid)
        load(sides, plain(next_in), own_in[...], edge, mid)
        upper[...] = own_in[...]
        for b in range(blocks):
            at, rows = slice(b * length, (b + 1) * length), slice(b * window, (b + 1) * window)
            product = stacked_dot(mid, slice(b * length, b * length + window), near_high[rows], near_low[rows])
            lower[:, at] = const[:, at] - product
        if len(rest) > 1:
            halo = rest[0].shape[1]
            start = pl.multiple_of(jnp.where(lax.axis_index("row") == 0, sites - halo, 0), 128)
            rest[0][...] = lower[:, pl.ds(start, halo)]


def step(both, high, low, late, lower):
    blocks = lower.shape[1] // high.shape[1]
    length, span = high.shape[1], high.shape[0] // blocks
    for b in range(blocks):
        at, rows = slice(b * length, (b + 1) * length), slice(b * span, (b + 1) * span)
        lower[:, at] = both[:, at] + stacked_dot(late, slice(b * length, b * length + span), high[rows], low[rows])


def load_rims(sides, next_in, sites, halo, late):
    for side in range(sides):
        on_right = 1 - jnp.minimum(lax.axis_index("row"), 1).astype(jnp.int32) if sides == 1 else side
        if next_in.shape[-1] == halo:
            value = next_in[...]
        else:
            value = plain(next_in)(side, pl.ds(pl.multiple_of((1 - on_right) * (sites - halo), 128), halo))
        keep(late, pl.multiple_of(on_right * (halo + sites), 128), value)


def rim_kernel(mine, sides, next_in, both, high, low, _late, late, base):
    sites, length = base.shape[1], high.shape[1]
    blocks = sites // length
    span = high.shape[0] // blocks
    halo = (late.shape[1] - sites) // 2
    edge = halo - length

    @pl.when(lax.axis_index("tm") == 2 * mine)
    def _():
        load_rims(sides, next_in, sites, halo, late)
        if sides == 1 and blocks == 2:
            left = lax.axis_index("row") != 0
            wide = halo - edge
            pieces = []
            for count, on_left, on_right in (
                (edge, (0, 0), (span - edge, span - edge)),
                (edge, (span, length), (2 * span - halo, length + span - halo)),
                (wide, (edge, edge), (2 * span - wide, length + span - wide)),
            ):
                rows, source = (pl.multiple_of(jnp.where(left, x, y), edge) for x, y in zip(on_left, on_right))
                cut = pl.ds(rows, count)
                pieces.append(stacked_dot(late, pl.ds(source, count), high[cut], low[cut]))
            base[:, :length] = both[:, :length] + pieces[0] + jnp.where(left, pieces[2], 0.0)
            base[:, length:] = both[:, length:] + pieces[1] + jnp.where(left, 0.0, pieces[2])
            return
        cuts = [cuts_of(blocks, length, sites, span, last) for last in (False, True)]
        for b in range(blocks):
            value = both[:, b * length : (b + 1) * length]
            if sides == 2:
                for lo, hi, _ in (cuts[0][b], cuts[1][b]):
                    rows = slice(b * span + lo, b * span + hi)
                    value += stacked_dot(late, slice(b * length + lo, b * length + hi), high[rows], low[rows])
            else:
                on_left = lax.axis_index("row") != 0
                counts = [cut[b][1] - cut[b][0] for cut in cuts]
                for chunk in range(0, max(counts), edge):
                    starts = [cut[b][0] + chunk if chunk < count else 0 for cut, count in zip(cuts, counts)]
                    start = pl.multiple_of(jnp.where(on_left, starts[0], starts[1]), edge)
                    rows = pl.ds(b * span + start, edge)
                    product = stacked_dot(late, pl.ds(b * length + start, edge), high[rows], low[rows])
                    if chunk >= min(counts):
                        product = jnp.where(on_left == (counts[0] > counts[1]), product, 0.0)
                    value += product
            base[:, b * length : (b + 1) * length] = value


def add_own(own_in, base, high, low, late, lower):
    sites, length = lower.shape[1], high.shape[1]
    blocks = sites // length
    span = high.shape[0] // blocks
    halo = (late.shape[1] - sites) // 2
    keep(late, halo, own_in[...])
    for b in range(blocks):
        at, start = slice(b * length, (b + 1) * length), halo - b * length
        rows = slice(b * span + start, b * span + start + sites)
        lower[:, at] = base[:, at] + stacked_dot(late, slice(halo, halo + sites), high[rows], low[rows])


def chain_kernel(mine, own_in, base, high, low, _late, _lower, late, lower, near=None):
    @pl.when(lax.axis_index("tm") == 2 * mine)
    def _():
        add_own(own_in, base, high, low, late, lower)
        if near is not None:
            sites, halo = lower.shape[1], near.shape[1]
            start = pl.multiple_of(jnp.where(lax.axis_index("row") == 0, sites - halo, 0), 128)
            near[...] = lower[:, pl.ds(start, halo)]


def rows_kernel(own_rows, other_rows, own_high, own_low, other_high, other_low):
    own_high[...], own_low[...] = halves(own_rows[: own_high.shape[0]])
    other_high[...], other_low[...] = halves(other_rows[...])


def add_parts(lower, own_rows, own_high, own_low, other_high, other_low, to_next, to_own, mid, far_mid, span):
    cols, sites = lower.shape
    length = own_rows.shape[1]
    blocks = sites // length
    halo = to_own.shape[1] - sites
    edge = halo - length
    row = lax.axis_index("row")
    keep(mid, 0, lower[...])
    near = pl.multiple_of(jnp.where(row == 0, sites - halo, 0), edge)
    for b in range(blocks):
        at, rows = slice(b * length, (b + 1) * length), slice(b * sites, (b + 1) * sites)
        const = slice(blocks * sites + b * cols, blocks * sites + (b + 1) * cols)
        to_own[:, at] = own_rows[const] + stacked_dot(mid, slice(0, sites), own_high[rows], own_low[rows])
    to_next[:, :halo] = to_own[:, pl.ds(near, halo)]
    pieces = []
    for rows, from_last, from_first in (
        (slice(0, edge), sites - halo, 0),
        (slice(edge, halo), sites - length, 0),
        (slice(halo, halo + edge), sites - edge, length),
    ):
        source = pl.multiple_of(jnp.where(row == 0, from_last, from_first), edge)
        pieces.append(stacked_dot(mid, pl.ds(source, rows.stop - rows.start), other_high[rows], other_low[rows]))
    far_mid[:, :length] = pieces[0] + jnp.where(row == 0, pieces[1], 0.0)
    far_mid[:, length:] = pieces[2] + jnp.where(row == 0, 0.0, pieces[1])
    to_next[:, halo:] = far_mid[...]
    away = pl.multiple_of(jnp.where(row == 0, 0, sites - halo), edge)
    to_own[:, sites:] = far_mid[:, pl.ds(away, halo)]


def jump_kernel(mine, own_in, base, high, low, *rest):
    ship, (_late, _lower, late, lower, to_next, to_own, to_last, *scratch) = rest[:-9], rest[-9:]

    @pl.when(lax.axis_index("tm") == 2 * mine)
    def _():
        add_own(own_in, base, high, low, late, lower)
        add_parts(lower, *ship, to_next, to_own, *scratch, high.shape[0] * high.shape[1] // own_in.shape[1])
        to_last[...] = to_next[...]

    @pl.when(lax.axis_index("tm") != 2 * mine)
    def _():
        for part in (to_next, to_own, to_last):
            part[...] = jnp.zeros_like(part)


def parts_kernel(mine, span, lower, *rest):
    ship, parts = rest[:-4], rest[-4:]

    @pl.when(lax.axis_index("tm") == 2 * mine)
    def _():
        add_parts(lower, *ship, *parts, span)

    @pl.when(lax.axis_index("tm") != 2 * mine)
    def _():
        for part in parts[:2]:
            part[...] = jnp.zeros_like(part)


def last_kernel(jumps, both, high, low, late, _lower, lower):
    device = lax.axis_index("tm")
    pl.when((device == 0) | (device == 2) if jumps else device == 0)(lambda: step(both, high, low, late, lower))


def upper_kernel(sides, top, *rest):
    far, far_high, far_low, _late, _upper, late, upper = rest[-7:]
    cols, sites = upper.shape
    length = far.shape[1]
    blocks = sites // length
    window = far_high.shape[0] // blocks
    halo = (late.shape[1] - sites) // 2
    at_window = halo - (window - length) // 2
    messages = rest[:-7]

    if len(messages) == 2:

        @pl.when(lax.axis_index("tm") == 0)
        def _():
            load(sides, plain(messages[1]), messages[0][...], halo, late)

    sums = ((messages[0], messages[2], messages[1]), messages[3:]) if len(messages) > 2 else ()
    for mine, (*next_in, own_in) in enumerate(sums):

        @pl.when(lax.axis_index("tm") == 2 * mine)
        def _():
            from_next = next_in[0][...] + next_in[1][...] if len(next_in) == 2 else next_in[0][...]
            own = own_in[:, :sites] + from_next[:, halo:]
            near = own_in[:, sites:] + from_next[:, :halo]
            load(sides, lambda side, cut: near, own, halo, late)

    @pl.when(lax.axis_index("tm") != 2 * top)
    def _():
        for b in range(blocks):
            rows = slice(b * window, (b + 1) * window)
            at = blocks * window + b * cols
            start = at_window + b * length
            upper[:, b * length : (b + 1) * length] = far[at : at + cols] - stacked_dot(
                late, slice(start, start + window), far_high[rows], far_low[rows]
            )


def local(normals, inv_diag, lag_coupling, fill_mask):
    times, rows = lax.axis_size("tm"), lax.axis_size("row")
    device = lax.axis_index("tm")
    cols, sites = normals.shape[1:]
    blocks, length = inv_diag.shape[1:3]
    window = lag_coupling.shape[2]
    edge = (window - length) // 2
    halo = length + edge
    sides = 1 if rows == 2 else 2
    pairs = times // 2
    f32, bf16 = jnp.float32, jnp.bfloat16
    shape = jax.ShapeDtypeStruct

    def link(source, target):
        return [(s * rows + r, t * rows + r) for s, t in zip(source, target) for r in range(rows)]

    def cross(value, source, target, split=False):
        if sides == 1:
            perm = [(s * rows + r, t * rows + 1 - r) for s, t in zip(source, target) for r in range(2)]
            return lax.ppermute(value, BOTH, perm)
        moved = []
        for side, step in enumerate((1, -1)):
            perm = [
                (s * rows + r, t * rows + r + step)
                for s, t in zip(source, target)
                for r in range(rows)
                if 0 <= r + step < rows
            ]
            moved.append(lax.ppermute(value[side : side + 1] if split else value[None], BOTH, perm))
        return jnp.concatenate(moved)

    tall = blocks * window
    jump = 2
    jumps = rows == 2 and pairs > 5 and blocks == 2
    const, inv_high, inv_low = pl.pallas_call(
        const_kernel,
        out_shape=(
            shape((cols, sites), f32),
            shape((blocks, length, length), bf16), shape((blocks, length, length), bf16),
        ),
        in_specs=[HBM] * 2,
        out_specs=(VMEM,) * 3,
        scratch_shapes=[
            pltpu.VMEM(normals.shape[1:], f32),
            pltpu.VMEM(inv_diag.shape[1:], f32),
            pltpu.SemaphoreType.DMA((1 + blocks,)),
        ],
        compiler_params=PARAMS,
    )(*[pltpu.with_memory_space_constraint(a, pltpu.HBM) for a in (normals, inv_diag)])
    again = pl.pallas_call(
        again_kernel,
        out_shape=shape((cols, sites), f32),
        in_specs=[VMEM],
        out_specs=VMEM,
        compiler_params=PARAMS,
        cost_estimate=pl.CostEstimate(flops=5 * 10**9, bytes_accessed=0, transcendentals=0),
    )(const)
    odd, even = range(1, times, 2), range(0, times, 2)
    first_next = cross(again, odd[-1:], even[-1:])
    first_own = lax.ppermute(const, BOTH, link(odd[-1:], even[-1:]))

    def fused(late, extra, after=()):
        return pl.pallas_call(
            functools.partial(fuse_kernel, (2 * pairs - 4, late)),
            out_shape=(shape((tall, length), bf16), shape((tall, length), bf16), *extra),
            in_specs=[VMEM] * (5 + len(after)),
            out_specs=(VMEM,) * (2 + len(extra)),
            compiler_params=PARAMS,
            cost_estimate=pl.CostEstimate(
                flops=6 * (tall + cols * blocks) * length * length, bytes_accessed=16 * tall * length, transcendentals=0
            ),
        )(fill_mask, const, inv_high, inv_low, lag_coupling, *after)

    near_high, near_low, near = fused(False, (shape((tall + blocks * cols, length), f32),))
    edges = pl.pallas_call(
        functools.partial(edge_kernel, sides, blocks, cols),
        out_shape=shape((sides, window + cols, edge), f32),
        in_specs=[VMEM],
        out_specs=VMEM,
        compiler_params=PARAMS,
    )(near)
    near = pl.pallas_call(
        lambda _own, _edges, own: None,
        out_shape=shape(near.shape, f32),
        in_specs=[VMEM] * 2,
        out_specs=VMEM,
        input_output_aliases={0: 0},
        compiler_params=PARAMS,
    )(near, edges)
    rim = cross(edges, odd[:-1], even[:-1], True)
    far = lax.ppermute(near, BOTH, link(odd[:-1], even[:-1]))

    blank = jnp.zeros((cols, sites), f32)
    near_shape = (shape((cols, halo), f32),) if sides == 1 else ()
    upper, lower, *near = pl.pallas_call(
        functools.partial(top_kernel, pairs - 1, sides),
        out_shape=(shape((cols, sites), f32),) * 2 + near_shape,
        in_specs=[VMEM] * 7,
        out_specs=(VMEM,) * (2 + len(near_shape)),
        scratch_shapes=[pltpu.VMEM((2 * cols, sites + 2 * edge), bf16)],
        input_output_aliases={5: 0, 6: 1},
        compiler_params=PARAMS,
        cost_estimate=pl.CostEstimate(flops=50 * 10**9, bytes_accessed=0, transcendentals=0),
    )(first_next, first_own, const, near_high, near_low, blank, blank)
    far_high, far_low = pl.pallas_call(
        split_kernel,
        out_shape=(shape((tall, length), bf16), shape((tall, length), bf16)),
        in_specs=[VMEM],
        out_specs=(VMEM,) * 2,
        compiler_params=PARAMS,
    )(far)
    packs = (shape((blocks * (sites + cols), length), f32), shape((halo + edge, length), f32)) if jumps else ()

    def pair_matrix(first, jumps, packs, mine):
        return pl.pallas_call(
            functools.partial(pair_kernel, (pairs - 2, first), jumps),
            out_shape=(
                shape((2 * tall, length), bf16), shape((2 * tall, length), bf16), shape((cols, sites), f32), *packs
            ),
            in_specs=[VMEM] * 7,
            out_specs=(VMEM,) * (3 + len(packs)),
            scratch_shapes=[pltpu.VMEM((2 * window, length), f32)],
            compiler_params=PARAMS,
            cost_estimate=pl.CostEstimate(flops=10**9, bytes_accessed=0, transcendentals=0),
        )(far, rim, far_high, far_low, *mine, const)

    early = pair_matrix(True, False, (), fused(True, (), (lower,)))
    high, low, both, *packs = pair_matrix(False, jumps, packs, (near_high, near_low))
    if jumps:
        source, target = [2 * jump - 2, 2 * jump], [2 * jump, 2 * jump + 2]
        own_rows = lax.ppermute(packs[0], BOTH, link(source, target))
        other_rows = cross(packs[1], source, target)
        ship = pl.pallas_call(
            rows_kernel,
            out_shape=(shape((blocks * sites, length), bf16),) * 2 + (shape(other_rows.shape, bf16),) * 2,
            in_specs=[VMEM] * 2,
            out_specs=(VMEM,) * 4,
            compiler_params=PARAMS,
        )(own_rows, other_rows)

    def turn(kernel, given, state, scratch=(), extra=(), flops=0):
        return pl.pallas_call(
            kernel,
            out_shape=tuple(shape(v.shape, v.dtype) for v in state) + tuple(extra),
            in_specs=[VMEM] * (len(given) + len(state)),
            out_specs=(VMEM,) * (len(state) + len(extra)),
            scratch_shapes=list(scratch),
            input_output_aliases={len(given) + i: i for i in range(len(state))},
            compiler_params=PARAMS,
            cost_estimate=pl.CostEstimate(flops=flops, bytes_accessed=0, transcendentals=0) if flops else None,
        )(*given, *state)

    parts = (shape((cols, sites + halo), f32),) * 2
    parts_scratch = [pltpu.VMEM((2 * cols, sites), bf16), pltpu.VMEM((cols, sites), f32)]
    late = jnp.zeros((2 * cols, sites + 2 * halo), bf16)
    mine = pairs - 1
    while mine > 0:
        if jumps and mine == jump:
            source, target = [2 * mine], [2 * mine - 4]
            first_in = lax.ppermute(to_next, BOTH, [(2 * source[0] + 1, 2 * target[0])])
            own_in = lax.ppermute(to_own, BOTH, link(source, target))
            next_in = lax.ppermute(to_last, BOTH, [(2 * source[0], 2 * target[0] + 1)])
            break
        source, target = [2 * mine], [2 * mine - 2]
        next_in = cross(near[0] if near else lower, source, target)
        own_in = lax.ppermute(lower, BOTH, link(source, target))
        if jumps and mine == jump + 1:
            beside = pl.pallas_call(
                functools.partial(parts_kernel, mine, 2 * window),
                out_shape=parts,
                in_specs=[VMEM] * 6,
                out_specs=(VMEM,) * 2,
                scratch_shapes=parts_scratch,
                compiler_params=PARAMS,
            )(lower, own_rows, *ship)
            source, target = [2 * mine], [2 * mine - 4]
            beside_next = cross(beside[0], source, target)
            beside_own = lax.ppermute(beside[1], BOTH, link(source, target))
        mine -= 1
        if mine == 0:
            break
        here = early if mine == pairs - 2 else (high, low, both)
        late, base = turn(
            functools.partial(rim_kernel, mine, sides),
            (next_in, here[2], *here[:2]),
            (late,),
            extra=[shape((cols, sites), f32)],
        )
        if jumps and mine == jump:
            late, lower, to_next, to_own, to_last = turn(
                functools.partial(jump_kernel, mine),
                (own_in, base, high, low, own_rows, *ship),
                (late, lower),
                parts_scratch,
                parts + parts[:1],
            )
        else:
            late, lower, *near = turn(
                functools.partial(chain_kernel, mine),
                (own_in, base, *here[:2]),
                (late, lower),
                extra=[shape((cols, halo), f32)] if sides == 1 and mine == pairs - 2 else [],
                flops=50 * 10**9 if jumps and mine == pairs - 3 else 0,
            )
    given = (first_in, own_in, next_in, beside_next, beside_own) if jumps else (own_in, next_in)
    late, upper = turn(
        functools.partial(upper_kernel, sides, pairs - 1), (*given, far, far_high, far_low), (late, upper)
    )
    returned = lax.ppermute(upper, BOTH, link(even, odd))
    lower = pl.pallas_call(
        functools.partial(last_kernel, jumps),
        out_shape=shape(lower.shape, f32),
        in_specs=[VMEM] * 5,
        out_specs=VMEM,
        input_output_aliases={4: 0},
        compiler_params=PARAMS,
        cost_estimate=pl.CostEstimate(flops=12 * cols * tall * length, bytes_accessed=8 * tall * length, transcendentals=0),
    )(both, high, low, late, lower)
    return jnp.where(device % 2 == 0, lower, returned)[None]


def solution(mesh):
    placed = (
        P("tm", None, "row"),
        P("tm", "row", None, None),
        P("tm", "row", None, None),
        P("tm", "row", None),
    )
    return jax.shard_map(
        local, mesh=mesh, in_specs=placed, out_specs=P("tm", None, "row"), check_vma=False
    )
```
